32 devices in a mesh: seq: 16 (over z, y, core), mp: 2 (over x).
Axes of the slice: x: 2, y: 2, z: 4, core: 2. Of those that a mesh axis runs over, the one named last changes fastest.
Arguments:
- queries: bfloat16 [4096, 8, 64], P('seq', 'mp'), may hold values from -6 to 6
- key_value: bfloat16 [4096, 8, 128], P('seq', 'mp'), may hold values from -6 to 6
- tile_fill: int32 [32], P('seq'), may hold values from 0 to 128, as said below
- out_weight: bfloat16 [8, 64, 768], P('mp'), may hold values from -0.75 to 0.75
- grad_output: bfloat16 [4096, 768], P('seq'), may hold values from -6 to 6
Outputs:
- attention_out: bfloat16 [4096, 768], P('seq')
- query_grad: float32 [4096, 8, 64], P('seq', 'mp')
- key_value_grad: float32 [4096, 8, 128], P('seq', 'mp')
- out_weight_grad: float32 [8, 64, 768], P('mp')
The draws below stay inside these ranges and needn't reach their ends.
Inputs may be any that keep to these rules, and one draw needn't show every extreme that they name: `tile_fill`: tile 0 is full, and the first tile of every block of 256 slots holds at least one active voxel.
All inputs are finite; a program needn't handle non-finite values.
Results may differ from the reference program's by a relative error of at most 0.03.
Values may be sent and summed in bfloat16 or wider, within the bound.
No kernel may reach another device: no remote copies, remote signals or barrier semaphores. Data moves between devices by JAX's collectives and lax.ppermute only.
A program may use at most 64 MiB of HBM per device.

```python
import jax
import jax.numpy as jnp
from jax import lax

D = 768
HEADS = 8
DH = 64
TILE = 128
TOK_DEV = 256
TOKENS = 4096


def rough_field(key, shape):
    return jnp.clip(jax.random.normal(key, shape, jnp.float32) * 1.58, -6.0, 6.0)


def draw_queries(key, part):
    values = rough_field(jax.random.fold_in(key, 1), (TOKENS, HEADS, DH))
    return values.astype(jnp.bfloat16)


def draw_key_value(key, part):
    values = rough_field(jax.random.fold_in(key, 2), (TOKENS, HEADS, 2 * DH))
    return values.astype(jnp.bfloat16)


def draw_tile_fill(key, part):
    tiles = TOKENS // TILE
    per_device = TOK_DEV // TILE
    devices = TOKENS // TOK_DEV
    level_key, fill_key, empty_key = jax.random.split(jax.random.fold_in(key, 11), 3)
    levels = jax.random.randint(level_key, (devices,), 1, 5)
    tile_index = jnp.arange(tiles, dtype=jnp.int32)
    tile_level = levels[tile_index // per_device]
    uniform_fill = jax.random.randint(fill_key, (tiles,), 0, TILE)
    empty_draw = jax.random.randint(empty_key, (tiles,), 0, 8)
    filled = TILE - uniform_fill * (5 - tile_level) // 8
    first_tile = tile_index % per_device == 0
    empty_tile = jnp.logical_and(empty_draw >= tile_level + 5, jnp.logical_not(first_tile))
    filled = jnp.where(empty_tile, 0, filled)
    filled = filled.at[0].set(TILE)
    return filled.astype(jnp.int32)


def steps_of(stream_key, shape, cuts, least, largest):
    factor_of, own = 1.0, jax.random.fold_in(stream_key, 6)
    for axis_at, shards_of in cuts:
        draws = jnp.exp(jax.random.uniform(jax.random.fold_in(own, axis_at), (shards_of,), jnp.float32, least / len(cuts), largest / len(cuts)))
        factor_of = factor_of * jnp.repeat(draws, shape[axis_at] // shards_of).reshape([-1 if axis == axis_at else 1 for axis in range(len(shape))])
    return factor_of


def gaussian(stream_key, extent, deviation, reach, cuts=(), kind=jnp.bfloat16):
    level = steps_of(stream_key, extent, cuts, -0.22, 0.18) if cuts else 1.0
    result = jax.random.normal(stream_key, extent, jnp.float32) * deviation * level
    return jnp.minimum(jnp.maximum(result, -reach), reach).astype(kind)


def setup_inputs(seed: int = 0) -> dict:
    splits = jax.random.split(jax.random.key(seed), 6)
    return {
        "queries": draw_queries(jax.random.fold_in(splits[5], 71), 0),
        "key_value": draw_key_value(jax.random.fold_in(splits[5], 71), 0),
        "tile_fill": draw_tile_fill(jax.random.fold_in(splits[5], 71), 0),
        "out_weight": gaussian(splits[3], (HEADS, DH, D), DH ** -0.5, 0.75, ((0, 2),)),
        "grad_output": gaussian(splits[4], (TOKENS, D), 1.0, 6.0, ((0, 16),)),
    }


def live_slots(tile_fill):
    within = lax.iota(jnp.int32, TILE)
    return (within[None, :] < tile_fill[:, None]).reshape(-1)


def reference(queries, key_value, tile_fill, out_weight, grad_output):
    live_mask = live_slots(tile_fill)
    score_scale = DH ** -0.5
    number = TOKENS // TOK_DEV
    q_heads = jnp.transpose(queries, (1, 0, 2))
    k_heads = jnp.transpose(key_value[:, :, :DH], (1, 0, 2))
    v_heads = jnp.transpose(key_value[:, :, DH:], (1, 0, 2))

    def forward_head(operands):
        q_one, k_one, v_one = operands

        def forward_block(q_block):
            scores = jnp.dot(q_block, k_one.T, preferred_element_type=jnp.float32) * score_scale
            masked = jnp.where(live_mask[None, :], scores, -jnp.inf)
            row_peak = jnp.max(masked, axis=1)
            log_total = row_peak + jnp.log(jnp.sum(jnp.exp(masked - row_peak[:, None]), axis=1))
            weights = jnp.where(live_mask[None, :], jnp.exp(scores - log_total[:, None]), 0.0).astype(jnp.bfloat16)
            attended = jnp.dot(weights, v_one, preferred_element_type=jnp.float32).astype(jnp.bfloat16)
            return attended, log_total

        attended, log_total = lax.map(forward_block, q_one.reshape(number, TOK_DEV, DH))
        return attended.reshape(TOKENS, DH), log_total.reshape(TOKENS)

    attended, log_total = lax.map(forward_head, (q_heads, k_heads, v_heads))
    live_float = live_mask.astype(jnp.float32)
    projected = jnp.einsum("hqd,hde->qe", attended.astype(jnp.float32), out_weight.astype(jnp.float32))
    attention_out = (projected * live_float[:, None]).astype(jnp.bfloat16)
    grad_mixed = grad_output * live_mask[:, None].astype(jnp.bfloat16)
    grad_attn = jnp.einsum("qe,hde->hqd", grad_mixed.astype(jnp.float32), out_weight.astype(jnp.float32)).astype(jnp.bfloat16)
    out_weight_grad = jnp.einsum("hqd,qe->hde", attended.astype(jnp.float32), grad_mixed.astype(jnp.float32))
    inner_sum = jnp.sum(grad_attn.astype(jnp.float32) * attended.astype(jnp.float32), axis=2)

    def backward_head(operands):
        q_one, k_one, v_one, log_one, grad_one, inner_one = operands

        def backward_block(carried, pieces):
            grad_keys, grad_values = carried
            q_block, log_block, grad_block, inner_block = pieces
            scores = jnp.dot(q_block, k_one.T, preferred_element_type=jnp.float32) * score_scale
            prob_rows = jnp.where(live_mask[None, :], jnp.exp(scores - log_block[:, None]), 0.0)
            grad_probs = jnp.dot(grad_block, v_one.T, preferred_element_type=jnp.float32)
            grad_scores = (prob_rows * (grad_probs - inner_block[:, None])).astype(jnp.bfloat16)
            grad_query = jnp.dot(grad_scores, k_one, preferred_element_type=jnp.float32) * score_scale
            grad_keys = grad_keys + jnp.dot(grad_scores.T, q_block, preferred_element_type=jnp.float32) * score_scale
            grad_values = grad_values + jnp.dot(prob_rows.astype(jnp.bfloat16).T, grad_block, preferred_element_type=jnp.float32)
            return (grad_keys, grad_values), grad_query

        start_zero = jnp.zeros((TOKENS, DH), jnp.float32)
        blocked = (q_one.reshape(number, TOK_DEV, DH), log_one.reshape(number, TOK_DEV),
                   grad_one.reshape(number, TOK_DEV, DH), inner_one.reshape(number, TOK_DEV))
        (grad_keys, grad_values), grad_query = lax.scan(backward_block, (start_zero, start_zero), blocked)
        return grad_query.reshape(TOKENS, DH), grad_keys, grad_values

    grad_query, grad_keys, grad_values = lax.map(backward_head, (q_heads, k_heads, v_heads, log_total, grad_attn, inner_sum))
    query_grad = jnp.transpose(grad_query, (1, 0, 2))
    key_value_grad = jnp.concatenate([jnp.transpose(grad_keys, (1, 0, 2)), jnp.transpose(grad_values, (1, 0, 2))], axis=2)
    return attention_out, query_grad, key_value_grad, out_weight_grad
```

```python
import functools

import jax
import jax.numpy as jnp
from jax import lax
from jax.experimental import pallas as pl
from jax.experimental.pallas import tpu as pltpu
from jax.sharding import PartitionSpec as P

TILE = 128
DEAD = 1024.0
BIAS = -1e30
F32 = jnp.float32
BF16 = jnp.bfloat16
VMEM = pl.BlockSpec(memory_space=pltpu.VMEM)
SMEM = pl.BlockSpec(memory_space=pltpu.SMEM)
LIMIT = 48 * 1024 * 1024


def dot(a, b):
    return lax.dot_general(a, b, (((1,), (0,)), ((), ())), preferred_element_type=F32)


def dot_nt(a, b):
    return lax.dot_general(a, b, (((1,), (1,)), ((), ())), preferred_element_type=F32)


def call(kernel, outs, scratch=(), n_in=1, smem_first=False, flops=0, moved=0):
    specs = [VMEM] * n_in
    if smem_first:
        specs[0] = SMEM
    return pl.pallas_call(
        kernel,
        out_shape=[jax.ShapeDtypeStruct(shape, kind) for shape, kind in outs],
        in_specs=specs,
        out_specs=[VMEM] * len(outs),
        scratch_shapes=list(scratch),
        compiler_params=pltpu.CompilerParams(vmem_limit_bytes=LIMIT),
        cost_estimate=pl.CostEstimate(flops=flops, bytes_accessed=moved, transcendentals=0),
    )


def live_column(fill_ref, rows):
    parts = []
    within = lax.broadcasted_iota(jnp.int32, (TILE, 1), 0)
    for tile in range(rows // TILE):
        parts.append(jnp.where(within < fill_ref[tile], 1.0, 0.0))
    return jnp.concatenate(parts, axis=0) if len(parts) > 1 else parts[0]


def pack_kernel(heads, rows, dim, a_of, fill_ref, q_ref, kv_ref, w_ref, go_ref, *rest):
    kv_out, qg_out = rest[:heads], rest[heads : 2 * heads]
    kv_all, qg_all = rest[2 * heads :]
    live = live_column(fill_ref, rows)
    mixed = jnp.where(live > 0, go_ref[...].astype(F32), 0.0).astype(BF16)
    lane = lax.broadcasted_iota(jnp.int32, (rows, 2 * dim), 1)
    mark = jnp.where(lane == 0, DEAD, 0.0)
    for head in range(heads):
        grad = dot_nt(w_ref[head], mixed).astype(BF16)
        scaled = (q_ref[head].astype(F32) * dim**-0.5).astype(BF16)
        qg_all[head] = jnp.concatenate([scaled, grad], axis=0)
        pair = kv_ref[:, head, :].astype(F32)
        kv_all[head] = jnp.where(live > 0, pair, mark).astype(BF16)
    me = a_of()
    for slot in range(heads):
        kv_out[slot][...] = kv_all[me ^ slot]
        qg_out[slot][...] = qg_all[me ^ slot]


def forward_kernel(slots, columns, rows, dim, *refs):
    blocks, refs = refs[:columns], refs[columns:]
    qg_in, refs = refs[:slots], refs[slots:]
    att_out, refs = refs[:slots], refs[slots:]
    log_ref, k_ref, v_ref, q_aug, g_aug, vt_ref = refs
    block = slots * rows
    lane = lax.broadcasted_iota(jnp.int32, (block, 2 * dim), 1)
    for column in range(columns):
        pair = blocks[column][...].astype(F32)
        dead = pair[:, 0:1] >= DEAD
        here = pl.ds(column * block, block)
        keys = jnp.where(lane < dim, pair, 0.0)
        k_ref[here, :] = jnp.where(dead, jnp.where(lane == dim, BIAS, 0.0), keys).astype(BF16)
        values = jnp.where(lane >= dim, pair, jnp.where(lane <= 1, 1.0, 0.0))
        values = jnp.where(dead, 0.0, values)
        v_ref[here, :] = values.astype(BF16)
        vt_ref[:, here] = values.T.astype(BF16)
    row = lax.broadcasted_iota(jnp.int32, (2 * dim, rows), 0)
    for slot in range(slots):
        mixed = qg_in[slot][...].astype(F32)
        queries = jnp.where(row < dim, mixed, jnp.where(row == dim, 1.0, 0.0)).astype(BF16)
        q_aug[slot] = queries
        peak = jnp.full((1, rows), BIAS, F32)
        total = jnp.zeros((2 * dim, rows), F32)
        for column in range(columns):
            here = pl.ds(column * block, block)
            scores = dot(k_ref[here, :], queries)
            new_peak = jnp.maximum(peak, jnp.max(scores, axis=0, keepdims=True))
            exps = jnp.exp(scores - new_peak).astype(BF16)
            total = total * jnp.exp(peak - new_peak) + dot(vt_ref[:, here], exps)
            peak = new_peak
        weight = total[0:1, :]
        log_ref[slot] = peak + jnp.log(weight)
        attended = (total / weight).astype(BF16)
        att_out[slot][...] = attended[dim:, :]
        terms = jnp.where(row >= dim, mixed * attended.astype(F32), 0.0)
        inner = jnp.sum(terms, axis=0, keepdims=True)
        high = inner.astype(BF16).astype(F32)
        low = inner - high
        filled = jnp.where(row == 0, -high, jnp.where(row == 1, -low, 0.0))
        g_aug[slot] = jnp.where(row >= dim, mixed, filled).astype(BF16)


def backward_kernel(slots, columns, rows, dim, key_block, log_ref, k_ref, v_ref, q_aug, g_aug, *refs):
    dkv_out, dq_out, (kt_ref, dq_acc) = refs[:columns], refs[columns : columns + slots], refs[columns + slots :]
    block = slots * rows
    for column in range(columns):
        here = pl.ds(column * block, block)
        kt_ref[:, here] = k_ref[here, :].astype(F32).T.astype(BF16)
    lane = lax.broadcasted_iota(jnp.int32, (key_block, 2 * dim), 1)
    dq_acc[...] = jnp.zeros_like(dq_acc)
    for column in range(columns):
        for part in range(block // key_block):
            start = column * block + part * key_block
            here = pl.ds(start, key_block)
            keys, values = k_ref[here, :], v_ref[here, :]
            grad_k = jnp.zeros((key_block, 2 * dim), F32)
            grad_v = jnp.zeros((key_block, 2 * dim), F32)
            for slot in range(slots):
                probs = jnp.exp(dot(keys, q_aug[slot]) - log_ref[slot])
                grads = (probs * dot(values, g_aug[slot])).astype(BF16)
                grad_v = grad_v + dot_nt(probs.astype(BF16), g_aug[slot])
                grad_k = grad_k + dot_nt(grads, q_aug[slot])
                dq_acc[slot] += dot(kt_ref[:, here], grads)
            dkv_out[column][pl.ds(part * key_block, key_block), :] = jnp.where(lane < dim, grad_k, grad_v).astype(BF16)
    for slot in range(slots):
        dq_out[slot][...] = (dq_acc[slot, 0:dim, :] * dim**-0.5).astype(BF16)


def project_kernel(slots, rows, dim, a_of, fill_ref, w_ref, go_ref, *refs):
    att, (terms_ref, wt_ref) = refs[:slots], refs[slots:]
    live = live_column(fill_ref, rows)
    mixed = jnp.where(live > 0, go_ref[...].astype(F32), 0.0).astype(BF16)
    me = a_of()
    total = None
    for slot in range(slots):
        head = me ^ slot
        wt_ref[head] = dot(att[slot][...], mixed).astype(BF16)
        term = dot(att[slot][...].astype(F32).T.astype(BF16), w_ref[head])
        total = term if total is None else total + term
    terms_ref[...] = (total * live).astype(BF16)


def unpack_kernel(slots, rows, dim, a_of, *refs):
    dkv, dq = refs[:slots], refs[slots : 2 * slots]
    kv_out, q_out, kv_all = refs[2 * slots :]
    me = a_of()
    for slot in range(slots):
        q_out[me ^ slot] = dq[slot][...].astype(F32)
        kv_all[me ^ slot] = dkv[slot][...].astype(F32)
    for head in range(slots):
        kv_out[:, head, :] = kv_all[head]


def split_kernel(columns, b_of, wt_ref, *outs):
    me = b_of()
    for column in range(columns):
        outs[column][...] = wt_ref[me ^ column]


def sum_split_kernel(columns, slots, piece, a_of, *refs):
    parts, outs = refs[:columns], refs[columns : columns + slots]
    (held,) = refs[columns + slots :]
    total = parts[0][...].astype(F32)
    for part in parts[1:]:
        total = total + part[...].astype(F32)
    held[...] = total
    me = a_of()
    for slot in range(slots):
        start = pl.multiple_of((me ^ slot) * piece, piece)
        outs[slot][...] = held[pl.ds(start, piece), :].astype(BF16)


def sum_kernel(*refs):
    total = refs[0][...].astype(F32)
    for part in refs[1:-1]:
        total = total + part[...].astype(F32)
    refs[-1][...] = total.astype(refs[-1].dtype)


def place_kernel(columns, slots, piece, a_of, b_of, *refs):
    parts, (out_ref,) = refs[:columns], refs[columns:]
    me_a, me_b = a_of(), b_of()
    for column in range(columns):
        for slot in range(slots):
            start = pl.multiple_of((me_a ^ slot) * piece, piece)
            out_ref[me_b ^ column, pl.ds(start, piece), :] = parts[column][pl.ds(slot * piece, piece), :].astype(F32)


def shards(seq, mp, queries, key_value, tile_fill, out_weight, grad_output):
    rows, heads, dim = queries.shape
    width = grad_output.shape[1]
    slots = heads
    columns = seq // slots
    assert slots * columns == seq and columns & (columns - 1) == 0 and slots & (slots - 1) == 0
    a_of = lambda: lax.axis_index("seq") // columns
    b_of = lambda: lax.axis_index("seq") % columns

    def swap(array, mask, axis="seq", size=seq):
        return lax.ppermute(array, axis, [(i, i ^ mask) for i in range(size)])

    qt = jnp.transpose(queries, (1, 2, 0))
    packed = call(
        functools.partial(pack_kernel, heads, rows, dim, a_of),
        [((rows, 2 * dim), BF16)] * slots + [((2 * dim, rows), BF16)] * slots,
        [pltpu.VMEM((heads, rows, 2 * dim), BF16), pltpu.VMEM((heads, 2 * dim, rows), BF16)],
        n_in=5, smem_first=True,
        flops=2 * rows * heads * dim * width, moved=4 * rows * width,
    )(tile_fill, qt, key_value, out_weight, grad_output)
    kv_send, qg_send = packed[:slots], packed[slots:]
    kv_mine = [kv_send[0]] + [swap(kv_send[s], s * columns) for s in range(1, slots)]
    qg_mine = [qg_send[0]] + [swap(qg_send[s], s * columns) for s in range(1, slots)]
    own = jnp.concatenate(kv_mine, axis=0) if slots > 1 else kv_mine[0]

    blocks = {0: own}
    bit = columns // 2
    while bit:
        for r in sorted(blocks):
            blocks[r ^ bit] = swap(blocks[r], bit)
        bit //= 2

    keys = seq * rows
    block = slots * rows
    mults = slots * rows * keys * 2 * dim
    forward = call(
        functools.partial(forward_kernel, slots, columns, rows, dim),
        [((dim, rows), BF16)] * slots
        + [((slots, 1, rows), F32), ((keys, 2 * dim), BF16), ((keys, 2 * dim), BF16),
           ((slots, 2 * dim, rows), BF16), ((slots, 2 * dim, rows), BF16)],
        [pltpu.VMEM((2 * dim, keys), BF16)],
        n_in=columns + slots, flops=4 * mults, moved=4 * keys * 2 * dim,
    )(*[blocks[r] for r in range(columns)], *qg_mine)
    att_send, saved = forward[:slots], forward[slots:]
    att_mine = [att_send[0]] + [swap(att_send[s], s * columns) for s in range(1, slots)]

    terms, weight_terms = call(
        functools.partial(project_kernel, slots, rows, dim, a_of),
        [((rows, width), BF16), ((heads, dim, width), BF16)],
        n_in=3 + slots, smem_first=True, flops=4 * rows * heads * dim * width, moved=4 * rows * width,
    )(tile_fill, out_weight, grad_output, *att_mine)
    bit = 1
    while bit < mp:
        terms = call(sum_kernel, [((rows, width), BF16)], n_in=2, moved=6 * rows * width)(
            terms, swap(terms, bit, "mp", mp))[0]
        bit *= 2

    if columns == heads:
        piece = dim // slots
        split = call(functools.partial(split_kernel, columns, b_of), [((dim, width), BF16)] * columns)(weight_terms)
        got = [split[0]] + [swap(split[r], r) for r in range(1, columns)]
        split = call(
            functools.partial(sum_split_kernel, columns, slots, piece, a_of),
            [((piece, width), BF16)] * slots, [pltpu.VMEM((dim, width), F32)], n_in=columns)(*got)
        got = [split[0]] + [swap(split[s], s * columns) for s in range(1, slots)]
        summed = call(sum_kernel, [((piece, width), BF16)], n_in=slots)(*got)[0]
        quarter = jnp.concatenate([summed] + [swap(summed, s * columns) for s in range(1, slots)], axis=0)
        whole = [quarter] + [swap(quarter, r) for r in range(1, columns)]
        weight_grad = call(
            functools.partial(place_kernel, columns, slots, piece, a_of, b_of),
            [((heads, dim, width), F32)], n_in=columns)(*whole)[0]
    else:
        weight_grad = lax.psum(weight_terms.astype(F32), "seq")

    key_block = min(block, 512)
    backward = call(
        functools.partial(backward_kernel, slots, columns, rows, dim, key_block),
        [((block, 2 * dim), BF16)] * columns + [((dim, rows), BF16)] * slots,
        [pltpu.VMEM((2 * dim, keys), BF16), pltpu.VMEM((slots, 2 * dim, rows), F32)],
        n_in=5, flops=10 * mults, moved=4 * keys * 2 * dim,
    )(*saved)
    dkv, dq = dict(enumerate(backward[:columns])), backward[columns:]
    dq_mine = [dq[0]] + [swap(dq[s], s * columns) for s in range(1, slots)]
    bit = 1
    while bit < columns:
        kept = sorted(r for r in dkv if not r & bit)
        dkv = {
            r: call(sum_kernel, [((block, 2 * dim), BF16)], n_in=2, moved=12 * block * dim)(
                dkv[r], swap(dkv[r ^ bit], bit))[0]
            for r in kept
        }
        bit *= 2
    parts = [dkv[0][s * rows : (s + 1) * rows] for s in range(slots)]
    dkv_mine = [parts[0]] + [swap(parts[s], s * columns) for s in range(1, slots)]
    key_value_grad, query_grad = call(
        functools.partial(unpack_kernel, slots, rows, dim, a_of),
        [((rows, heads, 2 * dim), F32), ((heads, dim, rows), F32)],
        [pltpu.VMEM((heads, rows, 2 * dim), F32)],
        n_in=2 * slots, moved=8 * rows * heads * dim,
    )(*dkv_mine, *dq_mine)
    return terms, jnp.transpose(query_grad, (2, 0, 1)), key_value_grad, weight_grad


def solution(mesh):
    return jax.shard_map(
        functools.partial(shards, mesh.shape["seq"], mesh.shape["mp"]),
        mesh=mesh,
        in_specs=(
            P("seq", "mp", None),
            P("seq", "mp", None),
            P("seq"),
            P("mp", None, None),
            P("seq", None),
        ),
        out_specs=(P("seq", None), P("seq", "mp", None), P("seq", "mp", None), P("mp", None, None)),
        check_vma=False,
    )
```

```python
import functools

import jax
import jax.numpy as jnp
from jax import lax
from jax.experimental import pallas as pl
from jax.experimental.pallas import tpu as pltpu
from jax.sharding import PartitionSpec as P

TILE = 128
DEAD = 1024.0
BIAS = -1e30
F32 = jnp.float32
BF16 = jnp.bfloat16
VMEM = pl.BlockSpec(memory_space=pltpu.VMEM)
SMEM = pl.BlockSpec(memory_space=pltpu.SMEM)
LIMIT = 48 * 1024 * 1024


def dot(a, b):
    return lax.dot_general(a, b, (((1,), (0,)), ((), ())), preferred_element_type=F32)


def dot_nt(a, b):
    return lax.dot_general(a, b, (((1,), (1,)), ((), ())), preferred_element_type=F32)


def call(kernel, outs, scratch=(), n_in=1, smem_first=False, flops=0, moved=0):
    specs = [VMEM] * n_in
    if smem_first:
        specs[0] = SMEM
    return pl.pallas_call(
        kernel,
        out_shape=[jax.ShapeDtypeStruct(shape, kind) for shape, kind in outs],
        in_specs=specs,
        out_specs=[VMEM] * len(outs),
        scratch_shapes=list(scratch),
        compiler_params=pltpu.CompilerParams(vmem_limit_bytes=LIMIT),
        cost_estimate=pl.CostEstimate(flops=flops, bytes_accessed=moved, transcendentals=0),
    )


def live_column(fill_ref, rows):
    parts = []
    within = lax.broadcasted_iota(jnp.int32, (TILE, 1), 0)
    for tile in range(rows // TILE):
        parts.append(jnp.where(within < fill_ref[tile], 1.0, 0.0))
    return jnp.concatenate(parts, axis=0) if len(parts) > 1 else parts[0]


def pack_kernel(heads, rows, dim, fill_ref, q_ref, kv_ref, w_ref, go_ref, out_ref):
    live = live_column(fill_ref, rows)
    mixed = jnp.where(live > 0, go_ref[...].astype(F32), 0.0).astype(BF16)
    lane = lax.broadcasted_iota(jnp.int32, (rows, 2 * dim), 1)
    mark = jnp.where(lane == 0, DEAD, 0.0)
    for head in range(heads):
        grad = dot_nt(w_ref[head], mixed).astype(BF16)
        scaled = (q_ref[head].astype(F32) * dim**-0.5).astype(BF16)
        pair = kv_ref[:, head, :].astype(F32)
        out_ref[head, 0:rows, :] = jnp.where(live > 0, pair, mark).astype(BF16)
        both = jnp.concatenate([scaled, grad], axis=0)
        for part in range(rows // (2 * dim)):
            across = slice(part * 2 * dim, (part + 1) * 2 * dim)
            out_ref[head, rows + part * 2 * dim : rows + (part + 1) * 2 * dim, :] = both[:, across]


def forward_kernel(slots, columns, rows, dim, *refs):
    blocks, refs = refs[:columns], refs[columns:]
    got_ref, att_out, log_ref, k_ref, v_ref, q_aug, g_aug, vt_ref = refs
    block = slots * rows
    lane = lax.broadcasted_iota(jnp.int32, (block, 2 * dim), 1)
    for column in range(columns):
        pair = blocks[column][...].astype(F32)
        dead = pair[:, 0:1] >= DEAD
        here = pl.ds(column * block, block)
        keys = jnp.where(lane < dim, pair, 0.0)
        k_ref[here, :] = jnp.where(dead, jnp.where(lane == dim, BIAS, 0.0), keys).astype(BF16)
        values = jnp.where(lane >= dim, pair, jnp.where(lane <= 1, 1.0, 0.0))
        values = jnp.where(dead, 0.0, values)
        v_ref[here, :] = values.astype(BF16)
        vt_ref[:, here] = values.T.astype(BF16)
    row = lax.broadcasted_iota(jnp.int32, (2 * dim, rows), 0)
    for slot in range(slots):
        pieces = [
            got_ref[slot, rows + part * 2 * dim : rows + (part + 1) * 2 * dim, :]
            for part in range(rows // (2 * dim))
        ]
        mixed = jnp.concatenate(pieces, axis=1).astype(F32)
        queries = jnp.where(row < dim, mixed, jnp.where(row == dim, 1.0, 0.0)).astype(BF16)
        q_aug[slot] = queries
        peak = jnp.full((1, rows), BIAS, F32)
        total = jnp.zeros((2 * dim, rows), F32)
        for column in range(columns):
            here = pl.ds(column * block, block)
            scores = dot(k_ref[here, :], queries)
            new_peak = jnp.maximum(peak, jnp.max(scores, axis=0, keepdims=True))
            exps = jnp.exp(scores - new_peak).astype(BF16)
            total = total * jnp.exp(peak - new_peak) + dot(vt_ref[:, here], exps)
            peak = new_peak
        weight = total[0:1, :]
        log_ref[slot] = peak + jnp.log(weight)
        attended = (total / weight).astype(BF16)
        att_out[slot] = attended[dim:, :]
        terms = jnp.where(row >= dim, mixed * attended.astype(F32), 0.0)
        inner = jnp.sum(terms, axis=0, keepdims=True)
        high = inner.astype(BF16).astype(F32)
        low = inner - high
        filled = jnp.where(row == 0, -high, jnp.where(row == 1, -low, 0.0))
        g_aug[slot] = jnp.where(row >= dim, mixed, filled).astype(BF16)


def backward_kernel(slots, columns, rows, dim, key_block, log_ref, k_ref, v_ref, q_aug, g_aug, *refs):
    dkv_out, dq_out, kt_ref, dq_acc = refs[:columns], *refs[columns:]
    block = slots * rows
    for column in range(columns):
        here = pl.ds(column * block, block)
        kt_ref[:, here] = k_ref[here, :].astype(F32).T.astype(BF16)
    lane = lax.broadcasted_iota(jnp.int32, (key_block, 2 * dim), 1)
    dq_acc[...] = jnp.zeros_like(dq_acc)
    for column in range(columns):
        for part in range(block // key_block):
            start = column * block + part * key_block
            here = pl.ds(start, key_block)
            keys, values = k_ref[here, :], v_ref[here, :]
            grad_k = jnp.zeros((key_block, 2 * dim), F32)
            grad_v = jnp.zeros((key_block, 2 * dim), F32)
            for slot in range(slots):
                probs = jnp.exp(dot(keys, q_aug[slot]) - log_ref[slot])
                grads = (probs * dot(values, g_aug[slot])).astype(BF16)
                grad_v = grad_v + dot_nt(probs.astype(BF16), g_aug[slot])
                grad_k = grad_k + dot_nt(grads, q_aug[slot])
                dq_acc[slot] += dot(kt_ref[:, here], grads)
            dkv_out[column][pl.ds(part * key_block, key_block), :] = jnp.where(lane < dim, grad_k, grad_v).astype(BF16)
    for slot in range(slots):
        grad = (dq_acc[slot, 0:dim, :] * dim**-0.5).astype(BF16)
        for part in range(rows // (2 * dim)):
            dq_out[slot, part * dim : (part + 1) * dim, :] = grad[:, part * 2 * dim : (part + 1) * 2 * dim]


def project_kernel(heads, rows, dim, fill_ref, w_ref, go_ref, att_ref, terms_ref, wt_ref):
    live = live_column(fill_ref, rows)
    mixed = jnp.where(live > 0, go_ref[...].astype(F32), 0.0).astype(BF16)
    total = None
    for head in range(heads):
        wt_ref[head] = dot(att_ref[head], mixed).astype(BF16)
        term = dot(att_ref[head].astype(F32).T.astype(BF16), w_ref[head])
        total = term if total is None else total + term
    terms_ref[...] = (total * live).astype(BF16)


def unpack_kernel(heads, rows, dim, got_ref, kv_out, q_out):
    for head in range(heads):
        kv_out[:, head, :] = got_ref[head, 0:rows, :].astype(F32)
        for part in range(rows // (2 * dim)):
            start = rows + part * dim
            q_out[head, :, part * 2 * dim : (part + 1) * 2 * dim] = got_ref[head, start : start + dim, :].astype(F32)


def add_send_kernel(slots, rows, kept_ref, came_ref, dq_ref, out_ref):
    for slot in range(slots):
        here = pl.ds(slot * rows, rows)
        total = kept_ref[here, :].astype(F32) + came_ref[here, :].astype(F32)
        out_ref[slot, 0:rows, :] = total.astype(BF16)
        out_ref[slot, rows:, :] = dq_ref[slot]


def halve_kernel(parts, bit, me_of, wt_ref, kept_ref, sent_ref):
    me = me_of()
    for relative in range(parts // 2):
        low = relative % bit + relative // bit * 2 * bit
        kept_ref[relative] = wt_ref[me ^ low]
        sent_ref[relative] = wt_ref[me ^ low ^ bit]


def sum_kernel(*refs):
    total = refs[0][...].astype(F32)
    for part in refs[1:-1]:
        total = total + part[...].astype(F32)
    refs[-1][...] = total.astype(refs[-1].dtype)


def sum_slots_kernel(slots, got_ref, out_ref):
    total = got_ref[0].astype(F32)
    for slot in range(1, slots):
        total = total + got_ref[slot].astype(F32)
    for slot in range(slots):
        out_ref[slot] = total.astype(BF16)


def place_kernel(columns, slots, piece, b_of, *refs):
    parts, (out_ref,) = refs[:columns], refs[columns:]
    me = b_of()
    for column in range(columns):
        for slot in range(slots):
            out_ref[me ^ column, slot * piece : (slot + 1) * piece, :] = parts[column][slot].astype(F32)


def shards(seq, mp, queries, key_value, tile_fill, out_weight, grad_output):
    rows, heads, dim = queries.shape
    width = grad_output.shape[1]
    slots = heads
    columns = seq // slots
    assert slots * columns == seq and columns & (columns - 1) == 0
    b_of = lambda: lax.axis_index("seq") % columns
    groups = [[a * columns + b for a in range(slots)] for b in range(columns)]

    def swap(array, mask, axis="seq", size=seq):
        return lax.ppermute(array, axis, [(i, i ^ mask) for i in range(size)])

    def exchange(array):
        if slots == 1:
            return array
        return lax.all_to_all(array, "seq", 0, 0, axis_index_groups=groups, tiled=True)

    block = slots * rows
    wide = 2 * dim
    qt = jnp.transpose(queries, (1, 2, 0))
    packed = call(
        functools.partial(pack_kernel, heads, rows, dim),
        [((heads, 2 * rows, wide), BF16)],
        n_in=5, smem_first=True,
        flops=2 * rows * heads * dim * width, moved=4 * rows * width,
    )(tile_fill, qt, key_value, out_weight, grad_output)[0]
    got = exchange(packed)
    own = got[:, :rows].reshape(block, wide)

    blocks = {0: own}
    bit = columns // 2
    while bit:
        for r in sorted(blocks):
            blocks[r ^ bit] = swap(blocks[r], bit)
        bit //= 2

    keys = seq * rows
    mults = block * keys * wide
    forward = call(
        functools.partial(forward_kernel, slots, columns, rows, dim),
        [((slots, dim, rows), BF16), ((slots, 1, rows), F32), ((keys, wide), BF16), ((keys, wide), BF16),
         ((slots, wide, rows), BF16), ((slots, wide, rows), BF16)],
        [pltpu.VMEM((wide, keys), BF16)],
        n_in=columns + 1, flops=4 * mults, moved=4 * keys * wide,
    )(*[blocks[r] for r in range(columns)], got)
    attended, saved = exchange(forward[0]), forward[1:]

    terms, weight_terms = call(
        functools.partial(project_kernel, heads, rows, dim),
        [((rows, width), BF16), ((heads, dim, width), BF16)],
        n_in=4, smem_first=True, flops=4 * rows * heads * dim * width, moved=4 * rows * width,
    )(tile_fill, out_weight, grad_output, attended)
    bit = 1
    while bit < mp:
        terms = call(sum_kernel, [((rows, width), BF16)], n_in=2, moved=6 * rows * width)(
            terms, swap(terms, bit, "mp", mp))[0]
        bit *= 2

    if columns == heads == 4:
        piece = dim // slots
        kept, sent = call(
            functools.partial(halve_kernel, columns, 1, b_of), [((columns // 2, dim, width), BF16)] * 2)(weight_terms)
        kept = call(sum_kernel, [((columns // 2, dim, width), BF16)], n_in=2)(kept, swap(sent, 1))[0]
        quarter = call(sum_kernel, [((dim, width), BF16)], n_in=2)(kept[0], swap(kept[1], 2))[0]
        summed = call(functools.partial(sum_slots_kernel, slots), [((slots, piece, width), BF16)])(
            exchange(quarter.reshape(slots, piece, width)))[0]
        mine = exchange(summed)
        across = swap(mine, 2)
        whole = [mine, swap(mine, 1), across, swap(across, 1)]
        weight_grad = call(
            functools.partial(place_kernel, columns, slots, piece, b_of),
            [((heads, dim, width), F32)], n_in=columns)(*whole)[0]
    else:
        weight_grad = lax.psum(weight_terms.astype(F32), "seq")

    key_block = min(block, 512)
    backward = call(
        functools.partial(backward_kernel, slots, columns, rows, dim, key_block),
        [((block, wide), BF16)] * columns + [((slots, rows // 2, wide), BF16)],
        [pltpu.VMEM((wide, keys), BF16), pltpu.VMEM((slots, wide, rows), F32)],
        n_in=5, flops=10 * mults, moved=4 * keys * wide,
    )(*saved)
    dkv, dq = dict(enumerate(backward[:columns])), backward[columns]
    bit = 1
    while 2 * bit < columns:
        kept = sorted(r for r in dkv if not r & bit)
        dkv = {
            r: call(sum_kernel, [((block, wide), BF16)], n_in=2, moved=12 * block * dim)(
                dkv[r], swap(dkv[r ^ bit], bit))[0]
            for r in kept
        }
        bit *= 2
    returned = call(
        functools.partial(add_send_kernel, slots, rows),
        [((slots, rows + rows // 2, wide), BF16)], n_in=3, moved=12 * block * dim,
    )(dkv[0], swap(dkv[bit], bit), dq)[0]
    key_value_grad, query_grad = call(
        functools.partial(unpack_kernel, heads, rows, dim),
        [((rows, heads, wide), F32), ((heads, dim, rows), F32)],
        moved=8 * rows * heads * dim,
    )(exchange(returned))
    return terms, jnp.transpose(query_grad, (2, 0, 1)), key_value_grad, weight_grad


def solution(mesh):
    return jax.shard_map(
        functools.partial(shards, mesh.shape["seq"], mesh.shape["mp"]),
        mesh=mesh,
        in_specs=(
            P("seq", "mp", None),
            P("seq", "mp", None),
            P("seq"),
            P("mp", None, None),
            P("seq", None),
        ),
        out_specs=(P("seq", None), P("seq", "mp", None), P("seq", "mp", None), P("mp", None, None)),
        check_vma=False,
    )
```

```python
import functools

import jax
import jax.numpy as jnp
from jax import lax
from jax.experimental import pallas as pl
from jax.experimental.pallas import tpu as pltpu
from jax.sharding import PartitionSpec as P

TILE = 128
DEAD = 1024.0
BIAS = -1e30
F32 = jnp.float32
BF16 = jnp.bfloat16
VMEM = pl.BlockSpec(memory_space=pltpu.VMEM)
SMEM = pl.BlockSpec(memory_space=pltpu.SMEM)
MIB = 1024 * 1024


def dot(a, b):
    return lax.dot_general(a, b, (((1,), (0,)), ((), ())), preferred_element_type=F32)


def dot_nt(a, b):
    return lax.dot_general(a, b, (((1,), (1,)), ((), ())), preferred_element_type=F32)


def call(kernel, outs, scratch=(), n_in=1, smem_first=False, any_last=False, flops=0, moved=0, limit=16):
    specs = [VMEM] * n_in
    if smem_first:
        specs[0] = SMEM
    if any_last:
        specs[-1] = pl.BlockSpec(memory_space=pl.ANY)
    return pl.pallas_call(
        kernel,
        out_shape=[jax.ShapeDtypeStruct(shape, kind) for shape, kind in outs],
        in_specs=specs,
        out_specs=[VMEM] * len(outs),
        scratch_shapes=list(scratch),
        compiler_params=pltpu.CompilerParams(vmem_limit_bytes=limit * MIB),
        cost_estimate=pl.CostEstimate(flops=flops, bytes_accessed=moved, transcendentals=0),
    )


def live_column(fill_ref, rows):
    parts = []
    within = lax.broadcasted_iota(jnp.int32, (TILE, 1), 0)
    for tile in range(rows // TILE):
        parts.append(jnp.where(within < fill_ref[tile], 1.0, 0.0))
    return jnp.concatenate(parts, axis=0) if len(parts) > 1 else parts[0]


def pack_kv_kernel(heads, rows, dim, a_of, fill_ref, kv_ref, *refs):
    outs, (held,) = refs[:heads], refs[heads:]
    live = live_column(fill_ref, rows)
    lane = lax.broadcasted_iota(jnp.int32, (rows, 2 * dim), 1)
    mark = jnp.where(lane == 0, DEAD, 0.0)
    for head in range(heads):
        held[head] = jnp.where(live > 0, kv_ref[:, head, :].astype(F32), mark).astype(BF16)
    me = a_of()
    for slot in range(heads):
        outs[slot][...] = held[me ^ slot]


def pack_qg_kernel(heads, rows, dim, a_of, fill_ref, q_ref, w_ref, go_ref, *refs):
    outs, (held,) = refs[:heads], refs[heads:]
    live = live_column(fill_ref, rows)
    mixed = jnp.where(live > 0, go_ref[...].astype(F32), 0.0).astype(BF16)
    for head in range(heads):
        held[head, 0:dim, :] = (q_ref[head].astype(F32) * dim**-0.5).astype(BF16)
        held[head, dim:, :] = dot_nt(w_ref[head], mixed).astype(BF16)
    me = a_of()
    for slot in range(heads):
        outs[slot][...] = held[me ^ slot]


def forward_kernel(slots, columns, rows, dim, step, *refs):
    blocks, refs = refs[:columns], refs[columns:]
    qg_in, refs = refs[:slots], refs[slots:]
    att_out, refs = refs[:slots], refs[slots:]
    exp_ref, wide_ref, kt_ref, q_ref, g_ref, vt_ref, score_ref, qa_ref = refs
    block, wide = slots * rows, 2 * dim
    keys = block * columns
    lane = lax.broadcasted_iota(jnp.int32, (step, wide), 1)
    ones = jnp.where(lane <= 2, jnp.where(lane == 0, 0.0, 1.0), 0.0)
    for start in range(0, keys, step):
        column, inside = start // block, start % block
        pair = blocks[column][inside : inside + step, :]
        full = pair.astype(F32)
        wide_ref[start : start + step, 0:wide] = pair
        bias = jnp.where(full[:, 0:1] >= DEAD, BIAS, 0.0)
        wide_ref[start : start + step, wide:] = jnp.where(lane == 0, bias, ones).astype(BF16)
        turned = full.T.astype(BF16)
        kt_ref[:, start : start + step] = turned[:dim, :]
        vt_ref[0:dim, start : start + step] = turned[dim:, :]
        vt_ref[dim:, start : start + step] = jnp.ones((16, step), BF16)
    row = lax.broadcasted_iota(jnp.int32, (wide, rows), 0)
    bias_row = jnp.where(row == 0, 1.0, 0.0).astype(BF16)
    for slot in range(slots):
        here = slice(slot * rows, (slot + 1) * rows)
        queries = qg_in[slot][0:dim, :]
        q_ref[:, here] = queries
        qa_ref[0:dim, here] = queries
        qa_ref[dim:wide, here] = jnp.zeros((dim, rows), BF16)
        qa_ref[wide:, here] = bias_row
    peak = None
    for turn in range(slots + 1):
        here = slice(turn * rows, (turn + 1) * rows)
        past = slice((turn - 1) * rows, turn * rows)
        top = jnp.full((8, rows), BIAS, F32)
        total = jnp.zeros((dim + 16, rows), F32)
        for start in range(0, keys, step):
            part = slice(start, start + step)
            if turn < slots:
                scores = dot(wide_ref[part, :], qa_ref[:, here])
                score_ref[turn % 2, part, :] = scores
                top = jnp.maximum(top, jnp.max(scores.reshape(step // 8, 8, rows), axis=0))
            if turn > 0:
                exps = jnp.exp(score_ref[(turn - 1) % 2, part, :] - peak).astype(BF16)
                exp_ref[part, past] = exps
                total = total + dot(vt_ref[:, part], exps)
        if turn > 0:
            inverse = 1.0 / total[dim : dim + 1, :]
            attended = (total[0:dim, :] * inverse).astype(BF16)
            att_out[turn - 1][...] = attended
            grad = qg_in[turn - 1][dim:, :].astype(F32)
            inner = jnp.sum(grad * attended.astype(F32), axis=0, keepdims=True) * inverse
            high = inner.astype(BF16).astype(F32)
            g_ref[0:dim, past] = jnp.zeros((dim, rows), BF16)
            g_ref[dim:wide, past] = (grad * inverse).astype(BF16)
            g_ref[wide:, past] = jnp.where(row == 1, -high, jnp.where(row == 2, high - inner, 0.0)).astype(BF16)
        peak = jnp.max(top, axis=0, keepdims=True)


def backward_kernel(slots, columns, rows, dim, step, exp_ref, wide_ref, kt_ref, q_ref, g_ref, _, *refs):
    dkv_out, dq_out, (dq_acc,) = refs[:columns], refs[columns : columns + slots], refs[columns + slots :]
    block, wide = slots * rows, 2 * dim
    for start in range(0, block * columns, step):
        column, inside = start // block, start % block
        part = slice(start, start + step)
        exps = exp_ref[part, :]
        grads = (exps.astype(F32) * dot(wide_ref[part, :], g_ref[...])).astype(BF16)
        dkv_out[column][dim:, inside : inside + step] = dot_nt(g_ref[dim:wide, :], exps).astype(BF16)
        dkv_out[column][0:dim, inside : inside + step] = dot_nt(q_ref[...], grads).astype(BF16)
        term = dot(kt_ref[:, part], grads)
        dq_acc[...] = term if start == 0 else dq_acc[...] + term
    for slot in range(slots):
        dq_out[slot][...] = (dq_acc[:, slot * rows : (slot + 1) * rows] * dim**-0.5).astype(BF16)


def project_kernel(slots, rows, dim, a_of, b_of, halves, fill_ref, w_ref, go_ref, *refs):
    att, refs = refs[:slots], refs[slots:]
    terms_ref, refs = refs[0], refs[1:]
    live = live_column(fill_ref, rows)
    mixed = jnp.where(live > 0, go_ref[...].astype(F32), 0.0).astype(BF16)
    me = a_of()
    held = refs[-1]
    total = None
    for slot in range(slots):
        head = me ^ slot
        held[head] = dot(att[slot][...], mixed).astype(BF16)
        term = dot(att[slot][...].astype(F32).T.astype(BF16), w_ref[head])
        total = term if total is None else total + term
    terms_ref[...] = (total * live).astype(BF16)
    if not halves:
        refs[0][...] = held[...]
        return
    me = b_of()
    kept_ref, sent_ref = refs[0], refs[1]
    for pair in range(slots // 2):
        kept_ref[pair] = held[me ^ (2 * pair)]
        sent_ref[pair] = held[me ^ (2 * pair) ^ 1]


def add_pairs_kernel(kept_ref, came_ref, first_ref, second_ref):
    for index, out_ref in enumerate((first_ref, second_ref)):
        out_ref[...] = (kept_ref[index].astype(F32) + came_ref[index].astype(F32)).astype(BF16)


def add_pieces_kernel(slots, rows, kept_ref, came_ref, *outs):
    for slot in range(slots):
        here = slice(slot * rows, (slot + 1) * rows)
        outs[slot][...] = (kept_ref[:, here].astype(F32) + came_ref[:, here].astype(F32)).astype(BF16)


def add_kernel(a_ref, b_ref, out_ref):
    out_ref[...] = (a_ref[...].astype(F32) + b_ref[...].astype(F32)).astype(out_ref.dtype)


def unpack_kernel(slots, rows, dim, a_of, *refs):
    dkv, dq = refs[:slots], refs[slots : 2 * slots]
    kv_out, q_out, held = refs[2 * slots :]
    me = a_of()
    for slot in range(slots):
        q_out[me ^ slot] = dq[slot][...].astype(F32)
        held[me ^ slot] = dkv[slot][...].astype(F32).T
    for head in range(slots):
        kv_out[:, head, :] = held[head]


def place_kernel(columns, b_of, *refs):
    parts, (out_ref,) = refs[:columns], refs[columns:]
    me = b_of()
    for column in range(columns):
        out_ref[me ^ column] = parts[column][...].astype(F32)


def shards(seq, mp, queries, key_value, tile_fill, out_weight, grad_output):
    rows, heads, dim = queries.shape
    width = grad_output.shape[1]
    slots = heads
    columns = seq // slots
    assert slots * columns == seq and columns & (columns - 1) == 0 and slots & (slots - 1) == 0
    a_of = lambda: lax.axis_index("seq") // columns
    b_of = lambda: lax.axis_index("seq") % columns

    def swap(array, mask, axis="seq", size=seq):
        return lax.ppermute(array, axis, [(i, i ^ mask) for i in range(size)])

    def exchange(pieces):
        return [pieces[0]] + [swap(pieces[s], s * columns) for s in range(1, slots)]

    block, wide = slots * rows, 2 * dim
    keys = seq * rows
    kv_mine = exchange(call(
        functools.partial(pack_kv_kernel, heads, rows, dim, a_of),
        [((rows, wide), BF16)] * slots, [pltpu.VMEM((heads, rows, wide), BF16)],
        n_in=2, smem_first=True, moved=4 * rows * heads * wide, limit=56,
    )(tile_fill, key_value))
    qg_mine = exchange(call(
        functools.partial(pack_qg_kernel, heads, rows, dim, a_of),
        [((wide, rows), BF16)] * slots, [pltpu.VMEM((heads, wide, rows), BF16)],
        n_in=4, smem_first=True, flops=2 * rows * heads * dim * width, moved=4 * rows * width, limit=56,
    )(tile_fill, jnp.transpose(queries, (1, 2, 0)), out_weight, grad_output))
    own = jnp.concatenate(kv_mine, axis=0) if slots > 1 else kv_mine[0]

    blocks = {0: own}
    bit = columns // 2
    while bit:
        for r in sorted(blocks):
            blocks[r ^ bit] = swap(blocks[r], bit)
        bit //= 2

    step = min(block, 512)
    mults = block * keys * wide
    forward = call(
        functools.partial(forward_kernel, slots, columns, rows, dim, step),
        [((dim, rows), BF16)] * slots
        + [((keys, block), BF16), ((keys, 2 * wide), BF16), ((dim, keys), BF16), ((dim, block), BF16), ((2 * wide, block), BF16)],
        [pltpu.VMEM((dim + 16, keys), BF16), pltpu.VMEM((min(slots, 2), keys, rows), F32), pltpu.VMEM((2 * wide, block), BF16)],
        n_in=columns + slots, flops=4 * mults, moved=4 * keys * wide, limit=24,
    )(*[blocks[r] for r in range(columns)], *qg_mine)
    att_mine, saved = exchange(forward[:slots]), forward[slots:]

    halves = columns == heads == 4
    terms, *weight_terms = call(
        functools.partial(project_kernel, slots, rows, dim, a_of, b_of, halves),
        [((rows, width), BF16)] + ([((2, dim, width), BF16)] * 2 if halves else [((heads, dim, width), BF16)]),
        [pltpu.VMEM((heads, dim, width), BF16)],
        n_in=3 + slots, smem_first=True, flops=4 * rows * heads * dim * width, moved=4 * rows * width,
    )(tile_fill, out_weight, grad_output, *att_mine)

    backward = call(
        functools.partial(backward_kernel, slots, columns, rows, dim, min(step, 256)),
        [((wide, block), BF16)] * columns + [((dim, rows), BF16)] * slots,
        [pltpu.VMEM((dim, block), F32)],
        n_in=6, any_last=True, flops=5 * mults, moved=4 * keys * wide, limit=24,
    )(*saved, terms)

    bit = 1
    while bit < mp:
        terms = call(add_kernel, [((rows, width), BF16)], n_in=2, moved=6 * rows * width)(
            terms, swap(terms, bit, "mp", mp))[0]
        bit *= 2

    if halves:
        kept, sent = weight_terms
        kept, sent = call(add_pairs_kernel, [((dim, width), BF16)] * 2, n_in=2)(kept, swap(sent, 1))
        add = call(add_kernel, [((dim, width), BF16)], n_in=2)
        kept = add(kept, swap(sent, 2))[0]
        bit = columns
        while bit < seq:
            kept = add(kept, swap(kept, bit))[0]
            bit *= 2
        across = swap(kept, 2)
        weight_grad = call(
            functools.partial(place_kernel, columns, b_of), [((heads, dim, width), F32)], n_in=columns,
        )(kept, swap(kept, 1), across, swap(across, 1))[0]
    else:
        weight_grad = lax.psum(weight_terms[0].astype(F32), "seq")

    dkv, dq_mine = dict(enumerate(backward[:columns])), exchange(backward[columns:])
    bit = 1
    while 2 * bit < columns:
        dkv = {
            r: call(add_kernel, [((wide, block), BF16)], n_in=2, moved=12 * block * dim)(
                dkv[r], swap(dkv[r ^ bit], bit))[0]
            for r in sorted(dkv) if not r & bit
        }
        bit *= 2
    dkv_mine = exchange(call(
        functools.partial(add_pieces_kernel, slots, rows), [((wide, rows), BF16)] * slots, n_in=2, moved=12 * block * dim,
    )(dkv[0], swap(dkv[bit], bit)))
    key_value_grad, query_grad = call(
        functools.partial(unpack_kernel, slots, rows, dim, a_of),
        [((rows, heads, wide), F32), ((heads, dim, rows), F32)],
        [pltpu.VMEM((heads, rows, wide), F32)],
        n_in=2 * slots, moved=8 * rows * heads * dim,
    )(*dkv_mine, *dq_mine)
    return terms, jnp.transpose(query_grad, (2, 0, 1)), key_value_grad, weight_grad


def solution(mesh):
    return jax.shard_map(
        functools.partial(shards, mesh.shape["seq"], mesh.shape["mp"]),
        mesh=mesh,
        in_specs=(
            P("seq", "mp", None),
            P("seq", "mp", None),
            P("seq"),
            P("mp", None, None),
            P("seq", None),
        ),
        out_specs=(P("seq", None), P("seq", "mp", None), P("seq", "mp", None), P("mp", None, None)),
        check_vma=False,
    )
```

```python
import functools

import jax
import jax.numpy as jnp
from jax import lax
from jax.experimental import pallas as pl
from jax.experimental.pallas import tpu as pltpu
from jax.sharding import PartitionSpec as P

TILE = 128
DEAD = 1024.0
BIAS = -1e30
F32 = jnp.float32
BF16 = jnp.bfloat16
VMEM = pl.BlockSpec(memory_space=pltpu.VMEM)
SMEM = pl.BlockSpec(memory_space=pltpu.SMEM)
MIB = 1024 * 1024


def dot(a, b):
    return lax.dot_general(a, b, (((1,), (0,)), ((), ())), preferred_element_type=F32)


def dot_nt(a, b):
    return lax.dot_general(a, b, (((1,), (1,)), ((), ())), preferred_element_type=F32)


def call(kernel, outs, scratch=(), n_in=1, smem_first=False, after=0, micros=0.3, limit=16):
    specs = [SMEM if smem_first else VMEM] + [VMEM] * (n_in - 1) + [pl.BlockSpec(memory_space=pl.ANY)] * after
    return pl.pallas_call(
        kernel,
        out_shape=[jax.ShapeDtypeStruct(shape, kind) for shape, kind in outs],
        in_specs=specs,
        out_specs=[VMEM] * len(outs),
        scratch_shapes=list(scratch),
        compiler_params=pltpu.CompilerParams(vmem_limit_bytes=limit * MIB),
        cost_estimate=pl.CostEstimate(flops=int(micros * 1.15e9), bytes_accessed=0, transcendentals=0),
    )


def live_column(fill_ref, rows):
    parts = []
    within = lax.broadcasted_iota(jnp.int32, (TILE, 1), 0)
    for tile in range(rows // TILE):
        parts.append(jnp.where(within < fill_ref[tile], 1.0, 0.0))
    return jnp.concatenate(parts, axis=0) if len(parts) > 1 else parts[0]


def pack_kv_kernel(heads, rows, dim, a_of, fill_ref, kv_ref, *refs):
    outs, (held,) = refs[:heads], refs[heads:]
    live = live_column(fill_ref, rows)
    lane = lax.broadcasted_iota(jnp.int32, (rows, 2 * dim), 1)
    mark = jnp.where(lane == 0, DEAD, 0.0)
    for head in range(heads):
        held[head] = jnp.where(live > 0, kv_ref[:, head, :].astype(F32), mark).astype(BF16)
    me = a_of()
    for slot in range(heads):
        outs[slot][...] = held[me ^ slot]


def pack_qg_kernel(heads, rows, dim, a_of, fill_ref, q_ref, w_ref, go_ref, *refs):
    outs, (held,) = refs[:heads], refs[heads:]
    live = live_column(fill_ref, rows)
    mixed = jnp.where(live > 0, go_ref[...].astype(F32), 0.0).astype(BF16)
    for head in range(heads):
        held[head, 0:dim, :] = (q_ref[head].astype(F32) * dim**-0.5).astype(BF16)
        held[head, dim:, :] = dot_nt(w_ref[head], mixed).astype(BF16)
    me = a_of()
    for slot in range(heads):
        outs[slot][...] = held[me ^ slot]


def join_kernel(pieces, *refs):
    out_ref = refs[-1]
    rows = refs[0].shape[0]
    for index in range(pieces):
        out_ref[index * rows : (index + 1) * rows, :] = refs[index][...]


def join_q_kernel(slots, rows, dim, *refs):
    pieces, (qa_ref, g_ref) = refs[:slots], refs[slots:]
    wide = 2 * dim
    row = lax.broadcasted_iota(jnp.int32, (wide, slots * rows), 0)
    qa_ref[dim:wide, :] = jnp.zeros((dim, slots * rows), BF16)
    qa_ref[wide:, :] = jnp.where(row == 0, 1.0, 0.0).astype(BF16)
    for slot in range(slots):
        here = slice(slot * rows, (slot + 1) * rows)
        qa_ref[0:dim, here] = pieces[slot][0:dim, :]
        g_ref[:, here] = pieces[slot][dim:, :]


def prep_kernel(dim, pair_ref, wide_ref, kt_ref, vt_ref):
    wide = 2 * dim
    keys = pair_ref.shape[0]
    pair = pair_ref[...]
    full = pair.astype(F32)
    lane = lax.broadcasted_iota(jnp.int32, (keys, wide), 1)
    ones = jnp.where(lane <= 2, 1.0, 0.0)
    bias = jnp.where(full[:, 0:1] >= DEAD, BIAS, 0.0)
    wide_ref[:, 0:wide] = pair
    wide_ref[:, wide:] = jnp.where(lane == 0, bias, ones).astype(BF16)
    turned = full.T.astype(BF16)
    kt_ref[...] = turned[:dim, :]
    vt_ref[0:dim, :] = turned[dim:, :]
    vt_ref[dim:, :] = jnp.ones((16, keys), BF16)


def score_kernel(slots, rows, dim, step, wide_ref, vt_ref, qa_ref, exp_ref, peak_ref, total_ref, score_ref):
    keys = wide_ref.shape[0]
    peak = None
    for turn in range(slots + 1):
        here = slice(turn * rows, (turn + 1) * rows)
        past = slice((turn - 1) * rows, turn * rows)
        top = jnp.full((8, rows), BIAS, F32)
        total = jnp.zeros((dim + 16, rows), F32)
        for start in range(0, keys, step):
            part = slice(start, start + step)
            if turn < slots:
                scores = dot(wide_ref[part, :], qa_ref[:, here])
                score_ref[turn % 2, part, :] = scores
                top = jnp.maximum(top, jnp.max(scores.reshape(step // 8, 8, rows), axis=0))
            if turn > 0:
                exps = jnp.exp(score_ref[(turn - 1) % 2, part, :] - peak).astype(BF16)
                exp_ref[part, past] = exps
                total = total + dot(vt_ref[:, part], exps)
        if turn > 0:
            total_ref[:, past] = total
            peak_ref[:, past] = peak
        peak = jnp.max(top, axis=0, keepdims=True)


def combine_kernel(slots, columns, rows, dim, *refs):
    peaks, totals, (g_ref,), outs = refs[:columns], refs[columns : 2 * columns], refs[2 * columns : 2 * columns + 1], refs[2 * columns + 1 :]
    att_out, factors_out, inner_ref = outs[:slots], outs[slots : slots + columns], outs[-1]
    peak = functools.reduce(jnp.maximum, [ref[...] for ref in peaks])
    factors = [jnp.exp(ref[...] - peak) for ref in peaks]
    total = sum(factor * ref[...] for factor, ref in zip(factors, totals))
    inverse = 1.0 / total[dim : dim + 1, :]
    attended = (total[0:dim, :] * inverse).astype(BF16)
    for slot in range(slots):
        att_out[slot][...] = attended[:, slot * rows : (slot + 1) * rows]
    for factor, ref in zip(factors, factors_out):
        ref[...] = factor * inverse
    inner_ref[...] = jnp.sum(g_ref[...].astype(F32) * attended.astype(F32), axis=0, keepdims=True)


def back_kernel(dim, step, first, exp_ref, wide_ref, kt_ref, qa_ref, g_ref, factor_ref, inner_ref, *refs):
    dkv_ref, dq_ref, ga_ref = refs[-3:]
    wide = 2 * dim
    keys = wide_ref.shape[0]
    factor = factor_ref[...]
    inner = inner_ref[...] * factor
    high = inner.astype(BF16).astype(F32)
    ga_ref[0:dim, :] = jnp.zeros((dim, g_ref.shape[1]), BF16)
    ga_ref[dim:wide, :] = (g_ref[...].astype(F32) * factor).astype(BF16)
    row = lax.broadcasted_iota(jnp.int32, (wide, g_ref.shape[1]), 0)
    ga_ref[wide:, :] = jnp.where(row == 1, -high, jnp.where(row == 2, high - inner, 0.0)).astype(BF16)
    total = None if first else refs[0][...]
    for start in range(0, keys, step):
        part = slice(start, start + step)
        exps = exp_ref[part, :]
        grads = (exps.astype(F32) * dot(wide_ref[part, :], ga_ref[...])).astype(BF16)
        dkv_ref[part, :] = (dot_nt(exps, ga_ref[0:wide, :]) + dot_nt(grads, qa_ref[0:wide, :])).astype(BF16)
        term = dot(kt_ref[:, part], grads)
        total = term if total is None else total + term
    dq_ref[...] = total


def project_kernel(slots, rows, dim, a_of, b_of, halves, fill_ref, w_ref, go_ref, *refs):
    att, refs = refs[:slots], refs[slots + 1 :]
    terms_ref, refs = refs[0], refs[1:]
    live = live_column(fill_ref, rows)
    mixed = jnp.where(live > 0, go_ref[...].astype(F32), 0.0).astype(BF16)
    me = a_of()
    held = refs[-1]
    total = None
    for slot in range(slots):
        head = me ^ slot
        held[head] = dot(att[slot][...], mixed).astype(BF16)
        term = dot(att[slot][...].astype(F32).T.astype(BF16), w_ref[head])
        total = term if total is None else total + term
    terms_ref[...] = (total * live).astype(BF16)
    if not halves:
        refs[0][...] = held[...]
        return
    me = b_of()
    kept_ref, sent_ref = refs[0], refs[1]
    for pair in range(slots // 2):
        kept_ref[pair] = held[me ^ (2 * pair)]
        sent_ref[pair] = held[me ^ (2 * pair) ^ 1]


def add_pairs_kernel(kept_ref, came_ref, first_ref, second_ref):
    for index, out_ref in enumerate((first_ref, second_ref)):
        out_ref[...] = (kept_ref[index].astype(F32) + came_ref[index].astype(F32)).astype(BF16)


def add_pieces_kernel(slots, rows, dim, kept_ref, came_ref, dq_ref, *outs):
    wide = 2 * dim
    for slot in range(slots):
        here = slice(slot * rows, (slot + 1) * rows)
        outs[slot][0:rows, :] = (kept_ref[here, :].astype(F32) + came_ref[here, :].astype(F32)).astype(BF16)
        for part in range(rows // wide):
            start = slot * rows + part * wide
            grad = dq_ref[:, start : start + wide] * dim**-0.5
            outs[slot][rows + part * dim : rows + (part + 1) * dim, :] = grad.astype(BF16)


def add_kernel(a_ref, b_ref, out_ref):
    out_ref[...] = (a_ref[...].astype(F32) + b_ref[...].astype(F32)).astype(out_ref.dtype)


def unpack_kernel(slots, rows, dim, a_of, *refs):
    pieces, (kv_out, q_out, held) = refs[:slots], refs[slots:]
    wide = 2 * dim
    me = a_of()
    for slot in range(slots):
        held[me ^ slot] = pieces[slot][0:rows, :].astype(F32)
        for part in range(rows // wide):
            start = rows + part * dim
            q_out[me ^ slot, :, part * wide : (part + 1) * wide] = pieces[slot][start : start + dim, :].astype(F32)
    for head in range(slots):
        kv_out[:, head, :] = held[head]


def place_kernel(columns, b_of, *refs):
    parts, (out_ref,) = refs[:columns], refs[columns:]
    me = b_of()
    for column in range(columns):
        out_ref[me ^ column] = parts[column][...].astype(F32)


def shards(seq, mp, queries, key_value, tile_fill, out_weight, grad_output):
    rows, heads, dim = queries.shape
    width = grad_output.shape[1]
    slots = heads
    columns = seq // slots
    assert slots * columns == seq and columns & (columns - 1) == 0 and slots & (slots - 1) == 0
    a_of = lambda: lax.axis_index("seq") // columns
    b_of = lambda: lax.axis_index("seq") % columns

    def swap(array, mask, axis="seq", size=seq):
        return lax.ppermute(array, axis, [(i, i ^ mask) for i in range(size)])

    def exchange(pieces):
        came = {s: swap(pieces[s], s * columns) for s in sorted(range(1, slots), key=lambda s: (s < slots // 2, s))}
        return [pieces[0]] + [came[s] for s in range(1, slots)]

    block, wide = slots * rows, 2 * dim
    kv_mine = exchange(call(
        functools.partial(pack_kv_kernel, heads, rows, dim, a_of),
        [((rows, wide), BF16)] * slots, [pltpu.VMEM((heads, rows, wide), BF16)],
        n_in=2, smem_first=True, micros=0.8,
    )(tile_fill, key_value))
    qg_send = call(
        functools.partial(pack_qg_kernel, heads, rows, dim, a_of),
        [((wide, rows), BF16)] * slots, [pltpu.VMEM((heads, wide, rows), BF16)],
        n_in=4, smem_first=True, micros=1,
    )(tile_fill, jnp.transpose(queries, (1, 2, 0)), out_weight, grad_output)
    qg_mine = exchange(qg_send)
    own = call(
        functools.partial(join_kernel, slots), [((block, wide), BF16)], n_in=slots, after=1,
    )(*kv_mine, qg_send[0])[0]

    blocks = {0: own}
    bit = columns // 2
    while bit:
        for r in sorted(blocks):
            blocks[r ^ bit] = swap(blocks[r], bit)
        bit //= 2

    qa, grads = call(
        functools.partial(join_q_kernel, slots, rows, dim), [((2 * wide, block), BF16), ((dim, block), BF16)], n_in=slots,
    )(*qg_mine)
    step = min(block, 512)
    prepared, scored = {}, {}
    for r in range(columns):
        prepared[r] = call(
            functools.partial(prep_kernel, dim),
            [((block, 2 * wide), BF16), ((dim, block), BF16), ((dim + 16, block), BF16)], micros=0.5,
        )(blocks[r])
        wide_keys, _, values = prepared[r]
        scored[r] = call(
            functools.partial(score_kernel, slots, rows, dim, step),
            [((block, block), BF16), ((1, block), F32), ((dim + 16, block), F32)],
            [pltpu.VMEM((min(slots, 2), block, rows), F32)], n_in=3, micros=2,
        )(wide_keys, values, qa)
    combined = call(
        functools.partial(combine_kernel, slots, columns, rows, dim),
        [((dim, rows), BF16)] * slots + [((1, block), F32)] * (columns + 1), n_in=2 * columns + 1, micros=0.5,
    )(*[scored[r][1] for r in range(columns)], *[scored[r][2] for r in range(columns)], grads)
    att_mine, factors, inner = exchange(combined[:slots]), combined[slots:-1], combined[-1]

    halves = columns == heads == 4
    order = sorted(range(columns), key=lambda r: -int(f"{r:032b}"[::-1], 2))
    dkv, dq = {}, None
    for at, r in enumerate(order):
        if at == columns // 2:
            terms, *weight_terms = call(
                functools.partial(project_kernel, slots, rows, dim, a_of, b_of, halves),
                [((rows, width), BF16)] + ([((2, dim, width), BF16)] * 2 if halves else [((heads, dim, width), BF16)]),
                [pltpu.VMEM((heads, dim, width), BF16)],
                n_in=3 + slots, smem_first=True, after=1, micros=1,
            )(tile_fill, out_weight, grad_output, *att_mine, dkv[order[at - 1]])
        operands = [scored[r][0], prepared[r][0], prepared[r][1], qa, grads, factors[r], inner] + ([] if dq is None else [dq])
        later = [terms] if at == columns // 2 else []
        dkv[r], dq = call(
            functools.partial(back_kernel, dim, min(step, 256), dq is None),
            [((block, wide), BF16), ((dim, block), F32)], [pltpu.VMEM((2 * wide, block), BF16)],
            n_in=len(operands), after=len(later), micros=2,
        )(*operands, *later)

    bit = 1
    while bit < mp:
        terms = call(add_kernel, [((rows, width), BF16)], n_in=2)(terms, swap(terms, bit, "mp", mp))[0]
        bit *= 2

    if halves:
        kept, sent = weight_terms
        kept, sent = call(add_pairs_kernel, [((dim, width), BF16)] * 2, n_in=2)(kept, swap(sent, 1))
        add = call(add_kernel, [((dim, width), BF16)], n_in=2)
        kept = add(kept, swap(sent, 2))[0]
        bit = columns
        while bit < seq:
            kept = add(kept, swap(kept, bit))[0]
            bit *= 2
        across = swap(kept, 2)
        weight_grad = call(
            functools.partial(place_kernel, columns, b_of), [((heads, dim, width), F32)], n_in=columns, micros=0.5,
        )(kept, swap(kept, 1), across, swap(across, 1))[0]
    else:
        weight_grad = lax.psum(weight_terms[0].astype(F32), "seq")

    bit = 1
    while 2 * bit < columns:
        dkv = {
            r: call(add_kernel, [((block, wide), BF16)], n_in=2)(dkv[r], swap(dkv[r ^ bit], bit))[0]
            for r in order if r in dkv and not r & bit
        }
        bit *= 2
    returned = exchange(call(
        functools.partial(add_pieces_kernel, slots, rows, dim), [((rows + rows // 2, wide), BF16)] * slots, n_in=3,
    )(dkv[0], swap(dkv[bit], bit), dq))
    key_value_grad, query_grad = call(
        functools.partial(unpack_kernel, slots, rows, dim, a_of),
        [((rows, heads, wide), F32), ((heads, dim, rows), F32)],
        [pltpu.VMEM((heads, rows, wide), F32)], n_in=slots, micros=1,
    )(*returned)
    return terms, jnp.transpose(query_grad, (2, 0, 1)), key_value_grad, weight_grad


def solution(mesh):
    return jax.shard_map(
        functools.partial(shards, mesh.shape["seq"], mesh.shape["mp"]),
        mesh=mesh,
        in_specs=(
            P("seq", "mp", None),
            P("seq", "mp", None),
            P("seq"),
            P("mp", None, None),
            P("seq", None),
        ),
        out_specs=(P("seq", None), P("seq", "mp", None), P("seq", "mp", None), P("mp", None, None)),
        check_vma=False,
    )
```

```python
import functools

import jax
import jax.numpy as jnp
from jax import lax
from jax.experimental import pallas as pl
from jax.experimental.pallas import tpu as pltpu
from jax.sharding import PartitionSpec as P

TILE = 128
DEAD = 1024.0
BIAS = -1e30
F32 = jnp.float32
BF16 = jnp.bfloat16
VMEM = pl.BlockSpec(memory_space=pltpu.VMEM)
HBM = pl.BlockSpec(memory_space=pltpu.HBM)
SMEM = pl.BlockSpec(memory_space=pltpu.SMEM)
MIB = 1024 * 1024


def dot(a, b):
    return lax.dot_general(a, b, (((1,), (0,)), ((), ())), preferred_element_type=F32)


def dot_nt(a, b):
    return lax.dot_general(a, b, (((1,), (1,)), ((), ())), preferred_element_type=F32)


def call(kernel, outs, scratch=(), n_in=1, smem_first=False, far=False, after=0, micros=0.3, limit=16):
    specs = [SMEM if smem_first else VMEM] + [HBM if far else VMEM] * (n_in - 1)
    specs += [pl.BlockSpec(memory_space=pl.ANY)] * after
    return pl.pallas_call(
        kernel,
        out_shape=[jax.ShapeDtypeStruct(shape, kind) for shape, kind in outs],
        in_specs=specs,
        out_specs=[VMEM] * len(outs),
        scratch_shapes=list(scratch),
        compiler_params=pltpu.CompilerParams(vmem_limit_bytes=limit * MIB),
        cost_estimate=pl.CostEstimate(flops=int(micros * 1.15e9), bytes_accessed=0, transcendentals=0),
    )


def live_column(fill_ref, rows):
    parts = []
    within = lax.broadcasted_iota(jnp.int32, (TILE, 1), 0)
    for tile in range(rows // TILE):
        parts.append(jnp.where(within < fill_ref[tile], 1.0, 0.0))
    return jnp.concatenate(parts, axis=0) if len(parts) > 1 else parts[0]


def pack_kernel(heads, rows, dim, a_of, fill_ref, q_hbm, kv_hbm, *refs):
    outs, (held, q_ref, kv_ref, q_sem, kv_sem) = refs[:heads], refs[heads:]
    q_copy = pltpu.make_async_copy(q_hbm, q_ref, q_sem)
    kv_copy = pltpu.make_async_copy(kv_hbm, kv_ref, kv_sem)
    kv_copy.start()
    q_copy.start()
    wide = 2 * dim
    live = live_column(fill_ref, rows)
    lane = lax.broadcasted_iota(jnp.int32, (rows, wide), 1)
    mark = jnp.where(lane == 0, DEAD, 0.0)
    kv_copy.wait()
    for head in range(heads):
        held[head, 0:rows, :] = jnp.where(live > 0, kv_ref[:, head, :].astype(F32), mark).astype(BF16)
    q_copy.wait()
    for head in range(heads):
        scaled = (q_ref[head].astype(F32) * dim**-0.5).astype(BF16)
        for part in range(rows // wide):
            start = rows + part * dim
            held[head, start : start + dim, :] = scaled[:, part * wide : (part + 1) * wide]
    me = a_of()
    for slot in range(heads):
        outs[slot][...] = held[me ^ slot]


def pack_grad_kernel(heads, rows, dim, a_of, fill_ref, w_ref, go_ref, *refs):
    outs, (held,) = refs[:heads], refs[heads:]
    live = live_column(fill_ref, rows)
    mixed = jnp.where(live > 0, go_ref[...].astype(F32), 0.0).astype(BF16)
    for head in range(heads):
        held[head] = dot_nt(w_ref[head], mixed).astype(BF16)
    me = a_of()
    for slot in range(heads):
        outs[slot][...] = held[me ^ slot]


def join_kernel(pieces, rows, *refs):
    out_ref = refs[-1]
    for index in range(pieces):
        out_ref[index * rows : (index + 1) * rows, :] = refs[index][0:rows, :]


def join_q_kernel(slots, rows, dim, *refs):
    pieces, (qa_ref,) = refs[:slots], refs[slots:]
    wide = 2 * dim
    row = lax.broadcasted_iota(jnp.int32, (wide, slots * rows), 0)
    qa_ref[dim:wide, :] = jnp.zeros((dim, slots * rows), BF16)
    qa_ref[wide:, :] = jnp.where(row == 0, 1.0, 0.0).astype(BF16)
    for slot in range(slots):
        for part in range(rows // wide):
            start, across = rows + part * dim, slot * rows + part * wide
            qa_ref[0:dim, across : across + wide] = pieces[slot][start : start + dim, :]


def prep_kernel(dim, pair_ref, wide_ref, kt_ref, vt_ref):
    wide = 2 * dim
    keys = pair_ref.shape[0]
    pair = pair_ref[...]
    full = pair.astype(F32)
    lane = lax.broadcasted_iota(jnp.int32, (keys, wide), 1)
    ones = jnp.where(lane <= 2, 1.0, 0.0)
    bias = jnp.where(full[:, 0:1] >= DEAD, BIAS, 0.0)
    wide_ref[:, 0:wide] = pair
    wide_ref[:, wide:] = jnp.where(lane == 0, bias, ones).astype(BF16)
    turned = full.T.astype(BF16)
    kt_ref[...] = turned[:dim, :]
    vt_ref[0:dim, :] = turned[dim:, :]
    vt_ref[dim:, :] = jnp.ones((16, keys), BF16)


def score_kernel(slots, rows, dim, step, wide_ref, vt_ref, qa_ref, exp_ref, peak_ref, total_ref, score_ref):
    keys = wide_ref.shape[0]
    peak = None
    for turn in range(slots + 1):
        here = slice(turn * rows, (turn + 1) * rows)
        past = slice((turn - 1) * rows, turn * rows)
        top = jnp.full((8, rows), BIAS, F32)
        total = jnp.zeros((dim + 16, rows), F32)
        for start in range(0, keys, step):
            part = slice(start, start + step)
            if turn < slots:
                scores = dot(wide_ref[part, :], qa_ref[:, here])
                score_ref[turn % 2, part, :] = scores
                top = jnp.maximum(top, jnp.max(scores.reshape(step // 8, 8, rows), axis=0))
            if turn > 0:
                exps = jnp.exp(score_ref[(turn - 1) % 2, part, :] - peak).astype(BF16)
                exp_ref[part, past] = exps
                total = total + dot(vt_ref[:, part], exps)
        if turn > 0:
            total_ref[:, past] = total
            peak_ref[:, past] = peak
        peak = jnp.max(top, axis=0, keepdims=True)


def combine_kernel(slots, columns, rows, dim, *refs):
    peaks, totals, refs = refs[:columns], refs[columns : 2 * columns], refs[2 * columns :]
    grads, outs = refs[:slots], refs[slots:]
    att_out, factors_out, (inner_ref, g_ref) = outs[:slots], outs[slots : slots + columns], outs[slots + columns :]
    peak = functools.reduce(jnp.maximum, [ref[...] for ref in peaks])
    factors = [jnp.exp(ref[...] - peak) for ref in peaks]
    total = sum(factor * ref[...] for factor, ref in zip(factors, totals))
    inverse = 1.0 / total[dim : dim + 1, :]
    attended = (total[0:dim, :] * inverse).astype(BF16)
    for slot in range(slots):
        att_out[slot][...] = attended[:, slot * rows : (slot + 1) * rows]
        g_ref[:, slot * rows : (slot + 1) * rows] = grads[slot][...]
    for factor, ref in zip(factors, factors_out):
        ref[...] = factor * inverse
    inner_ref[...] = jnp.sum(g_ref[...].astype(F32) * attended.astype(F32), axis=0, keepdims=True)


def back_kernel(dim, step, first, exp_ref, wide_ref, kt_ref, qa_ref, g_ref, factor_ref, inner_ref, *refs):
    dkv_ref, dq_ref, ga_ref = refs[-3:]
    wide = 2 * dim
    keys = wide_ref.shape[0]
    factor = factor_ref[...]
    inner = inner_ref[...] * factor
    high = inner.astype(BF16).astype(F32)
    ga_ref[0:dim, :] = jnp.zeros((dim, g_ref.shape[1]), BF16)
    ga_ref[dim:wide, :] = (g_ref[...].astype(F32) * factor).astype(BF16)
    row = lax.broadcasted_iota(jnp.int32, (wide, g_ref.shape[1]), 0)
    ga_ref[wide:, :] = jnp.where(row == 1, -high, jnp.where(row == 2, high - inner, 0.0)).astype(BF16)
    total = None if first else refs[0][...]
    ahead = dot(wide_ref[0:step, :], ga_ref[...])
    for start in range(0, keys, step):
        part = slice(start, start + step)
        products = ahead
        if start + step < keys:
            ahead = dot(wide_ref[start + step : start + 2 * step, :], ga_ref[...])
        exps = exp_ref[part, :]
        grads = (exps.astype(F32) * products).astype(BF16)
        dkv_ref[dim:, part] = dot_nt(ga_ref[dim:wide, :], exps).astype(BF16)
        dkv_ref[0:dim, part] = dot_nt(qa_ref[0:dim, :], grads).astype(BF16)
        term = dot(kt_ref[:, part], grads)
        total = term if total is None else total + term
    dq_ref[...] = total


def project_kernel(slots, rows, dim, a_of, b_of, halves, fill_ref, w_ref, go_ref, *refs):
    att, refs = refs[:slots], refs[slots + 1 :]
    terms_ref, refs = refs[0], refs[1:]
    live = live_column(fill_ref, rows)
    mixed = jnp.where(live > 0, go_ref[...].astype(F32), 0.0).astype(BF16)
    me = a_of()
    held = refs[-1]
    total = None
    for slot in range(slots):
        head = me ^ slot
        held[head] = dot(att[slot][...], mixed).astype(BF16)
        term = dot(att[slot][...].astype(F32).T.astype(BF16), w_ref[head])
        total = term if total is None else total + term
    terms_ref[...] = (total * live).astype(BF16)
    if not halves:
        refs[0][...] = held[...]
        return
    me = b_of()
    kept_ref, sent_ref = refs[0], refs[1]
    for pair in range(slots // 2):
        kept_ref[pair] = held[me ^ (2 * pair)]
        sent_ref[pair] = held[me ^ (2 * pair) ^ 1]


def add_pairs_kernel(kept_ref, came_ref, _, first_ref, second_ref):
    for index, out_ref in enumerate((first_ref, second_ref)):
        out_ref[...] = (kept_ref[index].astype(F32) + came_ref[index].astype(F32)).astype(BF16)


def add_pieces_kernel(slots, rows, dim, kept_ref, came_ref, dq_ref, *outs):
    wide = 2 * dim
    for slot in range(slots):
        here = slice(slot * rows, (slot + 1) * rows)
        outs[slot][0:wide, :] = (kept_ref[:, here].astype(F32) + came_ref[:, here].astype(F32)).astype(BF16)
        outs[slot][wide:, :] = (dq_ref[:, here] * dim**-0.5).astype(BF16)


def add_kernel(a_ref, b_ref, out_ref):
    out_ref[...] = (a_ref[...].astype(F32) + b_ref[...].astype(F32)).astype(out_ref.dtype)


def unpack_kernel(slots, rows, dim, a_of, *refs):
    pieces, (kv_out, q_out, held) = refs[:slots], refs[slots:]
    wide = 2 * dim
    me = a_of()
    for slot in range(slots):
        held[me ^ slot] = pieces[slot][0:wide, :].astype(F32).T
        q_out[me ^ slot] = pieces[slot][wide:, :].astype(F32)
    for head in range(slots):
        kv_out[:, head, :] = held[head]


def place_kernel(columns, b_of, *refs):
    parts, (out_ref,) = refs[:columns], refs[columns:]
    me = b_of()
    for column in range(columns):
        out_ref[me ^ column] = parts[column][...].astype(F32)


def shards(seq, mp, queries, key_value, tile_fill, out_weight, grad_output):
    rows, heads, dim = queries.shape
    width = grad_output.shape[1]
    slots = heads
    columns = seq // slots
    assert slots * columns == seq and columns & (columns - 1) == 0 and slots & (slots - 1) == 0
    a_of = lambda: lax.axis_index("seq") // columns
    b_of = lambda: lax.axis_index("seq") % columns

    def swap(array, mask, axis="seq", size=seq):
        return lax.ppermute(array, axis, [(i, i ^ mask) for i in range(size)])

    def exchange(pieces):
        came = {s: swap(pieces[s], s * columns) for s in sorted(range(1, slots), key=lambda s: (s < slots // 2, s))}
        return [pieces[0]] + [came[s] for s in range(1, slots)]

    block, wide = slots * rows, 2 * dim
    sent = call(
        functools.partial(pack_kernel, heads, rows, dim, a_of),
        [((rows + rows // 2, wide), BF16)] * slots,
        [pltpu.VMEM((heads, rows + rows // 2, wide), BF16), pltpu.VMEM((heads, dim, rows), BF16),
         pltpu.VMEM((rows, heads, wide), BF16), pltpu.SemaphoreType.DMA, pltpu.SemaphoreType.DMA],
        n_in=3, smem_first=True, far=True, micros=1.5, limit=56,
    )(tile_fill, jnp.transpose(queries, (1, 2, 0)), key_value)
    mine = exchange(sent)
    grad_sent = call(
        functools.partial(pack_grad_kernel, heads, rows, dim, a_of),
        [((dim, rows), BF16)] * slots, [pltpu.VMEM((heads, dim, rows), BF16)],
        n_in=3, smem_first=True, micros=1,
    )(tile_fill, out_weight, grad_output)
    grads = exchange(grad_sent)
    own = call(
        functools.partial(join_kernel, slots, rows), [((block, wide), BF16)], n_in=slots, after=1,
    )(*mine, grad_sent[0])[0]

    blocks = {0: own}
    bit = columns // 2
    while bit:
        for r in sorted(blocks):
            blocks[r ^ bit] = swap(blocks[r], bit)
        bit //= 2

    qa = call(
        functools.partial(join_q_kernel, slots, rows, dim), [((2 * wide, block), BF16)], n_in=slots,
    )(*mine)[0]
    step = min(block, 512)
    prepared, scored = {}, {}
    for r in range(columns):
        prepared[r] = call(
            functools.partial(prep_kernel, dim),
            [((block, 2 * wide), BF16), ((dim, block), BF16), ((dim + 16, block), BF16)], micros=0.5,
        )(blocks[r])
        wide_keys, _, values = prepared[r]
        scored[r] = call(
            functools.partial(score_kernel, slots, rows, dim, step),
            [((block, block), BF16), ((1, block), F32), ((dim + 16, block), F32)],
            [pltpu.VMEM((min(slots, 2), block, rows), F32)], n_in=3, micros=2,
        )(wide_keys, values, qa)
    combined = call(
        functools.partial(combine_kernel, slots, columns, rows, dim),
        [((dim, rows), BF16)] * slots + [((1, block), F32)] * (columns + 1) + [((dim, block), BF16)],
        n_in=2 * columns + slots, micros=0.5,
    )(*[scored[r][1] for r in range(columns)], *[scored[r][2] for r in range(columns)], *grads)
    att_mine, factors, (inner, grads) = exchange(combined[:slots]), combined[slots : slots + columns], combined[slots + columns :]

    halves = columns == heads == 4
    order = sorted(range(columns), key=lambda r: -int(f"{r:032b}"[::-1], 2))
    dkv, dq = {}, None
    for at, r in enumerate(order):
        later = []
        if at == min(1, columns - 1):
            terms, *weight_terms = call(
                functools.partial(project_kernel, slots, rows, dim, a_of, b_of, halves),
                [((rows, width), BF16)] + ([((2, dim, width), BF16)] * 2 if halves else [((heads, dim, width), BF16)]),
                [pltpu.VMEM((heads, dim, width), BF16)],
                n_in=3 + slots, smem_first=True, after=1, micros=1,
            )(tile_fill, out_weight, grad_output, *att_mine, dkv[order[at - 1]])
            later = [terms]
        if at == 2 and halves:
            kept, sent = weight_terms
            kept, sent = call(add_pairs_kernel, [((dim, width), BF16)] * 2, n_in=2, after=1)(
                kept, swap(sent, 1), dkv[order[at - 1]])
            later = [kept]
        operands = [scored[r][0], prepared[r][0], prepared[r][1], qa, grads, factors[r], inner] + ([] if dq is None else [dq])
        dkv[r], dq = call(
            functools.partial(back_kernel, dim, min(step, 256), dq is None),
            [((wide, block), BF16), ((dim, block), F32)], [pltpu.VMEM((2 * wide, block), BF16)],
            n_in=len(operands), after=len(later), micros=2,
        )(*operands, *later)

    bit = 1
    while bit < mp:
        terms = call(add_kernel, [((rows, width), BF16)], n_in=2)(terms, swap(terms, bit, "mp", mp))[0]
        bit *= 2

    if halves:
        add = call(add_kernel, [((dim, width), BF16)], n_in=2)
        kept = add(kept, swap(sent, 2))[0]
        bit = columns
        while bit < seq:
            kept = add(kept, swap(kept, bit))[0]
            bit *= 2
        across = swap(kept, 2)
        weight_grad = call(
            functools.partial(place_kernel, columns, b_of), [((heads, dim, width), F32)], n_in=columns, micros=0.5,
        )(kept, swap(kept, 1), across, swap(across, 1))[0]
    else:
        weight_grad = lax.psum(weight_terms[0].astype(F32), "seq")

    bit = 1
    while 2 * bit < columns:
        dkv = {
            r: call(add_kernel, [((wide, block), BF16)], n_in=2)(dkv[r], swap(dkv[r ^ bit], bit))[0]
            for r in order if r in dkv and not r & bit
        }
        bit *= 2
    returned = exchange(call(
        functools.partial(add_pieces_kernel, slots, rows, dim), [((wide + dim, rows), BF16)] * slots, n_in=3,
    )(dkv[0], swap(dkv[bit], bit), dq))
    key_value_grad, query_grad = call(
        functools.partial(unpack_kernel, slots, rows, dim, a_of),
        [((rows, heads, wide), F32), ((heads, dim, rows), F32)],
        [pltpu.VMEM((heads, rows, wide), F32)], n_in=slots, micros=1,
    )(*returned)
    return terms, jnp.transpose(query_grad, (2, 0, 1)), key_value_grad, weight_grad


def solution(mesh):
    return jax.shard_map(
        functools.partial(shards, mesh.shape["seq"], mesh.shape["mp"]),
        mesh=mesh,
        in_specs=(
            P("seq", "mp", None),
            P("seq", "mp", None),
            P("seq"),
            P("mp", None, None),
            P("seq", None),
        ),
        out_specs=(P("seq", None), P("seq", "mp", None), P("seq", "mp", None), P("mp", None, None)),
        check_vma=False,
    )
```

```python
import functools

import jax
import jax.numpy as jnp
from jax import lax
from jax.experimental import pallas as pl
from jax.experimental.pallas import tpu as pltpu
from jax.sharding import PartitionSpec as P

TILE = 128
DEAD = 1024.0
BIAS = -1e30
LOG2_E = 1.4426950408889634
SAFE = 64.0
F32 = jnp.float32
BF16 = jnp.bfloat16
VMEM = pl.BlockSpec(memory_space=pltpu.VMEM)
SMEM = pl.BlockSpec(memory_space=pltpu.SMEM)
MIB = 1024 * 1024


def dot(a, b):
    return lax.dot_general(a, b, (((1,), (0,)), ((), ())), preferred_element_type=F32)


def dot_nt(a, b):
    return lax.dot_general(a, b, (((1,), (1,)), ((), ())), preferred_element_type=F32)


def call(kernel, outs, scratch=(), n_in=1, smem_first=False, after=0, micros=0.01, limit=16):
    specs = [SMEM if smem_first else VMEM] + [VMEM] * (n_in - 1) + [pl.BlockSpec(memory_space=pl.ANY)] * after
    return pl.pallas_call(
        kernel,
        out_shape=[jax.ShapeDtypeStruct(shape, kind) for shape, kind in outs],
        in_specs=specs,
        out_specs=[VMEM] * len(outs),
        scratch_shapes=list(scratch),
        compiler_params=pltpu.CompilerParams(vmem_limit_bytes=limit * MIB),
        cost_estimate=pl.CostEstimate(flops=int(micros * 1.15e9), bytes_accessed=0, transcendentals=0),
    )


def live_column(fill_ref, rows):
    parts = []
    within = lax.broadcasted_iota(jnp.int32, (TILE, 1), 0)
    for tile in range(rows // TILE):
        parts.append(jnp.where(within < fill_ref[tile], 1.0, 0.0))
    return jnp.concatenate(parts, axis=0) if len(parts) > 1 else parts[0]


def pack_kv_kernel(heads, rows, dim, a_of, fill_ref, kv_ref, *refs):
    outs, (held,) = refs[:heads], refs[heads:]
    live = live_column(fill_ref, rows)
    lane = lax.broadcasted_iota(jnp.int32, (rows, 2 * dim), 1)
    mark = jnp.where(lane == 0, DEAD, 0.0)
    for head in range(heads):
        held[head] = jnp.where(live > 0, kv_ref[:, head, :].astype(F32), mark).astype(BF16)
    me = a_of()
    for slot in range(heads):
        outs[slot][...] = held[me ^ slot]


def pack_qg_kernel(heads, rows, dim, a_of, fill_ref, q_ref, w_ref, go_ref, *refs):
    outs, (held,) = refs[:heads], refs[heads:]
    live = live_column(fill_ref, rows)
    mixed = jnp.where(live > 0, go_ref[...].astype(F32), 0.0).astype(BF16)
    for head in range(heads):
        held[head, 0:dim, :] = (q_ref[head].astype(F32) * dim**-0.5).astype(BF16)
        held[head, dim:, :] = dot_nt(w_ref[head], mixed).astype(BF16)
    me = a_of()
    for slot in range(heads):
        outs[slot][...] = held[me ^ slot]


def join_kernel(pieces, *refs):
    out_ref = refs[-1]
    rows = refs[0].shape[0]
    for index in range(pieces):
        out_ref[index * rows : (index + 1) * rows, :] = refs[index][...]


def join_q_kernel(slots, rows, dim, *refs):
    pieces, (qa_ref, q_ref, g_ref, norm_ref) = refs[:slots], refs[slots:]
    wide = 2 * dim
    row = lax.broadcasted_iota(jnp.int32, (dim, slots * rows), 0)
    qa_ref[dim:wide, :] = jnp.zeros((dim, slots * rows), BF16)
    qa_ref[wide : wide + dim, :] = jnp.where(row == 0, 1.0, 0.0).astype(BF16)
    for slot in range(slots):
        here = slice(slot * rows, (slot + 1) * rows)
        queries = pieces[slot][0:dim, :]
        q_ref[:, here] = queries
        g_ref[:, here] = pieces[slot][dim:, :]
        scaled = queries.astype(F32) * LOG2_E
        high = scaled.astype(BF16)
        qa_ref[0:dim, here] = high
        qa_ref[wide + dim :, here] = (scaled - high.astype(F32)).astype(BF16)
        norm_ref[:, here] = jnp.sum(scaled * scaled, axis=0, keepdims=True)


def prep_kernel(dim, pair_ref, wide_ref, kt_ref, vt_ref, norm_ref):
    wide = 2 * dim
    keys = pair_ref.shape[0]
    pair = pair_ref[...]
    full = pair.astype(F32)
    lane = lax.broadcasted_iota(jnp.int32, (keys, wide), 1)
    ones = jnp.where(lane <= 2, 1.0, 0.0)
    bias = jnp.where(full[:, 0:1] >= DEAD, BIAS, 0.0)
    extra = jnp.where(lane == 0, bias, ones)
    wide_ref[:, 0:wide] = pair
    wide_ref[:, wide:] = jnp.where(lane < dim, extra, pltpu.roll(full, dim, 1)).astype(BF16)
    turned = full.T
    kt_ref[...] = turned[:dim, :].astype(BF16)
    vt_ref[0:dim, :] = turned[dim:, :].astype(BF16)
    vt_ref[dim:, :] = jnp.ones((16, keys), BF16)
    norm = jnp.sum(turned[:dim, :] * turned[:dim, :], axis=0, keepdims=True)
    norm_ref[...] = jnp.where(turned[0:1, :] >= DEAD, 0.0, norm)


def score_kernel(slots, rows, dim, step, wide_ref, vt_ref, norm_ref, qa_ref, q_norm_ref, exp_ref, peak_ref, total_ref, score_ref):
    keys = wide_ref.shape[0]
    small = jnp.max(norm_ref[...]) * jnp.max(q_norm_ref[...]) <= SAFE * SAFE

    @pl.when(small)
    def _():
        peak_ref[...] = jnp.zeros_like(peak_ref)
        ahead = dot(wide_ref[...], qa_ref[:, 0:rows])
        for slot in range(slots):
            here = slice(slot * rows, (slot + 1) * rows)
            scores = ahead
            if slot + 1 < slots:
                ahead = dot(wide_ref[...], qa_ref[:, (slot + 1) * rows : (slot + 2) * rows])
            exps = jnp.exp2(scores).astype(BF16)
            exp_ref[:, here] = exps
            total_ref[:, here] = dot(vt_ref[...], exps)

    @pl.when(jnp.logical_not(small))
    def _():
        for slot in range(slots):
            here = slice(slot * rows, (slot + 1) * rows)
            top = jnp.full((8, rows), BIAS, F32)
            for start in range(0, keys, step):
                part = slice(start, start + step)
                scores = dot(wide_ref[part, :], qa_ref[:, here])
                score_ref[part, :] = scores
                top = jnp.maximum(top, jnp.max(scores.reshape(step // 8, 8, rows), axis=0))
            peak = jnp.max(top, axis=0, keepdims=True)
            peak_ref[:, here] = peak
            total = jnp.zeros((dim + 16, rows), F32)
            for start in range(0, keys, step):
                part = slice(start, start + step)
                exps = jnp.exp2(score_ref[part, :] - peak).astype(BF16)
                exp_ref[part, here] = exps
                total = total + dot(vt_ref[:, part], exps)
            total_ref[:, here] = total


def combine_kernel(slots, columns, rows, dim, *refs):
    peaks, totals, (g_ref,), outs = refs[:columns], refs[columns : 2 * columns], refs[2 * columns : 2 * columns + 1], refs[2 * columns + 1 :]
    att_out, factors_out, inner_ref = outs[:slots], outs[slots : slots + columns], outs[-1]
    peak = functools.reduce(jnp.maximum, [ref[...] for ref in peaks])
    factors = [jnp.exp2(ref[...] - peak) for ref in peaks]
    total = sum(factor * ref[...] for factor, ref in zip(factors, totals))
    inverse = 1.0 / total[dim : dim + 1, :]
    attended = (total[0:dim, :] * inverse).astype(BF16)
    for slot in range(slots):
        att_out[slot][...] = attended[:, slot * rows : (slot + 1) * rows]
    for factor, ref in zip(factors, factors_out):
        ref[...] = factor * inverse
    inner_ref[...] = jnp.sum(g_ref[...].astype(F32) * attended.astype(F32), axis=0, keepdims=True)


def back_kernel(slots, rows, dim, first, exp_ref, wide_ref, kt_ref, q_ref, g_ref, factor_ref, inner_ref, *refs):
    dkv_ref, dq_ref, ga_ref = refs[-3:]
    wide = 2 * dim
    block = g_ref.shape[1]
    factor = factor_ref[...]
    inner = inner_ref[...] * factor
    high = inner.astype(BF16).astype(F32)
    row = lax.broadcasted_iota(jnp.int32, (dim, block), 0)
    ga_ref[0:dim, :] = jnp.zeros((dim, block), BF16)
    ga_ref[dim:wide, :] = (g_ref[...].astype(F32) * factor).astype(BF16)
    ga_ref[wide : wide + dim, :] = jnp.where(row == 1, -high, jnp.where(row == 2, high - inner, 0.0)).astype(BF16)
    ga_ref[wide + dim :, :] = jnp.zeros((dim, block), BF16)
    grad_k = grad_v = None
    ahead = dot(wide_ref[...], ga_ref[:, 0:rows])
    for slot in range(slots):
        here = slice(slot * rows, (slot + 1) * rows)
        products = ahead
        if slot + 1 < slots:
            ahead = dot(wide_ref[...], ga_ref[:, (slot + 1) * rows : (slot + 2) * rows])
        exps = exp_ref[:, here]
        grads = exps * products.astype(BF16)
        term_v = dot_nt(ga_ref[dim:wide, here], exps)
        term_k = dot_nt(q_ref[:, here], grads)
        grad_v = term_v if grad_v is None else grad_v + term_v
        grad_k = term_k if grad_k is None else grad_k + term_k
        term = dot(kt_ref[...], grads)
        dq_ref[:, here] = term if first else refs[0][:, here] + term
    dkv_ref[dim:, :] = grad_v.astype(BF16)
    dkv_ref[0:dim, :] = grad_k.astype(BF16)


def project_grad_kernel(slots, rows, a_of, b_of, halves, fill_ref, go_ref, *refs):
    att, refs = refs[:slots], refs[slots + 1 :]
    live = live_column(fill_ref, rows)
    mixed = jnp.where(live > 0, go_ref[...].astype(F32), 0.0).astype(BF16)
    me = a_of()
    held = refs[-1]
    for slot in range(slots):
        held[me ^ slot] = dot(att[slot][...], mixed).astype(BF16)
    if not halves:
        refs[0][...] = held[...]
        return
    me = b_of()
    kept_ref, sent_ref = refs[0], refs[1]
    for pair in range(slots // 2):
        kept_ref[pair] = held[me ^ (2 * pair)]
        sent_ref[pair] = held[me ^ (2 * pair) ^ 1]


def project_kernel(slots, rows, a_of, fill_ref, w_ref, *refs):
    att, terms_ref = refs[:slots], refs[-1]
    me = a_of()
    total = None
    for slot in range(slots):
        term = dot(att[slot][...].astype(F32).T.astype(BF16), w_ref[me ^ slot])
        total = term if total is None else total + term
    terms_ref[...] = (total * live_column(fill_ref, rows)).astype(BF16)


def add_pairs_kernel(kept_ref, came_ref, _, first_ref, second_ref):
    for index, out_ref in enumerate((first_ref, second_ref)):
        out_ref[...] = (kept_ref[index].astype(F32) + came_ref[index].astype(F32)).astype(BF16)


def add_pieces_kernel(slots, rows, dim, kept_ref, came_ref, dq_ref, _, *outs):
    wide = 2 * dim
    for slot in range(slots):
        here = slice(slot * rows, (slot + 1) * rows)
        outs[slot][0:wide, :] = (kept_ref[:, here].astype(F32) + came_ref[:, here].astype(F32)).astype(BF16)
        outs[slot][wide:, :] = (dq_ref[:, here] * dim**-0.5).astype(BF16)


def add_out_kernel(a_ref, b_ref, out_ref, done_ref):
    out_ref[...] = (a_ref[...].astype(F32) + b_ref[...].astype(F32)).astype(out_ref.dtype)
    done_ref[...] = jnp.zeros_like(done_ref)


def add_kernel(a_ref, b_ref, *refs):
    refs[-1][...] = (a_ref[...].astype(F32) + b_ref[...].astype(F32)).astype(refs[-1].dtype)


def unpack_kernel(slots, rows, dim, a_of, *refs):
    pieces, (kv_out, q_out, held) = refs[:slots], refs[slots:]
    wide = 2 * dim
    me = a_of()
    for slot in range(slots):
        held[me ^ slot] = pieces[slot][0:wide, :].astype(F32).T
        q_out[me ^ slot] = pieces[slot][wide:, :].astype(F32)
    for head in range(slots):
        kv_out[:, head, :] = held[head]


def place_kernel(columns, b_of, *refs):
    parts, (out_ref,) = refs[:columns], refs[columns:]
    me = b_of()
    for column in range(columns):
        out_ref[me ^ column] = parts[column][...].astype(F32)


def shards(seq, mp, queries, key_value, tile_fill, out_weight, grad_output):
    rows, heads, dim = queries.shape
    width = grad_output.shape[1]
    slots = heads
    columns = seq // slots
    assert slots * columns == seq and columns & (columns - 1) == 0 and slots & (slots - 1) == 0
    a_of = lambda: lax.axis_index("seq") // columns
    b_of = lambda: lax.axis_index("seq") % columns

    def swap(array, mask, axis="seq", size=seq):
        return lax.ppermute(array, axis, [(i, i ^ mask) for i in range(size)])

    def exchange(pieces):
        came = {s: swap(pieces[s], s * columns) for s in sorted(range(1, slots), key=lambda s: (s < slots // 2, s))}
        return [pieces[0]] + [came[s] for s in range(1, slots)]

    block, wide = slots * rows, 2 * dim
    kv_mine = exchange(call(
        functools.partial(pack_kv_kernel, heads, rows, dim, a_of),
        [((rows, wide), BF16)] * slots, [pltpu.VMEM((heads, rows, wide), BF16)],
        n_in=2, smem_first=True, micros=1.5, limit=56,
    )(tile_fill, key_value))
    qg_send = call(
        functools.partial(pack_qg_kernel, heads, rows, dim, a_of),
        [((wide, rows), BF16)] * slots, [pltpu.VMEM((heads, wide, rows), BF16)],
        n_in=4, smem_first=True, micros=1,
    )(tile_fill, jnp.transpose(queries, (1, 2, 0)), out_weight, grad_output)
    qg_mine = exchange(qg_send)
    own = call(
        functools.partial(join_kernel, slots), [((block, wide), BF16)], n_in=slots, after=1,
    )(*kv_mine, qg_send[0])[0]

    blocks = {0: own}
    bit = columns // 2
    while bit:
        for r in sorted(blocks):
            blocks[r ^ bit] = swap(blocks[r], bit)
        bit //= 2

    qa, q_all, grads, q_norm = call(
        functools.partial(join_q_kernel, slots, rows, dim),
        [((2 * wide, block), BF16), ((dim, block), BF16), ((dim, block), BF16), ((1, block), F32)], n_in=slots,
    )(*qg_mine)
    step = min(block, 512)
    prepared, scored = {}, {}
    for r in range(columns):
        *prepared[r], values, norm = call(
            functools.partial(prep_kernel, dim),
            [((block, 2 * wide), BF16), ((dim, block), BF16), ((dim + 16, block), BF16), ((1, block), F32)],
        )(blocks[r])
        scored[r] = call(
            functools.partial(score_kernel, slots, rows, dim, step),
            [((block, block), BF16), ((1, block), F32), ((dim + 16, block), F32)],
            [pltpu.VMEM((block, rows), F32)], n_in=5, micros=1.5,
        )(prepared[r][0], values, norm, qa, q_norm)
    combined = call(
        functools.partial(combine_kernel, slots, columns, rows, dim),
        [((dim, rows), BF16)] * slots + [((1, block), F32)] * (columns + 1), n_in=2 * columns + 1,
    )(*[scored[r][1] for r in range(columns)], *[scored[r][2] for r in range(columns)], grads)
    att_mine, factors, inner = exchange(combined[:slots]), combined[slots:-1], combined[-1]

    halves = columns == heads == 4
    order = sorted(range(columns), key=lambda r: -int(f"{r:032b}"[::-1], 2))
    dkv, dq, terms, kept = {}, None, None, None
    for at, r in enumerate(order):
        later = []
        if at == columns // 2:
            weight_terms = call(
                functools.partial(project_grad_kernel, slots, rows, a_of, b_of, halves),
                [((2, dim, width), BF16)] * 2 if halves else [((heads, dim, width), BF16)],
                [pltpu.VMEM((heads, dim, width), BF16)],
                n_in=2 + slots, smem_first=True, after=1, micros=0.7,
            )(tile_fill, grad_output, *att_mine, dkv[order[at - 1]])
            terms = call(
                functools.partial(project_kernel, slots, rows, a_of), [((rows, width), BF16)],
                n_in=2 + slots, smem_first=True, after=1, micros=0.7,
            )(tile_fill, out_weight, *att_mine, weight_terms[-1])[0]
            later = [terms]
            if halves:
                kept, sent = call(add_pairs_kernel, [((dim, width), BF16)] * 2, n_in=2, after=1)(
                    weight_terms[0], swap(weight_terms[1], 1), terms)
                later = [kept]
        if at == columns - 1 and halves:
            kept = call(add_kernel, [((dim, width), BF16)], n_in=2, after=1)(kept, swap(sent, 2), dkv[order[at - 1]])[0]
            later = [kept]
        operands = [scored[r][0], *prepared[r], q_all, grads, factors[r], inner] + ([] if dq is None else [dq])
        dkv[r], dq = call(
            functools.partial(back_kernel, slots, rows, dim, dq is None),
            [((wide, block), BF16), ((dim, block), F32)], [pltpu.VMEM((2 * wide, block), BF16)],
            n_in=len(operands), after=len(later), micros=2,
        )(*operands, *later)

    bit, done = 1, terms
    while bit < mp:
        terms, done = call(add_out_kernel, [((rows, width), BF16), ((8, 128), F32)], n_in=2)(
            terms, swap(terms, bit, "mp", mp))
        bit *= 2

    dkv_last = dkv[order[-1]]
    bit = 1
    while 2 * bit < columns:
        dkv = {
            r: call(add_kernel, [((wide, block), BF16)], n_in=2)(dkv[r], swap(dkv[r ^ bit], bit))[0]
            for r in order if r in dkv and not r & bit
        }
        bit *= 2
    returned = exchange(call(
        functools.partial(add_pieces_kernel, slots, rows, dim), [((wide + dim, rows), BF16)] * slots, n_in=3, after=1,
    )(dkv[0], swap(dkv[bit], bit), dq, done))
    if halves:
        bit, last = columns, dkv_last
        while bit < seq:
            kept = call(add_kernel, [((dim, width), BF16)], n_in=2, after=1)(kept, swap(kept, bit), last)[0]
            bit *= 2
        across = swap(kept, 2)
        weight_grad = call(
            functools.partial(place_kernel, columns, b_of), [((heads, dim, width), F32)], n_in=columns, micros=0.5,
        )(kept, swap(kept, 1), across, swap(across, 1))[0]
    else:
        weight_grad = lax.psum(weight_terms[0].astype(F32), "seq")

    key_value_grad, query_grad = call(
        functools.partial(unpack_kernel, slots, rows, dim, a_of),
        [((rows, heads, wide), F32), ((heads, dim, rows), F32)],
        [pltpu.VMEM((heads, rows, wide), F32)], n_in=slots, micros=1,
    )(*returned)
    return terms, jnp.transpose(query_grad, (2, 0, 1)), key_value_grad, weight_grad


def solution(mesh):
    return jax.shard_map(
        functools.partial(shards, mesh.shape["seq"], mesh.shape["mp"]),
        mesh=mesh,
        in_specs=(
            P("seq", "mp", None),
            P("seq", "mp", None),
            P("seq"),
            P("mp", None, None),
            P("seq", None),
        ),
        out_specs=(P("seq", None), P("seq", "mp", None), P("seq", "mp", None), P("mp", None, None)),
        check_vma=False,
    )
```

```python
import functools

import jax
import jax.numpy as jnp
from jax import lax
from jax.experimental import pallas as pl
from jax.experimental.pallas import tpu as pltpu
from jax.sharding import PartitionSpec as P

TILE = 128
DEAD = 1024.0
BIAS = -1e30
LOG2_E = 1.4426950408889634
SAFE = 64.0
F32 = jnp.float32
BF16 = jnp.bfloat16
VMEM = pl.BlockSpec(memory_space=pltpu.VMEM)
SMEM = pl.BlockSpec(memory_space=pltpu.SMEM)
MIB = 1024 * 1024


def dot(a, b):
    return lax.dot_general(a, b, (((1,), (0,)), ((), ())), preferred_element_type=F32)


def dot_nt(a, b):
    return lax.dot_general(a, b, (((1,), (1,)), ((), ())), preferred_element_type=F32)


def call(kernel, outs, scratch=(), n_in=1, smem_first=False, after=0, micros=0.01, limit=16):
    specs = [SMEM if smem_first else VMEM] + [VMEM] * (n_in - 1) + [pl.BlockSpec(memory_space=pl.ANY)] * after
    return pl.pallas_call(
        kernel,
        out_shape=[jax.ShapeDtypeStruct(shape, kind) for shape, kind in outs],
        in_specs=specs,
        out_specs=[VMEM] * len(outs),
        scratch_shapes=list(scratch),
        compiler_params=pltpu.CompilerParams(vmem_limit_bytes=limit * MIB),
        cost_estimate=pl.CostEstimate(flops=int(micros * 1.15e9), bytes_accessed=0, transcendentals=0),
    )


def live_column(fill_ref, rows):
    parts = []
    within = lax.broadcasted_iota(jnp.int32, (TILE, 1), 0)
    for tile in range(rows // TILE):
        parts.append(jnp.where(within < fill_ref[tile], 1.0, 0.0))
    return jnp.concatenate(parts, axis=0) if len(parts) > 1 else parts[0]


def spread(slots):
    return [0] + sorted(range(1, slots), key=lambda mask: (mask < slots // 2, mask))


def pack_kv_kernel(heads, rows, dim, a_of, fill_ref, kv_ref, *refs):
    outs, (held,) = refs[:heads], refs[heads:]
    live = live_column(fill_ref, rows)
    lane = lax.broadcasted_iota(jnp.int32, (rows, 2 * dim), 1)
    mark = jnp.where(lane == 0, DEAD * (1.0 - live), 0.0).astype(BF16)
    live = live.astype(BF16)
    for head in range(heads):
        held[head] = kv_ref[:, head, :] * live + mark
    me = a_of()
    for slot, mask in enumerate(spread(heads)):
        outs[slot][...] = held[me ^ mask]


def pack_qg_kernel(heads, rows, dim, a_of, fill_ref, q_ref, w_ref, go_ref, *refs):
    outs, (held,) = refs[:heads], refs[heads:]
    mixed = go_ref[...] * live_column(fill_ref, rows).astype(BF16)
    grads = dot_nt(w_ref[...].reshape(heads * dim, mixed.shape[1]), mixed).astype(BF16)
    for head in range(heads):
        held[head, 0:dim, :] = (q_ref[head].astype(F32) * dim**-0.5).astype(BF16)
        held[head, dim:, :] = grads[head * dim : (head + 1) * dim, :]
    me = a_of()
    for slot, mask in enumerate(spread(heads)):
        outs[slot][...] = held[me ^ mask]


def join_kernel(pieces, *refs):
    out_ref = refs[-1]
    rows = refs[0].shape[0]
    for index in range(pieces):
        out_ref[index * rows : (index + 1) * rows, :] = refs[index][...]


def join_q_kernel(slots, rows, dim, *refs):
    pieces, (qa_ref, q_ref, g_ref, norm_ref) = refs[:slots], refs[slots:]
    wide = 2 * dim
    row = lax.broadcasted_iota(jnp.int32, (dim, slots * rows), 0)
    qa_ref[dim:wide, :] = jnp.zeros((dim, slots * rows), BF16)
    qa_ref[wide : wide + dim, :] = jnp.where(row == 0, 1.0, 0.0).astype(BF16)
    for slot in range(slots):
        here = slice(slot * rows, (slot + 1) * rows)
        queries = pieces[slot][0:dim, :]
        q_ref[:, here] = queries
        g_ref[:, here] = pieces[slot][dim:, :]
        scaled = queries.astype(F32) * LOG2_E
        high = scaled.astype(BF16)
        qa_ref[0:dim, here] = high
        qa_ref[wide + dim :, here] = (scaled - high.astype(F32)).astype(BF16)
        norm_ref[:, here] = jnp.sum(scaled * scaled, axis=0, keepdims=True)


def prep_kernel(dim, pair_ref, wide_ref, kt_ref, vt_ref, norm_ref):
    wide = 2 * dim
    keys = pair_ref.shape[0]
    pair = pair_ref[...]
    full = pair.astype(F32)
    lane = lax.broadcasted_iota(jnp.int32, (keys, wide), 1)
    ones = jnp.where(lane <= 2, 1.0, 0.0)
    bias = jnp.where(full[:, 0:1] >= DEAD, BIAS, 0.0)
    extra = jnp.where(lane == 0, bias, ones)
    wide_ref[:, 0:wide] = pair
    wide_ref[:, wide:] = jnp.where(lane < dim, extra, pltpu.roll(full, dim, 1)).astype(BF16)
    turned = full.T
    kt_ref[...] = turned[:dim, :].astype(BF16)
    vt_ref[0:dim, :] = turned[dim:, :].astype(BF16)
    vt_ref[dim:, :] = jnp.ones((16, keys), BF16)
    norm = jnp.sum(turned[:dim, :] * turned[:dim, :], axis=0, keepdims=True)
    norm_ref[...] = jnp.where(turned[0:1, :] >= DEAD, 0.0, norm)


def score_kernel(slots, rows, dim, step, wide_ref, vt_ref, norm_ref, qa_ref, q_norm_ref, exp_ref, peak_ref, total_ref, score_ref):
    keys = wide_ref.shape[0]
    small = jnp.max(norm_ref[...]) * jnp.max(q_norm_ref[...]) <= SAFE * SAFE

    @pl.when(small)
    def _():
        peak_ref[...] = jnp.zeros_like(peak_ref)
        ahead = dot(wide_ref[...], qa_ref[:, 0:rows])
        for slot in range(slots):
            here = slice(slot * rows, (slot + 1) * rows)
            scores = ahead
            if slot + 1 < slots:
                ahead = dot(wide_ref[...], qa_ref[:, (slot + 1) * rows : (slot + 2) * rows])
            exps = jnp.exp2(scores).astype(BF16)
            exp_ref[:, here] = exps
            total_ref[:, here] = dot(vt_ref[...], exps)

    @pl.when(jnp.logical_not(small))
    def _():
        for slot in range(slots):
            here = slice(slot * rows, (slot + 1) * rows)
            top = jnp.full((8, rows), BIAS, F32)
            for start in range(0, keys, step):
                part = slice(start, start + step)
                scores = dot(wide_ref[part, :], qa_ref[:, here])
                score_ref[part, :] = scores
                top = jnp.maximum(top, jnp.max(scores.reshape(step // 8, 8, rows), axis=0))
            peak = jnp.max(top, axis=0, keepdims=True)
            peak_ref[:, here] = peak
            total = jnp.zeros((dim + 16, rows), F32)
            for start in range(0, keys, step):
                part = slice(start, start + step)
                exps = jnp.exp2(score_ref[part, :] - peak).astype(BF16)
                exp_ref[part, here] = exps
                total = total + dot(vt_ref[:, part], exps)
            total_ref[:, here] = total


def combine_kernel(slots, columns, rows, dim, *refs):
    peaks, totals, (g_ref,), outs = refs[:columns], refs[columns : 2 * columns], refs[2 * columns : 2 * columns + 1], refs[2 * columns + 1 :]
    att_out, factors_out, inner_ref = outs[:slots], outs[slots : slots + columns], outs[-1]
    peak = functools.reduce(jnp.maximum, [ref[...] for ref in peaks])
    factors = [jnp.exp2(ref[...] - peak) for ref in peaks]
    total = sum(factor * ref[...] for factor, ref in zip(factors, totals))
    inverse = 1.0 / total[dim : dim + 1, :]
    attended = (total[0:dim, :] * inverse).astype(BF16)
    for slot in range(slots):
        att_out[slot][...] = attended[:, slot * rows : (slot + 1) * rows]
    for factor, ref in zip(factors, factors_out):
        ref[...] = factor * inverse
    inner_ref[...] = jnp.sum(g_ref[...].astype(F32) * attended.astype(F32), axis=0, keepdims=True)


def back_kernel(slots, rows, dim, first, exp_ref, wide_ref, kt_ref, q_ref, g_ref, factor_ref, inner_ref, *refs):
    dkv_ref, dq_ref, ga_ref = refs[-3:]
    wide = 2 * dim
    block = g_ref.shape[1]
    factor = factor_ref[...]
    inner = inner_ref[...] * factor
    high = inner.astype(BF16).astype(F32)
    row = lax.broadcasted_iota(jnp.int32, (dim, block), 0)
    ga_ref[0:dim, :] = jnp.zeros((dim, block), BF16)
    ga_ref[dim:wide, :] = (g_ref[...].astype(F32) * factor).astype(BF16)
    ga_ref[wide : wide + dim, :] = jnp.where(row == 1, -high, jnp.where(row == 2, high - inner, 0.0)).astype(BF16)
    ga_ref[wide + dim :, :] = jnp.zeros((dim, block), BF16)
    grad_k = grad_v = None
    ahead = dot(wide_ref[...], ga_ref[:, 0:rows])
    for slot in range(slots):
        here = slice(slot * rows, (slot + 1) * rows)
        products = ahead
        if slot + 1 < slots:
            ahead = dot(wide_ref[...], ga_ref[:, (slot + 1) * rows : (slot + 2) * rows])
        exps = exp_ref[:, here]
        grads = exps * products.astype(BF16)
        term_v = dot_nt(ga_ref[dim:wide, here], exps)
        term_k = dot_nt(q_ref[:, here], grads)
        grad_v = term_v if grad_v is None else grad_v + term_v
        grad_k = term_k if grad_k is None else grad_k + term_k
        term = dot(kt_ref[...], grads)
        dq_ref[:, here] = term if first else refs[0][:, here] + term
    dkv_ref[dim:, :] = grad_v.astype(BF16)
    dkv_ref[0:dim, :] = grad_k.astype(BF16)


def project_grad_kernel(slots, rows, a_of, b_of, halves, fill_ref, go_ref, *refs):
    att, refs = refs[:slots], refs[slots + 1 :]
    mixed = go_ref[...] * live_column(fill_ref, rows).astype(BF16)
    me = a_of()
    held = refs[-1]
    dim = held.shape[1]
    grads = dot(jnp.concatenate([ref[...] for ref in att], axis=0), mixed).astype(BF16)
    for slot, mask in enumerate(spread(slots)):
        held[me ^ mask] = grads[slot * dim : (slot + 1) * dim, :]
    if not halves:
        refs[0][...] = held[...]
        return
    me = b_of()
    kept_ref, sent_ref = refs[0], refs[1]
    for pair in range(slots // 2):
        kept_ref[pair] = held[me ^ (2 * pair)]
        sent_ref[pair] = held[me ^ (2 * pair) ^ 1]


def project_kernel(slots, rows, a_of, fill_ref, w_ref, *refs):
    att, terms_ref = refs[:slots], refs[-1]
    me = a_of()
    rows_in = jnp.concatenate([ref[...] for ref in att], axis=0).astype(F32).T.astype(BF16)
    weights = jnp.concatenate([w_ref[me ^ mask] for mask in spread(slots)], axis=0)
    terms_ref[...] = (dot(rows_in, weights) * live_column(fill_ref, rows)).astype(BF16)


def add_pairs_kernel(kept_ref, came_ref, _, first_ref, second_ref):
    for index, out_ref in enumerate((first_ref, second_ref)):
        out_ref[...] = (kept_ref[index].astype(F32) + came_ref[index].astype(F32)).astype(BF16)


def add_pieces_kernel(slots, rows, dim, kept_ref, came_ref, dq_ref, _, *outs):
    wide = 2 * dim
    for slot in range(slots):
        here = slice(slot * rows, (slot + 1) * rows)
        outs[slot][0:wide, :] = (kept_ref[:, here].astype(F32) + came_ref[:, here].astype(F32)).astype(BF16)
        outs[slot][wide:, :] = (dq_ref[:, here] * dim**-0.5).astype(BF16)


def add_out_kernel(a_ref, b_ref, out_ref, done_ref):
    out_ref[...] = (a_ref[...].astype(F32) + b_ref[...].astype(F32)).astype(out_ref.dtype)
    done_ref[...] = jnp.zeros_like(done_ref)


def add_kernel(a_ref, b_ref, *refs):
    refs[-1][...] = (a_ref[...].astype(F32) + b_ref[...].astype(F32)).astype(refs[-1].dtype)


def unpack_kernel(slots, rows, dim, a_of, *refs):
    pieces, (kv_out, q_out, held) = refs[:slots], refs[slots:]
    wide = 2 * dim
    me = a_of()
    for slot, mask in enumerate(spread(slots)):
        held[me ^ mask] = pieces[slot][0:wide, :].astype(F32).T
        q_out[me ^ mask] = pieces[slot][wide:, :].astype(F32)
    for head in range(slots):
        kv_out[:, head, :] = held[head]


def place_kernel(columns, b_of, *refs):
    parts, (out_ref,) = refs[:columns], refs[columns:]
    me = b_of()
    for column in range(columns):
        out_ref[me ^ column] = parts[column][...].astype(F32)


def shards(seq, mp, queries, key_value, tile_fill, out_weight, grad_output):
    rows, heads, dim = queries.shape
    width = grad_output.shape[1]
    slots = heads
    columns = seq // slots
    assert slots * columns == seq and columns & (columns - 1) == 0 and slots & (slots - 1) == 0
    a_of = lambda: lax.axis_index("seq") // columns
    b_of = lambda: lax.axis_index("seq") % columns

    def swap(array, mask, axis="seq", size=seq):
        return lax.ppermute(array, axis, [(i, i ^ mask) for i in range(size)])

    def exchange(pieces):
        return [pieces[0]] + [swap(piece, mask * columns) for piece, mask in zip(pieces[1:], spread(slots)[1:])]

    block, wide = slots * rows, 2 * dim
    kv_mine = exchange(call(
        functools.partial(pack_kv_kernel, heads, rows, dim, a_of),
        [((rows, wide), BF16)] * slots, [pltpu.VMEM((heads, rows, wide), BF16)],
        n_in=2, smem_first=True, micros=1.5, limit=56,
    )(tile_fill, key_value))
    qg_send = call(
        functools.partial(pack_qg_kernel, heads, rows, dim, a_of),
        [((wide, rows), BF16)] * slots, [pltpu.VMEM((heads, wide, rows), BF16)],
        n_in=4, smem_first=True, micros=1,
    )(tile_fill, jnp.transpose(queries, (1, 2, 0)), out_weight, grad_output)
    qg_mine = exchange(qg_send)
    own = call(
        functools.partial(join_kernel, slots), [((block, wide), BF16)], n_in=slots, after=1,
    )(*kv_mine, qg_mine[-1])[0]

    blocks = {0: own}
    bit = columns // 2
    while bit:
        for r in sorted(blocks):
            blocks[r ^ bit] = swap(blocks[r], bit)
        bit //= 2

    qa, q_all, grads, q_norm = call(
        functools.partial(join_q_kernel, slots, rows, dim),
        [((2 * wide, block), BF16), ((dim, block), BF16), ((dim, block), BF16), ((1, block), F32)], n_in=slots,
    )(*qg_mine)
    step = min(block, 512)
    prepared, scored = {}, {}
    for r in range(columns):
        *prepared[r], values, norm = call(
            functools.partial(prep_kernel, dim),
            [((block, 2 * wide), BF16), ((dim, block), BF16), ((dim + 16, block), BF16), ((1, block), F32)],
        )(blocks[r])
        scored[r] = call(
            functools.partial(score_kernel, slots, rows, dim, step),
            [((block, block), BF16), ((1, block), F32), ((dim + 16, block), F32)],
            [pltpu.VMEM((block, rows), F32)], n_in=5, micros=1.5,
        )(prepared[r][0], values, norm, qa, q_norm)
    combined = call(
        functools.partial(combine_kernel, slots, columns, rows, dim),
        [((dim, rows), BF16)] * slots + [((1, block), F32)] * (columns + 1), n_in=2 * columns + 1,
    )(*[scored[r][1] for r in range(columns)], *[scored[r][2] for r in range(columns)], grads)
    att_mine, factors, inner = exchange(combined[:slots]), combined[slots:-1], combined[-1]

    halves = columns == heads == 4
    order = sorted(range(columns), key=lambda r: -int(f"{r:032b}"[::-1], 2))
    dkv, dq, terms, kept = {}, None, None, None
    for at, r in enumerate(order):
        later = []
        if at == columns // 2:
            weight_terms = call(
                functools.partial(project_grad_kernel, slots, rows, a_of, b_of, halves),
                [((2, dim, width), BF16)] * 2 if halves else [((heads, dim, width), BF16)],
                [pltpu.VMEM((heads, dim, width), BF16)],
                n_in=2 + slots, smem_first=True, after=1, micros=0.7,
            )(tile_fill, grad_output, *att_mine, dkv[order[at - 1]])
            terms = call(
                functools.partial(project_kernel, slots, rows, a_of), [((rows, width), BF16)],
                n_in=2 + slots, smem_first=True, after=1, micros=0.7,
            )(tile_fill, out_weight, *att_mine, weight_terms[-1])[0]
            later = [terms]
            if halves:
                kept, sent = call(add_pairs_kernel, [((dim, width), BF16)] * 2, n_in=2, after=1)(
                    weight_terms[0], swap(weight_terms[1], 1), terms)
                later = [kept]
        if at == columns - 1 and halves:
            kept = call(add_kernel, [((dim, width), BF16)], n_in=2, after=1)(kept, swap(sent, 2), dkv[order[at - 1]])[0]
            later = [kept]
        operands = [scored[r][0], *prepared[r], q_all, grads, factors[r], inner] + ([] if dq is None else [dq])
        dkv[r], dq = call(
            functools.partial(back_kernel, slots, rows, dim, dq is None),
            [((wide, block), BF16), ((dim, block), F32)], [pltpu.VMEM((2 * wide, block), BF16)],
            n_in=len(operands), after=len(later), micros=2,
        )(*operands, *later)

    bit, done = 1, terms
    while bit < mp:
        terms, done = call(add_out_kernel, [((rows, width), BF16), ((8, 128), F32)], n_in=2)(
            terms, swap(terms, bit, "mp", mp))
        bit *= 2

    dkv_last = dkv[order[-1]]
    bit = 1
    while 2 * bit < columns:
        dkv = {
            r: call(add_kernel, [((wide, block), BF16)], n_in=2)(dkv[r], swap(dkv[r ^ bit], bit))[0]
            for r in order if r in dkv and not r & bit
        }
        bit *= 2
    returned = exchange(call(
        functools.partial(add_pieces_kernel, slots, rows, dim), [((wide + dim, rows), BF16)] * slots, n_in=3, after=1,
    )(dkv[0], swap(dkv[bit], bit), dq, done))
    if halves:
        for mask in [seq >> step for step in range(1, slots.bit_length())]:
            kept = call(add_kernel, [((dim, width), BF16)], n_in=2, after=1)(kept, swap(kept, mask), dkv_last)[0]
        across = swap(kept, 2)
        weight_grad = call(
            functools.partial(place_kernel, columns, b_of), [((heads, dim, width), F32)], n_in=columns, micros=0.5,
        )(kept, swap(kept, 1), across, swap(across, 1))[0]
    else:
        weight_grad = lax.psum(weight_terms[0].astype(F32), "seq")

    key_value_grad, query_grad = call(
        functools.partial(unpack_kernel, slots, rows, dim, a_of),
        [((rows, heads, wide), F32), ((heads, dim, rows), F32)],
        [pltpu.VMEM((heads, rows, wide), F32)], n_in=slots, micros=1,
    )(*returned)
    return terms, jnp.transpose(query_grad, (2, 0, 1)), key_value_grad, weight_grad


def solution(mesh):
    return jax.shard_map(
        functools.partial(shards, mesh.shape["seq"], mesh.shape["mp"]),
        mesh=mesh,
        in_specs=(
            P("seq", "mp", None),
            P("seq", "mp", None),
            P("seq"),
            P("mp", None, None),
            P("seq", None),
        ),
        out_specs=(P("seq", None), P("seq", "mp", None), P("seq", "mp", None), P("mp", None, None)),
        check_vma=False,
    )
```

```python
import functools

import jax
import jax.numpy as jnp
from jax import lax
from jax.experimental import pallas as pl
from jax.experimental.pallas import tpu as pltpu
from jax.sharding import PartitionSpec as P

TILE = 128
DEAD = 1024.0
BIAS = -1e30
LOG2_E = 1.4426950408889634
SAFE = 64.0
F32 = jnp.float32
BF16 = jnp.bfloat16
VMEM = pl.BlockSpec(memory_space=pltpu.VMEM)
SMEM = pl.BlockSpec(memory_space=pltpu.SMEM)
MIB = 1024 * 1024


def dot(a, b):
    return lax.dot_general(a, b, (((1,), (0,)), ((), ())), preferred_element_type=F32)


def dot_nt(a, b):
    return lax.dot_general(a, b, (((1,), (1,)), ((), ())), preferred_element_type=F32)


def call(kernel, outs, scratch=(), n_in=1, smem_first=False, after=0, micros=0.01, limit=16):
    specs = [SMEM if smem_first else VMEM] + [VMEM] * (n_in - 1) + [pl.BlockSpec(memory_space=pl.ANY)] * after
    return pl.pallas_call(
        kernel,
        out_shape=[jax.ShapeDtypeStruct(shape, kind) for shape, kind in outs],
        in_specs=specs,
        out_specs=[VMEM] * len(outs),
        scratch_shapes=list(scratch),
        compiler_params=pltpu.CompilerParams(vmem_limit_bytes=limit * MIB),
        cost_estimate=pl.CostEstimate(flops=int(micros * 1.15e9), bytes_accessed=0, transcendentals=0),
    )


def live_column(fill_ref, rows):
    parts = []
    within = lax.broadcasted_iota(jnp.int32, (TILE, 1), 0)
    for tile in range(rows // TILE):
        parts.append(jnp.where(within < fill_ref[tile], 1.0, 0.0))
    return jnp.concatenate(parts, axis=0) if len(parts) > 1 else parts[0]


def spread(slots):
    return [0] + sorted(range(1, slots), key=lambda mask: (mask < slots // 2, mask))


def pack_kv_kernel(heads, rows, dim, a_of, fill_ref, kv_ref, *refs):
    outs, (held,) = refs[:heads], refs[heads:]
    live = live_column(fill_ref, rows)
    lane = lax.broadcasted_iota(jnp.int32, (rows, 2 * dim), 1)
    mark = jnp.where(lane == 0, DEAD * (1.0 - live), 0.0).astype(BF16)
    live = live.astype(BF16)
    for head in range(heads):
        held[head] = kv_ref[:, head, :] * live + mark
    me = a_of()
    for slot, mask in enumerate(spread(heads)):
        outs[slot][...] = held[me ^ mask]


def pack_qg_kernel(heads, rows, dim, a_of, fill_ref, q_ref, w_ref, go_ref, *refs):
    outs, (held,) = refs[:heads], refs[heads:]
    mixed = go_ref[...] * live_column(fill_ref, rows).astype(BF16)
    grads = dot_nt(w_ref[...].reshape(heads * dim, mixed.shape[1]), mixed).astype(BF16)
    for head in range(heads):
        held[head, 0:dim, :] = (q_ref[head].astype(F32) * dim**-0.5).astype(BF16)
        held[head, dim:, :] = grads[head * dim : (head + 1) * dim, :]
    me = a_of()
    for slot, mask in enumerate(spread(heads)):
        outs[slot][...] = held[me ^ mask]


def join_kernel(pieces, *refs):
    out_ref = refs[-1]
    rows = refs[0].shape[0]
    for index in range(pieces):
        out_ref[index * rows : (index + 1) * rows, :] = refs[index][...]


def join_q_kernel(slots, rows, dim, *refs):
    pieces, (qa_ref, q_ref, g_ref, norm_ref) = refs[:slots], refs[slots:]
    wide = 2 * dim
    row = lax.broadcasted_iota(jnp.int32, (dim, slots * rows), 0)
    qa_ref[dim:wide, :] = jnp.zeros((dim, slots * rows), BF16)
    qa_ref[wide : wide + dim, :] = jnp.where(row == 0, 1.0, 0.0).astype(BF16)
    for slot in range(slots):
        here = slice(slot * rows, (slot + 1) * rows)
        queries = pieces[slot][0:dim, :]
        q_ref[:, here] = queries
        g_ref[:, here] = pieces[slot][dim:, :]
        scaled = queries.astype(F32) * LOG2_E
        high = scaled.astype(BF16)
        qa_ref[0:dim, here] = high
        qa_ref[wide + dim :, here] = (scaled - high.astype(F32)).astype(BF16)
        norm_ref[:, here] = jnp.sum(scaled * scaled, axis=0, keepdims=True)


def prep_kernel(dim, pair_ref, wide_ref, kt_ref, vt_ref, norm_ref):
    wide = 2 * dim
    keys = pair_ref.shape[0]
    pair = pair_ref[...]
    full = pair.astype(F32)
    lane = lax.broadcasted_iota(jnp.int32, (keys, wide), 1)
    ones = jnp.where(lane <= 2, 1.0, 0.0)
    bias = jnp.where(full[:, 0:1] >= DEAD, BIAS, 0.0)
    extra = jnp.where(lane == 0, bias, ones)
    wide_ref[:, 0:wide] = pair
    wide_ref[:, wide:] = jnp.where(lane < dim, extra, pltpu.roll(full, dim, 1)).astype(BF16)
    turned = full.T
    kt_ref[...] = turned[:dim, :].astype(BF16)
    vt_ref[0:dim, :] = turned[dim:, :].astype(BF16)
    vt_ref[dim:, :] = jnp.ones((16, keys), BF16)
    norm = jnp.sum(turned[:dim, :] * turned[:dim, :], axis=0, keepdims=True)
    norm_ref[...] = jnp.where(turned[0:1, :] >= DEAD, 0.0, norm)


def score_kernel(slots, rows, dim, step, wide_ref, vt_ref, norm_ref, qa_ref, q_norm_ref, exp_ref, peak_ref, total_ref, score_ref):
    keys = wide_ref.shape[0]
    small = jnp.max(norm_ref[...]) * jnp.max(q_norm_ref[...]) <= SAFE * SAFE

    @pl.when(small)
    def _():
        peak_ref[...] = jnp.zeros_like(peak_ref)
        ahead = dot(wide_ref[...], qa_ref[:, 0:rows])
        for slot in range(slots):
            here = slice(slot * rows, (slot + 1) * rows)
            scores = ahead
            if slot + 1 < slots:
                ahead = dot(wide_ref[...], qa_ref[:, (slot + 1) * rows : (slot + 2) * rows])
            exps = jnp.exp2(scores).astype(BF16)
            exp_ref[:, here] = exps
            total_ref[:, here] = dot(vt_ref[...], exps)

    @pl.when(jnp.logical_not(small))
    def _():
        for slot in range(slots):
            here = slice(slot * rows, (slot + 1) * rows)
            top = jnp.full((8, rows), BIAS, F32)
            for start in range(0, keys, step):
                part = slice(start, start + step)
                scores = dot(wide_ref[part, :], qa_ref[:, here])
                score_ref[part, :] = scores
                top = jnp.maximum(top, jnp.max(scores.reshape(step // 8, 8, rows), axis=0))
            peak = jnp.max(top, axis=0, keepdims=True)
            peak_ref[:, here] = peak
            total = jnp.zeros((dim + 16, rows), F32)
            for start in range(0, keys, step):
                part = slice(start, start + step)
                exps = jnp.exp2(score_ref[part, :] - peak).astype(BF16)
                exp_ref[part, here] = exps
                total = total + dot(vt_ref[:, part], exps)
            total_ref[:, here] = total


def combine_kernel(slots, columns, rows, dim, *refs):
    peaks, totals, (g_ref,), outs = refs[:columns], refs[columns : 2 * columns], refs[2 * columns : 2 * columns + 1], refs[2 * columns + 1 :]
    att_out, factors_out, inner_ref = outs[:slots], outs[slots : slots + columns], outs[-1]
    peak = functools.reduce(jnp.maximum, [ref[...] for ref in peaks])
    factors = [jnp.exp2(ref[...] - peak) for ref in peaks]
    total = sum(factor * ref[...] for factor, ref in zip(factors, totals))
    inverse = 1.0 / total[dim : dim + 1, :]
    attended = (total[0:dim, :] * inverse).astype(BF16)
    for slot in range(slots):
        att_out[slot][...] = attended[:, slot * rows : (slot + 1) * rows]
    for factor, ref in zip(factors, factors_out):
        ref[...] = factor * inverse
    inner_ref[...] = jnp.sum(g_ref[...].astype(F32) * attended.astype(F32), axis=0, keepdims=True)


def back_kernel(slots, rows, dim, first, exp_ref, wide_ref, kt_ref, q_ref, g_ref, factor_ref, inner_ref, *refs):
    dkv_ref, dq_ref, ga_ref = refs[-3:]
    wide = 2 * dim
    block = g_ref.shape[1]
    factor = factor_ref[...]
    inner = inner_ref[...] * factor
    high = inner.astype(BF16).astype(F32)
    row = lax.broadcasted_iota(jnp.int32, (dim, block), 0)
    ga_ref[0:dim, :] = jnp.zeros((dim, block), BF16)
    ga_ref[dim:wide, :] = (g_ref[...].astype(F32) * factor).astype(BF16)
    ga_ref[wide : wide + dim, :] = jnp.where(row == 1, -high, jnp.where(row == 2, high - inner, 0.0)).astype(BF16)
    ga_ref[wide + dim :, :] = jnp.zeros((dim, block), BF16)
    grad_k = grad_v = None
    ahead = dot(wide_ref[...], ga_ref[:, 0:rows])
    for slot in range(slots):
        here = slice(slot * rows, (slot + 1) * rows)
        products = ahead
        if slot + 1 < slots:
            ahead = dot(wide_ref[...], ga_ref[:, (slot + 1) * rows : (slot + 2) * rows])
        exps = exp_ref[:, here]
        grads = exps * products.astype(BF16)
        term_v = dot_nt(ga_ref[dim:wide, here], exps)
        term_k = dot_nt(q_ref[:, here], grads)
        grad_v = term_v if grad_v is None else grad_v + term_v
        grad_k = term_k if grad_k is None else grad_k + term_k
        term = dot(kt_ref[...], grads)
        dq_ref[:, here] = term if first else refs[0][:, here] + term
    dkv_ref[dim:, :] = grad_v.astype(BF16)
    dkv_ref[0:dim, :] = grad_k.astype(BF16)


def project_grad_kernel(slots, rows, a_of, b_of, halves, fill_ref, go_ref, *refs):
    att, refs = refs[:slots], refs[slots + 1 :]
    mixed = go_ref[...] * live_column(fill_ref, rows).astype(BF16)
    me = a_of()
    held = refs[-1]
    dim = held.shape[1]
    grads = dot(jnp.concatenate([ref[...] for ref in att], axis=0), mixed).astype(BF16)
    for slot, mask in enumerate(spread(slots)):
        held[me ^ mask] = grads[slot * dim : (slot + 1) * dim, :]
    if not halves:
        refs[0][...] = held[...]
        return
    me = b_of()
    kept_ref, sent_ref = refs[0], refs[1]
    for pair in range(slots // 2):
        kept_ref[pair] = held[me ^ (2 * pair)]
        sent_ref[pair] = held[me ^ (2 * pair) ^ 1]


def project_kernel(slots, rows, a_of, fill_ref, w_ref, *refs):
    att, terms_ref = refs[:slots], refs[-1]
    me = a_of()
    rows_in = jnp.concatenate([ref[...] for ref in att], axis=0).astype(F32).T.astype(BF16)
    weights = jnp.concatenate([w_ref[me ^ mask] for mask in spread(slots)], axis=0)
    terms_ref[...] = (dot(rows_in, weights) * live_column(fill_ref, rows)).astype(BF16)


def add_pairs_kernel(kept_ref, came_ref, _, first_ref, second_ref):
    for index, out_ref in enumerate((first_ref, second_ref)):
        out_ref[...] = (kept_ref[index].astype(F32) + came_ref[index].astype(F32)).astype(BF16)


def add_pieces_kernel(slots, rows, dim, kept_ref, came_ref, dq_ref, _, *outs):
    wide = 2 * dim
    for slot in range(slots):
        here = slice(slot * rows, (slot + 1) * rows)
        outs[slot][0:wide, :] = (kept_ref[:, here].astype(F32) + came_ref[:, here].astype(F32)).astype(BF16)
        outs[slot][wide:, :] = (dq_ref[:, here] * dim**-0.5).astype(BF16)


def add_out_kernel(a_ref, b_ref, out_ref, done_ref):
    out_ref[...] = (a_ref[...].astype(F32) + b_ref[...].astype(F32)).astype(out_ref.dtype)
    done_ref[...] = jnp.zeros_like(done_ref)


def add_kernel(a_ref, b_ref, *refs):
    refs[-1][...] = (a_ref[...].astype(F32) + b_ref[...].astype(F32)).astype(refs[-1].dtype)


def unpack_kernel(slots, rows, dim, a_of, *refs):
    pieces, (kv_out, q_out, held) = refs[:slots], refs[slots:]
    wide = 2 * dim
    me = a_of()
    for slot, mask in enumerate(spread(slots)):
        held[me ^ mask] = pieces[slot][0:wide, :].astype(F32).T
        q_out[me ^ mask] = pieces[slot][wide:, :].astype(F32)
    for head in range(slots):
        kv_out[:, head, :] = held[head]


def place_kernel(columns, b_of, *refs):
    parts, (out_ref,) = refs[:columns], refs[columns:]
    me = b_of()
    for column in range(columns):
        out_ref[me ^ column] = parts[column][...].astype(F32)


def shards(seq, mp, queries, key_value, tile_fill, out_weight, grad_output):
    rows, heads, dim = queries.shape
    width = grad_output.shape[1]
    slots = heads
    columns = seq // slots
    assert slots * columns == seq and columns & (columns - 1) == 0 and slots & (slots - 1) == 0
    a_of = lambda: lax.axis_index("seq") // columns
    b_of = lambda: lax.axis_index("seq") % columns

    def swap(array, mask, axis="seq", size=seq):
        return lax.ppermute(array, axis, [(i, i ^ mask) for i in range(size)])

    def exchange(pieces):
        return [pieces[0]] + [swap(piece, mask * columns) for piece, mask in zip(pieces[1:], spread(slots)[1:])]

    block, wide = slots * rows, 2 * dim
    kv_mine = exchange(call(
        functools.partial(pack_kv_kernel, heads, rows, dim, a_of),
        [((rows, wide), BF16)] * slots, [pltpu.VMEM((heads, rows, wide), BF16)],
        n_in=2, smem_first=True, micros=1.5, limit=56,
    )(tile_fill, key_value))
    qg_send = call(
        functools.partial(pack_qg_kernel, heads, rows, dim, a_of),
        [((wide, rows), BF16)] * slots, [pltpu.VMEM((heads, wide, rows), BF16)],
        n_in=4, smem_first=True, micros=1,
    )(tile_fill, jnp.transpose(queries, (1, 2, 0)), out_weight, grad_output)
    qg_mine = exchange(qg_send)
    own = call(
        functools.partial(join_kernel, slots), [((block, wide), BF16)], n_in=slots, after=1,
    )(*kv_mine, qg_send[0])[0]

    blocks = {0: own}
    bit = columns // 2
    while bit:
        for r in sorted(blocks):
            blocks[r ^ bit] = swap(blocks[r], bit)
        bit //= 2

    qa, q_all, grads, q_norm = call(
        functools.partial(join_q_kernel, slots, rows, dim),
        [((2 * wide, block), BF16), ((dim, block), BF16), ((dim, block), BF16), ((1, block), F32)], n_in=slots,
    )(*qg_mine)
    step = min(block, 512)
    prepared, scored = {}, {}
    for r in range(columns):
        *prepared[r], values, norm = call(
            functools.partial(prep_kernel, dim),
            [((block, 2 * wide), BF16), ((dim, block), BF16), ((dim + 16, block), BF16), ((1, block), F32)], micros=2,
        )(blocks[r])
        scored[r] = call(
            functools.partial(score_kernel, slots, rows, dim, step),
            [((block, block), BF16), ((1, block), F32), ((dim + 16, block), F32)],
            [pltpu.VMEM((block, rows), F32)], n_in=5, micros=4,
        )(prepared[r][0], values, norm, qa, q_norm)
    combined = call(
        functools.partial(combine_kernel, slots, columns, rows, dim),
        [((dim, rows), BF16)] * slots + [((1, block), F32)] * (columns + 1), n_in=2 * columns + 1,
    )(*[scored[r][1] for r in range(columns)], *[scored[r][2] for r in range(columns)], grads)
    att_mine, factors, inner = exchange(combined[:slots]), combined[slots:-1], combined[-1]

    halves = columns == heads == 4
    order = sorted(range(columns), key=lambda r: -int(f"{r:032b}"[::-1], 2))
    dkv, dq, terms, kept = {}, None, None, None
    for at, r in enumerate(order):
        later = []
        if at == columns // 2:
            weight_terms = call(
                functools.partial(project_grad_kernel, slots, rows, a_of, b_of, halves),
                [((2, dim, width), BF16)] * 2 if halves else [((heads, dim, width), BF16)],
                [pltpu.VMEM((heads, dim, width), BF16)],
                n_in=2 + slots, smem_first=True, after=1, micros=0.7,
            )(tile_fill, grad_output, *att_mine, dkv[order[at - 1]])
            terms = call(
                functools.partial(project_kernel, slots, rows, a_of), [((rows, width), BF16)],
                n_in=2 + slots, smem_first=True, after=1, micros=0.7,
            )(tile_fill, out_weight, *att_mine, weight_terms[-1])[0]
            later = [terms]
            if halves:
                kept, sent = call(add_pairs_kernel, [((dim, width), BF16)] * 2, n_in=2, after=1)(
                    weight_terms[0], swap(weight_terms[1], 1), terms)
                later = [kept]
        if at == columns - 1 and halves:
            kept = call(add_kernel, [((dim, width), BF16)], n_in=2, after=1)(kept, swap(sent, 2), dkv[order[at - 1]])[0]
            later = [kept]
        operands = [scored[r][0], *prepared[r], q_all, grads, factors[r], inner] + ([] if dq is None else [dq])
        dkv[r], dq = call(
            functools.partial(back_kernel, slots, rows, dim, dq is None),
            [((wide, block), BF16), ((dim, block), F32)], [pltpu.VMEM((2 * wide, block), BF16)],
            n_in=len(operands), after=len(later), micros=2,
        )(*operands, *later)

    bit, done = 1, terms
    while bit < mp:
        terms, done = call(add_out_kernel, [((rows, width), BF16), ((8, 128), F32)], n_in=2)(
            terms, swap(terms, bit, "mp", mp))
        bit *= 2

    dkv_last = dkv[order[-1]]
    bit = 1
    while 2 * bit < columns:
        dkv = {
            r: call(add_kernel, [((wide, block), BF16)], n_in=2)(dkv[r], swap(dkv[r ^ bit], bit))[0]
            for r in order if r in dkv and not r & bit
        }
        bit *= 2
    returned = exchange(call(
        functools.partial(add_pieces_kernel, slots, rows, dim), [((wide + dim, rows), BF16)] * slots, n_in=3, after=1,
    )(dkv[0], swap(dkv[bit], bit), dq, done))
    if halves:
        for mask in [seq >> step for step in range(1, slots.bit_length())]:
            kept = call(add_kernel, [((dim, width), BF16)], n_in=2, after=1)(kept, swap(kept, mask), dkv_last)[0]
        across = swap(kept, 2)
        weight_grad = call(
            functools.partial(place_kernel, columns, b_of), [((heads, dim, width), F32)], n_in=columns, micros=0.5,
        )(kept, swap(kept, 1), across, swap(across, 1))[0]
    else:
        weight_grad = lax.psum(weight_terms[0].astype(F32), "seq")

    key_value_grad, query_grad = call(
        functools.partial(unpack_kernel, slots, rows, dim, a_of),
        [((rows, heads, wide), F32), ((heads, dim, rows), F32)],
        [pltpu.VMEM((heads, rows, wide), F32)], n_in=slots, micros=1,
    )(*returned)
    return terms, jnp.transpose(query_grad, (2, 0, 1)), key_value_grad, weight_grad


def solution(mesh):
    return jax.shard_map(
        functools.partial(shards, mesh.shape["seq"], mesh.shape["mp"]),
        mesh=mesh,
        in_specs=(
            P("seq", "mp", None),
            P("seq", "mp", None),
            P("seq"),
            P("mp", None, None),
            P("seq", None),
        ),
        out_specs=(P("seq", None), P("seq", "mp", None), P("seq", "mp", None), P("mp", None, None)),
        check_vma=False,
    )
```

```python
import functools

import jax
import jax.numpy as jnp
from jax import lax
from jax.experimental import pallas as pl
from jax.experimental.pallas import tpu as pltpu
from jax.sharding import PartitionSpec as P

TILE = 128
DEAD = 1024.0
BIAS = -1e30
LOG2_E = 1.4426950408889634
SAFE = 64.0
F32 = jnp.float32
BF16 = jnp.bfloat16
VMEM = pl.BlockSpec(memory_space=pltpu.VMEM)
SMEM = pl.BlockSpec(memory_space=pltpu.SMEM)
MIB = 1024 * 1024


def dot(a, b):
    return lax.dot_general(a, b, (((1,), (0,)), ((), ())), preferred_element_type=F32)


def dot_nt(a, b):
    return lax.dot_general(a, b, (((1,), (1,)), ((), ())), preferred_element_type=F32)


def call(kernel, outs, scratch=(), n_in=1, smem_first=False, after=0, micros=0.01, limit=16):
    specs = [SMEM if smem_first else VMEM] + [VMEM] * (n_in - 1) + [pl.BlockSpec(memory_space=pl.ANY)] * after
    return pl.pallas_call(
        kernel,
        out_shape=[jax.ShapeDtypeStruct(shape, kind) for shape, kind in outs],
        in_specs=specs,
        out_specs=[VMEM] * len(outs),
        scratch_shapes=list(scratch),
        compiler_params=pltpu.CompilerParams(vmem_limit_bytes=limit * MIB),
        cost_estimate=pl.CostEstimate(flops=int(micros * 1.15e9), bytes_accessed=0, transcendentals=0),
    )


def live_column(fill_ref, rows):
    parts = []
    within = lax.broadcasted_iota(jnp.int32, (TILE, 1), 0)
    for tile in range(rows // TILE):
        parts.append(jnp.where(within < fill_ref[tile], 1.0, 0.0))
    return jnp.concatenate(parts, axis=0) if len(parts) > 1 else parts[0]


def spread(slots):
    return [0] + sorted(range(1, slots), key=lambda mask: (mask < slots // 2, mask))


def pack_kv_kernel(heads, rows, dim, a_of, fill_ref, kv_ref, *refs):
    outs, (held,) = refs[:heads], refs[heads:]
    live = live_column(fill_ref, rows)
    lane = lax.broadcasted_iota(jnp.int32, (rows, 2 * dim), 1)
    mark = jnp.where(lane == 0, DEAD * (1.0 - live), 0.0).astype(BF16)
    live = live.astype(BF16)
    for head in range(heads):
        held[head] = kv_ref[:, head, :] * live + mark
    me = a_of()
    for slot, mask in enumerate(spread(heads)):
        outs[slot][...] = held[me ^ mask]


def pack_qg_kernel(heads, rows, dim, a_of, fill_ref, q_ref, w_ref, go_ref, *refs):
    outs, (held,) = refs[:heads], refs[heads:]
    mixed = go_ref[...] * live_column(fill_ref, rows).astype(BF16)
    grads = dot_nt(w_ref[...].reshape(heads * dim, mixed.shape[1]), mixed).astype(BF16)
    for head in range(heads):
        held[head, 0:dim, :] = (q_ref[head].astype(F32) * dim**-0.5).astype(BF16)
        held[head, dim:, :] = grads[head * dim : (head + 1) * dim, :]
    me = a_of()
    for slot, mask in enumerate(spread(heads)):
        outs[slot][...] = held[me ^ mask]


def join_kernel(pieces, *refs):
    out_ref = refs[-1]
    rows = refs[0].shape[0]
    for index in range(pieces):
        out_ref[index * rows : (index + 1) * rows, :] = refs[index][...]


def join_q_kernel(slots, rows, dim, *refs):
    pieces, (qa_ref, q_ref, g_ref, norm_ref) = refs[:slots], refs[slots:]
    wide = 2 * dim
    row = lax.broadcasted_iota(jnp.int32, (dim, slots * rows), 0)
    qa_ref[dim:wide, :] = jnp.zeros((dim, slots * rows), BF16)
    qa_ref[wide : wide + dim, :] = jnp.where(row == 0, 1.0, 0.0).astype(BF16)
    for slot in range(slots):
        here = slice(slot * rows, (slot + 1) * rows)
        queries = pieces[slot][0:dim, :]
        q_ref[:, here] = queries
        g_ref[:, here] = pieces[slot][dim:, :]
        scaled = queries.astype(F32) * LOG2_E
        high = scaled.astype(BF16)
        qa_ref[0:dim, here] = high
        qa_ref[wide + dim :, here] = (scaled - high.astype(F32)).astype(BF16)
        norm_ref[:, here] = jnp.sum(scaled * scaled, axis=0, keepdims=True)


def prep_kernel(dim, pair_ref, wide_ref, kt_ref, vt_ref, norm_ref):
    wide = 2 * dim
    keys = pair_ref.shape[0]
    pair = pair_ref[...]
    full = pair.astype(F32)
    lane = lax.broadcasted_iota(jnp.int32, (keys, wide), 1)
    ones = jnp.where(lane <= 2, 1.0, 0.0)
    bias = jnp.where(full[:, 0:1] >= DEAD, BIAS, 0.0)
    extra = jnp.where(lane == 0, bias, ones)
    wide_ref[:, 0:wide] = pair
    wide_ref[:, wide:] = jnp.where(lane < dim, extra, pltpu.roll(full, dim, 1)).astype(BF16)
    turned = full.T
    kt_ref[...] = turned[:dim, :].astype(BF16)
    vt_ref[0:dim, :] = turned[dim:, :].astype(BF16)
    vt_ref[dim:, :] = jnp.ones((16, keys), BF16)
    norm = jnp.sum(turned[:dim, :] * turned[:dim, :], axis=0, keepdims=True)
    norm_ref[...] = jnp.where(turned[0:1, :] >= DEAD, 0.0, norm)


def score_kernel(slots, rows, dim, step, wide_ref, vt_ref, norm_ref, qa_ref, q_norm_ref, exp_ref, peak_ref, total_ref, score_ref):
    keys = wide_ref.shape[0]
    small = jnp.max(norm_ref[...]) * jnp.max(q_norm_ref[...]) <= SAFE * SAFE

    @pl.when(small)
    def _():
        peak_ref[...] = jnp.zeros_like(peak_ref)
        ahead = dot(wide_ref[...], qa_ref[:, 0:rows])
        for slot in range(slots):
            here = slice(slot * rows, (slot + 1) * rows)
            scores = ahead
            if slot + 1 < slots:
                ahead = dot(wide_ref[...], qa_ref[:, (slot + 1) * rows : (slot + 2) * rows])
            exps = jnp.exp2(scores).astype(BF16)
            exp_ref[:, here] = exps
            total_ref[:, here] = dot(vt_ref[...], exps)

    @pl.when(jnp.logical_not(small))
    def _():
        for slot in range(slots):
            here = slice(slot * rows, (slot + 1) * rows)
            top = jnp.full((8, rows), BIAS, F32)
            for start in range(0, keys, step):
                part = slice(start, start + step)
                scores = dot(wide_ref[part, :], qa_ref[:, here])
                score_ref[part, :] = scores
                top = jnp.maximum(top, jnp.max(scores.reshape(step // 8, 8, rows), axis=0))
            peak = jnp.max(top, axis=0, keepdims=True)
            peak_ref[:, here] = peak
            total = jnp.zeros((dim + 16, rows), F32)
            for start in range(0, keys, step):
                part = slice(start, start + step)
                exps = jnp.exp2(score_ref[part, :] - peak).astype(BF16)
                exp_ref[part, here] = exps
                total = total + dot(vt_ref[:, part], exps)
            total_ref[:, here] = total


def combine_kernel(slots, columns, rows, dim, *refs):
    peaks, totals, (g_ref,), outs = refs[:columns], refs[columns : 2 * columns], refs[2 * columns : 2 * columns + 1], refs[2 * columns + 1 :]
    att_out, factors_out, inner_ref = outs[:slots], outs[slots : slots + columns], outs[-1]
    peak = functools.reduce(jnp.maximum, [ref[...] for ref in peaks])
    factors = [jnp.exp2(ref[...] - peak) for ref in peaks]
    total = sum(factor * ref[...] for factor, ref in zip(factors, totals))
    inverse = 1.0 / total[dim : dim + 1, :]
    attended = (total[0:dim, :] * inverse).astype(BF16)
    for slot in range(slots):
        att_out[slot][...] = attended[:, slot * rows : (slot + 1) * rows]
    for factor, ref in zip(factors, factors_out):
        ref[...] = factor * inverse
    inner_ref[...] = jnp.sum(g_ref[...].astype(F32) * attended.astype(F32), axis=0, keepdims=True)


def back_kernel(slots, rows, dim, first, exp_ref, wide_ref, kt_ref, q_ref, g_ref, factor_ref, inner_ref, *refs):
    dkv_ref, dq_ref, ga_ref = refs[-3:]
    wide = 2 * dim
    block = g_ref.shape[1]
    factor = factor_ref[...]
    inner = inner_ref[...] * factor
    high = inner.astype(BF16).astype(F32)
    row = lax.broadcasted_iota(jnp.int32, (dim, block), 0)
    ga_ref[0:dim, :] = jnp.zeros((dim, block), BF16)
    ga_ref[dim:wide, :] = (g_ref[...].astype(F32) * factor).astype(BF16)
    ga_ref[wide : wide + dim, :] = jnp.where(row == 1, -high, jnp.where(row == 2, high - inner, 0.0)).astype(BF16)
    ga_ref[wide + dim :, :] = jnp.zeros((dim, block), BF16)
    grad_k = grad_v = None
    ahead = dot(wide_ref[...], ga_ref[:, 0:rows])
    for slot in range(slots):
        here = slice(slot * rows, (slot + 1) * rows)
        products = ahead
        if slot + 1 < slots:
            ahead = dot(wide_ref[...], ga_ref[:, (slot + 1) * rows : (slot + 2) * rows])
        exps = exp_ref[:, here]
        grads = exps * products.astype(BF16)
        term_v = dot_nt(ga_ref[dim:wide, here], exps)
        term_k = dot_nt(q_ref[:, here], grads)
        grad_v = term_v if grad_v is None else grad_v + term_v
        grad_k = term_k if grad_k is None else grad_k + term_k
        term = dot(kt_ref[...], grads)
        dq_ref[:, here] = term if first else refs[0][:, here] + term
    dkv_ref[dim:, :] = grad_v.astype(BF16)
    dkv_ref[0:dim, :] = grad_k.astype(BF16)


def project_grad_kernel(slots, rows, a_of, b_of, halves, fill_ref, go_ref, *refs):
    att, refs = refs[:slots], refs[slots + 1 :]
    mixed = go_ref[...] * live_column(fill_ref, rows).astype(BF16)
    me = a_of()
    held = refs[-1]
    dim = held.shape[1]
    grads = dot(jnp.concatenate([ref[...] for ref in att], axis=0), mixed).astype(BF16)
    for slot, mask in enumerate(spread(slots)):
        held[me ^ mask] = grads[slot * dim : (slot + 1) * dim, :]
    if not halves:
        refs[0][...] = held[...]
        return
    me = b_of()
    kept_ref, sent_ref = refs[0], refs[1]
    for pair in range(slots // 2):
        kept_ref[pair] = held[me ^ (2 * pair)]
        sent_ref[pair] = held[me ^ (2 * pair) ^ 1]


def project_kernel(slots, rows, a_of, fill_ref, w_ref, *refs):
    att, terms_ref = refs[:slots], refs[-1]
    me = a_of()
    rows_in = jnp.concatenate([ref[...] for ref in att], axis=0).astype(F32).T.astype(BF16)
    weights = jnp.concatenate([w_ref[me ^ mask] for mask in spread(slots)], axis=0)
    terms_ref[...] = (dot(rows_in, weights) * live_column(fill_ref, rows)).astype(BF16)


def add_pairs_kernel(kept_ref, came_ref, _, first_ref, second_ref):
    for index, out_ref in enumerate((first_ref, second_ref)):
        out_ref[...] = (kept_ref[index].astype(F32) + came_ref[index].astype(F32)).astype(BF16)


def add_pieces_kernel(slots, rows, dim, kept_ref, came_ref, dq_ref, *outs):
    wide = 2 * dim
    for slot in range(slots):
        here = slice(slot * rows, (slot + 1) * rows)
        outs[slot][0:wide, :] = (kept_ref[:, here].astype(F32) + came_ref[:, here].astype(F32)).astype(BF16)
        outs[slot][wide:, :] = (dq_ref[:, here] * dim**-0.5).astype(BF16)


def add_kernel(a_ref, b_ref, *refs):
    refs[-1][...] = (a_ref[...].astype(F32) + b_ref[...].astype(F32)).astype(refs[-1].dtype)


def unpack_kernel(slots, rows, dim, a_of, *refs):
    pieces, (kv_out, q_out, held) = refs[:slots], refs[slots:]
    wide = 2 * dim
    me = a_of()
    for slot, mask in enumerate(spread(slots)):
        held[me ^ mask] = pieces[slot][0:wide, :].astype(F32).T
        q_out[me ^ mask] = pieces[slot][wide:, :].astype(F32)
    for head in range(slots):
        kv_out[:, head, :] = held[head]


def place_kernel(columns, b_of, *refs):
    parts, (out_ref,) = refs[:columns], refs[columns:]
    me = b_of()
    for column in range(columns):
        out_ref[me ^ column] = parts[column][...].astype(F32)


def shards(seq, mp, queries, key_value, tile_fill, out_weight, grad_output):
    rows, heads, dim = queries.shape
    width = grad_output.shape[1]
    slots = heads
    columns = seq // slots
    assert slots * columns == seq and columns & (columns - 1) == 0 and slots & (slots - 1) == 0
    a_of = lambda: lax.axis_index("seq") // columns
    b_of = lambda: lax.axis_index("seq") % columns

    def swap(array, mask, axis="seq", size=seq):
        return lax.ppermute(array, axis, [(i, i ^ mask) for i in range(size)])

    def exchange(pieces):
        return [pieces[0]] + [swap(piece, mask * columns) for piece, mask in zip(pieces[1:], spread(slots)[1:])]

    block, wide = slots * rows, 2 * dim
    kv_mine = exchange(call(
        functools.partial(pack_kv_kernel, heads, rows, dim, a_of),
        [((rows, wide), BF16)] * slots, [pltpu.VMEM((heads, rows, wide), BF16)],
        n_in=2, smem_first=True, micros=1.5, limit=56,
    )(tile_fill, key_value))
    qg_send = call(
        functools.partial(pack_qg_kernel, heads, rows, dim, a_of),
        [((wide, rows), BF16)] * slots, [pltpu.VMEM((heads, wide, rows), BF16)],
        n_in=4, smem_first=True, micros=1,
    )(tile_fill, jnp.transpose(queries, (1, 2, 0)), out_weight, grad_output)
    qg_mine = exchange(qg_send)
    own = call(
        functools.partial(join_kernel, slots), [((block, wide), BF16)], n_in=slots, after=1,
    )(*kv_mine, qg_send[0])[0]

    blocks = {0: own}
    bit = columns // 2
    while bit:
        for r in sorted(blocks):
            blocks[r ^ bit] = swap(blocks[r], bit)
        bit //= 2

    qa, q_all, grads, q_norm = call(
        functools.partial(join_q_kernel, slots, rows, dim),
        [((2 * wide, block), BF16), ((dim, block), BF16), ((dim, block), BF16), ((1, block), F32)], n_in=slots,
    )(*qg_mine)
    step = min(block, 512)
    prepared, scored = {}, {}
    for r in range(columns):
        *prepared[r], values, norm = call(
            functools.partial(prep_kernel, dim),
            [((block, 2 * wide), BF16), ((dim, block), BF16), ((dim + 16, block), BF16), ((1, block), F32)], micros=2,
        )(blocks[r])
        scored[r] = call(
            functools.partial(score_kernel, slots, rows, dim, step),
            [((block, block), BF16), ((1, block), F32), ((dim + 16, block), F32)],
            [pltpu.VMEM((block, rows), F32)], n_in=5, micros=4,
        )(prepared[r][0], values, norm, qa, q_norm)
    combined = call(
        functools.partial(combine_kernel, slots, columns, rows, dim),
        [((dim, rows), BF16)] * slots + [((1, block), F32)] * (columns + 1), n_in=2 * columns + 1,
    )(*[scored[r][1] for r in range(columns)], *[scored[r][2] for r in range(columns)], grads)
    att_mine, factors, inner = exchange(combined[:slots]), combined[slots:-1], combined[-1]

    halves = columns == heads == 4
    order = sorted(range(columns), reverse=True)
    add = call(add_kernel, [((dim, width), BF16)], n_in=2, after=1)
    add_halves = call(add_kernel, [((wide, block), BF16)], n_in=2)
    far_masks = [seq >> level for level in range(1, slots.bit_length())]
    dkv, dq, kept, summed, later = {}, None, None, {}, []
    for at, r in enumerate(order):
        if at and not halves and at == columns - 1 or halves and at == 1:
            weight_terms = call(
                functools.partial(project_grad_kernel, slots, rows, a_of, b_of, halves),
                [((2, dim, width), BF16)] * 2 if halves else [((heads, dim, width), BF16)],
                [pltpu.VMEM((heads, dim, width), BF16)],
                n_in=2 + slots, smem_first=True, after=1, micros=0.7,
            )(tile_fill, grad_output, *att_mine, dkv[order[at - 1]])
            terms = call(
                functools.partial(project_kernel, slots, rows, a_of), [((rows, width), BF16)],
                n_in=2 + slots, smem_first=True, after=1, micros=0.7,
            )(tile_fill, out_weight, *att_mine, weight_terms[-1])[0]
            later = [terms]
            if halves:
                kept, sent = call(add_pairs_kernel, [((dim, width), BF16)] * 2, n_in=2, after=1)(
                    weight_terms[0], swap(weight_terms[1], 1), terms)
                later = [kept]
        if at == 2 and halves:
            kept = add(kept, swap(sent, 2), dkv[order[at - 1]])[0]
            later = [kept]
        if at == 3 and halves:
            kept = add(kept, swap(kept, far_masks[0]), dkv[order[at - 1]])[0]
            later = [kept, summed[2]]
        operands = [scored[r][0], *prepared[r], q_all, grads, factors[r], inner] + ([] if dq is None else [dq])
        dkv[r], dq = call(
            functools.partial(back_kernel, slots, rows, dim, dq is None),
            [((wide, block), BF16), ((dim, block), F32)], [pltpu.VMEM((2 * wide, block), BF16)],
            n_in=len(operands), after=len(later), micros=2,
        )(*operands, *later)
        later = []
        if columns == 4 and r == 2:
            summed[2] = swap(add_halves(dkv[2], swap(dkv[3], 1))[0], 2)

    attention_out = lax.psum(terms, "mp") if mp > 1 else terms

    if columns == 4:
        halved = add_halves(dkv[0], swap(dkv[1], 1))[0], summed[2]
    else:
        bit = 1
        while 2 * bit < columns:
            dkv = {r: add_halves(dkv[r], swap(dkv[r ^ bit], bit))[0] for r in order if r in dkv and not r & bit}
            bit *= 2
        halved = dkv[0], swap(dkv[bit], bit)
    pieces = call(
        functools.partial(add_pieces_kernel, slots, rows, dim), [((wide + dim, rows), BF16)] * slots, n_in=3,
    )(*halved, dq)
    returned = exchange(pieces)

    if halves:
        for mask in far_masks[1:]:
            kept = add(kept, swap(kept, mask), dkv[0])[0]
        across = swap(kept, 2)
        weight_grad = call(
            functools.partial(place_kernel, columns, b_of), [((heads, dim, width), F32)], n_in=columns, micros=0.5,
        )(kept, swap(kept, 1), across, swap(across, 1))[0]
    else:
        weight_grad = lax.psum(weight_terms[0].astype(F32), "seq")

    key_value_grad, query_grad = call(
        functools.partial(unpack_kernel, slots, rows, dim, a_of),
        [((rows, heads, wide), F32), ((heads, dim, rows), F32)],
        [pltpu.VMEM((heads, rows, wide), F32)], n_in=slots, micros=1,
    )(*returned)
    return attention_out, jnp.transpose(query_grad, (2, 0, 1)), key_value_grad, weight_grad


def solution(mesh):
    return jax.shard_map(
        functools.partial(shards, mesh.shape["seq"], mesh.shape["mp"]),
        mesh=mesh,
        in_specs=(
            P("seq", "mp", None),
            P("seq", "mp", None),
            P("seq"),
            P("mp", None, None),
            P("seq", None),
        ),
        out_specs=(P("seq", None), P("seq", "mp", None), P("seq", "mp", None), P("mp", None, None)),
        check_vma=False,
    )
```

```python
import functools

import jax
import jax.numpy as jnp
from jax import lax
from jax.experimental import pallas as pl
from jax.experimental.pallas import tpu as pltpu
from jax.sharding import PartitionSpec as P

TILE = 128
DEAD = 1024.0
BIAS = -1e30
LOG2_E = 1.4426950408889634
SAFE = 64.0
F32 = jnp.float32
BF16 = jnp.bfloat16
VMEM = pl.BlockSpec(memory_space=pltpu.VMEM)
SMEM = pl.BlockSpec(memory_space=pltpu.SMEM)
MIB = 1024 * 1024


def dot(a, b):
    return lax.dot_general(a, b, (((1,), (0,)), ((), ())), preferred_element_type=F32)


def dot_nt(a, b):
    return lax.dot_general(a, b, (((1,), (1,)), ((), ())), preferred_element_type=F32)


def call(kernel, outs, scratch=(), n_in=1, smem_first=False, after=0, micros=0.01, limit=16):
    specs = [SMEM if smem_first else VMEM] + [VMEM] * (n_in - 1) + [pl.BlockSpec(memory_space=pl.ANY)] * after
    return pl.pallas_call(
        kernel,
        out_shape=[jax.ShapeDtypeStruct(shape, kind) for shape, kind in outs],
        in_specs=specs,
        out_specs=[VMEM] * len(outs),
        scratch_shapes=list(scratch),
        compiler_params=pltpu.CompilerParams(vmem_limit_bytes=limit * MIB),
        cost_estimate=pl.CostEstimate(flops=int(micros * 1.15e9), bytes_accessed=0, transcendentals=0),
    )


def live_column(fill_ref, rows):
    parts = []
    within = lax.broadcasted_iota(jnp.int32, (TILE, 1), 0)
    for tile in range(rows // TILE):
        parts.append(jnp.where(within < fill_ref[tile], 1.0, 0.0))
    return jnp.concatenate(parts, axis=0) if len(parts) > 1 else parts[0]


def spread(slots):
    return [0] + sorted(range(1, slots), key=lambda mask: (mask < slots // 2, mask))


def pack_kv_kernel(heads, rows, dim, a_of, fill_ref, kv_ref, *refs):
    outs, (held,) = refs[:heads], refs[heads:]
    live = live_column(fill_ref, rows)
    lane = lax.broadcasted_iota(jnp.int32, (rows, 2 * dim), 1)
    mark = jnp.where(lane == 0, DEAD * (1.0 - live), 0.0)
    held[...] = kv_ref[...].astype(F32)
    me = a_of()
    for slot, mask in enumerate(spread(heads)):
        outs[slot][...] = (held[pl.ds(me ^ mask, rows, stride=heads), :] * live + mark).astype(BF16)


def pack_qg_kernel(heads, rows, dim, a_of, fill_ref, q_ref, w_ref, go_ref, *refs):
    outs, (held,) = refs[:heads], refs[heads:]
    mixed = go_ref[...] * live_column(fill_ref, rows).astype(BF16)
    grads = dot_nt(w_ref[...].reshape(heads * dim, mixed.shape[1]), mixed).astype(BF16)
    for head in range(heads):
        held[head, 0:dim, :] = (q_ref[head].astype(F32) * dim**-0.5).astype(BF16)
        held[head, dim:, :] = grads[head * dim : (head + 1) * dim, :]
    me = a_of()
    for slot, mask in enumerate(spread(heads)):
        outs[slot][...] = held[me ^ mask]


def join_kernel(pieces, *refs):
    out_ref = refs[-1]
    rows = refs[0].shape[0]
    for index in range(pieces):
        out_ref[index * rows : (index + 1) * rows, :] = refs[index][...]


def join_q_kernel(slots, rows, dim, *refs):
    pieces, (qa_ref, q_ref, g_ref, norm_ref) = refs[:slots], refs[slots:]
    wide = 2 * dim
    row = lax.broadcasted_iota(jnp.int32, (dim, slots * rows), 0)
    qa_ref[dim:wide, :] = jnp.zeros((dim, slots * rows), BF16)
    qa_ref[wide : wide + dim, :] = jnp.where(row == 0, 1.0, 0.0).astype(BF16)
    for slot in range(slots):
        here = slice(slot * rows, (slot + 1) * rows)
        queries = pieces[slot][0:dim, :]
        q_ref[:, here] = queries
        g_ref[:, here] = pieces[slot][dim:, :]
        scaled = queries.astype(F32) * LOG2_E
        high = scaled.astype(BF16)
        qa_ref[0:dim, here] = high
        qa_ref[wide + dim :, here] = (scaled - high.astype(F32)).astype(BF16)
        norm_ref[:, here] = jnp.sum(scaled * scaled, axis=0, keepdims=True)


def prep_kernel(dim, pair_ref, *refs):
    wide_ref, kt_ref, vt_ref, norm_ref = refs[-4:]
    wide = 2 * dim
    keys = pair_ref.shape[0]
    pair = pair_ref[...]
    full = pair.astype(F32)
    lane = lax.broadcasted_iota(jnp.int32, (keys, wide), 1)
    ones = jnp.where(lane <= 2, 1.0, 0.0)
    bias = jnp.where(full[:, 0:1] >= DEAD, BIAS, 0.0)
    extra = jnp.where(lane == 0, bias, ones)
    wide_ref[:, 0:wide] = pair
    wide_ref[:, wide:] = jnp.where(lane < dim, extra, pltpu.roll(full, dim, 1)).astype(BF16)
    turned = full.T
    kt_ref[...] = turned[:dim, :].astype(BF16)
    vt_ref[0:dim, :] = turned[dim:, :].astype(BF16)
    vt_ref[dim:, :] = jnp.ones((16, keys), BF16)
    norm = jnp.sum(turned[:dim, :] * turned[:dim, :], axis=0, keepdims=True)
    norm_ref[...] = jnp.where(turned[0:1, :] >= DEAD, 0.0, norm)


def score_kernel(slots, rows, dim, step, wide_ref, vt_ref, norm_ref, qa_ref, q_norm_ref, exp_ref, peak_ref, total_ref, score_ref):
    keys = wide_ref.shape[0]
    small = jnp.max(norm_ref[...]) * jnp.max(q_norm_ref[...]) <= SAFE * SAFE

    @pl.when(small)
    def _():
        peak_ref[...] = jnp.zeros_like(peak_ref)
        ahead = dot(wide_ref[...], qa_ref[:, 0:rows])
        for slot in range(slots):
            here = slice(slot * rows, (slot + 1) * rows)
            scores = ahead
            if slot + 1 < slots:
                ahead = dot(wide_ref[...], qa_ref[:, (slot + 1) * rows : (slot + 2) * rows])
            exps = jnp.exp2(scores).astype(BF16)
            exp_ref[:, here] = exps
            total_ref[:, here] = dot(vt_ref[...], exps)

    @pl.when(jnp.logical_not(small))
    def _():
        for slot in range(slots):
            here = slice(slot * rows, (slot + 1) * rows)
            top = jnp.full((8, rows), BIAS, F32)
            for start in range(0, keys, step):
                part = slice(start, start + step)
                scores = dot(wide_ref[part, :], qa_ref[:, here])
                score_ref[part, :] = scores
                top = jnp.maximum(top, jnp.max(scores.reshape(step // 8, 8, rows), axis=0))
            peak = jnp.max(top, axis=0, keepdims=True)
            peak_ref[:, here] = peak
            total = jnp.zeros((dim + 16, rows), F32)
            for start in range(0, keys, step):
                part = slice(start, start + step)
                exps = jnp.exp2(score_ref[part, :] - peak).astype(BF16)
                exp_ref[part, here] = exps
                total = total + dot(vt_ref[:, part], exps)
            total_ref[:, here] = total


def combine_kernel(slots, columns, rows, dim, *refs):
    peaks, totals, (g_ref,), outs = refs[:columns], refs[columns : 2 * columns], refs[2 * columns : 2 * columns + 1], refs[2 * columns + 1 :]
    att_out, factors_out, inner_ref = outs[:slots], outs[slots : slots + columns], outs[-1]
    peak = functools.reduce(jnp.maximum, [ref[...] for ref in peaks])
    factors = [jnp.exp2(ref[...] - peak) for ref in peaks]
    total = sum(factor * ref[...] for factor, ref in zip(factors, totals))
    inverse = 1.0 / total[dim : dim + 1, :]
    attended = (total[0:dim, :] * inverse).astype(BF16)
    for slot in range(slots):
        att_out[slot][...] = attended[:, slot * rows : (slot + 1) * rows]
    for factor, ref in zip(factors, factors_out):
        ref[...] = factor * inverse
    inner_ref[...] = jnp.sum(g_ref[...].astype(F32) * attended.astype(F32), axis=0, keepdims=True)


def back_kernel(slots, rows, dim, first, exp_ref, wide_ref, kt_ref, q_ref, g_ref, factor_ref, inner_ref, *refs):
    dkv_ref, dq_ref, ga_ref = refs[-3:]
    wide = 2 * dim
    block = g_ref.shape[1]
    factor = factor_ref[...]
    inner = inner_ref[...] * factor
    high = inner.astype(BF16).astype(F32)
    row = lax.broadcasted_iota(jnp.int32, (dim, block), 0)
    ga_ref[0:dim, :] = jnp.zeros((dim, block), BF16)
    ga_ref[dim:wide, :] = (g_ref[...].astype(F32) * factor).astype(BF16)
    ga_ref[wide : wide + dim, :] = jnp.where(row == 1, -high, jnp.where(row == 2, high - inner, 0.0)).astype(BF16)
    ga_ref[wide + dim :, :] = jnp.zeros((dim, block), BF16)
    grad_k = grad_v = None
    ahead = dot(wide_ref[...], ga_ref[:, 0:rows])
    for slot in range(slots):
        here = slice(slot * rows, (slot + 1) * rows)
        products = ahead
        if slot + 1 < slots:
            ahead = dot(wide_ref[...], ga_ref[:, (slot + 1) * rows : (slot + 2) * rows])
        exps = exp_ref[:, here]
        grads = exps * products.astype(BF16)
        term_v = dot_nt(ga_ref[dim:wide, here], exps)
        term_k = dot_nt(q_ref[:, here], grads)
        grad_v = term_v if grad_v is None else grad_v + term_v
        grad_k = term_k if grad_k is None else grad_k + term_k
        term = dot(kt_ref[...], grads)
        dq_ref[:, here] = term if first else refs[0][:, here] + term
    dkv_ref[dim:, :] = grad_v.astype(BF16)
    dkv_ref[0:dim, :] = grad_k.astype(BF16)


def project_grad_kernel(slots, rows, a_of, b_of, halves, fill_ref, go_ref, *refs):
    att, refs = refs[:slots], refs[slots + 1 :]
    mixed = go_ref[...] * live_column(fill_ref, rows).astype(BF16)
    me = a_of()
    held = refs[-1]
    dim = held.shape[1]
    grads = dot(jnp.concatenate([ref[...] for ref in att], axis=0), mixed).astype(BF16)
    for slot, mask in enumerate(spread(slots)):
        held[me ^ mask] = grads[slot * dim : (slot + 1) * dim, :]
    if not halves:
        refs[0][...] = held[...]
        return
    me = b_of()
    kept_ref, sent_ref = refs[0], refs[1]
    for pair in range(slots // 2):
        kept_ref[pair] = held[me ^ (2 * pair)]
        sent_ref[pair] = held[me ^ (2 * pair) ^ 1]


def project_kernel(slots, rows, a_of, fill_ref, w_ref, *refs):
    att, terms_ref = refs[:slots], refs[-1]
    me = a_of()
    rows_in = jnp.concatenate([ref[...] for ref in att], axis=0).astype(F32).T.astype(BF16)
    weights = jnp.concatenate([w_ref[me ^ mask] for mask in spread(slots)], axis=0)
    terms_ref[...] = (dot(rows_in, weights) * live_column(fill_ref, rows)).astype(BF16)


def add_pairs_kernel(kept_ref, came_ref, _, first_ref, second_ref):
    for index, out_ref in enumerate((first_ref, second_ref)):
        out_ref[...] = (kept_ref[index].astype(F32) + came_ref[index].astype(F32)).astype(BF16)


def add_pieces_kernel(slots, rows, dim, kept_ref, came_ref, dq_ref, *outs):
    wide = 2 * dim
    for slot in range(slots):
        here = slice(slot * rows, (slot + 1) * rows)
        outs[slot][0:wide, :] = (kept_ref[:, here].astype(F32) + came_ref[:, here].astype(F32)).astype(BF16)
        outs[slot][wide:, :] = (dq_ref[:, here] * dim**-0.5).astype(BF16)


def add_out_kernel(a_ref, b_ref, out_ref, done_ref):
    out_ref[...] = (a_ref[...].astype(F32) + b_ref[...].astype(F32)).astype(out_ref.dtype)
    done_ref[...] = jnp.zeros_like(done_ref)


def add_kernel(a_ref, b_ref, *refs):
    refs[-1][...] = (a_ref[...].astype(F32) + b_ref[...].astype(F32)).astype(refs[-1].dtype)


def unpack_kernel(slots, rows, dim, a_of, *refs):
    pieces, (kv_out, q_out) = refs[:slots], refs[-2:]
    wide = 2 * dim
    me = a_of()
    for slot, mask in enumerate(spread(slots)):
        kv_out[pl.ds(me ^ mask, rows, stride=slots), :] = pieces[slot][0:wide, :].astype(F32).T
        q_out[me ^ mask] = pieces[slot][wide:, :].astype(F32)


def place_kernel(columns, b_of, *refs):
    parts, (out_ref,) = refs[:columns], refs[columns:]
    me = b_of()
    for column in range(columns):
        out_ref[me ^ column] = parts[column][...].astype(F32)


def shards(seq, mp, queries, key_value, tile_fill, out_weight, grad_output):
    rows, heads, dim = queries.shape
    width = grad_output.shape[1]
    slots = heads
    columns = seq // slots
    assert slots * columns == seq and columns & (columns - 1) == 0 and slots & (slots - 1) == 0
    a_of = lambda: lax.axis_index("seq") // columns
    b_of = lambda: lax.axis_index("seq") % columns

    def swap(array, mask, axis="seq", size=seq):
        return lax.ppermute(array, axis, [(i, i ^ mask) for i in range(size)])

    def exchange(pieces):
        return [pieces[0]] + [swap(piece, mask * columns) for piece, mask in zip(pieces[1:], spread(slots)[1:])]

    block, wide = slots * rows, 2 * dim
    kv_mine = exchange(call(
        functools.partial(pack_kv_kernel, heads, rows, dim, a_of),
        [((rows, wide), BF16)] * slots, [pltpu.VMEM((rows * heads, wide), F32)],
        n_in=2, smem_first=True, micros=1.5, limit=56,
    )(tile_fill, key_value.reshape(rows * heads, wide)))
    qg_send = call(
        functools.partial(pack_qg_kernel, heads, rows, dim, a_of),
        [((wide, rows), BF16)] * slots, [pltpu.VMEM((heads, wide, rows), BF16)],
        n_in=4, smem_first=True, micros=1,
    )(tile_fill, jnp.transpose(queries, (1, 2, 0)), out_weight, grad_output)
    qg_mine = exchange(qg_send)
    own = call(
        functools.partial(join_kernel, slots), [((block, wide), BF16)], n_in=slots, after=1,
    )(*kv_mine, qg_send[0])[0]

    blocks = {0: own}
    bit = columns // 2
    while bit:
        for r in sorted(blocks):
            blocks[r ^ bit] = swap(blocks[r], bit)
        bit //= 2

    qa, q_all, grads, q_norm = call(
        functools.partial(join_q_kernel, slots, rows, dim),
        [((2 * wide, block), BF16), ((dim, block), BF16), ((dim, block), BF16), ((1, block), F32)], n_in=slots,
    )(*qg_mine)
    step = min(block, 512)
    prepared, scored = {}, {}
    for r in range(columns):
        *prepared[r], values, norm = call(
            functools.partial(prep_kernel, dim),
            [((block, 2 * wide), BF16), ((dim, block), BF16), ((dim + 16, block), BF16), ((1, block), F32)],
            after=min(r, 1), micros=2,
        )(blocks[r], *([scored[r - 1][1]] if r else []))
        scored[r] = call(
            functools.partial(score_kernel, slots, rows, dim, step),
            [((block, block), BF16), ((1, block), F32), ((dim + 16, block), F32)],
            [pltpu.VMEM((block, rows), F32)], n_in=5, micros=4,
        )(prepared[r][0], values, norm, qa, q_norm)
    combined = call(
        functools.partial(combine_kernel, slots, columns, rows, dim),
        [((dim, rows), BF16)] * slots + [((1, block), F32)] * (columns + 1), n_in=2 * columns + 1,
    )(*[scored[r][1] for r in range(columns)], *[scored[r][2] for r in range(columns)], grads)
    att_mine, factors, inner = exchange(combined[:slots]), combined[slots:-1], combined[-1]

    halves = columns == heads == 4
    order = sorted(range(columns), reverse=True)
    add = call(add_kernel, [((dim, width), BF16)], n_in=2, after=1)
    add_halves = call(add_kernel, [((wide, block), BF16)], n_in=2)
    far_masks = [seq >> level for level in range(1, slots.bit_length())]
    dkv, dq, kept, summed, later = {}, None, None, {}, []
    for at, r in enumerate(order):
        if at and not halves and at == columns - 1 or halves and at == 1:
            weight_terms = call(
                functools.partial(project_grad_kernel, slots, rows, a_of, b_of, halves),
                [((2, dim, width), BF16)] * 2 if halves else [((heads, dim, width), BF16)],
                [pltpu.VMEM((heads, dim, width), BF16)],
                n_in=2 + slots, smem_first=True, after=1, micros=0.7,
            )(tile_fill, grad_output, *att_mine, dkv[order[at - 1]])
            terms = call(
                functools.partial(project_kernel, slots, rows, a_of), [((rows, width), BF16)],
                n_in=2 + slots, smem_first=True, after=1, micros=0.7,
            )(tile_fill, out_weight, *att_mine, weight_terms[-1])[0]
            later, bit, done = [terms], 1, terms
            first_terms = terms
            while bit < mp:
                terms, done = call(add_out_kernel, [((rows, width), BF16), ((8, 128), F32)], n_in=2)(
                    terms, swap(terms, bit, "mp", mp))
                bit *= 2
            if halves:
                kept, sent = call(add_pairs_kernel, [((dim, width), BF16)] * 2, n_in=2, after=1)(
                    weight_terms[0], swap(weight_terms[1], 1), first_terms)
                later = [kept]
        if at == 2 and halves:
            kept = add(kept, swap(sent, 2), dkv[order[at - 1]])[0]
            later = [kept]
        if at == 3 and halves:
            kept = add(kept, swap(kept, far_masks[0]), dkv[order[at - 1]])[0]
            later = [kept, summed[2], done]
        operands = [scored[r][0], *prepared[r], q_all, grads, factors[r], inner] + ([] if dq is None else [dq])
        dkv[r], dq = call(
            functools.partial(back_kernel, slots, rows, dim, dq is None),
            [((wide, block), BF16), ((dim, block), F32)], [pltpu.VMEM((2 * wide, block), BF16)],
            n_in=len(operands), after=len(later), micros=2,
        )(*operands, *later)
        later = []
        if columns == 4 and r == 2:
            summed[2] = swap(add_halves(dkv[2], swap(dkv[3], 1))[0], 2)

    if columns == 4:
        halved = add_halves(dkv[0], swap(dkv[1], 1))[0], summed[2]
    else:
        bit = 1
        while 2 * bit < columns:
            dkv = {r: add_halves(dkv[r], swap(dkv[r ^ bit], bit))[0] for r in order if r in dkv and not r & bit}
            bit *= 2
        halved = dkv[0], swap(dkv[bit], bit)
    pieces = call(
        functools.partial(add_pieces_kernel, slots, rows, dim), [((wide + dim, rows), BF16)] * slots, n_in=3,
    )(*halved, dq)
    returned = exchange(pieces)

    if halves:
        for mask in far_masks[1:]:
            kept = add(kept, swap(kept, mask), pieces[0])[0]
        across = swap(kept, 2)
        weight_grad = call(
            functools.partial(place_kernel, columns, b_of), [((heads, dim, width), F32)], n_in=columns, micros=0.5,
        )(kept, swap(kept, 1), across, swap(across, 1))[0]
    else:
        weight_grad = lax.psum(weight_terms[0].astype(F32), "seq")

    key_value_grad, query_grad = call(
        functools.partial(unpack_kernel, slots, rows, dim, a_of),
        [((rows * heads, wide), F32), ((heads, dim, rows), F32)],
        n_in=slots, micros=1,
    )(*returned)
    return terms, jnp.transpose(query_grad, (2, 0, 1)), key_value_grad.reshape(rows, heads, wide), weight_grad


def solution(mesh):
    return jax.shard_map(
        functools.partial(shards, mesh.shape["seq"], mesh.shape["mp"]),
        mesh=mesh,
        in_specs=(
            P("seq", "mp", None),
            P("seq", "mp", None),
            P("seq"),
            P("mp", None, None),
            P("seq", None),
        ),
        out_specs=(P("seq", None), P("seq", "mp", None), P("seq", "mp", None), P("mp", None, None)),
        check_vma=False,
    )
```

```python
import functools

import jax
import jax.numpy as jnp
from jax import lax
from jax.experimental import pallas as pl
from jax.experimental.pallas import tpu as pltpu
from jax.sharding import PartitionSpec as P

TILE = 128
DEAD = 1024.0
BIAS = -1e30
LOG2_E = 1.4426950408889634
SAFE = 64.0
F32 = jnp.float32
BF16 = jnp.bfloat16
VMEM = pl.BlockSpec(memory_space=pltpu.VMEM)
SMEM = pl.BlockSpec(memory_space=pltpu.SMEM)
MIB = 1024 * 1024


def dot(a, b):
    return lax.dot_general(a, b, (((1,), (0,)), ((), ())), preferred_element_type=F32)


def dot_nt(a, b):
    return lax.dot_general(a, b, (((1,), (1,)), ((), ())), preferred_element_type=F32)


def call(kernel, outs, scratch=(), n_in=1, smem_first=False, after=0, micros=0.01, limit=16):
    specs = [SMEM if smem_first else VMEM] + [VMEM] * (n_in - 1) + [pl.BlockSpec(memory_space=pl.ANY)] * after
    return pl.pallas_call(
        kernel,
        out_shape=[jax.ShapeDtypeStruct(shape, kind) for shape, kind in outs],
        in_specs=specs,
        out_specs=[VMEM] * len(outs),
        scratch_shapes=list(scratch),
        compiler_params=pltpu.CompilerParams(vmem_limit_bytes=limit * MIB),
        cost_estimate=pl.CostEstimate(flops=int(micros * 1.15e9), bytes_accessed=0, transcendentals=0),
    )


def live_column(fill_ref, rows):
    parts = []
    within = lax.broadcasted_iota(jnp.int32, (TILE, 1), 0)
    for tile in range(rows // TILE):
        parts.append(jnp.where(within < fill_ref[tile], 1.0, 0.0))
    return jnp.concatenate(parts, axis=0) if len(parts) > 1 else parts[0]


def spread(slots):
    return [0] + sorted(range(1, slots), key=lambda mask: (mask < slots // 2, mask))


def pack_kv_kernel(heads, rows, dim, a_of, fill_ref, kv_ref, *refs):
    outs, (held,) = refs[:heads], refs[heads:]
    live = live_column(fill_ref, rows)
    lane = lax.broadcasted_iota(jnp.int32, (rows, 2 * dim), 1)
    mark = jnp.where(lane == 0, DEAD * (1.0 - live), 0.0)
    held[...] = kv_ref[...].astype(F32)
    me = a_of()
    for slot, mask in enumerate(spread(heads)):
        outs[slot][...] = (held[pl.ds(me ^ mask, rows, stride=heads), :] * live + mark).astype(BF16)


def pack_qg_kernel(heads, rows, dim, a_of, fill_ref, q_ref, w_ref, go_ref, *refs):
    outs, (held,) = refs[:heads], refs[heads:]
    mixed = go_ref[...] * live_column(fill_ref, rows).astype(BF16)
    grads = dot_nt(w_ref[...].reshape(heads * dim, mixed.shape[1]), mixed).astype(BF16)
    for head in range(heads):
        held[head, 0:dim, :] = (q_ref[head].astype(F32) * dim**-0.5).astype(BF16)
        held[head, dim:, :] = grads[head * dim : (head + 1) * dim, :]
    me = a_of()
    for slot, mask in enumerate(spread(heads)):
        outs[slot][...] = held[me ^ mask]


def join_kernel(pieces, *refs):
    out_ref = refs[-1]
    rows = refs[0].shape[0]
    for index in range(pieces):
        out_ref[index * rows : (index + 1) * rows, :] = refs[index][...]


def join_q_kernel(slots, rows, dim, *refs):
    pieces, (qa_ref, q_ref, g_ref, norm_ref) = refs[:slots], refs[slots:]
    wide = 2 * dim
    row = lax.broadcasted_iota(jnp.int32, (dim, slots * rows), 0)
    qa_ref[dim:wide, :] = jnp.zeros((dim, slots * rows), BF16)
    qa_ref[wide : wide + dim, :] = jnp.where(row == 0, 1.0, 0.0).astype(BF16)
    for slot in range(slots):
        here = slice(slot * rows, (slot + 1) * rows)
        queries = pieces[slot][0:dim, :]
        q_ref[:, here] = queries
        g_ref[:, here] = pieces[slot][dim:, :]
        scaled = queries.astype(F32) * LOG2_E
        high = scaled.astype(BF16)
        qa_ref[0:dim, here] = high
        qa_ref[wide + dim :, here] = (scaled - high.astype(F32)).astype(BF16)
        norm_ref[:, here] = jnp.sum(scaled * scaled, axis=0, keepdims=True)


def prep_kernel(dim, pair_ref, *refs):
    wide_ref, kt_ref, vt_ref, norm_ref = refs[-4:]
    wide = 2 * dim
    keys = pair_ref.shape[0]
    pair = pair_ref[...]
    full = pair.astype(F32)
    lane = lax.broadcasted_iota(jnp.int32, (keys, wide), 1)
    ones = jnp.where(lane <= 2, 1.0, 0.0)
    bias = jnp.where(full[:, 0:1] >= DEAD, BIAS, 0.0)
    extra = jnp.where(lane == 0, bias, ones)
    wide_ref[:, 0:wide] = pair
    wide_ref[:, wide:] = jnp.where(lane < dim, extra, pltpu.roll(full, dim, 1)).astype(BF16)
    turned = full.T
    kt_ref[...] = turned[:dim, :].astype(BF16)
    vt_ref[0:dim, :] = turned[dim:, :].astype(BF16)
    vt_ref[dim:, :] = jnp.ones((16, keys), BF16)
    norm = jnp.sum(turned[:dim, :] * turned[:dim, :], axis=0, keepdims=True)
    norm_ref[...] = jnp.where(turned[0:1, :] >= DEAD, 0.0, norm)


def score_kernel(slots, rows, dim, step, wide_ref, vt_ref, norm_ref, qa_ref, q_norm_ref, exp_ref, peak_ref, total_ref, score_ref):
    keys = wide_ref.shape[0]
    small = jnp.max(norm_ref[...]) * jnp.max(q_norm_ref[...]) <= SAFE * SAFE

    @pl.when(small)
    def _():
        peak_ref[...] = jnp.zeros_like(peak_ref)
        ahead = dot(wide_ref[...], qa_ref[:, 0:rows])
        for slot in range(slots):
            here = slice(slot * rows, (slot + 1) * rows)
            scores = ahead
            if slot + 1 < slots:
                ahead = dot(wide_ref[...], qa_ref[:, (slot + 1) * rows : (slot + 2) * rows])
            exps = jnp.exp2(scores).astype(BF16)
            exp_ref[:, here] = exps
            total_ref[:, here] = dot(vt_ref[...], exps)

    @pl.when(jnp.logical_not(small))
    def _():
        for slot in range(slots):
            here = slice(slot * rows, (slot + 1) * rows)
            top = jnp.full((8, rows), BIAS, F32)
            for start in range(0, keys, step):
                part = slice(start, start + step)
                scores = dot(wide_ref[part, :], qa_ref[:, here])
                score_ref[part, :] = scores
                top = jnp.maximum(top, jnp.max(scores.reshape(step // 8, 8, rows), axis=0))
            peak = jnp.max(top, axis=0, keepdims=True)
            peak_ref[:, here] = peak
            total = jnp.zeros((dim + 16, rows), F32)
            for start in range(0, keys, step):
                part = slice(start, start + step)
                exps = jnp.exp2(score_ref[part, :] - peak).astype(BF16)
                exp_ref[part, here] = exps
                total = total + dot(vt_ref[:, part], exps)
            total_ref[:, here] = total


def combine_kernel(slots, columns, rows, dim, *refs):
    peaks, totals, (g_ref,), outs = refs[:columns], refs[columns : 2 * columns], refs[2 * columns : 2 * columns + 1], refs[2 * columns + 1 :]
    att_out, factors_out, inner_ref = outs[:slots], outs[slots : slots + columns], outs[-1]
    peak = functools.reduce(jnp.maximum, [ref[...] for ref in peaks])
    factors = [jnp.exp2(ref[...] - peak) for ref in peaks]
    total = sum(factor * ref[...] for factor, ref in zip(factors, totals))
    inverse = 1.0 / total[dim : dim + 1, :]
    attended = (total[0:dim, :] * inverse).astype(BF16)
    for slot in range(slots):
        att_out[slot][...] = attended[:, slot * rows : (slot + 1) * rows]
    for factor, ref in zip(factors, factors_out):
        ref[...] = factor * inverse
    inner_ref[...] = jnp.sum(g_ref[...].astype(F32) * attended.astype(F32), axis=0, keepdims=True)


def back_kernel(slots, rows, dim, first, exp_ref, wide_ref, kt_ref, q_ref, g_ref, factor_ref, inner_ref, *refs):
    dkv_ref, dq_ref, ga_ref = refs[-3:]
    wide = 2 * dim
    block = g_ref.shape[1]
    factor = factor_ref[...]
    inner = inner_ref[...] * factor
    high = inner.astype(BF16).astype(F32)
    row = lax.broadcasted_iota(jnp.int32, (dim, block), 0)
    ga_ref[0:dim, :] = jnp.zeros((dim, block), BF16)
    ga_ref[dim:wide, :] = (g_ref[...].astype(F32) * factor).astype(BF16)
    ga_ref[wide : wide + dim, :] = jnp.where(row == 1, -high, jnp.where(row == 2, high - inner, 0.0)).astype(BF16)
    ga_ref[wide + dim :, :] = jnp.zeros((dim, block), BF16)
    grad_k = grad_v = None
    ahead = dot(wide_ref[...], ga_ref[:, 0:rows])
    for slot in range(slots):
        here = slice(slot * rows, (slot + 1) * rows)
        products = ahead
        if slot + 1 < slots:
            ahead = dot(wide_ref[...], ga_ref[:, (slot + 1) * rows : (slot + 2) * rows])
        exps = exp_ref[:, here]
        grads = exps * products.astype(BF16)
        term_v = dot_nt(ga_ref[dim:wide, here], exps)
        term_k = dot_nt(q_ref[:, here], grads)
        grad_v = term_v if grad_v is None else grad_v + term_v
        grad_k = term_k if grad_k is None else grad_k + term_k
        term = dot(kt_ref[...], grads)
        dq_ref[:, here] = term if first else refs[0][:, here] + term
    dkv_ref[dim:, :] = grad_v.astype(BF16)
    dkv_ref[0:dim, :] = grad_k.astype(BF16)


def project_grad_kernel(slots, rows, a_of, b_of, halves, fill_ref, go_ref, *refs):
    att, refs = refs[:slots], refs[slots + 1 :]
    mixed = go_ref[...] * live_column(fill_ref, rows).astype(BF16)
    me = a_of()
    held = refs[-1]
    dim = held.shape[1]
    grads = dot(jnp.concatenate([ref[...] for ref in att], axis=0), mixed).astype(BF16)
    for slot, mask in enumerate(spread(slots)):
        held[me ^ mask] = grads[slot * dim : (slot + 1) * dim, :]
    if not halves:
        refs[0][...] = held[...]
        return
    me = b_of()
    kept_ref, sent_ref = refs[0], refs[1]
    for pair in range(slots // 2):
        kept_ref[pair] = held[me ^ (2 * pair)]
        sent_ref[pair] = held[me ^ (2 * pair) ^ 1]


def project_kernel(slots, rows, a_of, fill_ref, w_ref, *refs):
    att, terms_ref = refs[:slots], refs[-1]
    me = a_of()
    rows_in = jnp.concatenate([ref[...] for ref in att], axis=0).astype(F32).T.astype(BF16)
    weights = jnp.concatenate([w_ref[me ^ mask] for mask in spread(slots)], axis=0)
    terms_ref[...] = (dot(rows_in, weights) * live_column(fill_ref, rows)).astype(BF16)


def add_pairs_kernel(kept_ref, came_ref, _, first_ref, second_ref):
    for index, out_ref in enumerate((first_ref, second_ref)):
        out_ref[...] = (kept_ref[index].astype(F32) + came_ref[index].astype(F32)).astype(BF16)


def add_pieces_kernel(slots, rows, dim, a_of, kept_ref, came_ref, dq_ref, out_ref):
    wide = 2 * dim
    me = a_of()
    for slot, mask in enumerate(spread(slots)):
        here = slice(slot * rows, (slot + 1) * rows)
        out_ref[me ^ mask, 0:wide, :] = (kept_ref[:, here].astype(F32) + came_ref[:, here].astype(F32)).astype(BF16)
        out_ref[me ^ mask, wide:, :] = (dq_ref[:, here] * dim**-0.5).astype(BF16)


def add_out_kernel(a_ref, b_ref, out_ref, done_ref):
    out_ref[...] = (a_ref[...].astype(F32) + b_ref[...].astype(F32)).astype(out_ref.dtype)
    done_ref[...] = jnp.zeros_like(done_ref)


def add_kernel(a_ref, b_ref, *refs):
    refs[-1][...] = (a_ref[...].astype(F32) + b_ref[...].astype(F32)).astype(refs[-1].dtype)


def finish_kernel(slots, rows, dim, columns, b_of, got_ref, *refs):
    parts, (kv_out, q_out, *outs) = refs[:columns], refs[columns:]
    wide = 2 * dim
    if columns:
        me = b_of()
        for column in range(columns):
            outs[-1][me ^ column] = parts[column][...].astype(F32)
    for head in range(slots):
        kv_out[pl.ds(head, rows, stride=slots), :] = got_ref[head, 0:wide, :].astype(F32).T
        q_out[head] = got_ref[head, wide:, :].astype(F32)


def shards(seq, mp, queries, key_value, tile_fill, out_weight, grad_output):
    rows, heads, dim = queries.shape
    width = grad_output.shape[1]
    slots = heads
    columns = seq // slots
    assert slots * columns == seq and columns & (columns - 1) == 0 and slots & (slots - 1) == 0
    a_of = lambda: lax.axis_index("seq") // columns
    b_of = lambda: lax.axis_index("seq") % columns

    def swap(array, mask, axis="seq", size=seq):
        return lax.ppermute(array, axis, [(i, i ^ mask) for i in range(size)])

    def exchange(pieces):
        return [pieces[0]] + [swap(piece, mask * columns) for piece, mask in zip(pieces[1:], spread(slots)[1:])]

    block, wide = slots * rows, 2 * dim
    kv_mine = exchange(call(
        functools.partial(pack_kv_kernel, heads, rows, dim, a_of),
        [((rows, wide), BF16)] * slots, [pltpu.VMEM((rows * heads, wide), F32)],
        n_in=2, smem_first=True, micros=1.5, limit=56,
    )(tile_fill, key_value.reshape(rows * heads, wide)))
    qg_send = call(
        functools.partial(pack_qg_kernel, heads, rows, dim, a_of),
        [((wide, rows), BF16)] * slots, [pltpu.VMEM((heads, wide, rows), BF16)],
        n_in=4, smem_first=True, micros=1,
    )(tile_fill, jnp.transpose(queries, (1, 2, 0)), out_weight, grad_output)
    qg_mine = exchange(qg_send)
    own = call(
        functools.partial(join_kernel, slots), [((block, wide), BF16)], n_in=slots, after=1,
    )(*kv_mine, qg_send[0])[0]

    blocks = {0: own}
    bit = columns // 2
    while bit:
        for r in sorted(blocks):
            blocks[r ^ bit] = swap(blocks[r], bit)
        bit //= 2

    qa, q_all, grads, q_norm = call(
        functools.partial(join_q_kernel, slots, rows, dim),
        [((2 * wide, block), BF16), ((dim, block), BF16), ((dim, block), BF16), ((1, block), F32)], n_in=slots,
    )(*qg_mine)
    step = min(block, 512)
    prepared, scored = {}, {}
    for r in range(columns):
        *prepared[r], values, norm = call(
            functools.partial(prep_kernel, dim),
            [((block, 2 * wide), BF16), ((dim, block), BF16), ((dim + 16, block), BF16), ((1, block), F32)],
            after=min(r, 1), micros=2,
        )(blocks[r], *([scored[r - 1][1]] if r else []))
        scored[r] = call(
            functools.partial(score_kernel, slots, rows, dim, step),
            [((block, block), BF16), ((1, block), F32), ((dim + 16, block), F32)],
            [pltpu.VMEM((block, rows), F32)], n_in=5, micros=4,
        )(prepared[r][0], values, norm, qa, q_norm)
    combined = call(
        functools.partial(combine_kernel, slots, columns, rows, dim),
        [((dim, rows), BF16)] * slots + [((1, block), F32)] * (columns + 1), n_in=2 * columns + 1,
    )(*[scored[r][1] for r in range(columns)], *[scored[r][2] for r in range(columns)], grads)
    att_mine, factors, inner = exchange(combined[:slots]), combined[slots:-1], combined[-1]

    halves = columns == heads == 4
    order = sorted(range(columns), reverse=True)
    add = call(add_kernel, [((dim, width), BF16)], n_in=2, after=1)
    add_halves = call(add_kernel, [((wide, block), BF16)], n_in=2)
    far_masks = [seq >> level for level in range(1, slots.bit_length())]
    dkv, dq, kept, summed, later = {}, None, None, {}, []
    for at, r in enumerate(order):
        if at and not halves and at == columns - 1 or halves and at == 1:
            weight_terms = call(
                functools.partial(project_grad_kernel, slots, rows, a_of, b_of, halves),
                [((2, dim, width), BF16)] * 2 if halves else [((heads, dim, width), BF16)],
                [pltpu.VMEM((heads, dim, width), BF16)],
                n_in=2 + slots, smem_first=True, after=1, micros=0.7,
            )(tile_fill, grad_output, *att_mine, dkv[order[at - 1]])
            terms = call(
                functools.partial(project_kernel, slots, rows, a_of), [((rows, width), BF16)],
                n_in=2 + slots, smem_first=True, after=1, micros=0.7,
            )(tile_fill, out_weight, *att_mine, weight_terms[-1])[0]
            later, bit, done = [terms], 1, terms
            first_terms = terms
            while bit < mp:
                terms, done = call(add_out_kernel, [((rows, width), BF16), ((8, 128), F32)], n_in=2)(
                    terms, swap(terms, bit, "mp", mp))
                bit *= 2
            if halves:
                kept, sent = call(add_pairs_kernel, [((dim, width), BF16)] * 2, n_in=2, after=1)(
                    weight_terms[0], swap(weight_terms[1], 1), first_terms)
                later = [kept]
        if at == 2 and halves:
            kept = add(kept, swap(sent, 2), dkv[order[at - 1]])[0]
            later = [kept]
        if at == 3 and halves:
            kept = add(kept, swap(kept, far_masks[0]), dkv[order[at - 1]])[0]
            later = [kept, summed[2], done]
        operands = [scored[r][0], *prepared[r], q_all, grads, factors[r], inner] + ([] if dq is None else [dq])
        dkv[r], dq = call(
            functools.partial(back_kernel, slots, rows, dim, dq is None),
            [((wide, block), BF16), ((dim, block), F32)], [pltpu.VMEM((2 * wide, block), BF16)],
            n_in=len(operands), after=len(later), micros=2,
        )(*operands, *later)
        later = []
        if columns == 4 and r == 2:
            summed[2] = swap(add_halves(dkv[2], swap(dkv[3], 1))[0], 2)

    if columns == 4:
        halved = add_halves(dkv[0], swap(dkv[1], 1))[0], summed[2]
    else:
        bit = 1
        while 2 * bit < columns:
            dkv = {r: add_halves(dkv[r], swap(dkv[r ^ bit], bit))[0] for r in order if r in dkv and not r & bit}
            bit *= 2
        halved = dkv[0], swap(dkv[bit], bit)
    pieces = call(
        functools.partial(add_pieces_kernel, slots, rows, dim, a_of), [((slots, wide + dim, rows), BF16)], n_in=3,
    )(*halved, dq)[0]
    got = pieces
    if slots > 1:
        groups = [[a * columns + b for a in range(slots)] for b in range(columns)]
        got = lax.all_to_all(pieces, "seq", 0, 0, axis_index_groups=groups, tiled=True)

    if halves:
        for mask in far_masks[1:]:
            kept = add(kept, swap(kept, mask), pieces)[0]
        across = swap(kept, 2)
        parts = [kept, swap(kept, 1), across, swap(across, 1)]
    else:
        parts, weight_grad = [], lax.psum(weight_terms[0].astype(F32), "seq")
    outs = [((rows * heads, wide), F32), ((heads, dim, rows), F32)]
    outs += [((heads, dim, width), F32)] if parts else []
    key_value_grad, query_grad, *outs = call(
        functools.partial(finish_kernel, slots, rows, dim, len(parts), b_of), outs,
        n_in=1 + len(parts), micros=1,
    )(got, *parts)
    weight_grad = outs[0] if parts else weight_grad
    return terms, jnp.transpose(query_grad, (2, 0, 1)), key_value_grad.reshape(rows, heads, wide), weight_grad


def solution(mesh):
    return jax.shard_map(
        functools.partial(shards, mesh.shape["seq"], mesh.shape["mp"]),
        mesh=mesh,
        in_specs=(
            P("seq", "mp", None),
            P("seq", "mp", None),
            P("seq"),
            P("mp", None, None),
            P("seq", None),
        ),
        out_specs=(P("seq", None), P("seq", "mp", None), P("seq", "mp", None), P("mp", None, None)),
        check_vma=False,
    )
```

```python
import functools

import jax
import jax.numpy as jnp
from jax import lax
from jax.experimental import pallas as pl
from jax.experimental.pallas import tpu as pltpu
from jax.sharding import PartitionSpec as P

TILE = 128
DEAD = 1024.0
BIAS = -1e30
LOG2_E = 1.4426950408889634
SAFE = 64.0
F32 = jnp.float32
BF16 = jnp.bfloat16
VMEM = pl.BlockSpec(memory_space=pltpu.VMEM)
SMEM = pl.BlockSpec(memory_space=pltpu.SMEM)
MIB = 1024 * 1024


def dot(a, b):
    return lax.dot_general(a, b, (((1,), (0,)), ((), ())), preferred_element_type=F32)


def dot_nt(a, b):
    return lax.dot_general(a, b, (((1,), (1,)), ((), ())), preferred_element_type=F32)


def call(kernel, outs, scratch=(), n_in=1, smem_first=False, after=0, micros=0.01, limit=16):
    specs = [SMEM if smem_first else VMEM] + [VMEM] * (n_in - 1) + [pl.BlockSpec(memory_space=pl.ANY)] * after
    return pl.pallas_call(
        kernel,
        out_shape=[jax.ShapeDtypeStruct(shape, kind) for shape, kind in outs],
        in_specs=specs,
        out_specs=[VMEM] * len(outs),
        scratch_shapes=list(scratch),
        compiler_params=pltpu.CompilerParams(vmem_limit_bytes=limit * MIB),
        cost_estimate=pl.CostEstimate(flops=int(micros * 1.15e9), bytes_accessed=0, transcendentals=0),
    )


def live_column(fill_ref, rows):
    parts = []
    within = lax.broadcasted_iota(jnp.int32, (TILE, 1), 0)
    for tile in range(rows // TILE):
        parts.append(jnp.where(within < fill_ref[tile], 1.0, 0.0))
    return jnp.concatenate(parts, axis=0) if len(parts) > 1 else parts[0]


def live_row(fill_ref, rows):
    within = lax.broadcasted_iota(jnp.int32, (1, TILE), 1)
    parts = [jnp.where(within < fill_ref[tile], 1.0, 0.0) for tile in range(rows // TILE)]
    return jnp.concatenate(parts, axis=1) if len(parts) > 1 else parts[0]


def spread(slots):
    return [0] + sorted(range(1, slots), key=lambda mask: (mask < slots // 2, mask))


def pack_kv_kernel(heads, rows, dim, a_of, fill_ref, kv_ref, *refs):
    outs, (held,) = refs[:heads], refs[heads:]
    live = live_column(fill_ref, rows)
    lane = lax.broadcasted_iota(jnp.int32, (rows, 2 * dim), 1)
    mark = jnp.where(lane == 0, DEAD * (1.0 - live), 0.0)
    held[...] = kv_ref[...].astype(F32)
    me = a_of()
    for slot, mask in enumerate(spread(heads)):
        outs[slot][...] = (held[pl.ds(me ^ mask, rows, stride=heads), :] * live + mark).astype(BF16)


def pack_qg_kernel(heads, rows, dim, a_of, fill_ref, q_ref, w_ref, go_ref, *refs):
    outs, (held,) = refs[:heads], refs[heads:]
    grads = dot_nt(w_ref[...].reshape(heads * dim, go_ref.shape[1]), go_ref[...])
    grads = (grads * live_row(fill_ref, rows)).astype(BF16)
    for head in range(heads):
        held[head, 0:dim, :] = (q_ref[head].astype(F32) * dim**-0.5).astype(BF16)
        held[head, dim:, :] = grads[head * dim : (head + 1) * dim, :]
    me = a_of()
    for slot, mask in enumerate(spread(heads)):
        outs[slot][...] = held[me ^ mask]


def join_kernel(pieces, *refs):
    out_ref = refs[-1]
    rows = refs[0].shape[0]
    for index in range(pieces):
        out_ref[index * rows : (index + 1) * rows, :] = refs[index][...]


def join_q_kernel(slots, rows, dim, *refs):
    pieces, (qa_ref, q_ref, g_ref, norm_ref) = refs[:slots], refs[slots:]
    wide = 2 * dim
    row = lax.broadcasted_iota(jnp.int32, (dim, slots * rows), 0)
    qa_ref[wide : wide + dim, :] = jnp.zeros((dim, slots * rows), BF16)
    qa_ref[wide + dim :, :] = jnp.where(row == 0, 1.0, 0.0).astype(BF16)
    for slot in range(slots):
        here = slice(slot * rows, (slot + 1) * rows)
        queries = pieces[slot][0:dim, :]
        q_ref[:, here] = queries
        g_ref[:, here] = pieces[slot][dim:, :]
        scaled = queries.astype(F32) * LOG2_E
        high = scaled.astype(BF16)
        qa_ref[0:dim, here] = high
        qa_ref[dim:wide, here] = (scaled - high.astype(F32)).astype(BF16)
        norm_ref[:, here] = jnp.sum(scaled * scaled, axis=0, keepdims=True)


def score_kernel(slots, rows, dim, step, pair_ref, qa_ref, q_norm_ref, *refs):
    exp_ref, peak_ref, total_ref, v_ref, kt_ref, wide_ref, vt_ref, score_ref = refs[-8:]
    wide = 2 * dim
    keys = pair_ref.shape[0]
    full = pair_ref[...].astype(F32)
    turned = full.T
    norm = jnp.sum(turned[:dim, :] * turned[:dim, :], axis=0, keepdims=True)
    norm = jnp.where(turned[0:1, :] >= DEAD, 0.0, norm)
    small = jnp.max(norm) * jnp.max(q_norm_ref[...]) <= SAFE * SAFE
    lane = lax.broadcasted_iota(jnp.int32, (keys, wide), 1)
    bias = jnp.where(full[:, 0:1] >= DEAD, BIAS, 0.0)
    extra = jnp.where(lane == dim, bias, jnp.where(lane <= dim + 2, 1.0, 0.0))
    rolled = pltpu.roll(full, dim, 1)
    values = jnp.where(lane < dim, rolled, extra).astype(BF16)
    wide_ref[:, 0:wide] = jnp.where(lane < dim, full, rolled).astype(BF16)
    wide_ref[:, wide:] = values
    v_ref[...] = values
    kt_ref[...] = turned[:dim, :].astype(BF16)
    vt_ref[0:dim, :] = turned[dim:, :].astype(BF16)
    vt_ref[dim:, :] = jnp.ones((16, keys), BF16)

    @pl.when(small)
    def _():
        peak_ref[...] = jnp.zeros_like(peak_ref)
        ahead = dot(wide_ref[...], qa_ref[:, 0:rows])
        for slot in range(slots):
            here = slice(slot * rows, (slot + 1) * rows)
            scores = ahead
            if slot + 1 < slots:
                ahead = dot(wide_ref[...], qa_ref[:, (slot + 1) * rows : (slot + 2) * rows])
            exps = jnp.exp2(scores).astype(BF16)
            exp_ref[:, here] = exps
            total_ref[:, here] = dot(vt_ref[...], exps)

    @pl.when(jnp.logical_not(small))
    def _():
        for slot in range(slots):
            here = slice(slot * rows, (slot + 1) * rows)
            top = jnp.full((8, rows), BIAS, F32)
            for start in range(0, keys, step):
                part = slice(start, start + step)
                scores = dot(wide_ref[part, :], qa_ref[:, here])
                score_ref[part, :] = scores
                top = jnp.maximum(top, jnp.max(scores.reshape(step // 8, 8, rows), axis=0))
            peak = jnp.max(top, axis=0, keepdims=True)
            peak_ref[:, here] = peak
            total = jnp.zeros((dim + 16, rows), F32)
            for start in range(0, keys, step):
                part = slice(start, start + step)
                exps = jnp.exp2(score_ref[part, :] - peak).astype(BF16)
                exp_ref[part, here] = exps
                total = total + dot(vt_ref[:, part], exps)
            total_ref[:, here] = total


def combine_kernel(slots, columns, rows, dim, *refs):
    peaks, totals, (g_ref,), outs = refs[:columns], refs[columns : 2 * columns], refs[2 * columns : 2 * columns + 1], refs[2 * columns + 1 :]
    att_out, factors_out, inner_ref = outs[:slots], outs[slots : slots + columns], outs[-1]
    peak = functools.reduce(jnp.maximum, [ref[...] for ref in peaks])
    factors = [jnp.exp2(ref[...] - peak) for ref in peaks]
    total = sum(factor * ref[...] for factor, ref in zip(factors, totals))
    inverse = 1.0 / total[dim : dim + 1, :]
    attended = (total[0:dim, :] * inverse).astype(BF16)
    for slot in range(slots):
        att_out[slot][...] = attended[:, slot * rows : (slot + 1) * rows]
    for factor, ref in zip(factors, factors_out):
        ref[...] = factor * inverse
    inner_ref[...] = jnp.sum(g_ref[...].astype(F32) * attended.astype(F32), axis=0, keepdims=True)


def back_kernel(slots, rows, dim, first, exp_ref, v_ref, kt_ref, q_ref, g_ref, factor_ref, inner_ref, *refs):
    dkv_ref, dq_ref, ga_ref = refs[-3:]
    block = g_ref.shape[1]
    factor = factor_ref[...]
    inner = inner_ref[...] * factor
    high = inner.astype(BF16).astype(F32)
    row = lax.broadcasted_iota(jnp.int32, (dim, block), 0)
    ga_ref[0:dim, :] = (g_ref[...].astype(F32) * factor).astype(BF16)
    ga_ref[dim:, :] = jnp.where(row == 1, -high, jnp.where(row == 2, high - inner, 0.0)).astype(BF16)
    grad_k = grad_v = None
    ahead = dot(v_ref[...], ga_ref[:, 0:rows])
    for slot in range(slots):
        here = slice(slot * rows, (slot + 1) * rows)
        products = ahead
        if slot + 1 < slots:
            ahead = dot(v_ref[...], ga_ref[:, (slot + 1) * rows : (slot + 2) * rows])
        exps = exp_ref[:, here]
        grads = exps * products.astype(BF16)
        term_v = dot_nt(ga_ref[0:dim, here], exps)
        term_k = dot_nt(q_ref[:, here], grads)
        grad_v = term_v if grad_v is None else grad_v + term_v
        grad_k = term_k if grad_k is None else grad_k + term_k
        term = dot(kt_ref[...], grads)
        dq_ref[:, here] = term if first else refs[0][:, here] + term
    dkv_ref[dim:, :] = grad_v.astype(BF16)
    dkv_ref[0:dim, :] = grad_k.astype(BF16)


def project_grad_kernel(slots, rows, a_of, b_of, halves, fill_ref, go_ref, *refs):
    att, refs = refs[:slots], refs[slots + 1 :]
    me = a_of()
    held = refs[-1]
    dim = held.shape[1]
    live = live_row(fill_ref, rows).astype(BF16)
    grads = dot(jnp.concatenate([ref[...] * live for ref in att], axis=0), go_ref[...]).astype(BF16)
    for slot, mask in enumerate(spread(slots)):
        held[me ^ mask] = grads[slot * dim : (slot + 1) * dim, :]
    if not halves:
        refs[0][...] = held[...]
        return
    me = b_of()
    kept_ref, sent_ref = refs[0], refs[1]
    for pair in range(slots // 2):
        kept_ref[pair] = held[me ^ (2 * pair)]
        sent_ref[pair] = held[me ^ (2 * pair) ^ 1]


def project_kernel(slots, rows, a_of, fill_ref, w_ref, *refs):
    att, terms_ref = refs[:slots], refs[-1]
    me = a_of()
    live = live_row(fill_ref, rows)
    rows_in = jnp.concatenate([ref[...].astype(F32) * live for ref in att], axis=0).T.astype(BF16)
    weights = jnp.concatenate([w_ref[me ^ mask] for mask in spread(slots)], axis=0)
    terms_ref[...] = dot(rows_in, weights).astype(BF16)


def add_pairs_kernel(kept_ref, came_ref, _, first_ref, second_ref):
    for index, out_ref in enumerate((first_ref, second_ref)):
        out_ref[...] = (kept_ref[index].astype(F32) + came_ref[index].astype(F32)).astype(BF16)


def add_pieces_kernel(slots, rows, dim, kept_ref, came_ref, dq_ref, *outs):
    wide = 2 * dim
    for slot in range(slots):
        here = slice(slot * rows, (slot + 1) * rows)
        outs[slot][0:wide, :] = (kept_ref[:, here].astype(F32) + came_ref[:, here].astype(F32)).astype(BF16)
        outs[slot][wide:, :] = (dq_ref[:, here] * dim**-0.5).astype(BF16)


def add_out_kernel(a_ref, b_ref, out_ref, done_ref):
    out_ref[...] = (a_ref[...].astype(F32) + b_ref[...].astype(F32)).astype(out_ref.dtype)
    done_ref[...] = jnp.zeros_like(done_ref)


def add_kernel(a_ref, b_ref, *refs):
    refs[-1][...] = (a_ref[...].astype(F32) + b_ref[...].astype(F32)).astype(refs[-1].dtype)


def finish_kernel(slots, rows, dim, a_of, b_of, columns, *refs):
    pieces, parts, (kv_out, q_out, *outs) = refs[:slots], refs[slots : slots + columns], refs[slots + columns :]
    wide = 2 * dim
    if columns:
        me = b_of()
        for column in range(columns):
            outs[0][me ^ column] = parts[column][...].astype(F32)
    me = a_of()
    for slot, mask in enumerate(spread(slots)):
        kv_out[pl.ds(me ^ mask, rows, stride=slots), :] = pieces[slot][0:wide, :].astype(F32).T
        q_out[me ^ mask] = pieces[slot][wide:, :].astype(F32)


def shards(seq, mp, queries, key_value, tile_fill, out_weight, grad_output):
    rows, heads, dim = queries.shape
    width = grad_output.shape[1]
    slots = heads
    columns = seq // slots
    assert slots * columns == seq and columns & (columns - 1) == 0 and slots & (slots - 1) == 0
    a_of = lambda: lax.axis_index("seq") // columns
    b_of = lambda: lax.axis_index("seq") % columns

    def swap(array, mask, axis="seq", size=seq):
        return lax.ppermute(array, axis, [(i, i ^ mask) for i in range(size)])

    def exchange(pieces):
        return [pieces[0]] + [swap(piece, mask * columns) for piece, mask in zip(pieces[1:], spread(slots)[1:])]

    block, wide = slots * rows, 2 * dim
    kv_mine = exchange(call(
        functools.partial(pack_kv_kernel, heads, rows, dim, a_of),
        [((rows, wide), BF16)] * slots, [pltpu.VMEM((rows * heads, wide), F32)],
        n_in=2, smem_first=True, micros=1.5, limit=56,
    )(tile_fill, key_value.reshape(rows * heads, wide)))
    qg_send = call(
        functools.partial(pack_qg_kernel, heads, rows, dim, a_of),
        [((wide, rows), BF16)] * slots, [pltpu.VMEM((heads, wide, rows), BF16)],
        n_in=4, smem_first=True, micros=1,
    )(tile_fill, jnp.transpose(queries, (1, 2, 0)), out_weight, grad_output)
    qg_mine = exchange(qg_send)
    own = call(
        functools.partial(join_kernel, slots), [((block, wide), BF16)], n_in=slots, after=1,
    )(*kv_mine, qg_send[0])[0]

    blocks = {0: own}
    bit = columns // 2
    while bit:
        for r in sorted(blocks):
            blocks[r ^ bit] = swap(blocks[r], bit)
        bit //= 2

    qa, q_all, grads, q_norm = call(
        functools.partial(join_q_kernel, slots, rows, dim),
        [((2 * wide, block), BF16), ((dim, block), BF16), ((dim, block), BF16), ((1, block), F32)], n_in=slots,
    )(*qg_mine)
    step = min(block, 512)
    scored = {}
    for r in range(columns):
        scored[r] = call(
            functools.partial(score_kernel, slots, rows, dim, step),
            [((block, block), BF16), ((1, block), F32), ((dim + 16, block), F32), ((block, wide), BF16), ((dim, block), BF16)],
            [pltpu.VMEM((block, 2 * wide), BF16), pltpu.VMEM((dim + 16, block), BF16), pltpu.VMEM((block, rows), F32)],
            n_in=3, after=min(r, 1), micros=5,
        )(blocks[r], qa, q_norm, *([scored[r - 1][1]] if r else []))
    combined = call(
        functools.partial(combine_kernel, slots, columns, rows, dim),
        [((dim, rows), BF16)] * slots + [((1, block), F32)] * (columns + 1), n_in=2 * columns + 1,
    )(*[scored[r][1] for r in range(columns)], *[scored[r][2] for r in range(columns)], grads)
    att_mine, factors, inner = exchange(combined[:slots]), combined[slots:-1], combined[-1]

    halves = columns == heads == 4
    order = sorted(range(columns), reverse=True)
    add = call(add_kernel, [((dim, width), BF16)], n_in=2, after=1)
    add_halves = call(add_kernel, [((wide, block), BF16)], n_in=2)
    far_masks = [seq >> level for level in range(1, slots.bit_length())]
    dkv, dq, kept, summed, later = {}, None, None, {}, []
    for at, r in enumerate(order):
        if at and not halves and at == columns - 1 or halves and at == 1:
            weight_terms = call(
                functools.partial(project_grad_kernel, slots, rows, a_of, b_of, halves),
                [((2, dim, width), BF16)] * 2 if halves else [((heads, dim, width), BF16)],
                [pltpu.VMEM((heads, dim, width), BF16)],
                n_in=2 + slots, smem_first=True, after=1, micros=0.7,
            )(tile_fill, grad_output, *att_mine, dkv[order[at - 1]])
            terms = call(
                functools.partial(project_kernel, slots, rows, a_of), [((rows, width), BF16)],
                n_in=2 + slots, smem_first=True, after=1, micros=0.7,
            )(tile_fill, out_weight, *att_mine, weight_terms[-1])[0]
            later, bit, done = [terms], 1, terms
            first_terms = terms
            while bit < mp:
                terms, done = call(add_out_kernel, [((rows, width), BF16), ((8, 128), F32)], n_in=2)(
                    terms, swap(terms, bit, "mp", mp))
                bit *= 2
            if halves:
                kept, sent = call(add_pairs_kernel, [((dim, width), BF16)] * 2, n_in=2, after=1)(
                    weight_terms[0], swap(weight_terms[1], 1), first_terms)
                later = [kept]
        if at == 2 and halves:
            kept = add(kept, swap(sent, 2), dkv[order[at - 1]])[0]
            later = [kept]
        if at == 3 and halves:
            kept = add(kept, swap(kept, far_masks[0]), dkv[order[at - 1]])[0]
            later = [kept, summed[2], done]
        operands = [scored[r][0], *scored[r][3:], q_all, grads, factors[r], inner] + ([] if dq is None else [dq])
        dkv[r], dq = call(
            functools.partial(back_kernel, slots, rows, dim, dq is None),
            [((wide, block), BF16), ((dim, block), F32)], [pltpu.VMEM((wide, block), BF16)],
            n_in=len(operands), after=len(later), micros=2,
        )(*operands, *later)
        later = []
        if columns == 4 and r == 2:
            summed[2] = swap(add_halves(dkv[2], swap(dkv[3], 1))[0], 2)

    if columns == 4:
        halved = add_halves(dkv[0], swap(dkv[1], 1))[0], summed[2]
    else:
        bit = 1
        while 2 * bit < columns:
            dkv = {r: add_halves(dkv[r], swap(dkv[r ^ bit], bit))[0] for r in order if r in dkv and not r & bit}
            bit *= 2
        halved = dkv[0], swap(dkv[bit], bit)
    pieces = call(
        functools.partial(add_pieces_kernel, slots, rows, dim), [((wide + dim, rows), BF16)] * slots, n_in=3,
    )(*halved, dq)
    returned = exchange(pieces)

    if halves:
        for mask in far_masks[1:]:
            kept = add(kept, swap(kept, mask), pieces[0])[0]
        across = swap(kept, 2)
        parts = [kept, swap(kept, 1), across, swap(across, 1)]
    else:
        parts, weight_grad = [], lax.psum(weight_terms[0].astype(F32), "seq")
    key_value_grad, query_grad, *outs = call(
        functools.partial(finish_kernel, slots, rows, dim, a_of, b_of, len(parts)),
        [((rows * heads, wide), F32), ((heads, dim, rows), F32)] + ([((heads, dim, width), F32)] if parts else []),
        n_in=slots + len(parts), micros=1,
    )(*returned, *parts)
    weight_grad = outs[0] if parts else weight_grad
    return terms, jnp.transpose(query_grad, (2, 0, 1)), key_value_grad.reshape(rows, heads, wide), weight_grad


def solution(mesh):
    return jax.shard_map(
        functools.partial(shards, mesh.shape["seq"], mesh.shape["mp"]),
        mesh=mesh,
        in_specs=(
            P("seq", "mp", None),
            P("seq", "mp", None),
            P("seq"),
            P("mp", None, None),
            P("seq", None),
        ),
        out_specs=(P("seq", None), P("seq", "mp", None), P("seq", "mp", None), P("mp", None, None)),
        check_vma=False,
    )
```

```python
import functools

import jax
import jax.numpy as jnp
from jax import lax
from jax.experimental import pallas as pl
from jax.experimental.pallas import tpu as pltpu
from jax.sharding import PartitionSpec as P

TILE = 128
DEAD = 1024.0
BIAS = -1e30
LOG2_E = 1.4426950408889634
SAFE = 64.0
F32 = jnp.float32
BF16 = jnp.bfloat16
VMEM = pl.BlockSpec(memory_space=pltpu.VMEM)
SMEM = pl.BlockSpec(memory_space=pltpu.SMEM)
MIB = 1024 * 1024


def dot(a, b):
    return lax.dot_general(a, b, (((1,), (0,)), ((), ())), preferred_element_type=F32)


def dot_nt(a, b):
    return lax.dot_general(a, b, (((1,), (1,)), ((), ())), preferred_element_type=F32)


def call(kernel, outs, scratch=(), n_in=1, smem_first=False, after=0, micros=0.01, limit=16):
    specs = [SMEM if smem_first else VMEM] + [VMEM] * (n_in - 1) + [pl.BlockSpec(memory_space=pl.ANY)] * after
    return pl.pallas_call(
        kernel,
        out_shape=[jax.ShapeDtypeStruct(shape, kind) for shape, kind in outs],
        in_specs=specs,
        out_specs=[VMEM] * len(outs),
        scratch_shapes=list(scratch),
        compiler_params=pltpu.CompilerParams(vmem_limit_bytes=limit * MIB),
        cost_estimate=pl.CostEstimate(flops=int(micros * 1.15e9), bytes_accessed=0, transcendentals=0),
    )


def live_column(fill_ref, rows):
    parts = []
    within = lax.broadcasted_iota(jnp.int32, (TILE, 1), 0)
    for tile in range(rows // TILE):
        parts.append(jnp.where(within < fill_ref[tile], 1.0, 0.0))
    return jnp.concatenate(parts, axis=0) if len(parts) > 1 else parts[0]


def live_row(fill_ref, rows):
    within = lax.broadcasted_iota(jnp.int32, (1, TILE), 1)
    parts = [jnp.where(within < fill_ref[tile], 1.0, 0.0) for tile in range(rows // TILE)]
    return jnp.concatenate(parts, axis=1) if len(parts) > 1 else parts[0]


def spread(slots):
    return [0] + sorted(range(1, slots), key=lambda mask: (mask < slots // 2, mask))


def pack_kv_kernel(heads, rows, dim, a_of, fill_ref, kv_ref, *refs):
    outs, (held,) = refs[:heads], refs[heads:]
    live = live_column(fill_ref, rows)
    lane = lax.broadcasted_iota(jnp.int32, (rows, 2 * dim), 1)
    mark = jnp.where(lane == 0, DEAD * (1.0 - live), 0.0)
    held[...] = kv_ref[...].astype(F32)
    me = a_of()
    for slot, mask in enumerate(spread(heads)):
        outs[slot][...] = (held[pl.ds(me ^ mask, rows, stride=heads), :] * live + mark).astype(BF16)


def pack_qg_kernel(heads, rows, dim, a_of, fill_ref, q_ref, w_ref, go_ref, *refs):
    outs, (held,) = refs[:heads], refs[heads:]
    grads = dot_nt(w_ref[...].reshape(heads * dim, go_ref.shape[1]), go_ref[...])
    grads = (grads * live_row(fill_ref, rows)).astype(BF16)
    for head in range(heads):
        held[head, 0:dim, :] = (q_ref[head].astype(F32) * dim**-0.5).astype(BF16)
        held[head, dim:, :] = grads[head * dim : (head + 1) * dim, :]
    me = a_of()
    for slot, mask in enumerate(spread(heads)):
        outs[slot][...] = held[me ^ mask]


def join_kernel(pieces, *refs):
    out_ref = refs[-1]
    rows = refs[0].shape[0]
    for index in range(pieces):
        out_ref[index * rows : (index + 1) * rows, :] = refs[index][...]


def join_q_kernel(slots, rows, dim, *refs):
    pieces, (qa_ref, q_ref, g_ref, norm_ref) = refs[:slots], refs[slots:]
    wide = 2 * dim
    row = lax.broadcasted_iota(jnp.int32, (dim, slots * rows), 0)
    qa_ref[wide : wide + dim, :] = jnp.zeros((dim, slots * rows), BF16)
    qa_ref[wide + dim :, :] = jnp.where(row == 0, 1.0, 0.0).astype(BF16)
    for slot in range(slots):
        here = slice(slot * rows, (slot + 1) * rows)
        queries = pieces[slot][0:dim, :]
        q_ref[:, here] = queries
        g_ref[:, here] = pieces[slot][dim:, :]
        scaled = queries.astype(F32) * LOG2_E
        high = scaled.astype(BF16)
        qa_ref[0:dim, here] = high
        qa_ref[dim:wide, here] = (scaled - high.astype(F32)).astype(BF16)
        norm_ref[:, here] = jnp.sum(scaled * scaled, axis=0, keepdims=True)


def score_kernel(slots, rows, dim, step, pair_ref, qa_ref, q_norm_ref, *refs):
    exp_ref, peak_ref, total_ref, v_ref, kt_ref, wide_ref, vt_ref, score_ref = refs[-8:]
    wide = 2 * dim
    keys = pair_ref.shape[0]
    full = pair_ref[...].astype(F32)
    turned = full.T
    norm = jnp.sum(turned[:dim, :] * turned[:dim, :], axis=0, keepdims=True)
    norm = jnp.where(turned[0:1, :] >= DEAD, 0.0, norm)
    small = jnp.max(norm) * jnp.max(q_norm_ref[...]) <= SAFE * SAFE
    lane = lax.broadcasted_iota(jnp.int32, (keys, wide), 1)
    bias = jnp.where(full[:, 0:1] >= DEAD, BIAS, 0.0)
    extra = jnp.where(lane == dim, bias, jnp.where(lane <= dim + 2, 1.0, 0.0))
    rolled = pltpu.roll(full, dim, 1)
    values = jnp.where(lane < dim, rolled, extra).astype(BF16)
    wide_ref[:, 0:wide] = jnp.where(lane < dim, full, rolled).astype(BF16)
    wide_ref[:, wide:] = values
    v_ref[...] = values
    kt_ref[...] = turned[:dim, :].astype(BF16)
    vt_ref[0:dim, :] = turned[dim:, :].astype(BF16)
    vt_ref[dim:, :] = jnp.ones((16, keys), BF16)

    @pl.when(small)
    def _():
        peak_ref[...] = jnp.zeros_like(peak_ref)
        ahead = dot(wide_ref[...], qa_ref[:, 0:rows])
        for slot in range(slots):
            here = slice(slot * rows, (slot + 1) * rows)
            scores = ahead
            if slot + 1 < slots:
                ahead = dot(wide_ref[...], qa_ref[:, (slot + 1) * rows : (slot + 2) * rows])
            exps = jnp.exp2(scores).astype(BF16)
            exp_ref[:, here] = exps
            total_ref[:, here] = dot(vt_ref[...], exps)

    @pl.when(jnp.logical_not(small))
    def _():
        for slot in range(slots):
            here = slice(slot * rows, (slot + 1) * rows)
            top = jnp.full((8, rows), BIAS, F32)
            for start in range(0, keys, step):
                part = slice(start, start + step)
                scores = dot(wide_ref[part, :], qa_ref[:, here])
                score_ref[part, :] = scores
                top = jnp.maximum(top, jnp.max(scores.reshape(step // 8, 8, rows), axis=0))
            peak = jnp.max(top, axis=0, keepdims=True)
            peak_ref[:, here] = peak
            total = jnp.zeros((dim + 16, rows), F32)
            for start in range(0, keys, step):
                part = slice(start, start + step)
                exps = jnp.exp2(score_ref[part, :] - peak).astype(BF16)
                exp_ref[part, here] = exps
                total = total + dot(vt_ref[:, part], exps)
            total_ref[:, here] = total


def combine_kernel(slots, columns, rows, dim, *refs):
    peaks, totals, (g_ref,), outs = refs[:columns], refs[columns : 2 * columns], refs[2 * columns : 2 * columns + 1], refs[2 * columns + 1 :]
    att_out, factors_out, inner_ref = outs[:slots], outs[slots : slots + columns], outs[-1]
    peak = functools.reduce(jnp.maximum, [ref[...] for ref in peaks])
    factors = [jnp.exp2(ref[...] - peak) for ref in peaks]
    total = sum(factor * ref[...] for factor, ref in zip(factors, totals))
    inverse = 1.0 / total[dim : dim + 1, :]
    attended = (total[0:dim, :] * inverse).astype(BF16)
    for slot in range(slots):
        att_out[slot][...] = attended[:, slot * rows : (slot + 1) * rows]
    for factor, ref in zip(factors, factors_out):
        ref[...] = factor * inverse
    inner_ref[...] = jnp.sum(g_ref[...].astype(F32) * attended.astype(F32), axis=0, keepdims=True)


def back_kernel(slots, rows, dim, first, exp_ref, v_ref, kt_ref, q_ref, g_ref, factor_ref, inner_ref, *refs):
    dkv_ref, dq_ref, ga_ref = refs[-3:]
    block = g_ref.shape[1]
    factor = factor_ref[...]
    inner = inner_ref[...] * factor
    high = inner.astype(BF16).astype(F32)
    row = lax.broadcasted_iota(jnp.int32, (dim, block), 0)
    ga_ref[0:dim, :] = (g_ref[...].astype(F32) * factor).astype(BF16)
    ga_ref[dim:, :] = jnp.where(row == 1, -high, jnp.where(row == 2, high - inner, 0.0)).astype(BF16)
    grad_k = grad_v = None
    ahead = dot(v_ref[...], ga_ref[:, 0:rows])
    for slot in range(slots):
        here = slice(slot * rows, (slot + 1) * rows)
        products = ahead
        if slot + 1 < slots:
            ahead = dot(v_ref[...], ga_ref[:, (slot + 1) * rows : (slot + 2) * rows])
        exps = exp_ref[:, here]
        grads = exps * products.astype(BF16)
        term_v = dot_nt(ga_ref[0:dim, here], exps)
        term_k = dot_nt(q_ref[:, here], grads)
        grad_v = term_v if grad_v is None else grad_v + term_v
        grad_k = term_k if grad_k is None else grad_k + term_k
        term = dot(kt_ref[...], grads)
        dq_ref[:, here] = term if first else refs[0][:, here] + term
    dkv_ref[dim:, :] = grad_v.astype(BF16)
    dkv_ref[0:dim, :] = grad_k.astype(BF16)


def project_grad_kernel(slots, rows, a_of, b_of, halves, fill_ref, go_ref, *refs):
    att, refs = refs[:slots], refs[slots + 1 :]
    me = a_of()
    held = refs[-1]
    dim = held.shape[1]
    live = live_row(fill_ref, rows).astype(BF16)
    grads = dot(jnp.concatenate([ref[...] * live for ref in att], axis=0), go_ref[...]).astype(BF16)
    for slot, mask in enumerate(spread(slots)):
        held[me ^ mask] = grads[slot * dim : (slot + 1) * dim, :]
    if not halves:
        refs[0][...] = held[...]
        return
    me = b_of()
    kept_ref, sent_ref = refs[0], refs[1]
    for pair in range(slots // 2):
        kept_ref[pair] = held[me ^ (2 * pair)]
        sent_ref[pair] = held[me ^ (2 * pair) ^ 1]


def project_kernel(slots, rows, a_of, fill_ref, w_ref, *refs):
    att, terms_ref = refs[:slots], refs[-1]
    me = a_of()
    live = live_row(fill_ref, rows)
    rows_in = jnp.concatenate([ref[...].astype(F32) * live for ref in att], axis=0).T.astype(BF16)
    weights = jnp.concatenate([w_ref[me ^ mask] for mask in spread(slots)], axis=0)
    terms_ref[...] = dot(rows_in, weights).astype(BF16)


def add_pairs_kernel(kept_ref, came_ref, _, first_ref, second_ref):
    for index, out_ref in enumerate((first_ref, second_ref)):
        out_ref[...] = (kept_ref[index].astype(F32) + came_ref[index].astype(F32)).astype(BF16)


def add_pieces_kernel(slots, rows, dim, kept_ref, came_ref, dq_ref, *outs):
    wide = 2 * dim
    for slot in range(slots):
        here = slice(slot * rows, (slot + 1) * rows)
        outs[slot][0:wide, :] = (kept_ref[:, here].astype(F32) + came_ref[:, here].astype(F32)).astype(BF16)
        outs[slot][wide:, :] = (dq_ref[:, here] * dim**-0.5).astype(BF16)


def add_kernel(a_ref, b_ref, *refs):
    refs[-1][...] = (a_ref[...].astype(F32) + b_ref[...].astype(F32)).astype(refs[-1].dtype)


def unpack_kernel(slots, rows, dim, a_of, *refs):
    pieces, (kv_out, q_out) = refs[:slots], refs[slots:]
    wide = 2 * dim
    me = a_of()
    for slot, mask in enumerate(spread(slots)):
        kv_out[pl.ds(me ^ mask, rows, stride=slots), :] = pieces[slot][0:wide, :].astype(F32).T
        q_out[me ^ mask] = pieces[slot][wide:, :].astype(F32)


def place_kernel(columns, b_of, *refs):
    parts, (a_ref, b_ref), (sum_out, grad_out) = refs[:columns], refs[columns : columns + 2], refs[columns + 2 :]
    sum_out[...] = (a_ref[...].astype(F32) + b_ref[...].astype(F32)).astype(BF16)
    me = b_of()
    for column in range(columns):
        grad_out[me ^ column] = parts[column][...].astype(F32)


def shards(seq, mp, queries, key_value, tile_fill, out_weight, grad_output):
    rows, heads, dim = queries.shape
    width = grad_output.shape[1]
    slots = heads
    columns = seq // slots
    assert slots * columns == seq and columns & (columns - 1) == 0 and slots & (slots - 1) == 0
    a_of = lambda: lax.axis_index("seq") // columns
    b_of = lambda: lax.axis_index("seq") % columns

    def swap(array, mask, axis="seq", size=seq):
        return lax.ppermute(array, axis, [(i, i ^ mask) for i in range(size)])

    def exchange(pieces):
        return [pieces[0]] + [swap(piece, mask * columns) for piece, mask in zip(pieces[1:], spread(slots)[1:])]

    block, wide = slots * rows, 2 * dim
    kv_mine = exchange(call(
        functools.partial(pack_kv_kernel, heads, rows, dim, a_of),
        [((rows, wide), BF16)] * slots, [pltpu.VMEM((rows * heads, wide), F32)],
        n_in=2, smem_first=True, micros=1.5, limit=56,
    )(tile_fill, key_value.reshape(rows * heads, wide)))
    qg_send = call(
        functools.partial(pack_qg_kernel, heads, rows, dim, a_of),
        [((wide, rows), BF16)] * slots, [pltpu.VMEM((heads, wide, rows), BF16)],
        n_in=4, smem_first=True, micros=1,
    )(tile_fill, jnp.transpose(queries, (1, 2, 0)), out_weight, grad_output)
    qg_mine = exchange(qg_send)
    own = call(
        functools.partial(join_kernel, slots), [((block, wide), BF16)], n_in=slots, after=1,
    )(*kv_mine, qg_send[0])[0]

    qa, q_all, grads, q_norm = call(
        functools.partial(join_q_kernel, slots, rows, dim),
        [((2 * wide, block), BF16), ((dim, block), BF16), ((dim, block), BF16), ((1, block), F32)], n_in=slots,
    )(*qg_mine)
    step = min(block, 512)
    scored, blocks = {}, {0: own}
    bit = columns // 2
    while bit:
        for r in sorted(blocks):
            blocks[r ^ bit] = swap(blocks[r], bit)
        bit //= 2
    for r in range(columns):
        if r == 2 and columns == 4:
            blocks[2] = call(functools.partial(join_kernel, 1), [((block, wide), BF16)], after=1)(
                blocks[2], scored[1][1])[0]
            blocks[3] = swap(blocks[2], 1)
        scored[r] = call(
            functools.partial(score_kernel, slots, rows, dim, step),
            [((block, block), BF16), ((1, block), F32), ((dim + 16, block), F32), ((block, wide), BF16), ((dim, block), BF16)],
            [pltpu.VMEM((block, 2 * wide), BF16), pltpu.VMEM((dim + 16, block), BF16), pltpu.VMEM((block, rows), F32)],
            n_in=3, after=min(r, 1), micros=5,
        )(blocks[r], qa, q_norm, *([scored[r - 1][1]] if r else []))
    combined = call(
        functools.partial(combine_kernel, slots, columns, rows, dim),
        [((dim, rows), BF16)] * slots + [((1, block), F32)] * (columns + 1), n_in=2 * columns + 1,
    )(*[scored[r][1] for r in range(columns)], *[scored[r][2] for r in range(columns)], grads)
    att_mine, factors, inner = exchange(combined[:slots]), combined[slots:-1], combined[-1]

    halves = columns == heads == 4
    order = sorted(range(columns), reverse=True)
    add = call(add_kernel, [((dim, width), BF16)], n_in=2, after=1)
    add_halves = call(add_kernel, [((wide, block), BF16)], n_in=2)
    far_masks = [seq >> level for level in range(1, slots.bit_length())]
    dkv, dq, kept, summed, later = {}, None, None, {}, []
    for at, r in enumerate(order):
        if at and not halves and at == columns - 1 or halves and at == 1:
            weight_terms = call(
                functools.partial(project_grad_kernel, slots, rows, a_of, b_of, halves),
                [((2, dim, width), BF16)] * 2 if halves else [((heads, dim, width), BF16)],
                [pltpu.VMEM((heads, dim, width), BF16)],
                n_in=2 + slots, smem_first=True, after=1, micros=0.7,
            )(tile_fill, grad_output, *att_mine, dkv[order[at - 1]])
            terms = call(
                functools.partial(project_kernel, slots, rows, a_of), [((rows, width), BF16)],
                n_in=2 + slots, smem_first=True, after=1, micros=0.7,
            )(tile_fill, out_weight, *att_mine, weight_terms[-1])[0]
            later, bit, first_terms = [terms], 1, terms
            while bit < mp // 2:
                terms = call(add_kernel, [((rows, width), BF16)], n_in=2)(terms, swap(terms, bit, "mp", mp))[0]
                bit *= 2
            terms_came = swap(terms, bit, "mp", mp)
            if halves:
                kept, sent = call(add_pairs_kernel, [((dim, width), BF16)] * 2, n_in=2, after=1)(
                    weight_terms[0], swap(weight_terms[1], 1), first_terms)
                later = [kept]
        if at == 2 and halves:
            kept = add(kept, swap(sent, 2), dkv[order[at - 1]])[0]
            later = [kept]
        if at == 3 and halves:
            kept = add(kept, swap(kept, far_masks[0]), dkv[order[at - 1]])[0]
            later = [kept, summed[2], terms_came]
        operands = [scored[r][0], *scored[r][3:], q_all, grads, factors[r], inner] + ([] if dq is None else [dq])
        dkv[r], dq = call(
            functools.partial(back_kernel, slots, rows, dim, dq is None),
            [((wide, block), BF16), ((dim, block), F32)], [pltpu.VMEM((wide, block), BF16)],
            n_in=len(operands), after=len(later), micros=2,
        )(*operands, *later)
        later = []
        if columns == 4 and r == 2:
            summed[2] = swap(add_halves(dkv[2], swap(dkv[3], 1))[0], 2)

    if columns == 4:
        halved = add_halves(dkv[0], swap(dkv[1], 1))[0], summed[2]
    else:
        bit = 1
        while 2 * bit < columns:
            dkv = {r: add_halves(dkv[r], swap(dkv[r ^ bit], bit))[0] for r in order if r in dkv and not r & bit}
            bit *= 2
        halved = dkv[0], swap(dkv[bit], bit)
    pieces = call(
        functools.partial(add_pieces_kernel, slots, rows, dim), [((wide + dim, rows), BF16)] * slots, n_in=3,
    )(*halved, dq)
    returned = exchange(pieces)

    if halves:
        for mask in far_masks[1:]:
            kept = add(kept, swap(kept, mask), pieces[0])[0]
        across = swap(kept, 2)
        attention_out, weight_grad = call(
            functools.partial(place_kernel, columns, b_of),
            [((rows, width), BF16), ((heads, dim, width), F32)], n_in=columns + 2, micros=0.5,
        )(kept, swap(kept, 1), across, swap(across, 1), terms, terms_came)
    else:
        attention_out = call(add_kernel, [((rows, width), BF16)], n_in=2)(terms, terms_came)[0]
        weight_grad = lax.psum(weight_terms[0].astype(F32), "seq")
    key_value_grad, query_grad = call(
        functools.partial(unpack_kernel, slots, rows, dim, a_of),
        [((rows * heads, wide), F32), ((heads, dim, rows), F32)], n_in=slots, micros=1,
    )(*returned)
    return attention_out, jnp.transpose(query_grad, (2, 0, 1)), key_value_grad.reshape(rows, heads, wide), weight_grad


def solution(mesh):
    return jax.shard_map(
        functools.partial(shards, mesh.shape["seq"], mesh.shape["mp"]),
        mesh=mesh,
        in_specs=(
            P("seq", "mp", None),
            P("seq", "mp", None),
            P("seq"),
            P("mp", None, None),
            P("seq", None),
        ),
        out_specs=(P("seq", None), P("seq", "mp", None), P("seq", "mp", None), P("mp", None, None)),
        check_vma=False,
    )
```

```python
import functools

import jax
import jax.numpy as jnp
from jax import lax
from jax.experimental import pallas as pl
from jax.experimental.pallas import tpu as pltpu
from jax.sharding import PartitionSpec as P

TILE = 128
DEAD = 1024.0
BIAS = -1e30
LOG2_E = 1.4426950408889634
SAFE = 64.0
F32 = jnp.float32
BF16 = jnp.bfloat16
VMEM = pl.BlockSpec(memory_space=pltpu.VMEM)
SMEM = pl.BlockSpec(memory_space=pltpu.SMEM)
MIB = 1024 * 1024


def dot(a, b):
    return lax.dot_general(a, b, (((1,), (0,)), ((), ())), preferred_element_type=F32)


def dot_nt(a, b):
    return lax.dot_general(a, b, (((1,), (1,)), ((), ())), preferred_element_type=F32)


def call(kernel, outs, scratch=(), n_in=1, smem_first=False, after=0, micros=0.01, limit=16):
    specs = [SMEM if smem_first else VMEM] + [VMEM] * (n_in - 1) + [pl.BlockSpec(memory_space=pl.ANY)] * after
    return pl.pallas_call(
        kernel,
        out_shape=[jax.ShapeDtypeStruct(shape, kind) for shape, kind in outs],
        in_specs=specs,
        out_specs=[VMEM] * len(outs),
        scratch_shapes=list(scratch),
        compiler_params=pltpu.CompilerParams(vmem_limit_bytes=limit * MIB),
        cost_estimate=pl.CostEstimate(flops=int(micros * 1.15e9), bytes_accessed=0, transcendentals=0),
    )


def live_column(fill_ref, rows):
    parts = []
    within = lax.broadcasted_iota(jnp.int32, (TILE, 1), 0)
    for tile in range(rows // TILE):
        parts.append(jnp.where(within < fill_ref[tile], 1.0, 0.0))
    return jnp.concatenate(parts, axis=0) if len(parts) > 1 else parts[0]


def live_row(fill_ref, rows):
    within = lax.broadcasted_iota(jnp.int32, (1, TILE), 1)
    parts = [jnp.where(within < fill_ref[tile], 1.0, 0.0) for tile in range(rows // TILE)]
    return jnp.concatenate(parts, axis=1) if len(parts) > 1 else parts[0]


def spread(slots):
    return [0] + sorted(range(1, slots), key=lambda mask: (mask < slots // 2, mask))


def pack_kv_kernel(heads, rows, dim, a_of, fill_ref, kv_ref, *refs):
    outs, (held,) = refs[:heads], refs[heads:]
    live = live_column(fill_ref, rows)
    lane = lax.broadcasted_iota(jnp.int32, (rows, 2 * dim), 1)
    mark = jnp.where(lane == 0, DEAD * (1.0 - live), 0.0)
    held[...] = kv_ref[...].astype(F32)
    me = a_of()
    for slot, mask in enumerate(spread(heads)):
        outs[slot][...] = (held[pl.ds(me ^ mask, rows, stride=heads), :] * live + mark).astype(BF16)


def pack_qg_kernel(heads, rows, dim, a_of, fill_ref, q_ref, w_ref, go_ref, *refs):
    outs, (held,) = refs[:heads], refs[heads:]
    grads = dot_nt(w_ref[...].reshape(heads * dim, go_ref.shape[1]), go_ref[...])
    grads = (grads * live_row(fill_ref, rows)).astype(BF16)
    for head in range(heads):
        held[head, 0:dim, :] = (q_ref[head].astype(F32) * dim**-0.5).astype(BF16)
        held[head, dim:, :] = grads[head * dim : (head + 1) * dim, :]
    me = a_of()
    for slot, mask in enumerate(spread(heads)):
        outs[slot][...] = held[me ^ mask]


def join_kernel(pieces, *refs):
    out_ref = refs[-1]
    rows = refs[0].shape[0]
    for index in range(pieces):
        out_ref[index * rows : (index + 1) * rows, :] = refs[index][...]


def join_q_kernel(slots, rows, dim, *refs):
    pieces, (qa_ref, q_ref, g_ref, norm_ref) = refs[:slots], refs[slots:]
    wide = 2 * dim
    row = lax.broadcasted_iota(jnp.int32, (dim, slots * rows), 0)
    qa_ref[wide : wide + dim, :] = jnp.zeros((dim, slots * rows), BF16)
    qa_ref[wide + dim :, :] = jnp.where(row == 0, 1.0, 0.0).astype(BF16)
    for slot in range(slots):
        here = slice(slot * rows, (slot + 1) * rows)
        queries = pieces[slot][0:dim, :]
        q_ref[:, here] = queries
        g_ref[:, here] = pieces[slot][dim:, :]
        scaled = queries.astype(F32) * LOG2_E
        high = scaled.astype(BF16)
        qa_ref[0:dim, here] = high
        qa_ref[dim:wide, here] = (scaled - high.astype(F32)).astype(BF16)
        norm_ref[:, here] = jnp.sum(scaled * scaled, axis=0, keepdims=True)


def score_kernel(slots, rows, dim, step, pair_ref, qa_ref, q_norm_ref, *refs):
    exp_ref, peak_ref, total_ref, v_ref, kt_ref, wide_ref, vt_ref, score_ref = refs[-8:]
    wide = 2 * dim
    keys = pair_ref.shape[0]
    full = pair_ref[...].astype(F32)
    turned = full.T
    norm = jnp.sum(turned[:dim, :] * turned[:dim, :], axis=0, keepdims=True)
    norm = jnp.where(turned[0:1, :] >= DEAD, 0.0, norm)
    small = jnp.max(norm) * jnp.max(q_norm_ref[...]) <= SAFE * SAFE
    lane = lax.broadcasted_iota(jnp.int32, (keys, wide), 1)
    bias = jnp.where(full[:, 0:1] >= DEAD, BIAS, 0.0)
    extra = jnp.where(lane == dim, bias, jnp.where(lane <= dim + 2, 1.0, 0.0))
    rolled = pltpu.roll(full, dim, 1)
    values = jnp.where(lane < dim, rolled, extra).astype(BF16)
    wide_ref[:, 0:wide] = jnp.where(lane < dim, full, rolled).astype(BF16)
    wide_ref[:, wide:] = values
    v_ref[...] = values
    kt_ref[...] = turned[:dim, :].astype(BF16)
    vt_ref[0:dim, :] = turned[dim:, :].astype(BF16)
    vt_ref[dim:, :] = jnp.ones((16, keys), BF16)

    @pl.when(small)
    def _():
        peak_ref[...] = jnp.zeros_like(peak_ref)
        ahead = dot(wide_ref[...], qa_ref[:, 0:rows])
        for slot in range(slots):
            here = slice(slot * rows, (slot + 1) * rows)
            scores = ahead
            if slot + 1 < slots:
                ahead = dot(wide_ref[...], qa_ref[:, (slot + 1) * rows : (slot + 2) * rows])
            exps = jnp.exp2(scores).astype(BF16)
            exp_ref[:, here] = exps
            total_ref[:, here] = dot(vt_ref[...], exps)

    @pl.when(jnp.logical_not(small))
    def _():
        for slot in range(slots):
            here = slice(slot * rows, (slot + 1) * rows)
            top = jnp.full((8, rows), BIAS, F32)
            for start in range(0, keys, step):
                part = slice(start, start + step)
                scores = dot(wide_ref[part, :], qa_ref[:, here])
                score_ref[part, :] = scores
                top = jnp.maximum(top, jnp.max(scores.reshape(step // 8, 8, rows), axis=0))
            peak = jnp.max(top, axis=0, keepdims=True)
            peak_ref[:, here] = peak
            total = jnp.zeros((dim + 16, rows), F32)
            for start in range(0, keys, step):
                part = slice(start, start + step)
                exps = jnp.exp2(score_ref[part, :] - peak).astype(BF16)
                exp_ref[part, here] = exps
                total = total + dot(vt_ref[:, part], exps)
            total_ref[:, here] = total


def combine_kernel(slots, columns, rows, dim, *refs):
    peaks, totals, (g_ref,), outs = refs[:columns], refs[columns : 2 * columns], refs[2 * columns : 2 * columns + 1], refs[2 * columns + 1 :]
    att_out, factors_out, inner_ref = outs[:slots], outs[slots : slots + columns], outs[-1]
    peak = functools.reduce(jnp.maximum, [ref[...] for ref in peaks])
    factors = [jnp.exp2(ref[...] - peak) for ref in peaks]
    total = sum(factor * ref[...] for factor, ref in zip(factors, totals))
    inverse = 1.0 / total[dim : dim + 1, :]
    attended = (total[0:dim, :] * inverse).astype(BF16)
    for slot in range(slots):
        att_out[slot][...] = attended[:, slot * rows : (slot + 1) * rows]
    for factor, ref in zip(factors, factors_out):
        ref[...] = factor * inverse
    inner_ref[...] = jnp.sum(g_ref[...].astype(F32) * attended.astype(F32), axis=0, keepdims=True)


def back_kernel(slots, rows, dim, first, exp_ref, v_ref, kt_ref, q_ref, g_ref, factor_ref, inner_ref, *refs):
    dkv_ref, dq_ref, ga_ref = refs[-3:]
    block = g_ref.shape[1]
    factor = factor_ref[...]
    inner = inner_ref[...] * factor
    high = inner.astype(BF16).astype(F32)
    row = lax.broadcasted_iota(jnp.int32, (dim, block), 0)
    ga_ref[0:dim, :] = (g_ref[...].astype(F32) * factor).astype(BF16)
    ga_ref[dim:, :] = jnp.where(row == 1, -high, jnp.where(row == 2, high - inner, 0.0)).astype(BF16)
    grad_k = grad_v = None
    ahead = dot(v_ref[...], ga_ref[:, 0:rows])
    for slot in range(slots):
        here = slice(slot * rows, (slot + 1) * rows)
        products = ahead
        if slot + 1 < slots:
            ahead = dot(v_ref[...], ga_ref[:, (slot + 1) * rows : (slot + 2) * rows])
        exps = exp_ref[:, here]
        grads = exps * products.astype(BF16)
        term_v = dot_nt(ga_ref[0:dim, here], exps)
        term_k = dot_nt(q_ref[:, here], grads)
        grad_v = term_v if grad_v is None else grad_v + term_v
        grad_k = term_k if grad_k is None else grad_k + term_k
        term = dot(kt_ref[...], grads)
        dq_ref[:, here] = term if first else refs[0][:, here] + term
    dkv_ref[dim:, :] = grad_v.astype(BF16)
    dkv_ref[0:dim, :] = grad_k.astype(BF16)


def project_grad_kernel(slots, rows, a_of, b_of, halves, fill_ref, go_ref, *refs):
    att, refs = refs[:slots], refs[slots + 1 :]
    me = a_of()
    held = refs[-1]
    dim = held.shape[1]
    live = live_row(fill_ref, rows).astype(BF16)
    grads = dot(jnp.concatenate([ref[...] * live for ref in att], axis=0), go_ref[...]).astype(BF16)
    for slot, mask in enumerate(spread(slots)):
        held[me ^ mask] = grads[slot * dim : (slot + 1) * dim, :]
    if not halves:
        refs[0][...] = held[...]
        return
    me = b_of()
    kept_ref, sent_ref = refs[0], refs[1]
    for pair in range(slots // 2):
        kept_ref[pair] = held[me ^ (2 * pair)]
        sent_ref[pair] = held[me ^ (2 * pair) ^ 1]


def project_kernel(slots, rows, a_of, fill_ref, w_ref, *refs):
    att, terms_ref = refs[:slots], refs[-1]
    me = a_of()
    live = live_row(fill_ref, rows)
    rows_in = jnp.concatenate([ref[...].astype(F32) * live for ref in att], axis=0).T.astype(BF16)
    weights = jnp.concatenate([w_ref[me ^ mask] for mask in spread(slots)], axis=0)
    terms_ref[...] = dot(rows_in, weights).astype(BF16)


def add_pairs_kernel(kept_ref, came_ref, _, first_ref, second_ref):
    for index, out_ref in enumerate((first_ref, second_ref)):
        out_ref[...] = (kept_ref[index].astype(F32) + came_ref[index].astype(F32)).astype(BF16)


def add_pieces_kernel(slots, rows, dim, kept_ref, came_ref, dq_ref, *outs):
    wide = 2 * dim
    for slot in range(slots):
        here = slice(slot * rows, (slot + 1) * rows)
        outs[slot][0:wide, :] = (kept_ref[:, here].astype(F32) + came_ref[:, here].astype(F32)).astype(BF16)
        outs[slot][wide:, :] = (dq_ref[:, here] * dim**-0.5).astype(BF16)


def add_kernel(a_ref, b_ref, *refs):
    refs[-1][...] = (a_ref[...].astype(F32) + b_ref[...].astype(F32)).astype(refs[-1].dtype)


def unpack_kernel(slots, rows, dim, a_of, *refs):
    pieces, (a_ref, b_ref, kv_out, q_out, sum_out, done_ref) = refs[:slots], refs[slots:]
    sum_out[...] = (a_ref[...].astype(F32) + b_ref[...].astype(F32)).astype(BF16)
    done_ref[...] = jnp.zeros_like(done_ref)
    wide = 2 * dim
    me = a_of()
    for slot, mask in enumerate(spread(slots)):
        kv_out[pl.ds(me ^ mask, rows, stride=slots), :] = pieces[slot][0:wide, :].astype(F32).T
        q_out[me ^ mask] = pieces[slot][wide:, :].astype(F32)


def place_kernel(columns, b_of, *refs):
    parts, (grad_out,) = refs[:columns], refs[columns:]
    me = b_of()
    for column in range(columns):
        grad_out[me ^ column] = parts[column][...].astype(F32)


def shards(seq, mp, queries, key_value, tile_fill, out_weight, grad_output):
    rows, heads, dim = queries.shape
    width = grad_output.shape[1]
    slots = heads
    columns = seq // slots
    assert slots * columns == seq and columns & (columns - 1) == 0 and slots & (slots - 1) == 0
    a_of = lambda: lax.axis_index("seq") // columns
    b_of = lambda: lax.axis_index("seq") % columns

    def swap(array, mask, axis="seq", size=seq):
        return lax.ppermute(array, axis, [(i, i ^ mask) for i in range(size)])

    def exchange(pieces):
        return [pieces[0]] + [swap(piece, mask * columns) for piece, mask in zip(pieces[1:], spread(slots)[1:])]

    block, wide = slots * rows, 2 * dim
    kv_mine = exchange(call(
        functools.partial(pack_kv_kernel, heads, rows, dim, a_of),
        [((rows, wide), BF16)] * slots, [pltpu.VMEM((rows * heads, wide), F32)],
        n_in=2, smem_first=True, micros=1.5, limit=56,
    )(tile_fill, key_value.reshape(rows * heads, wide)))
    qg_send = call(
        functools.partial(pack_qg_kernel, heads, rows, dim, a_of),
        [((wide, rows), BF16)] * slots, [pltpu.VMEM((heads, wide, rows), BF16)],
        n_in=4, smem_first=True, micros=1,
    )(tile_fill, jnp.transpose(queries, (1, 2, 0)), out_weight, grad_output)
    qg_mine = exchange(qg_send)
    own = call(
        functools.partial(join_kernel, slots), [((block, wide), BF16)], n_in=slots, after=1,
    )(*kv_mine, qg_send[0])[0]

    qa, q_all, grads, q_norm = call(
        functools.partial(join_q_kernel, slots, rows, dim),
        [((2 * wide, block), BF16), ((dim, block), BF16), ((dim, block), BF16), ((1, block), F32)], n_in=slots,
    )(*qg_mine)
    step = min(block, 512)
    scored, blocks = {}, {0: own}
    bit = columns // 2
    while bit:
        for r in sorted(blocks):
            blocks[r ^ bit] = swap(blocks[r], bit)
        bit //= 2
    for r in range(columns):
        if r == 2 and columns == 4:
            blocks[2] = call(functools.partial(join_kernel, 1), [((block, wide), BF16)], after=1)(
                blocks[2], scored[1][1])[0]
            blocks[3] = swap(blocks[2], 1)
        scored[r] = call(
            functools.partial(score_kernel, slots, rows, dim, step),
            [((block, block), BF16), ((1, block), F32), ((dim + 16, block), F32), ((block, wide), BF16), ((dim, block), BF16)],
            [pltpu.VMEM((block, 2 * wide), BF16), pltpu.VMEM((dim + 16, block), BF16), pltpu.VMEM((block, rows), F32)],
            n_in=3, after=min(r, 1), micros=5,
        )(blocks[r], qa, q_norm, *([scored[r - 1][1]] if r else []))
    combined = call(
        functools.partial(combine_kernel, slots, columns, rows, dim),
        [((dim, rows), BF16)] * slots + [((1, block), F32)] * (columns + 1), n_in=2 * columns + 1,
    )(*[scored[r][1] for r in range(columns)], *[scored[r][2] for r in range(columns)], grads)
    att_mine, factors, inner = exchange(combined[:slots]), combined[slots:-1], combined[-1]

    halves = columns == heads == 4
    order = sorted(range(columns), reverse=True)
    add = call(add_kernel, [((dim, width), BF16)], n_in=2, after=1)
    add_halves = call(add_kernel, [((wide, block), BF16)], n_in=2)
    z_masks = [columns << level for level in range(slots.bit_length() - 1)]
    dkv, dq, kept, summed, later = {}, None, None, {}, []
    for at, r in enumerate(order):
        if at and not halves and at == columns - 1 or halves and at == 1:
            weight_terms = call(
                functools.partial(project_grad_kernel, slots, rows, a_of, b_of, halves),
                [((2, dim, width), BF16)] * 2 if halves else [((heads, dim, width), BF16)],
                [pltpu.VMEM((heads, dim, width), BF16)],
                n_in=2 + slots, smem_first=True, after=1, micros=0.7,
            )(tile_fill, grad_output, *att_mine, dkv[order[at - 1]])
            terms = call(
                functools.partial(project_kernel, slots, rows, a_of), [((rows, width), BF16)],
                n_in=2 + slots, smem_first=True, after=1, micros=0.7,
            )(tile_fill, out_weight, *att_mine, weight_terms[-1])[0]
            later, bit, first_terms = [terms], 1, terms
            while bit < mp // 2:
                terms = call(add_kernel, [((rows, width), BF16)], n_in=2)(terms, swap(terms, bit, "mp", mp))[0]
                bit *= 2
            terms_came = swap(terms, bit, "mp", mp)
            if halves:
                kept, sent = call(add_pairs_kernel, [((dim, width), BF16)] * 2, n_in=2, after=1)(
                    weight_terms[0], swap(weight_terms[1], 1), first_terms)
                later = [kept]
        if at == 2 and halves:
            kept = add(kept, swap(sent, 2), dkv[order[at - 1]])[0]
            later = [kept]
        if at == 3 and halves:
            kept = add(kept, swap(kept, z_masks[0]), dkv[order[at - 1]])[0]
            later = [kept, summed[2], terms_came]
        operands = [scored[r][0], *scored[r][3:], q_all, grads, factors[r], inner] + ([] if dq is None else [dq])
        dkv[r], dq = call(
            functools.partial(back_kernel, slots, rows, dim, dq is None),
            [((wide, block), BF16), ((dim, block), F32)], [pltpu.VMEM((wide, block), BF16)],
            n_in=len(operands), after=len(later), micros=2,
        )(*operands, *later)
        later = []
        if columns == 4 and r == 2:
            summed[2] = swap(add_halves(dkv[2], swap(dkv[3], 1))[0], 2)

    if columns == 4:
        halved = add_halves(dkv[0], swap(dkv[1], 1))[0], summed[2]
    else:
        bit = 1
        while 2 * bit < columns:
            dkv = {r: add_halves(dkv[r], swap(dkv[r ^ bit], bit))[0] for r in order if r in dkv and not r & bit}
            bit *= 2
        halved = dkv[0], swap(dkv[bit], bit)
    pieces = call(
        functools.partial(add_pieces_kernel, slots, rows, dim), [((wide + dim, rows), BF16)] * slots, n_in=3,
    )(*halved, dq)
    returned = exchange(pieces)

    key_value_grad, query_grad, attention_out, done = call(
        functools.partial(unpack_kernel, slots, rows, dim, a_of),
        [((rows * heads, wide), F32), ((heads, dim, rows), F32), ((rows, width), BF16), ((8, 128), F32)],
        n_in=slots + 2, micros=1,
    )(*returned, terms, terms_came)
    if halves:
        for mask in z_masks[1:]:
            kept = add(kept, swap(kept, mask), pieces[0])[0]
        across = call(functools.partial(join_kernel, 1), [((dim, width), BF16)], after=1)(swap(kept, 2), done)[0]
        weight_grad = call(
            functools.partial(place_kernel, columns, b_of), [((heads, dim, width), F32)], n_in=columns, micros=0.5,
        )(kept, swap(kept, 1), across, swap(across, 1))[0]
    else:
        weight_grad = lax.psum(weight_terms[0].astype(F32), "seq")
    return attention_out, jnp.transpose(query_grad, (2, 0, 1)), key_value_grad.reshape(rows, heads, wide), weight_grad


def solution(mesh):
    return jax.shard_map(
        functools.partial(shards, mesh.shape["seq"], mesh.shape["mp"]),
        mesh=mesh,
        in_specs=(
            P("seq", "mp", None),
            P("seq", "mp", None),
            P("seq"),
            P("mp", None, None),
            P("seq", None),
        ),
        out_specs=(P("seq", None), P("seq", "mp", None), P("seq", "mp", None), P("mp", None, None)),
        check_vma=False,
    )
```

```python
import functools

import jax
import jax.numpy as jnp
from jax import lax
from jax.experimental import pallas as pl
from jax.experimental.pallas import tpu as pltpu
from jax.sharding import PartitionSpec as P

TILE = 128
DEAD = 1024.0
BIAS = -1e30
LOG2_E = 1.4426950408889634
SAFE = 64.0
F32 = jnp.float32
BF16 = jnp.bfloat16
VMEM = pl.BlockSpec(memory_space=pltpu.VMEM)
SMEM = pl.BlockSpec(memory_space=pltpu.SMEM)
MIB = 1024 * 1024


def dot(a, b):
    return lax.dot_general(a, b, (((1,), (0,)), ((), ())), preferred_element_type=F32)


def dot_nt(a, b):
    return lax.dot_general(a, b, (((1,), (1,)), ((), ())), preferred_element_type=F32)


def call(kernel, outs, scratch=(), n_in=1, smem_first=False, after=0, micros=0.01, limit=16):
    specs = ([SMEM if smem_first else VMEM] + [VMEM] * (n_in - 1))[:n_in] + [pl.BlockSpec(memory_space=pl.ANY)] * after
    return pl.pallas_call(
        kernel,
        out_shape=[jax.ShapeDtypeStruct(shape, kind) for shape, kind in outs],
        in_specs=specs,
        out_specs=[VMEM] * len(outs),
        scratch_shapes=list(scratch),
        compiler_params=pltpu.CompilerParams(vmem_limit_bytes=limit * MIB),
        cost_estimate=pl.CostEstimate(flops=int(micros * 1.15e9), bytes_accessed=0, transcendentals=0),
    )


def live_column(fill_ref, rows):
    parts = []
    within = lax.broadcasted_iota(jnp.int32, (TILE, 1), 0)
    for tile in range(rows // TILE):
        parts.append(jnp.where(within < fill_ref[tile], 1.0, 0.0))
    return jnp.concatenate(parts, axis=0) if len(parts) > 1 else parts[0]


def live_row(fill_ref, rows):
    within = lax.broadcasted_iota(jnp.int32, (1, TILE), 1)
    parts = [jnp.where(within < fill_ref[tile], 1.0, 0.0) for tile in range(rows // TILE)]
    return jnp.concatenate(parts, axis=1) if len(parts) > 1 else parts[0]


def spread(slots):
    return [0] + sorted(range(1, slots), key=lambda mask: (mask < slots // 2, mask))


def pack_kv_kernel(heads, rows, dim, a_of, fill_ref, kv_ref, *refs):
    outs, (held,) = refs[:heads], refs[heads:]
    live = live_column(fill_ref, rows)
    lane = lax.broadcasted_iota(jnp.int32, (rows, 2 * dim), 1)
    mark = jnp.where(lane == 0, DEAD * (1.0 - live), 0.0)
    held[...] = kv_ref[...].astype(F32)
    me = a_of()
    for slot, mask in enumerate(spread(heads)):
        outs[slot][...] = (held[pl.ds(me ^ mask, rows, stride=heads), :] * live + mark).astype(BF16)


def pack_qg_kernel(heads, rows, dim, a_of, fill_ref, q_ref, w_ref, go_ref, *refs):
    outs, (held,) = refs[:heads], refs[heads:]
    grads = dot_nt(w_ref[...].reshape(heads * dim, go_ref.shape[1]), go_ref[...])
    grads = (grads * live_row(fill_ref, rows)).astype(BF16)
    for head in range(heads):
        held[head, 0:dim, :] = (q_ref[head].astype(F32) * dim**-0.5).astype(BF16)
        held[head, dim:, :] = grads[head * dim : (head + 1) * dim, :]
    me = a_of()
    for slot, mask in enumerate(spread(heads)):
        outs[slot][...] = held[me ^ mask]


def join_kernel(pieces, *refs):
    out_ref = refs[-1]
    rows = refs[0].shape[0]
    for index in range(pieces):
        out_ref[index * rows : (index + 1) * rows, :] = refs[index][...]


def join_q_kernel(slots, rows, dim, *refs):
    pieces, (qa_ref, q_ref, g_ref, norm_ref) = refs[:slots], refs[slots:]
    wide = 2 * dim
    row = lax.broadcasted_iota(jnp.int32, (dim, slots * rows), 0)
    qa_ref[wide : wide + dim, :] = jnp.zeros((dim, slots * rows), BF16)
    qa_ref[wide + dim :, :] = jnp.where(row == 0, 1.0, 0.0).astype(BF16)
    for slot in range(slots):
        here = slice(slot * rows, (slot + 1) * rows)
        queries = pieces[slot][0:dim, :]
        q_ref[:, here] = queries
        g_ref[:, here] = pieces[slot][dim:, :]
        scaled = queries.astype(F32) * LOG2_E
        high = scaled.astype(BF16)
        qa_ref[0:dim, here] = high
        qa_ref[dim:wide, here] = (scaled - high.astype(F32)).astype(BF16)
        norm_ref[:, here] = jnp.sum(scaled * scaled, axis=0, keepdims=True)


def score_kernel(slots, rows, dim, step, pair_ref, qa_ref, q_norm_ref, *refs):
    exp_ref, peak_ref, total_ref, v_ref, kt_ref, wide_ref, vt_ref, score_ref = refs[-8:]
    wide = 2 * dim
    keys = pair_ref.shape[0]
    full = pair_ref[...].astype(F32)
    turned = full.T
    norm = jnp.sum(turned[:dim, :] * turned[:dim, :], axis=0, keepdims=True)
    norm = jnp.where(turned[0:1, :] >= DEAD, 0.0, norm)
    small = jnp.max(norm) * jnp.max(q_norm_ref[...]) <= SAFE * SAFE
    lane = lax.broadcasted_iota(jnp.int32, (keys, wide), 1)
    bias = jnp.where(full[:, 0:1] >= DEAD, BIAS, 0.0)
    extra = jnp.where(lane == dim, bias, jnp.where(lane <= dim + 2, 1.0, 0.0))
    rolled = pltpu.roll(full, dim, 1)
    values = jnp.where(lane < dim, rolled, extra).astype(BF16)
    wide_ref[:, 0:wide] = jnp.where(lane < dim, full, rolled).astype(BF16)
    wide_ref[:, wide:] = values
    v_ref[...] = values
    kt_ref[...] = turned[:dim, :].astype(BF16)
    vt_ref[0:dim, :] = turned[dim:, :].astype(BF16)
    vt_ref[dim:, :] = jnp.ones((16, keys), BF16)

    @pl.when(small)
    def _():
        peak_ref[...] = jnp.zeros_like(peak_ref)
        ahead = dot(wide_ref[...], qa_ref[:, 0:rows])
        for slot in range(slots):
            here = slice(slot * rows, (slot + 1) * rows)
            scores = ahead
            if slot + 1 < slots:
                ahead = dot(wide_ref[...], qa_ref[:, (slot + 1) * rows : (slot + 2) * rows])
            exps = jnp.exp2(scores).astype(BF16)
            exp_ref[:, here] = exps
            total_ref[:, here] = dot(vt_ref[...], exps)

    @pl.when(jnp.logical_not(small))
    def _():
        for slot in range(slots):
            here = slice(slot * rows, (slot + 1) * rows)
            top = jnp.full((8, rows), BIAS, F32)
            for start in range(0, keys, step):
                part = slice(start, start + step)
                scores = dot(wide_ref[part, :], qa_ref[:, here])
                score_ref[part, :] = scores
                top = jnp.maximum(top, jnp.max(scores.reshape(step // 8, 8, rows), axis=0))
            peak = jnp.max(top, axis=0, keepdims=True)
            peak_ref[:, here] = peak
            total = jnp.zeros((dim + 16, rows), F32)
            for start in range(0, keys, step):
                part = slice(start, start + step)
                exps = jnp.exp2(score_ref[part, :] - peak).astype(BF16)
                exp_ref[part, here] = exps
                total = total + dot(vt_ref[:, part], exps)
            total_ref[:, here] = total


def combine_kernel(slots, columns, rows, dim, *refs):
    peaks, totals, (g_ref,), outs = refs[:columns], refs[columns : 2 * columns], refs[2 * columns : 2 * columns + 1], refs[2 * columns + 1 :]
    att_out, factors_out, inner_ref = outs[:slots], outs[slots : slots + columns], outs[-1]
    peak = functools.reduce(jnp.maximum, [ref[...] for ref in peaks])
    factors = [jnp.exp2(ref[...] - peak) for ref in peaks]
    total = sum(factor * ref[...] for factor, ref in zip(factors, totals))
    inverse = 1.0 / total[dim : dim + 1, :]
    attended = (total[0:dim, :] * inverse).astype(BF16)
    for slot in range(slots):
        att_out[slot][...] = attended[:, slot * rows : (slot + 1) * rows]
    for factor, ref in zip(factors, factors_out):
        ref[...] = factor * inverse
    inner_ref[...] = jnp.sum(g_ref[...].astype(F32) * attended.astype(F32), axis=0, keepdims=True)


def back_kernel(slots, rows, dim, first, exp_ref, v_ref, kt_ref, q_ref, g_ref, factor_ref, inner_ref, *refs):
    dkv_ref, dq_ref, ga_ref = refs[-3:]
    block = g_ref.shape[1]
    factor = factor_ref[...]
    inner = inner_ref[...] * factor
    high = inner.astype(BF16).astype(F32)
    row = lax.broadcasted_iota(jnp.int32, (dim, block), 0)
    ga_ref[0:dim, :] = (g_ref[...].astype(F32) * factor).astype(BF16)
    ga_ref[dim:, :] = jnp.where(row == 1, -high, jnp.where(row == 2, high - inner, 0.0)).astype(BF16)
    grad_k = grad_v = None
    ahead = dot(v_ref[...], ga_ref[:, 0:rows])
    for slot in range(slots):
        here = slice(slot * rows, (slot + 1) * rows)
        products = ahead
        if slot + 1 < slots:
            ahead = dot(v_ref[...], ga_ref[:, (slot + 1) * rows : (slot + 2) * rows])
        exps = exp_ref[:, here]
        grads = exps * products.astype(BF16)
        term_v = dot_nt(ga_ref[0:dim, here], exps)
        term_k = dot_nt(q_ref[:, here], grads)
        grad_v = term_v if grad_v is None else grad_v + term_v
        grad_k = term_k if grad_k is None else grad_k + term_k
        term = dot(kt_ref[...], grads)
        dq_ref[:, here] = term if first else refs[0][:, here] + term
    dkv_ref[dim:, :] = grad_v.astype(BF16)
    dkv_ref[0:dim, :] = grad_k.astype(BF16)


def project_kernel(slots, rows, a_of, b_of, halves, fill_ref, go_ref, w_ref, *refs):
    att, refs = refs[:slots], refs[slots + 1 :]
    terms_ref, held = refs[0], refs[-1]
    me = a_of()
    dim = held.shape[1]
    stacked = jnp.concatenate([ref[...].astype(F32) for ref in att], axis=0) * live_row(fill_ref, rows)
    grads = dot(stacked.astype(BF16), go_ref[...]).astype(BF16)
    for slot, mask in enumerate(spread(slots)):
        held[me ^ mask] = grads[slot * dim : (slot + 1) * dim, :]
    weights = jnp.concatenate([w_ref[me ^ mask] for mask in spread(slots)], axis=0)
    terms_ref[...] = dot(stacked.T.astype(BF16), weights).astype(BF16)
    if not halves:
        refs[1][...] = held[...]
        return
    me = b_of()
    kept_ref, sent_ref = refs[1], refs[2]
    for pair in range(slots // 2):
        kept_ref[pair] = held[me ^ (2 * pair)]
        sent_ref[pair] = held[me ^ (2 * pair) ^ 1]


def add_pairs_kernel(kept_ref, came_ref, _, first_ref, second_ref):
    for index, out_ref in enumerate((first_ref, second_ref)):
        out_ref[...] = (kept_ref[index].astype(F32) + came_ref[index].astype(F32)).astype(BF16)


def add_pieces_kernel(slots, rows, dim, kept_ref, came_ref, dq_ref, *outs):
    wide = 2 * dim
    for slot in range(slots):
        here = slice(slot * rows, (slot + 1) * rows)
        outs[slot][0:wide, :] = (kept_ref[:, here].astype(F32) + came_ref[:, here].astype(F32)).astype(BF16)
        outs[slot][wide:, :] = (dq_ref[:, here] * dim**-0.5).astype(BF16)


def add_kernel(a_ref, b_ref, *refs):
    refs[-1][...] = (a_ref[...].astype(F32) + b_ref[...].astype(F32)).astype(refs[-1].dtype)


def unpack_kernel(slots, rows, dim, a_of, *refs):
    pieces, (a_ref, b_ref, _, kv_out, q_out, sum_out) = refs[:slots], refs[slots:]
    sum_out[...] = (a_ref[...].astype(F32) + b_ref[...].astype(F32)).astype(BF16)
    wide = 2 * dim
    me = a_of()
    for slot, mask in enumerate(spread(slots)):
        kv_out[pl.ds(me ^ mask, rows, stride=slots), :] = pieces[slot][0:wide, :].astype(F32).T
        q_out[me ^ mask] = pieces[slot][wide:, :].astype(F32)


def token_kernel(*refs):
    refs[-1][...] = jnp.zeros_like(refs[-1])


def place_kernel(columns, b_of, *refs):
    parts, (grad_out,) = refs[:columns], refs[columns:]
    me = b_of()
    for column in range(columns):
        grad_out[me ^ column] = parts[column][...].astype(F32)


def shards(seq, mp, queries, key_value, tile_fill, out_weight, grad_output):
    rows, heads, dim = queries.shape
    width = grad_output.shape[1]
    slots = heads
    columns = seq // slots
    assert slots * columns == seq and columns & (columns - 1) == 0 and slots & (slots - 1) == 0
    a_of = lambda: lax.axis_index("seq") // columns
    b_of = lambda: lax.axis_index("seq") % columns

    def swap(array, mask, axis="seq", size=seq):
        return lax.ppermute(array, axis, [(i, i ^ mask) for i in range(size)])

    def exchange(pieces):
        return [pieces[0]] + [swap(piece, mask * columns) for piece, mask in zip(pieces[1:], spread(slots)[1:])]

    block, wide = slots * rows, 2 * dim
    kv_mine = exchange(call(
        functools.partial(pack_kv_kernel, heads, rows, dim, a_of),
        [((rows, wide), BF16)] * slots, [pltpu.VMEM((rows * heads, wide), F32)],
        n_in=2, smem_first=True, micros=1.5, limit=56,
    )(tile_fill, key_value.reshape(rows * heads, wide)))
    qg_send = call(
        functools.partial(pack_qg_kernel, heads, rows, dim, a_of),
        [((wide, rows), BF16)] * slots, [pltpu.VMEM((heads, wide, rows), BF16)],
        n_in=4, smem_first=True, micros=1,
    )(tile_fill, jnp.transpose(queries, (1, 2, 0)), out_weight, grad_output)
    qg_mine = exchange(qg_send)
    own = call(
        functools.partial(join_kernel, slots), [((block, wide), BF16)], n_in=slots, after=1,
    )(*kv_mine, qg_send[0])[0]

    qa, q_all, grads, q_norm = call(
        functools.partial(join_q_kernel, slots, rows, dim),
        [((2 * wide, block), BF16), ((dim, block), BF16), ((dim, block), BF16), ((1, block), F32)], n_in=slots,
    )(*qg_mine)
    step = min(block, 512)
    scored, blocks = {}, {0: own}
    bit = columns // 2
    while bit:
        for r in sorted(blocks):
            blocks[r ^ bit] = swap(blocks[r], bit)
        bit //= 2
    for r in range(columns):
        if r == 2 and columns == 4:
            blocks[2] = call(functools.partial(join_kernel, 1), [((block, wide), BF16)], after=1)(
                blocks[2], scored[1][1])[0]
            blocks[3] = swap(blocks[2], 1)
        scored[r] = call(
            functools.partial(score_kernel, slots, rows, dim, step),
            [((block, block), BF16), ((1, block), F32), ((dim + 16, block), F32), ((block, wide), BF16), ((dim, block), BF16)],
            [pltpu.VMEM((block, 2 * wide), BF16), pltpu.VMEM((dim + 16, block), BF16), pltpu.VMEM((block, rows), F32)],
            n_in=3, after=min(r, 1), micros=5,
        )(blocks[r], qa, q_norm, *([scored[r - 1][1]] if r else []))
    combined = call(
        functools.partial(combine_kernel, slots, columns, rows, dim),
        [((dim, rows), BF16)] * slots + [((1, block), F32)] * (columns + 1), n_in=2 * columns + 1,
    )(*[scored[r][1] for r in range(columns)], *[scored[r][2] for r in range(columns)], grads)
    att_mine, factors, inner = exchange(combined[:slots]), combined[slots:-1], combined[-1]

    halves = columns == heads == 4
    order = sorted(range(columns), reverse=True)
    add = call(add_kernel, [((dim, width), BF16)], n_in=2, after=1)
    add_halves = call(add_kernel, [((wide, block), BF16)], n_in=2)
    z_masks = [columns << level for level in range(slots.bit_length() - 1)]
    dkv, dq, kept, summed, later = {}, None, None, {}, []
    for at, r in enumerate(order):
        if at and not halves and at == columns - 1 or halves and at == 1:
            terms, *weight_terms = call(
                functools.partial(project_kernel, slots, rows, a_of, b_of, halves),
                [((rows, width), BF16)] + ([((2, dim, width), BF16)] * 2 if halves else [((heads, dim, width), BF16)]),
                [pltpu.VMEM((heads, dim, width), BF16)],
                n_in=3 + slots, smem_first=True, after=1, micros=0.7,
            )(tile_fill, grad_output, out_weight, *att_mine, dkv[order[at - 1]])
            later, bit = [terms], 1
            while bit < mp // 2:
                terms = call(add_kernel, [((rows, width), BF16)], n_in=2)(terms, swap(terms, bit, "mp", mp))[0]
                bit *= 2
            terms_came = swap(terms, bit, "mp", mp)
            if halves:
                kept, sent = call(add_pairs_kernel, [((dim, width), BF16)] * 2, n_in=2, after=1)(
                    weight_terms[0], swap(weight_terms[1], 1), weight_terms[0])
                later = [kept]
        if at == 2 and halves:
            kept = add(kept, swap(sent, 2), dkv[order[at - 1]])[0]
            later = [kept]
        if at == 3 and halves:
            kept = add(kept, swap(kept, z_masks[0]), dkv[order[at - 1]])[0]
            later = [kept, summed[2], terms_came]
        operands = [scored[r][0], *scored[r][3:], q_all, grads, factors[r], inner] + ([] if dq is None else [dq])
        dkv[r], dq = call(
            functools.partial(back_kernel, slots, rows, dim, dq is None),
            [((wide, block), BF16), ((dim, block), F32)], [pltpu.VMEM((wide, block), BF16)],
            n_in=len(operands), after=len(later), micros=2,
        )(*operands, *later)
        later = []
        if columns == 4 and r == 2:
            summed[2] = swap(add_halves(dkv[2], swap(dkv[3], 1))[0], 2)

    if columns == 4:
        halved = add_halves(dkv[0], swap(dkv[1], 1))[0], summed[2]
    else:
        bit = 1
        while 2 * bit < columns:
            dkv = {r: add_halves(dkv[r], swap(dkv[r ^ bit], bit))[0] for r in order if r in dkv and not r & bit}
            bit *= 2
        halved = dkv[0], swap(dkv[bit], bit)
    pieces = call(
        functools.partial(add_pieces_kernel, slots, rows, dim), [((wide + dim, rows), BF16)] * slots, n_in=3,
    )(*halved, dq)
    returned = exchange(pieces)

    arrived = call(token_kernel, [((8, 128), F32)], n_in=0, after=slots)(*returned)[0]
    if halves:
        for mask in z_masks[1:]:
            kept = add(kept, swap(kept, mask), pieces[0])[0]
        across = call(functools.partial(join_kernel, 1), [((dim, width), BF16)], after=1)(swap(kept, 2), arrived)[0]
        weight_grad = call(
            functools.partial(place_kernel, columns, b_of), [((heads, dim, width), F32)], n_in=columns, micros=0.5,
        )(kept, swap(kept, 1), across, swap(across, 1))[0]
        arrived = across
    else:
        weight_grad = lax.psum(weight_terms[0].astype(F32), "seq")
    key_value_grad, query_grad, attention_out = call(
        functools.partial(unpack_kernel, slots, rows, dim, a_of),
        [((rows * heads, wide), F32), ((heads, dim, rows), F32), ((rows, width), BF16)],
        n_in=slots + 2, after=1, micros=5,
    )(*returned, terms, terms_came, arrived)
    return attention_out, jnp.transpose(query_grad, (2, 0, 1)), key_value_grad.reshape(rows, heads, wide), weight_grad


def solution(mesh):
    return jax.shard_map(
        functools.partial(shards, mesh.shape["seq"], mesh.shape["mp"]),
        mesh=mesh,
        in_specs=(
            P("seq", "mp", None),
            P("seq", "mp", None),
            P("seq"),
            P("mp", None, None),
            P("seq", None),
        ),
        out_specs=(P("seq", None), P("seq", "mp", None), P("seq", "mp", None), P("mp", None, None)),
        check_vma=False,
    )
```

```python
import functools

import jax
import jax.numpy as jnp
from jax import lax
from jax.experimental import pallas as pl
from jax.experimental.pallas import tpu as pltpu
from jax.sharding import PartitionSpec as P

TILE = 128
DEAD = 1024.0
BIAS = -1e30
LOG2_E = 1.4426950408889634
SAFE = 64.0
F32 = jnp.float32
BF16 = jnp.bfloat16
VMEM = pl.BlockSpec(memory_space=pltpu.VMEM)
SMEM = pl.BlockSpec(memory_space=pltpu.SMEM)
MIB = 1024 * 1024


def dot(a, b):
    return lax.dot_general(a, b, (((1,), (0,)), ((), ())), preferred_element_type=F32)


def dot_nt(a, b):
    return lax.dot_general(a, b, (((1,), (1,)), ((), ())), preferred_element_type=F32)


def call(kernel, outs, scratch=(), n_in=1, smem_first=False, after=0, micros=0.01, limit=16):
    specs = ([SMEM if smem_first else VMEM] + [VMEM] * (n_in - 1))[:n_in] + [pl.BlockSpec(memory_space=pl.ANY)] * after
    return pl.pallas_call(
        kernel,
        out_shape=[jax.ShapeDtypeStruct(shape, kind) for shape, kind in outs],
        in_specs=specs,
        out_specs=[VMEM] * len(outs),
        scratch_shapes=list(scratch),
        compiler_params=pltpu.CompilerParams(vmem_limit_bytes=limit * MIB),
        cost_estimate=pl.CostEstimate(flops=int(micros * 1.15e9), bytes_accessed=0, transcendentals=0),
    )


def live_column(fill_ref, rows):
    parts = []
    within = lax.broadcasted_iota(jnp.int32, (TILE, 1), 0)
    for tile in range(rows // TILE):
        parts.append(jnp.where(within < fill_ref[tile], 1.0, 0.0))
    return jnp.concatenate(parts, axis=0) if len(parts) > 1 else parts[0]


def live_row(fill_ref, rows):
    within = lax.broadcasted_iota(jnp.int32, (1, TILE), 1)
    parts = [jnp.where(within < fill_ref[tile], 1.0, 0.0) for tile in range(rows // TILE)]
    return jnp.concatenate(parts, axis=1) if len(parts) > 1 else parts[0]


def spread(slots):
    return [0] + list(range(slots - 1, 0, -1))


def pack_kv_kernel(heads, rows, dim, a_of, fill_ref, kv_ref, *refs):
    outs, (held,) = refs[:heads], refs[heads:]
    live = live_column(fill_ref, rows)
    lane = lax.broadcasted_iota(jnp.int32, (rows, 2 * dim), 1)
    mark = jnp.where(lane == 0, DEAD * (1.0 - live), 0.0)
    held[...] = kv_ref[...].astype(F32)
    me = a_of()
    for slot, mask in enumerate(spread(heads)):
        outs[slot][...] = (held[pl.ds(me ^ mask, rows, stride=heads), :] * live + mark).astype(BF16)


def pack_qg_kernel(heads, rows, dim, a_of, fill_ref, q_ref, w_ref, go_ref, *refs):
    outs, (held,) = refs[:heads], refs[heads:]
    grads = dot_nt(w_ref[...].reshape(heads * dim, go_ref.shape[1]), go_ref[...])
    grads = (grads * live_row(fill_ref, rows)).astype(BF16)
    for head in range(heads):
        held[head, 0:dim, :] = (q_ref[head].astype(F32) * dim**-0.5).astype(BF16)
        held[head, dim:, :] = grads[head * dim : (head + 1) * dim, :]
    me = a_of()
    for slot, mask in enumerate(spread(heads)):
        outs[slot][...] = held[me ^ mask]


def join_kernel(pieces, *refs):
    out_ref = refs[-1]
    rows = refs[0].shape[0]
    for index in range(pieces):
        out_ref[index * rows : (index + 1) * rows, :] = refs[index][...]


def join_q_kernel(slots, rows, dim, *refs):
    pieces, (qa_ref, q_ref, g_ref, norm_ref) = refs[:slots], refs[slots:]
    wide = 2 * dim
    row = lax.broadcasted_iota(jnp.int32, (dim, slots * rows), 0)
    qa_ref[wide : wide + dim, :] = jnp.zeros((dim, slots * rows), BF16)
    qa_ref[wide + dim :, :] = jnp.where(row == 0, 1.0, 0.0).astype(BF16)
    for slot in range(slots):
        here = slice(slot * rows, (slot + 1) * rows)
        queries = pieces[slot][0:dim, :]
        q_ref[:, here] = queries
        g_ref[:, here] = pieces[slot][dim:, :]
        scaled = queries.astype(F32) * LOG2_E
        high = scaled.astype(BF16)
        qa_ref[0:dim, here] = high
        qa_ref[dim:wide, here] = (scaled - high.astype(F32)).astype(BF16)
        norm_ref[:, here] = jnp.sum(scaled * scaled, axis=0, keepdims=True)


def score_kernel(slots, rows, dim, step, pair_ref, qa_ref, q_norm_ref, *refs):
    exp_ref, peak_ref, total_ref, v_ref, kt_ref, wide_ref, vt_ref, score_ref = refs[-8:]
    wide = 2 * dim
    keys = pair_ref.shape[0]
    full = pair_ref[...].astype(F32)
    turned = full.T
    norm = jnp.sum(turned[:dim, :] * turned[:dim, :], axis=0, keepdims=True)
    norm = jnp.where(turned[0:1, :] >= DEAD, 0.0, norm)
    small = jnp.max(norm) * jnp.max(q_norm_ref[...]) <= SAFE * SAFE
    lane = lax.broadcasted_iota(jnp.int32, (keys, wide), 1)
    bias = jnp.where(full[:, 0:1] >= DEAD, BIAS, 0.0)
    extra = jnp.where(lane == dim, bias, jnp.where(lane <= dim + 2, 1.0, 0.0))
    rolled = pltpu.roll(full, dim, 1)
    values = jnp.where(lane < dim, rolled, extra).astype(BF16)
    wide_ref[:, 0:wide] = jnp.where(lane < dim, full, rolled).astype(BF16)
    wide_ref[:, wide:] = values
    v_ref[...] = values
    kt_ref[...] = turned[:dim, :].astype(BF16)
    vt_ref[0:dim, :] = turned[dim:, :].astype(BF16)
    vt_ref[dim:, :] = jnp.ones((16, keys), BF16)

    @pl.when(small)
    def _():
        peak_ref[...] = jnp.zeros_like(peak_ref)
        ahead = dot(wide_ref[...], qa_ref[:, 0:rows])
        for slot in range(slots):
            here = slice(slot * rows, (slot + 1) * rows)
            scores = ahead
            if slot + 1 < slots:
                ahead = dot(wide_ref[...], qa_ref[:, (slot + 1) * rows : (slot + 2) * rows])
            exps = jnp.exp2(scores).astype(BF16)
            exp_ref[:, here] = exps
            total_ref[:, here] = dot(vt_ref[...], exps)

    @pl.when(jnp.logical_not(small))
    def _():
        for slot in range(slots):
            here = slice(slot * rows, (slot + 1) * rows)
            top = jnp.full((8, rows), BIAS, F32)
            for start in range(0, keys, step):
                part = slice(start, start + step)
                scores = dot(wide_ref[part, :], qa_ref[:, here])
                score_ref[part, :] = scores
                top = jnp.maximum(top, jnp.max(scores.reshape(step // 8, 8, rows), axis=0))
            peak = jnp.max(top, axis=0, keepdims=True)
            peak_ref[:, here] = peak
            total = jnp.zeros((dim + 16, rows), F32)
            for start in range(0, keys, step):
                part = slice(start, start + step)
                exps = jnp.exp2(score_ref[part, :] - peak).astype(BF16)
                exp_ref[part, here] = exps
                total = total + dot(vt_ref[:, part], exps)
            total_ref[:, here] = total


def combine_kernel(slots, columns, rows, dim, *refs):
    peaks, totals, (g_ref,), outs = refs[:columns], refs[columns : 2 * columns], refs[2 * columns : 2 * columns + 1], refs[2 * columns + 1 :]
    att_out, factors_out, inner_ref = outs[:slots], outs[slots : slots + columns], outs[-1]
    peak = functools.reduce(jnp.maximum, [ref[...] for ref in peaks])
    factors = [jnp.exp2(ref[...] - peak) for ref in peaks]
    total = sum(factor * ref[...] for factor, ref in zip(factors, totals))
    inverse = 1.0 / total[dim : dim + 1, :]
    attended = (total[0:dim, :] * inverse).astype(BF16)
    for slot in range(slots):
        att_out[slot][...] = attended[:, slot * rows : (slot + 1) * rows]
    for factor, ref in zip(factors, factors_out):
        ref[...] = factor * inverse
    inner_ref[...] = jnp.sum(g_ref[...].astype(F32) * attended.astype(F32), axis=0, keepdims=True)


def back_kernel(slots, rows, dim, first, exp_ref, v_ref, kt_ref, q_ref, g_ref, factor_ref, inner_ref, *refs):
    dkv_ref, dq_ref, ga_ref, ds_ref = refs[-4:]
    block = g_ref.shape[1]
    factor = factor_ref[...]
    inner = inner_ref[...] * factor
    high = inner.astype(BF16).astype(F32)
    row = lax.broadcasted_iota(jnp.int32, (dim, block), 0)
    ga_ref[0:dim, :] = (g_ref[...].astype(F32) * factor).astype(BF16)
    ga_ref[dim:, :] = jnp.where(row == 1, -high, jnp.where(row == 2, high - inner, 0.0)).astype(BF16)
    ahead = dot(v_ref[...], ga_ref[:, 0:rows])
    for slot in range(slots):
        here = slice(slot * rows, (slot + 1) * rows)
        products = ahead
        if slot + 1 < slots:
            ahead = dot(v_ref[...], ga_ref[:, (slot + 1) * rows : (slot + 2) * rows])
        grads = exp_ref[:, here] * products.astype(BF16)
        ds_ref[:, here] = grads
        term = dot(kt_ref[...], grads)
        dq_ref[:, here] = term if first else refs[0][:, here] + term
    dkv_ref[dim:, :] = dot_nt(ga_ref[0:dim, :], exp_ref[...]).astype(BF16)
    dkv_ref[0:dim, :] = dot_nt(q_ref[...], ds_ref[...]).astype(BF16)


def project_kernel(slots, rows, a_of, b_of, halves, fill_ref, go_ref, w_ref, *refs):
    att, refs = refs[:slots], refs[slots + 1 :]
    terms_ref, held = refs[0], refs[-1]
    me = a_of()
    dim = held.shape[1]
    stacked = jnp.concatenate([ref[...].astype(F32) for ref in att], axis=0) * live_row(fill_ref, rows)
    grads = dot(stacked.astype(BF16), go_ref[...]).astype(BF16)
    for slot, mask in enumerate(spread(slots)):
        held[me ^ mask] = grads[slot * dim : (slot + 1) * dim, :]
    weights = jnp.concatenate([w_ref[me ^ mask] for mask in spread(slots)], axis=0)
    terms_ref[...] = dot(stacked.T.astype(BF16), weights).astype(BF16)
    if not halves:
        refs[1][...] = held[...]
        return
    me = b_of()
    kept_ref, sent_ref = refs[1], refs[2]
    for pair in range(slots // 2):
        kept_ref[pair] = held[me ^ (2 * pair)]
        sent_ref[pair] = held[me ^ (2 * pair) ^ 1]


def add_pairs_kernel(kept_ref, came_ref, _, first_ref, second_ref):
    for index, out_ref in enumerate((first_ref, second_ref)):
        out_ref[...] = (kept_ref[index].astype(F32) + came_ref[index].astype(F32)).astype(BF16)


def add_pieces_kernel(slots, rows, dim, kept_ref, came_ref, dq_ref, *outs):
    wide = 2 * dim
    for slot in range(slots):
        here = slice(slot * rows, (slot + 1) * rows)
        outs[slot][0:wide, :] = (kept_ref[:, here].astype(F32) + came_ref[:, here].astype(F32)).astype(BF16)
        outs[slot][wide:, :] = (dq_ref[:, here] * dim**-0.5).astype(BF16)


def add_kernel(a_ref, b_ref, *refs):
    refs[-1][...] = (a_ref[...].astype(F32) + b_ref[...].astype(F32)).astype(refs[-1].dtype)


def unpack_kernel(slots, rows, dim, a_of, *refs):
    pieces, (a_ref, b_ref, _, kv_out, q_out, sum_out) = refs[:slots], refs[slots:]
    sum_out[...] = (a_ref[...].astype(F32) + b_ref[...].astype(F32)).astype(BF16)
    wide = 2 * dim
    me = a_of()
    for slot, mask in enumerate(spread(slots)):
        kv_out[pl.ds(me ^ mask, rows, stride=slots), :] = pieces[slot][0:wide, :].astype(F32).T
        q_out[me ^ mask] = pieces[slot][wide:, :].astype(F32)


def token_kernel(*refs):
    refs[-1][...] = jnp.zeros_like(refs[-1])


def place_kernel(columns, b_of, *refs):
    parts, (grad_out,) = refs[:columns], refs[columns:]
    me = b_of()
    for column in range(columns):
        grad_out[me ^ column] = parts[column][...].astype(F32)


def shards(seq, mp, queries, key_value, tile_fill, out_weight, grad_output):
    rows, heads, dim = queries.shape
    width = grad_output.shape[1]
    slots = heads
    columns = seq // slots
    assert slots * columns == seq and columns & (columns - 1) == 0 and slots & (slots - 1) == 0
    a_of = lambda: lax.axis_index("seq") // columns
    b_of = lambda: lax.axis_index("seq") % columns

    def swap(array, mask, axis="seq", size=seq):
        return lax.ppermute(array, axis, [(i, i ^ mask) for i in range(size)])

    def exchange(pieces):
        return [pieces[0]] + [swap(piece, mask * columns) for piece, mask in zip(pieces[1:], spread(slots)[1:])]

    block, wide = slots * rows, 2 * dim
    kv_mine = exchange(call(
        functools.partial(pack_kv_kernel, heads, rows, dim, a_of),
        [((rows, wide), BF16)] * slots, [pltpu.VMEM((rows * heads, wide), F32)],
        n_in=2, smem_first=True, micros=1.5, limit=56,
    )(tile_fill, key_value.reshape(rows * heads, wide)))
    qg_send = call(
        functools.partial(pack_qg_kernel, heads, rows, dim, a_of),
        [((wide, rows), BF16)] * slots, [pltpu.VMEM((heads, wide, rows), BF16)],
        n_in=4, smem_first=True, micros=1,
    )(tile_fill, jnp.transpose(queries, (1, 2, 0)), out_weight, grad_output)
    qg_mine = exchange(qg_send)
    own = call(
        functools.partial(join_kernel, slots), [((block, wide), BF16)], n_in=slots, after=1,
    )(*kv_mine, qg_send[0])[0]

    qa, q_all, grads, q_norm = call(
        functools.partial(join_q_kernel, slots, rows, dim),
        [((2 * wide, block), BF16), ((dim, block), BF16), ((dim, block), BF16), ((1, block), F32)], n_in=slots,
    )(*qg_mine)
    step = min(block, 512)
    scored, blocks = {}, {0: own}
    bit = columns // 2
    while bit:
        for r in sorted(blocks):
            blocks[r ^ bit] = swap(blocks[r], bit)
        bit //= 2
    for r in range(columns):
        if r == 2 and columns == 4:
            blocks[2] = call(functools.partial(join_kernel, 1), [((block, wide), BF16)], after=1)(
                blocks[2], scored[1][1])[0]
            blocks[3] = swap(blocks[2], 1)
        scored[r] = call(
            functools.partial(score_kernel, slots, rows, dim, step),
            [((block, block), BF16), ((1, block), F32), ((dim + 16, block), F32), ((block, wide), BF16), ((dim, block), BF16)],
            [pltpu.VMEM((block, 2 * wide), BF16), pltpu.VMEM((dim + 16, block), BF16), pltpu.VMEM((block, rows), F32)],
            n_in=3, after=min(r, 1), micros=5,
        )(blocks[r], qa, q_norm, *([scored[r - 1][1]] if r else []))
    combined = call(
        functools.partial(combine_kernel, slots, columns, rows, dim),
        [((dim, rows), BF16)] * slots + [((1, block), F32)] * (columns + 1), n_in=2 * columns + 1,
    )(*[scored[r][1] for r in range(columns)], *[scored[r][2] for r in range(columns)], grads)
    att_mine, factors, inner = exchange(combined[:slots]), combined[slots:-1], combined[-1]

    halves = columns == heads == 4
    order = sorted(range(columns), reverse=True)
    add = call(add_kernel, [((dim, width), BF16)], n_in=2, after=1)
    add_halves = call(add_kernel, [((wide, block), BF16)], n_in=2)
    z_masks = [columns << level for level in range(slots.bit_length() - 1)]
    dkv, dq, kept, summed, later = {}, None, None, {}, []
    for at, r in enumerate(order):
        if at and not halves and at == columns - 1 or halves and at == 1:
            terms, *weight_terms = call(
                functools.partial(project_kernel, slots, rows, a_of, b_of, halves),
                [((rows, width), BF16)] + ([((2, dim, width), BF16)] * 2 if halves else [((heads, dim, width), BF16)]),
                [pltpu.VMEM((heads, dim, width), BF16)],
                n_in=3 + slots, smem_first=True, after=1, micros=0.7,
            )(tile_fill, grad_output, out_weight, *att_mine, dkv[order[at - 1]])
            later, bit = [terms], 1
            while bit < mp // 2:
                terms = call(add_kernel, [((rows, width), BF16)], n_in=2)(terms, swap(terms, bit, "mp", mp))[0]
                bit *= 2
            terms_came = swap(terms, bit, "mp", mp)
            if halves:
                kept, sent = call(add_pairs_kernel, [((dim, width), BF16)] * 2, n_in=2, after=1)(
                    weight_terms[0], swap(weight_terms[1], 1), weight_terms[0])
                later = [kept]
        if at == 2 and halves:
            kept = add(kept, swap(sent, 2), dkv[order[at - 1]])[0]
            later = [kept]
        if at == 3 and halves:
            kept = add(kept, swap(kept, z_masks[0]), dkv[order[at - 1]])[0]
            later = [kept, summed[2], terms_came]
        operands = [scored[r][0], *scored[r][3:], q_all, grads, factors[r], inner] + ([] if dq is None else [dq])
        dkv[r], dq = call(
            functools.partial(back_kernel, slots, rows, dim, dq is None),
            [((wide, block), BF16), ((dim, block), F32)], [pltpu.VMEM((wide, block), BF16), pltpu.VMEM((block, block), BF16)],
            n_in=len(operands), after=len(later), micros=2,
        )(*operands, *later)
        later = []
        if columns == 4 and r == 2:
            summed[2] = swap(add_halves(dkv[2], swap(dkv[3], 1))[0], 2)

    if columns == 4:
        halved = add_halves(dkv[0], swap(dkv[1], 1))[0], summed[2]
    else:
        bit = 1
        while 2 * bit < columns:
            dkv = {r: add_halves(dkv[r], swap(dkv[r ^ bit], bit))[0] for r in order if r in dkv and not r & bit}
            bit *= 2
        halved = dkv[0], swap(dkv[bit], bit)
    pieces = call(
        functools.partial(add_pieces_kernel, slots, rows, dim), [((wide + dim, rows), BF16)] * slots, n_in=3,
    )(*halved, dq)
    returned = exchange(pieces)

    arrived = call(token_kernel, [((8, 128), F32)], n_in=0, after=slots)(*returned)[0]
    if halves:
        for mask in z_masks[1:]:
            kept = add(kept, swap(kept, mask), pieces[0])[0]
        across = call(functools.partial(join_kernel, 1), [((dim, width), BF16)], after=1)(swap(kept, 2), arrived)[0]
        weight_grad = call(
            functools.partial(place_kernel, columns, b_of), [((heads, dim, width), F32)], n_in=columns, micros=0.5,
        )(kept, swap(kept, 1), across, swap(across, 1))[0]
        arrived = across
    else:
        weight_grad = lax.psum(weight_terms[0].astype(F32), "seq")
    key_value_grad, query_grad, attention_out = call(
        functools.partial(unpack_kernel, slots, rows, dim, a_of),
        [((rows * heads, wide), F32), ((heads, dim, rows), F32), ((rows, width), BF16)],
        n_in=slots + 2, after=1, micros=5,
    )(*returned, terms, terms_came, arrived)
    return attention_out, jnp.transpose(query_grad, (2, 0, 1)), key_value_grad.reshape(rows, heads, wide), weight_grad


def solution(mesh):
    return jax.shard_map(
        functools.partial(shards, mesh.shape["seq"], mesh.shape["mp"]),
        mesh=mesh,
        in_specs=(
            P("seq", "mp", None),
            P("seq", "mp", None),
            P("seq"),
            P("mp", None, None),
            P("seq", None),
        ),
        out_specs=(P("seq", None), P("seq", "mp", None), P("seq", "mp", None), P("mp", None, None)),
        check_vma=False,
    )
```

```python
import functools

import jax
import jax.numpy as jnp
from jax import lax
from jax.experimental import pallas as pl
from jax.experimental.pallas import tpu as pltpu
from jax.sharding import PartitionSpec as P

TILE = 128
DEAD = 1024.0
BIAS = -1e30
LOG2_E = 1.4426950408889634
SAFE = 64.0
F32 = jnp.float32
BF16 = jnp.bfloat16
VMEM = pl.BlockSpec(memory_space=pltpu.VMEM)
SMEM = pl.BlockSpec(memory_space=pltpu.SMEM)
MIB = 1024 * 1024


def dot(a, b):
    return lax.dot_general(a, b, (((1,), (0,)), ((), ())), preferred_element_type=F32)


def dot_nt(a, b):
    return lax.dot_general(a, b, (((1,), (1,)), ((), ())), preferred_element_type=F32)


def call(kernel, outs, scratch=(), n_in=1, smem_first=False, after=0, micros=0.01, limit=16):
    specs = ([SMEM if smem_first else VMEM] + [VMEM] * (n_in - 1))[:n_in] + [pl.BlockSpec(memory_space=pl.ANY)] * after
    return pl.pallas_call(
        kernel,
        out_shape=[jax.ShapeDtypeStruct(shape, kind) for shape, kind in outs],
        in_specs=specs,
        out_specs=[VMEM] * len(outs),
        scratch_shapes=list(scratch),
        compiler_params=pltpu.CompilerParams(vmem_limit_bytes=limit * MIB),
        cost_estimate=pl.CostEstimate(flops=int(micros * 1.15e9), bytes_accessed=0, transcendentals=0),
    )


def live_column(fill_ref, rows):
    parts = []
    within = lax.broadcasted_iota(jnp.int32, (TILE, 1), 0)
    for tile in range(rows // TILE):
        parts.append(jnp.where(within < fill_ref[tile], 1.0, 0.0))
    return jnp.concatenate(parts, axis=0) if len(parts) > 1 else parts[0]


def live_row(fill_ref, rows):
    within = lax.broadcasted_iota(jnp.int32, (1, TILE), 1)
    parts = [jnp.where(within < fill_ref[tile], 1.0, 0.0) for tile in range(rows // TILE)]
    return jnp.concatenate(parts, axis=1) if len(parts) > 1 else parts[0]


def spread(slots):
    return [0] + list(range(slots - 1, 0, -1))


def pack_kv_kernel(heads, rows, dim, a_of, fill_ref, kv_hbm, *refs):
    outs, (kv_ref, held, made, in_sems, out_sems) = refs[:heads], refs[heads:]
    half = rows * heads // 2
    parts = [pl.ds(0, half), pl.ds(half, half)]
    loads = [pltpu.make_async_copy(kv_hbm.at[part], kv_ref.at[part], in_sems.at[i]) for i, part in enumerate(parts)]
    for load in loads:
        load.start()
    live = live_column(fill_ref, rows)
    lane = lax.broadcasted_iota(jnp.int32, (rows, 2 * dim), 1)
    mark = jnp.where(lane == 0, DEAD * (1.0 - live), 0.0)
    for load, part in zip(loads, parts):
        load.wait()
        held[part, :] = kv_ref[part, :].astype(F32)
    me = a_of()
    stores = [pltpu.make_async_copy(made.at[slot], outs[slot], out_sems.at[slot]) for slot in range(heads)]
    masks = spread(heads)
    for slot in [*range(1, heads), 0]:
        made[slot] = (held[pl.ds(me ^ masks[slot], rows, stride=heads), :] * live + mark).astype(BF16)
        stores[slot].start()
    for store in stores:
        store.wait()


def pack_qg_kernel(heads, rows, dim, a_of, fill_ref, q_ref, w_ref, go_ref, *refs):
    outs, (held,) = refs[:heads], refs[heads:]
    grads = dot_nt(w_ref[...].reshape(heads * dim, go_ref.shape[1]), go_ref[...])
    grads = (grads * live_row(fill_ref, rows)).astype(BF16)
    for head in range(heads):
        held[head, 0:dim, :] = (q_ref[head].astype(F32) * dim**-0.5).astype(BF16)
        held[head, dim:, :] = grads[head * dim : (head + 1) * dim, :]
    me = a_of()
    for slot, mask in enumerate(spread(heads)):
        outs[slot][...] = held[me ^ mask]


def join_kernel(pieces, *refs):
    out_ref = refs[-1]
    rows = refs[0].shape[0]
    for index in range(pieces):
        out_ref[index * rows : (index + 1) * rows, :] = refs[index][...]


def join_q_kernel(slots, rows, dim, *refs):
    pieces, (qa_ref, q_ref, g_ref, norm_ref) = refs[:slots], refs[slots:]
    wide = 2 * dim
    row = lax.broadcasted_iota(jnp.int32, (dim, slots * rows), 0)
    qa_ref[wide : wide + dim, :] = jnp.zeros((dim, slots * rows), BF16)
    qa_ref[wide + dim :, :] = jnp.where(row == 0, 1.0, 0.0).astype(BF16)
    for slot in range(slots):
        here = slice(slot * rows, (slot + 1) * rows)
        queries = pieces[slot][0:dim, :]
        q_ref[:, here] = queries
        g_ref[:, here] = pieces[slot][dim:, :]
        scaled = queries.astype(F32) * LOG2_E
        high = scaled.astype(BF16)
        qa_ref[0:dim, here] = high
        qa_ref[dim:wide, here] = (scaled - high.astype(F32)).astype(BF16)
        norm_ref[:, here] = jnp.sum(scaled * scaled, axis=0, keepdims=True)


def score_kernel(slots, rows, dim, step, pair_ref, qa_ref, q_norm_ref, *refs):
    exp_ref, peak_ref, total_ref, v_ref, kt_ref, wide_ref, vt_ref, score_ref = refs[-8:]
    wide = 2 * dim
    keys = pair_ref.shape[0]
    full = pair_ref[...].astype(F32)
    turned = full.T
    norm = jnp.sum(turned[:dim, :] * turned[:dim, :], axis=0, keepdims=True)
    norm = jnp.where(turned[0:1, :] >= DEAD, 0.0, norm)
    small = jnp.max(norm) * jnp.max(q_norm_ref[...]) <= SAFE * SAFE
    lane = lax.broadcasted_iota(jnp.int32, (keys, wide), 1)
    bias = jnp.where(full[:, 0:1] >= DEAD, BIAS, 0.0)
    extra = jnp.where(lane == dim, bias, jnp.where(lane <= dim + 2, 1.0, 0.0))
    rolled = pltpu.roll(full, dim, 1)
    values = jnp.where(lane < dim, rolled, extra).astype(BF16)
    wide_ref[:, 0:wide] = jnp.where(lane < dim, full, rolled).astype(BF16)
    wide_ref[:, wide:] = values
    v_ref[...] = values
    kt_ref[...] = turned[:dim, :].astype(BF16)
    vt_ref[0:dim, :] = turned[dim:, :].astype(BF16)
    vt_ref[dim:, :] = jnp.ones((16, keys), BF16)

    @pl.when(small)
    def _():
        peak_ref[...] = jnp.zeros_like(peak_ref)
        ahead = dot(wide_ref[...], qa_ref[:, 0:rows])
        for slot in range(slots):
            here = slice(slot * rows, (slot + 1) * rows)
            scores = ahead
            if slot + 1 < slots:
                ahead = dot(wide_ref[...], qa_ref[:, (slot + 1) * rows : (slot + 2) * rows])
            exps = jnp.exp2(scores).astype(BF16)
            exp_ref[:, here] = exps
            total_ref[:, here] = dot(vt_ref[...], exps)

    @pl.when(jnp.logical_not(small))
    def _():
        for slot in range(slots):
            here = slice(slot * rows, (slot + 1) * rows)
            top = jnp.full((8, rows), BIAS, F32)
            for start in range(0, keys, step):
                part = slice(start, start + step)
                scores = dot(wide_ref[part, :], qa_ref[:, here])
                score_ref[part, :] = scores
                top = jnp.maximum(top, jnp.max(scores.reshape(step // 8, 8, rows), axis=0))
            peak = jnp.max(top, axis=0, keepdims=True)
            peak_ref[:, here] = peak
            total = jnp.zeros((dim + 16, rows), F32)
            for start in range(0, keys, step):
                part = slice(start, start + step)
                exps = jnp.exp2(score_ref[part, :] - peak).astype(BF16)
                exp_ref[part, here] = exps
                total = total + dot(vt_ref[:, part], exps)
            total_ref[:, here] = total


def combine_kernel(slots, columns, rows, dim, *refs):
    peaks, totals, (g_ref,), outs = refs[:columns], refs[columns : 2 * columns], refs[2 * columns : 2 * columns + 1], refs[2 * columns + 1 :]
    att_out, factors_out, inner_ref = outs[:slots], outs[slots : slots + columns], outs[-1]
    peak = functools.reduce(jnp.maximum, [ref[...] for ref in peaks])
    factors = [jnp.exp2(ref[...] - peak) for ref in peaks]
    total = sum(factor * ref[...] for factor, ref in zip(factors, totals))
    inverse = 1.0 / total[dim : dim + 1, :]
    attended = (total[0:dim, :] * inverse).astype(BF16)
    for slot in range(slots):
        att_out[slot][...] = attended[:, slot * rows : (slot + 1) * rows]
    for factor, ref in zip(factors, factors_out):
        ref[...] = factor * inverse
    inner_ref[...] = jnp.sum(g_ref[...].astype(F32) * attended.astype(F32), axis=0, keepdims=True)


def back_kernel(slots, rows, dim, first, exp_ref, v_ref, kt_ref, q_ref, g_ref, factor_ref, inner_ref, *refs):
    dkv_ref, dq_ref, ga_ref = refs[-3:]
    block = g_ref.shape[1]
    factor = factor_ref[...]
    inner = inner_ref[...] * factor
    high = inner.astype(BF16).astype(F32)
    row = lax.broadcasted_iota(jnp.int32, (dim, block), 0)
    ga_ref[0:dim, :] = (g_ref[...].astype(F32) * factor).astype(BF16)
    ga_ref[dim:, :] = jnp.where(row == 1, -high, jnp.where(row == 2, high - inner, 0.0)).astype(BF16)
    grad_k = grad_v = None
    ahead = dot(v_ref[...], ga_ref[:, 0:rows])
    for slot in range(slots):
        here = slice(slot * rows, (slot + 1) * rows)
        products = ahead
        if slot + 1 < slots:
            ahead = dot(v_ref[...], ga_ref[:, (slot + 1) * rows : (slot + 2) * rows])
        exps = exp_ref[:, here]
        grads = exps * products.astype(BF16)
        term_v = dot_nt(ga_ref[0:dim, here], exps)
        term_k = dot_nt(q_ref[:, here], grads)
        grad_v = term_v if grad_v is None else grad_v + term_v
        grad_k = term_k if grad_k is None else grad_k + term_k
        term = dot(kt_ref[...], grads)
        dq_ref[:, here] = term if first else refs[0][:, here] + term
    dkv_ref[dim:, :] = grad_v.astype(BF16)
    dkv_ref[0:dim, :] = grad_k.astype(BF16)


def project_kernel(slots, rows, a_of, b_of, halves, fill_ref, go_ref, w_ref, *refs):
    att, refs = refs[:slots], refs[slots + 1 :]
    terms_ref, held = refs[0], refs[-1]
    me = a_of()
    dim = held.shape[1]
    stacked = jnp.concatenate([ref[...].astype(F32) for ref in att], axis=0) * live_row(fill_ref, rows)
    grads = dot(stacked.astype(BF16), go_ref[...]).astype(BF16)
    for slot, mask in enumerate(spread(slots)):
        held[me ^ mask] = grads[slot * dim : (slot + 1) * dim, :]
    weights = jnp.concatenate([w_ref[me ^ mask] for mask in spread(slots)], axis=0)
    terms_ref[...] = dot(stacked.T.astype(BF16), weights).astype(BF16)
    if not halves:
        refs[1][...] = held[...]
        return
    me = b_of()
    kept_ref, sent_ref = refs[1], refs[2]
    for pair in range(slots // 2):
        kept_ref[pair] = held[me ^ (2 * pair)]
        sent_ref[pair] = held[me ^ (2 * pair) ^ 1]


def add_pairs_kernel(kept_ref, came_ref, _, first_ref, second_ref):
    for index, out_ref in enumerate((first_ref, second_ref)):
        out_ref[...] = (kept_ref[index].astype(F32) + came_ref[index].astype(F32)).astype(BF16)


def add_pieces_kernel(slots, rows, dim, kept_ref, came_ref, dq_ref, *outs):
    wide = 2 * dim
    for slot in range(slots):
        here = slice(slot * rows, (slot + 1) * rows)
        outs[slot][0:wide, :] = (kept_ref[:, here].astype(F32) + came_ref[:, here].astype(F32)).astype(BF16)
        outs[slot][wide:, :] = (dq_ref[:, here] * dim**-0.5).astype(BF16)


def add_kernel(a_ref, b_ref, *refs):
    refs[-1][...] = (a_ref[...].astype(F32) + b_ref[...].astype(F32)).astype(refs[-1].dtype)


def unpack_kernel(slots, rows, dim, a_of, *refs):
    pieces, (a_ref, b_ref, _, kv_out, q_out, sum_out) = refs[:slots], refs[slots:]
    sum_out[...] = (a_ref[...].astype(F32) + b_ref[...].astype(F32)).astype(BF16)
    wide = 2 * dim
    me = a_of()
    for slot, mask in enumerate(spread(slots)):
        kv_out[pl.ds(me ^ mask, rows, stride=slots), :] = pieces[slot][0:wide, :].astype(F32).T
        q_out[me ^ mask] = pieces[slot][wide:, :].astype(F32)


def token_kernel(*refs):
    refs[-1][...] = jnp.zeros_like(refs[-1])


def place_kernel(columns, b_of, *refs):
    parts, (grad_out,) = refs[:columns], refs[columns:]
    me = b_of()
    for column in range(columns):
        grad_out[me ^ column] = parts[column][...].astype(F32)


def shards(seq, mp, queries, key_value, tile_fill, out_weight, grad_output):
    rows, heads, dim = queries.shape
    width = grad_output.shape[1]
    slots = heads
    columns = seq // slots
    assert slots * columns == seq and columns & (columns - 1) == 0 and slots & (slots - 1) == 0
    a_of = lambda: lax.axis_index("seq") // columns
    b_of = lambda: lax.axis_index("seq") % columns

    def swap(array, mask, axis="seq", size=seq):
        return lax.ppermute(array, axis, [(i, i ^ mask) for i in range(size)])

    def exchange(pieces):
        return [pieces[0]] + [swap(piece, mask * columns) for piece, mask in zip(pieces[1:], spread(slots)[1:])]

    block, wide = slots * rows, 2 * dim
    kv_mine = exchange(pl.pallas_call(
        functools.partial(pack_kv_kernel, heads, rows, dim, a_of),
        out_shape=[jax.ShapeDtypeStruct((rows, wide), BF16)] * slots,
        in_specs=[SMEM, pl.BlockSpec(memory_space=pl.ANY)],
        out_specs=[pl.BlockSpec(memory_space=pl.ANY)] * slots,
        scratch_shapes=[
            pltpu.VMEM((rows * heads, wide), BF16), pltpu.VMEM((rows * heads, wide), F32), pltpu.VMEM((heads, rows, wide), BF16),
            pltpu.SemaphoreType.DMA((2,)), pltpu.SemaphoreType.DMA((heads,)),
        ],
        compiler_params=pltpu.CompilerParams(vmem_limit_bytes=56 * MIB),
        cost_estimate=pl.CostEstimate(flops=int(1.5 * 1.15e9), bytes_accessed=0, transcendentals=0),
    )(tile_fill, key_value.reshape(rows * heads, wide)))
    qg_send = call(
        functools.partial(pack_qg_kernel, heads, rows, dim, a_of),
        [((wide, rows), BF16)] * slots, [pltpu.VMEM((heads, wide, rows), BF16)],
        n_in=4, smem_first=True, micros=1,
    )(tile_fill, jnp.transpose(queries, (1, 2, 0)), out_weight, grad_output)
    qg_mine = exchange(qg_send)
    own = call(
        functools.partial(join_kernel, slots), [((block, wide), BF16)], n_in=slots, after=1,
    )(*kv_mine, qg_send[0])[0]

    qa, q_all, grads, q_norm = call(
        functools.partial(join_q_kernel, slots, rows, dim),
        [((2 * wide, block), BF16), ((dim, block), BF16), ((dim, block), BF16), ((1, block), F32)], n_in=slots,
    )(*qg_mine)
    step = min(block, 512)
    scored, blocks = {}, {0: own}
    bit = columns // 2
    while bit:
        for r in sorted(blocks):
            blocks[r ^ bit] = swap(blocks[r], bit)
        bit //= 2
    for r in range(columns):
        if r == 2 and columns == 4:
            blocks[2] = call(functools.partial(join_kernel, 1), [((block, wide), BF16)], after=1)(
                blocks[2], scored[1][1])[0]
            blocks[3] = swap(blocks[2], 1)
        scored[r] = call(
            functools.partial(score_kernel, slots, rows, dim, step),
            [((block, block), BF16), ((1, block), F32), ((dim + 16, block), F32), ((block, wide), BF16), ((dim, block), BF16)],
            [pltpu.VMEM((block, 2 * wide), BF16), pltpu.VMEM((dim + 16, block), BF16), pltpu.VMEM((block, rows), F32)],
            n_in=3, after=min(r, 1), micros=5,
        )(blocks[r], qa, q_norm, *([scored[r - 1][1]] if r else []))
    combined = call(
        functools.partial(combine_kernel, slots, columns, rows, dim),
        [((dim, rows), BF16)] * slots + [((1, block), F32)] * (columns + 1), n_in=2 * columns + 1,
    )(*[scored[r][1] for r in range(columns)], *[scored[r][2] for r in range(columns)], grads)
    att_mine, factors, inner = exchange(combined[:slots]), combined[slots:-1], combined[-1]

    halves = columns == heads == 4
    order = sorted(range(columns), reverse=True)
    add = call(add_kernel, [((dim, width), BF16)], n_in=2, after=1)
    add_halves = call(add_kernel, [((wide, block), BF16)], n_in=2)
    z_masks = [columns << level for level in range(slots.bit_length() - 1)]
    dkv, dq, kept, summed, later = {}, None, None, {}, []
    for at, r in enumerate(order):
        if at and not halves and at == columns - 1 or halves and at == 1:
            terms, *weight_terms = call(
                functools.partial(project_kernel, slots, rows, a_of, b_of, halves),
                [((rows, width), BF16)] + ([((2, dim, width), BF16)] * 2 if halves else [((heads, dim, width), BF16)]),
                [pltpu.VMEM((heads, dim, width), BF16)],
                n_in=3 + slots, smem_first=True, after=1, micros=0.7,
            )(tile_fill, grad_output, out_weight, *att_mine, dkv[order[at - 1]])
            later, bit = [terms], 1
            while bit < mp // 2:
                terms = call(add_kernel, [((rows, width), BF16)], n_in=2)(terms, swap(terms, bit, "mp", mp))[0]
                bit *= 2
            terms_came = swap(terms, bit, "mp", mp)
            if halves:
                kept, sent = call(add_pairs_kernel, [((dim, width), BF16)] * 2, n_in=2, after=1)(
                    weight_terms[0], swap(weight_terms[1], 1), weight_terms[0])
                later = [kept]
        if at == 2 and halves:
            kept = add(kept, swap(sent, 2), dkv[order[at - 1]])[0]
            later = [kept]
        if at == 3 and halves:
            kept = add(kept, swap(kept, z_masks[0]), dkv[order[at - 1]])[0]
            later = [kept, summed[2], terms_came]
        operands = [scored[r][0], *scored[r][3:], q_all, grads, factors[r], inner] + ([] if dq is None else [dq])
        dkv[r], dq = call(
            functools.partial(back_kernel, slots, rows, dim, dq is None),
            [((wide, block), BF16), ((dim, block), F32)], [pltpu.VMEM((wide, block), BF16)],
            n_in=len(operands), after=len(later), micros=2,
        )(*operands, *later)
        later = []
        if columns == 4 and r == 2:
            summed[2] = swap(add_halves(dkv[2], swap(dkv[3], 1))[0], 2)

    if columns == 4:
        halved = add_halves(dkv[0], swap(dkv[1], 1))[0], summed[2]
    else:
        bit = 1
        while 2 * bit < columns:
            dkv = {r: add_halves(dkv[r], swap(dkv[r ^ bit], bit))[0] for r in order if r in dkv and not r & bit}
            bit *= 2
        halved = dkv[0], swap(dkv[bit], bit)
    pieces = call(
        functools.partial(add_pieces_kernel, slots, rows, dim), [((wide + dim, rows), BF16)] * slots, n_in=3,
    )(*halved, dq)
    returned = exchange(pieces)

    arrived = call(token_kernel, [((8, 128), F32)], n_in=0, after=slots)(*returned)[0]
    if halves:
        for mask in z_masks[1:]:
            kept = add(kept, swap(kept, mask), pieces[0])[0]
        across = call(functools.partial(join_kernel, 1), [((dim, width), BF16)], after=1)(swap(kept, 2), arrived)[0]
        weight_grad = call(
            functools.partial(place_kernel, columns, b_of), [((heads, dim, width), F32)], n_in=columns, micros=0.5,
        )(kept, swap(kept, 1), across, swap(across, 1))[0]
        arrived = across
    else:
        weight_grad = lax.psum(weight_terms[0].astype(F32), "seq")
    key_value_grad, query_grad, attention_out = call(
        functools.partial(unpack_kernel, slots, rows, dim, a_of),
        [((rows * heads, wide), F32), ((heads, dim, rows), F32), ((rows, width), BF16)],
        n_in=slots + 2, after=1, micros=5,
    )(*returned, terms, terms_came, arrived)
    return attention_out, jnp.transpose(query_grad, (2, 0, 1)), key_value_grad.reshape(rows, heads, wide), weight_grad


def solution(mesh):
    return jax.shard_map(
        functools.partial(shards, mesh.shape["seq"], mesh.shape["mp"]),
        mesh=mesh,
        in_specs=(
            P("seq", "mp", None),
            P("seq", "mp", None),
            P("seq"),
            P("mp", None, None),
            P("seq", None),
        ),
        out_specs=(P("seq", None), P("seq", "mp", None), P("seq", "mp", None), P("mp", None, None)),
        check_vma=False,
    )
```

```python
import functools

import jax
import jax.numpy as jnp
from jax import lax
from jax.experimental import pallas as pl
from jax.experimental.pallas import tpu as pltpu
from jax.sharding import PartitionSpec as P

TILE = 128
DEAD = 1024.0
BIAS = -1e30
LOG2_E = 1.4426950408889634
SAFE = 64.0
F32 = jnp.float32
BF16 = jnp.bfloat16
VMEM = pl.BlockSpec(memory_space=pltpu.VMEM)
SMEM = pl.BlockSpec(memory_space=pltpu.SMEM)
MIB = 1024 * 1024


def dot(a, b):
    return lax.dot_general(a, b, (((1,), (0,)), ((), ())), preferred_element_type=F32)


def dot_nt(a, b):
    return lax.dot_general(a, b, (((1,), (1,)), ((), ())), preferred_element_type=F32)


def call(kernel, outs, scratch=(), n_in=1, smem_first=False, after=0, micros=0.01, limit=16):
    specs = ([SMEM if smem_first else VMEM] + [VMEM] * (n_in - 1))[:n_in] + [pl.BlockSpec(memory_space=pl.ANY)] * after
    return pl.pallas_call(
        kernel,
        out_shape=[jax.ShapeDtypeStruct(shape, kind) for shape, kind in outs],
        in_specs=specs,
        out_specs=[VMEM] * len(outs),
        scratch_shapes=list(scratch),
        compiler_params=pltpu.CompilerParams(vmem_limit_bytes=limit * MIB),
        cost_estimate=pl.CostEstimate(flops=int(micros * 1.15e9), bytes_accessed=0, transcendentals=0),
    )


def live_column(fill_ref, rows):
    parts = []
    within = lax.broadcasted_iota(jnp.int32, (TILE, 1), 0)
    for tile in range(rows // TILE):
        parts.append(jnp.where(within < fill_ref[tile], 1.0, 0.0))
    return jnp.concatenate(parts, axis=0) if len(parts) > 1 else parts[0]


def live_row(fill_ref, rows):
    within = lax.broadcasted_iota(jnp.int32, (1, TILE), 1)
    parts = [jnp.where(within < fill_ref[tile], 1.0, 0.0) for tile in range(rows // TILE)]
    return jnp.concatenate(parts, axis=1) if len(parts) > 1 else parts[0]


def spread(slots):
    return [0] + list(range(slots - 1, 0, -1))


def pack_kv_kernel(heads, rows, dim, a_of, fill_ref, kv_ref, *refs):
    outs, (held,) = refs[:heads], refs[heads:]
    live = live_column(fill_ref, rows)
    lane = lax.broadcasted_iota(jnp.int32, (rows, 2 * dim), 1)
    mark = jnp.where(lane == 0, DEAD * (1.0 - live), 0.0)
    held[...] = kv_ref[...].astype(F32)
    me = a_of()
    for slot, mask in enumerate(spread(heads)):
        outs[slot][...] = (held[pl.ds(me ^ mask, rows, stride=heads), :] * live + mark).astype(BF16)


def pack_qg_kernel(heads, rows, dim, a_of, fill_ref, q_ref, w_ref, go_ref, *refs):
    outs, (held,) = refs[:heads], refs[heads:]
    grads = dot_nt(w_ref[...].reshape(heads * dim, go_ref.shape[1]), go_ref[...])
    grads = (grads * live_row(fill_ref, rows)).astype(BF16)
    for head in range(heads):
        held[head, 0:dim, :] = (q_ref[head].astype(F32) * dim**-0.5).astype(BF16)
        held[head, dim:, :] = grads[head * dim : (head + 1) * dim, :]
    me = a_of()
    for slot, mask in enumerate(spread(heads)):
        outs[slot][...] = held[me ^ mask]


def join_kernel(pieces, *refs):
    out_ref = refs[-1]
    rows = refs[0].shape[0]
    for index in range(pieces):
        out_ref[index * rows : (index + 1) * rows, :] = refs[index][...]


def join_q_kernel(slots, rows, dim, *refs):
    pieces, (qa_ref, q_ref, g_ref, norm_ref) = refs[:slots], refs[slots:]
    wide = 2 * dim
    row = lax.broadcasted_iota(jnp.int32, (dim, slots * rows), 0)
    qa_ref[wide : wide + dim, :] = jnp.zeros((dim, slots * rows), BF16)
    qa_ref[wide + dim :, :] = jnp.where(row == 0, 1.0, 0.0).astype(BF16)
    for slot in range(slots):
        here = slice(slot * rows, (slot + 1) * rows)
        queries = pieces[slot][0:dim, :]
        q_ref[:, here] = queries
        g_ref[:, here] = pieces[slot][dim:, :]
        scaled = queries.astype(F32) * LOG2_E
        high = scaled.astype(BF16)
        qa_ref[0:dim, here] = high
        qa_ref[dim:wide, here] = (scaled - high.astype(F32)).astype(BF16)
        norm_ref[:, here] = jnp.sum(scaled * scaled, axis=0, keepdims=True)


def score_kernel(slots, rows, dim, step, pair_ref, qa_ref, q_norm_ref, *refs):
    exp_ref, peak_ref, total_ref, v_ref, kt_ref, wide_ref, vt_ref, score_ref = refs[-8:]
    wide = 2 * dim
    keys = pair_ref.shape[0]
    full = pair_ref[...].astype(F32)
    turned = full.T
    norm = jnp.sum(turned[:dim, :] * turned[:dim, :], axis=0, keepdims=True)
    norm = jnp.where(turned[0:1, :] >= DEAD, 0.0, norm)
    small = jnp.max(norm) * jnp.max(q_norm_ref[...]) <= SAFE * SAFE
    lane = lax.broadcasted_iota(jnp.int32, (keys, wide), 1)
    bias = jnp.where(full[:, 0:1] >= DEAD, BIAS, 0.0)
    extra = jnp.where(lane == dim, bias, jnp.where(lane <= dim + 2, 1.0, 0.0))
    rolled = pltpu.roll(full, dim, 1)
    values = jnp.where(lane < dim, rolled, extra).astype(BF16)
    wide_ref[:, 0:wide] = jnp.where(lane < dim, full, rolled).astype(BF16)
    wide_ref[:, wide:] = values
    v_ref[...] = values
    kt_ref[...] = turned[:dim, :].astype(BF16)
    vt_ref[0:dim, :] = turned[dim:, :].astype(BF16)
    vt_ref[dim:, :] = jnp.ones((16, keys), BF16)

    @pl.when(small)
    def _():
        peak_ref[...] = jnp.zeros_like(peak_ref)
        ahead = dot(wide_ref[...], qa_ref[:, 0:rows])
        for slot in range(slots):
            here = slice(slot * rows, (slot + 1) * rows)
            scores = ahead
            if slot + 1 < slots:
                ahead = dot(wide_ref[...], qa_ref[:, (slot + 1) * rows : (slot + 2) * rows])
            exps = jnp.exp2(scores).astype(BF16)
            exp_ref[:, here] = exps
            total_ref[:, here] = dot(vt_ref[...], exps)

    @pl.when(jnp.logical_not(small))
    def _():
        for slot in range(slots):
            here = slice(slot * rows, (slot + 1) * rows)
            top = jnp.full((8, rows), BIAS, F32)
            for start in range(0, keys, step):
                part = slice(start, start + step)
                scores = dot(wide_ref[part, :], qa_ref[:, here])
                score_ref[part, :] = scores
                top = jnp.maximum(top, jnp.max(scores.reshape(step // 8, 8, rows), axis=0))
            peak = jnp.max(top, axis=0, keepdims=True)
            peak_ref[:, here] = peak
            total = jnp.zeros((dim + 16, rows), F32)
            for start in range(0, keys, step):
                part = slice(start, start + step)
                exps = jnp.exp2(score_ref[part, :] - peak).astype(BF16)
                exp_ref[part, here] = exps
                total = total + dot(vt_ref[:, part], exps)
            total_ref[:, here] = total


def combine_kernel(slots, columns, rows, dim, *refs):
    peaks, totals, (g_ref,), outs = refs[:columns], refs[columns : 2 * columns], refs[2 * columns : 2 * columns + 1], refs[2 * columns + 1 :]
    att_out, factors_out, inner_ref = outs[:slots], outs[slots : slots + columns], outs[-1]
    peak = functools.reduce(jnp.maximum, [ref[...] for ref in peaks])
    factors = [jnp.exp2(ref[...] - peak) for ref in peaks]
    total = sum(factor * ref[...] for factor, ref in zip(factors, totals))
    inverse = 1.0 / total[dim : dim + 1, :]
    attended = (total[0:dim, :] * inverse).astype(BF16)
    for slot in range(slots):
        att_out[slot][...] = attended[:, slot * rows : (slot + 1) * rows]
    for factor, ref in zip(factors, factors_out):
        ref[...] = factor * inverse
    inner_ref[...] = jnp.sum(g_ref[...].astype(F32) * attended.astype(F32), axis=0, keepdims=True)


def back_kernel(slots, rows, dim, first, low, high_key, exp_ref, v_ref, kt_ref, q_ref, g_ref, factor_ref, inner_ref, *refs):
    dkv_ref, dq_ref, ga_ref = refs[-3:]
    part = slice(low, high_key)
    block = g_ref.shape[1]
    factor = factor_ref[...]
    inner = inner_ref[...] * factor
    high = inner.astype(BF16).astype(F32)
    row = lax.broadcasted_iota(jnp.int32, (dim, block), 0)
    ga_ref[0:dim, :] = (g_ref[...].astype(F32) * factor).astype(BF16)
    ga_ref[dim:, :] = jnp.where(row == 1, -high, jnp.where(row == 2, high - inner, 0.0)).astype(BF16)
    grad_k = grad_v = None
    ahead = dot(v_ref[part, :], ga_ref[:, 0:rows])
    for slot in range(slots):
        here = slice(slot * rows, (slot + 1) * rows)
        products = ahead
        if slot + 1 < slots:
            ahead = dot(v_ref[part, :], ga_ref[:, (slot + 1) * rows : (slot + 2) * rows])
        exps = exp_ref[part, here]
        grads = exps * products.astype(BF16)
        term_v = dot_nt(ga_ref[0:dim, here], exps)
        term_k = dot_nt(q_ref[:, here], grads)
        grad_v = term_v if grad_v is None else grad_v + term_v
        grad_k = term_k if grad_k is None else grad_k + term_k
        term = dot(kt_ref[:, part], grads)
        dq_ref[:, here] = term if first else refs[0][:, here] + term
    dkv_ref[dim:, :] = grad_v.astype(BF16)
    dkv_ref[0:dim, :] = grad_k.astype(BF16)


def project_kernel(slots, rows, a_of, b_of, halves, fill_ref, go_ref, w_ref, *refs):
    att, refs = refs[:slots], refs[slots + 1 :]
    terms_ref, held = refs[0], refs[-1]
    me = a_of()
    dim = held.shape[1]
    stacked = jnp.concatenate([ref[...].astype(F32) for ref in att], axis=0) * live_row(fill_ref, rows)
    grads = dot(stacked.astype(BF16), go_ref[...]).astype(BF16)
    for slot, mask in enumerate(spread(slots)):
        held[me ^ mask] = grads[slot * dim : (slot + 1) * dim, :]
    weights = jnp.concatenate([w_ref[me ^ mask] for mask in spread(slots)], axis=0)
    terms_ref[...] = dot(stacked.T.astype(BF16), weights).astype(BF16)
    if not halves:
        refs[1][...] = held[...]
        return
    me = b_of()
    kept_ref, sent_ref = refs[1], refs[2]
    for pair in range(slots // 2):
        kept_ref[pair] = held[me ^ (2 * pair)]
        sent_ref[pair] = held[me ^ (2 * pair) ^ 1]


def add_pairs_kernel(kept_ref, came_ref, _, first_ref, second_ref):
    for index, out_ref in enumerate((first_ref, second_ref)):
        out_ref[...] = (kept_ref[index].astype(F32) + came_ref[index].astype(F32)).astype(BF16)


def add_pieces_kernel(slots, rows, dim, kept_ref, came_ref, dq_ref, *outs):
    wide = 2 * dim
    for slot in range(slots):
        here = slice(slot * rows, (slot + 1) * rows)
        outs[slot][0:wide, :] = (kept_ref[:, here].astype(F32) + came_ref[:, here].astype(F32)).astype(BF16)
        outs[slot][wide:, :] = (dq_ref[:, here] * dim**-0.5).astype(BF16)


def add_parts_kernel(parts, *refs):
    start = 0
    for part in refs[:parts]:
        here = slice(start, start + part.shape[1])
        refs[-1][:, here] = (part[...].astype(F32) + refs[parts][:, here].astype(F32)).astype(BF16)
        start += part.shape[1]


def add_kernel(a_ref, b_ref, *refs):
    refs[-1][...] = (a_ref[...].astype(F32) + b_ref[...].astype(F32)).astype(refs[-1].dtype)


def unpack_kernel(slots, rows, dim, a_of, *refs):
    pieces, (a_ref, b_ref, _, kv_out, q_out, sum_out) = refs[:slots], refs[slots:]
    sum_out[...] = (a_ref[...].astype(F32) + b_ref[...].astype(F32)).astype(BF16)
    wide = 2 * dim
    me = a_of()
    for slot, mask in enumerate(spread(slots)):
        kv_out[pl.ds(me ^ mask, rows, stride=slots), :] = pieces[slot][0:wide, :].astype(F32).T
        q_out[me ^ mask] = pieces[slot][wide:, :].astype(F32)


def token_kernel(*refs):
    refs[-1][...] = jnp.zeros_like(refs[-1])


def place_kernel(columns, b_of, *refs):
    parts, (grad_out,) = refs[:columns], refs[columns:]
    me = b_of()
    for column in range(columns):
        grad_out[me ^ column] = parts[column][...].astype(F32)


def shards(seq, mp, queries, key_value, tile_fill, out_weight, grad_output):
    rows, heads, dim = queries.shape
    width = grad_output.shape[1]
    slots = heads
    columns = seq // slots
    assert slots * columns == seq and columns & (columns - 1) == 0 and slots & (slots - 1) == 0
    a_of = lambda: lax.axis_index("seq") // columns
    b_of = lambda: lax.axis_index("seq") % columns

    def swap(array, mask, axis="seq", size=seq):
        return lax.ppermute(array, axis, [(i, i ^ mask) for i in range(size)])

    def exchange(pieces):
        return [pieces[0]] + [swap(piece, mask * columns) for piece, mask in zip(pieces[1:], spread(slots)[1:])]

    block, wide = slots * rows, 2 * dim
    kv_mine = exchange(call(
        functools.partial(pack_kv_kernel, heads, rows, dim, a_of),
        [((rows, wide), BF16)] * slots, [pltpu.VMEM((rows * heads, wide), F32)],
        n_in=2, smem_first=True, micros=1.5, limit=56,
    )(tile_fill, key_value.reshape(rows * heads, wide)))
    qg_send = call(
        functools.partial(pack_qg_kernel, heads, rows, dim, a_of),
        [((wide, rows), BF16)] * slots, [pltpu.VMEM((heads, wide, rows), BF16)],
        n_in=4, smem_first=True, micros=1,
    )(tile_fill, jnp.transpose(queries, (1, 2, 0)), out_weight, grad_output)
    qg_mine = exchange(qg_send)
    own = call(
        functools.partial(join_kernel, slots), [((block, wide), BF16)], n_in=slots, after=1,
    )(*kv_mine, qg_send[0])[0]

    qa, q_all, grads, q_norm = call(
        functools.partial(join_q_kernel, slots, rows, dim),
        [((2 * wide, block), BF16), ((dim, block), BF16), ((dim, block), BF16), ((1, block), F32)], n_in=slots,
    )(*qg_mine)
    step = min(block, 512)
    scored, blocks = {}, {0: own}
    bit = columns // 2
    while bit:
        for r in sorted(blocks):
            blocks[r ^ bit] = swap(blocks[r], bit)
        bit //= 2
    for r in range(columns):
        if r == 2 and columns == 4:
            blocks[2] = call(functools.partial(join_kernel, 1), [((block, wide), BF16)], after=1)(
                blocks[2], scored[1][1])[0]
            blocks[3] = swap(blocks[2], 1)
        scored[r] = call(
            functools.partial(score_kernel, slots, rows, dim, step),
            [((block, block), BF16), ((1, block), F32), ((dim + 16, block), F32), ((block, wide), BF16), ((dim, block), BF16)],
            [pltpu.VMEM((block, 2 * wide), BF16), pltpu.VMEM((dim + 16, block), BF16), pltpu.VMEM((block, rows), F32)],
            n_in=3, after=min(r, 1), micros=5,
        )(blocks[r], qa, q_norm, *([scored[r - 1][1]] if r else []))
    combined = call(
        functools.partial(combine_kernel, slots, columns, rows, dim),
        [((dim, rows), BF16)] * slots + [((1, block), F32)] * (columns + 1), n_in=2 * columns + 1,
    )(*[scored[r][1] for r in range(columns)], *[scored[r][2] for r in range(columns)], grads)
    att_mine, factors, inner = exchange(combined[:slots]), combined[slots:-1], combined[-1]

    halves = columns == heads == 4
    order = sorted(range(columns), reverse=True)
    add = call(add_kernel, [((dim, width), BF16)], n_in=2, after=1)
    add_kernel_of = lambda parts: functools.partial(add_parts_kernel, parts)
    add_halves = call(add_kernel, [((wide, block), BF16)], n_in=2)
    z_masks = [columns << level for level in range(slots.bit_length() - 1)]
    dkv, dq, kept, summed, later = {}, None, None, {}, []
    for at, r in enumerate(order):
        if at and not halves and at == columns - 1 or halves and at == 1:
            terms, *weight_terms = call(
                functools.partial(project_kernel, slots, rows, a_of, b_of, halves),
                [((rows, width), BF16)] + ([((2, dim, width), BF16)] * 2 if halves else [((heads, dim, width), BF16)]),
                [pltpu.VMEM((heads, dim, width), BF16)],
                n_in=3 + slots, smem_first=True, after=1, micros=0.7,
            )(tile_fill, grad_output, out_weight, *att_mine, dkv[order[at - 1]])
            later, bit = [terms], 1
            while bit < mp // 2:
                terms = call(add_kernel, [((rows, width), BF16)], n_in=2)(terms, swap(terms, bit, "mp", mp))[0]
                bit *= 2
            terms_came = swap(terms, bit, "mp", mp)
            if halves:
                kept, sent = call(add_pairs_kernel, [((dim, width), BF16)] * 2, n_in=2, after=1)(
                    weight_terms[0], swap(weight_terms[1], 1), weight_terms[0])
                later = [kept]
        if at == 2 and halves:
            kept = add(kept, swap(sent, 2), dkv[order[at - 1]])[0]
            later = [kept]
        low = 0
        if at == 3 and halves:
            low = block // 2
            operands = [scored[r][0], *scored[r][3:], q_all, grads, factors[r], inner, dq]
            lower, dq = call(
                functools.partial(back_kernel, slots, rows, dim, False, 0, low),
                [((wide, low), BF16), ((dim, block), F32)], [pltpu.VMEM((wide, block), BF16)],
                n_in=len(operands), micros=2,
            )(*operands)
            kept = add(kept, swap(kept, z_masks[0]), lower)[0]
            later = [kept, summed[2], terms_came]
        operands = [scored[r][0], *scored[r][3:], q_all, grads, factors[r], inner] + ([] if dq is None else [dq])
        dkv[r], dq = call(
            functools.partial(back_kernel, slots, rows, dim, dq is None, low, block),
            [((wide, block - low), BF16), ((dim, block), F32)], [pltpu.VMEM((wide, block), BF16)],
            n_in=len(operands), after=len(later), micros=2,
        )(*operands, *later)
        later = []
        if columns == 4 and r == 2:
            summed[2] = swap(add_halves(dkv[2], swap(dkv[3], 1))[0], 2)

    if columns == 4:
        lowers = [lower] if halves else []
        halved = call(add_kernel_of(len(lowers) + 1), [((wide, block), BF16)], n_in=len(lowers) + 2)(
            *lowers, dkv[0], swap(dkv[1], 1))[0], summed[2]
    else:
        bit = 1
        while 2 * bit < columns:
            dkv = {r: add_halves(dkv[r], swap(dkv[r ^ bit], bit))[0] for r in order if r in dkv and not r & bit}
            bit *= 2
        halved = dkv[0], swap(dkv[bit], bit)
    pieces = call(
        functools.partial(add_pieces_kernel, slots, rows, dim), [((wide + dim, rows), BF16)] * slots, n_in=3,
    )(*halved, dq)
    returned = exchange(pieces)

    arrived = call(token_kernel, [((8, 128), F32)], n_in=0, after=slots)(*returned)[0]
    if halves:
        for mask in z_masks[1:]:
            kept = add(kept, swap(kept, mask), pieces[0])[0]
        across = call(functools.partial(join_kernel, 1), [((dim, width), BF16)], after=1)(swap(kept, 2), arrived)[0]
        weight_grad = call(
            functools.partial(place_kernel, columns, b_of), [((heads, dim, width), F32)], n_in=columns, micros=0.5,
        )(kept, swap(kept, 1), across, swap(across, 1))[0]
        arrived = across
    else:
        weight_grad = lax.psum(weight_terms[0].astype(F32), "seq")
    key_value_grad, query_grad, attention_out = call(
        functools.partial(unpack_kernel, slots, rows, dim, a_of),
        [((rows * heads, wide), F32), ((heads, dim, rows), F32), ((rows, width), BF16)],
        n_in=slots + 2, after=1, micros=5,
    )(*returned, terms, terms_came, arrived)
    return attention_out, jnp.transpose(query_grad, (2, 0, 1)), key_value_grad.reshape(rows, heads, wide), weight_grad


def solution(mesh):
    return jax.shard_map(
        functools.partial(shards, mesh.shape["seq"], mesh.shape["mp"]),
        mesh=mesh,
        in_specs=(
            P("seq", "mp", None),
            P("seq", "mp", None),
            P("seq"),
            P("mp", None, None),
            P("seq", None),
        ),
        out_specs=(P("seq", None), P("seq", "mp", None), P("seq", "mp", None), P("mp", None, None)),
        check_vma=False,
    )
```

```python
import functools

import jax
import jax.numpy as jnp
from jax import lax
from jax.experimental import pallas as pl
from jax.experimental.pallas import tpu as pltpu
from jax.sharding import PartitionSpec as P

TILE = 128
DEAD = 1024.0
BIAS = -1e30
LOG2_E = 1.4426950408889634
SAFE = 64.0
F32 = jnp.float32
BF16 = jnp.bfloat16
VMEM = pl.BlockSpec(memory_space=pltpu.VMEM)
SMEM = pl.BlockSpec(memory_space=pltpu.SMEM)
MIB = 1024 * 1024


def dot(a, b):
    return lax.dot_general(a, b, (((1,), (0,)), ((), ())), preferred_element_type=F32)


def dot_nt(a, b):
    return lax.dot_general(a, b, (((1,), (1,)), ((), ())), preferred_element_type=F32)


def call(kernel, outs, scratch=(), n_in=1, smem_first=False, after=0, micros=0.01, limit=16):
    specs = ([SMEM if smem_first else VMEM] + [VMEM] * (n_in - 1))[:n_in] + [pl.BlockSpec(memory_space=pl.ANY)] * after
    return pl.pallas_call(
        kernel,
        out_shape=[jax.ShapeDtypeStruct(shape, kind) for shape, kind in outs],
        in_specs=specs,
        out_specs=[VMEM] * len(outs),
        scratch_shapes=list(scratch),
        compiler_params=pltpu.CompilerParams(vmem_limit_bytes=limit * MIB),
        cost_estimate=pl.CostEstimate(flops=int(micros * 1.15e9), bytes_accessed=0, transcendentals=0),
    )


def live_column(fill_ref, rows):
    parts = []
    within = lax.broadcasted_iota(jnp.int32, (TILE, 1), 0)
    for tile in range(rows // TILE):
        parts.append(jnp.where(within < fill_ref[tile], 1.0, 0.0))
    return jnp.concatenate(parts, axis=0) if len(parts) > 1 else parts[0]


def live_row(fill_ref, rows):
    within = lax.broadcasted_iota(jnp.int32, (1, TILE), 1)
    parts = [jnp.where(within < fill_ref[tile], 1.0, 0.0) for tile in range(rows // TILE)]
    return jnp.concatenate(parts, axis=1) if len(parts) > 1 else parts[0]


def spread(slots):
    return [0] + list(range(slots - 1, 0, -1))


def pack_kv_kernel(heads, rows, dim, a_of, fill_ref, kv_ref, *refs):
    outs, (held,) = refs[:heads], refs[heads:]
    live = live_column(fill_ref, rows)
    lane = lax.broadcasted_iota(jnp.int32, (rows, 2 * dim), 1)
    mark = jnp.where(lane == 0, DEAD * (1.0 - live), 0.0)
    held[...] = kv_ref[...].astype(F32)
    me = a_of()
    for slot, mask in enumerate(spread(heads)):
        outs[slot][...] = (held[pl.ds(me ^ mask, rows, stride=heads), :] * live + mark).astype(BF16)


def pack_qg_kernel(heads, rows, dim, a_of, fill_ref, q_ref, w_ref, go_ref, *refs):
    outs, (held,) = refs[:heads], refs[heads:]
    grads = dot_nt(w_ref[...].reshape(heads * dim, go_ref.shape[1]), go_ref[...])
    grads = (grads * live_row(fill_ref, rows)).astype(BF16)
    for head in range(heads):
        held[head, 0:dim, :] = (q_ref[head].astype(F32) * dim**-0.5).astype(BF16)
        held[head, dim:, :] = grads[head * dim : (head + 1) * dim, :]
    me = a_of()
    for slot, mask in enumerate(spread(heads)):
        outs[slot][...] = held[me ^ mask]


def join_kernel(pieces, *refs):
    out_ref = refs[-1]
    rows = refs[0].shape[0]
    for index in range(pieces):
        out_ref[index * rows : (index + 1) * rows, :] = refs[index][...]


def join_q_kernel(slots, rows, dim, *refs):
    pieces, (qa_ref, q_ref, g_ref, norm_ref) = refs[:slots], refs[slots:]
    wide = 2 * dim
    row = lax.broadcasted_iota(jnp.int32, (dim, slots * rows), 0)
    qa_ref[wide : wide + dim, :] = jnp.zeros((dim, slots * rows), BF16)
    qa_ref[wide + dim :, :] = jnp.where(row == 0, 1.0, 0.0).astype(BF16)
    for slot in range(slots):
        here = slice(slot * rows, (slot + 1) * rows)
        queries = pieces[slot][0:dim, :]
        q_ref[:, here] = queries
        g_ref[:, here] = pieces[slot][dim:, :]
        scaled = queries.astype(F32) * LOG2_E
        high = scaled.astype(BF16)
        qa_ref[0:dim, here] = high
        qa_ref[dim:wide, here] = (scaled - high.astype(F32)).astype(BF16)
        norm_ref[:, here] = jnp.sum(scaled * scaled, axis=0, keepdims=True)


def score_kernel(slots, rows, dim, step, pair_ref, qa_ref, q_norm_ref, *refs):
    exp_ref, peak_ref, total_ref, v_ref, kt_ref, wide_ref, vt_ref, score_ref = refs[-8:]
    wide = 2 * dim
    keys = pair_ref.shape[0]
    full = pair_ref[...].astype(F32)
    turned = full.T
    norm = jnp.sum(turned[:dim, :] * turned[:dim, :], axis=0, keepdims=True)
    norm = jnp.where(turned[0:1, :] >= DEAD, 0.0, norm)
    small = jnp.max(norm) * jnp.max(q_norm_ref[...]) <= SAFE * SAFE
    lane = lax.broadcasted_iota(jnp.int32, (keys, wide), 1)
    bias = jnp.where(full[:, 0:1] >= DEAD, BIAS, 0.0)
    extra = jnp.where(lane == dim, bias, jnp.where(lane <= dim + 2, 1.0, 0.0))
    rolled = pltpu.roll(full, dim, 1)
    values = jnp.where(lane < dim, rolled, extra).astype(BF16)
    wide_ref[:, 0:wide] = jnp.where(lane < dim, full, rolled).astype(BF16)
    wide_ref[:, wide:] = values
    v_ref[...] = values
    kt_ref[...] = turned[:dim, :].astype(BF16)
    vt_ref[0:dim, :] = turned[dim:, :].astype(BF16)
    vt_ref[dim:, :] = jnp.ones((16, keys), BF16)

    @pl.when(small)
    def _():
        peak_ref[...] = jnp.zeros_like(peak_ref)
        ahead = dot(wide_ref[...], qa_ref[:, 0:rows])
        for slot in range(slots):
            here = slice(slot * rows, (slot + 1) * rows)
            scores = ahead
            if slot + 1 < slots:
                ahead = dot(wide_ref[...], qa_ref[:, (slot + 1) * rows : (slot + 2) * rows])
            exps = jnp.exp2(scores).astype(BF16)
            exp_ref[:, here] = exps
            total_ref[:, here] = dot(vt_ref[...], exps)

    @pl.when(jnp.logical_not(small))
    def _():
        for slot in range(slots):
            here = slice(slot * rows, (slot + 1) * rows)
            top = jnp.full((8, rows), BIAS, F32)
            for start in range(0, keys, step):
                part = slice(start, start + step)
                scores = dot(wide_ref[part, :], qa_ref[:, here])
                score_ref[part, :] = scores
                top = jnp.maximum(top, jnp.max(scores.reshape(step // 8, 8, rows), axis=0))
            peak = jnp.max(top, axis=0, keepdims=True)
            peak_ref[:, here] = peak
            total = jnp.zeros((dim + 16, rows), F32)
            for start in range(0, keys, step):
                part = slice(start, start + step)
                exps = jnp.exp2(score_ref[part, :] - peak).astype(BF16)
                exp_ref[part, here] = exps
                total = total + dot(vt_ref[:, part], exps)
            total_ref[:, here] = total


def combine_kernel(slots, columns, rows, dim, *refs):
    peaks, totals, (g_ref,), outs = refs[:columns], refs[columns : 2 * columns], refs[2 * columns : 2 * columns + 1], refs[2 * columns + 1 :]
    att_out, factors_out, inner_ref = outs[:slots], outs[slots : slots + columns], outs[-1]
    peak = functools.reduce(jnp.maximum, [ref[...] for ref in peaks])
    factors = [jnp.exp2(ref[...] - peak) for ref in peaks]
    total = sum(factor * ref[...] for factor, ref in zip(factors, totals))
    inverse = 1.0 / total[dim : dim + 1, :]
    attended = (total[0:dim, :] * inverse).astype(BF16)
    for slot in range(slots):
        att_out[slot][...] = attended[:, slot * rows : (slot + 1) * rows]
    for factor, ref in zip(factors, factors_out):
        ref[...] = factor * inverse
    inner_ref[...] = jnp.sum(g_ref[...].astype(F32) * attended.astype(F32), axis=0, keepdims=True)


def back_kernel(slots, rows, dim, first, exp_ref, v_ref, kt_ref, q_ref, g_ref, factor_ref, inner_ref, *refs):
    dkv_ref, dq_ref, ga_ref = refs[-3:]
    block = g_ref.shape[1]
    factor = factor_ref[...]
    inner = inner_ref[...] * factor
    high = inner.astype(BF16).astype(F32)
    row = lax.broadcasted_iota(jnp.int32, (dim, block), 0)
    ga_ref[0:dim, :] = (g_ref[...].astype(F32) * factor).astype(BF16)
    ga_ref[dim:, :] = jnp.where(row == 1, -high, jnp.where(row == 2, high - inner, 0.0)).astype(BF16)
    grad_k = grad_v = None
    ahead = dot(v_ref[...], ga_ref[:, 0:rows])
    for slot in range(slots):
        here = slice(slot * rows, (slot + 1) * rows)
        products = ahead
        if slot + 1 < slots:
            ahead = dot(v_ref[...], ga_ref[:, (slot + 1) * rows : (slot + 2) * rows])
        exps = exp_ref[:, here]
        grads = exps * products.astype(BF16)
        term_v = dot_nt(ga_ref[0:dim, here], exps)
        term_k = dot_nt(q_ref[:, here], grads)
        grad_v = term_v if grad_v is None else grad_v + term_v
        grad_k = term_k if grad_k is None else grad_k + term_k
        term = dot(kt_ref[...], grads)
        dq_ref[:, here] = term if first else refs[0][:, here] + term
    dkv_ref[dim:, :] = grad_v.astype(BF16)
    dkv_ref[0:dim, :] = grad_k.astype(BF16)


def project_kernel(slots, rows, a_of, b_of, halves, fill_ref, go_ref, w_ref, *refs):
    att, refs = refs[:slots], refs[slots + 1 :]
    terms_ref, held = refs[0], refs[-1]
    me = a_of()
    dim = held.shape[1]
    stacked = jnp.concatenate([ref[...].astype(F32) for ref in att], axis=0) * live_row(fill_ref, rows)
    grads = dot(stacked.astype(BF16), go_ref[...]).astype(BF16)
    for slot, mask in enumerate(spread(slots)):
        held[me ^ mask] = grads[slot * dim : (slot + 1) * dim, :]
    weights = jnp.concatenate([w_ref[me ^ mask] for mask in spread(slots)], axis=0)
    terms_ref[...] = dot(stacked.T.astype(BF16), weights).astype(BF16)
    if not halves:
        refs[1][...] = held[...]
        return
    me = b_of()
    kept_ref, sent_ref = refs[1], refs[2]
    for pair in range(slots // 2):
        kept_ref[pair] = held[me ^ (2 * pair)]
        sent_ref[pair] = held[me ^ (2 * pair) ^ 1]


def add_pairs_kernel(kept_ref, came_ref, _, first_ref, second_ref):
    for index, out_ref in enumerate((first_ref, second_ref)):
        out_ref[...] = (kept_ref[index].astype(F32) + came_ref[index].astype(F32)).astype(BF16)


def add_pieces_kernel(slots, rows, dim, kept_ref, came_ref, dq_ref, *outs):
    wide = 2 * dim
    for slot in range(slots):
        here = slice(slot * rows, (slot + 1) * rows)
        outs[slot][0:wide, :] = (kept_ref[:, here].astype(F32) + came_ref[:, here].astype(F32)).astype(BF16)
        outs[slot][wide:, :] = (dq_ref[:, here] * dim**-0.5).astype(BF16)


def add_kernel(a_ref, b_ref, *refs):
    refs[-1][...] = (a_ref[...].astype(F32) + b_ref[...].astype(F32)).astype(refs[-1].dtype)


def unpack_kernel(slots, rows, dim, a_of, *refs):
    pieces, (a_ref, b_ref, _, kv_out, q_out, sum_out) = refs[:slots], refs[slots:]
    sum_out[...] = (a_ref[...].astype(F32) + b_ref[...].astype(F32)).astype(BF16)
    wide = 2 * dim
    me = a_of()
    for slot, mask in enumerate(spread(slots)):
        kv_out[pl.ds(me ^ mask, rows, stride=slots), :] = pieces[slot][0:wide, :].astype(F32).T
        q_out[me ^ mask] = pieces[slot][wide:, :].astype(F32)


def token_kernel(*refs):
    refs[-1][...] = jnp.zeros_like(refs[-1])


def place_kernel(columns, b_of, *refs):
    parts, (grad_out,) = refs[:columns], refs[columns:]
    me = b_of()
    for column in range(columns):
        grad_out[me ^ column] = parts[column][...].astype(F32)


def shards(seq, mp, queries, key_value, tile_fill, out_weight, grad_output):
    rows, heads, dim = queries.shape
    width = grad_output.shape[1]
    slots = heads
    columns = seq // slots
    assert slots * columns == seq and columns & (columns - 1) == 0 and slots & (slots - 1) == 0
    a_of = lambda: lax.axis_index("seq") // columns
    b_of = lambda: lax.axis_index("seq") % columns

    def swap(array, mask, axis="seq", size=seq):
        return lax.ppermute(array, axis, [(i, i ^ mask) for i in range(size)])

    def exchange(pieces):
        return [pieces[0]] + [swap(piece, mask * columns) for piece, mask in zip(pieces[1:], spread(slots)[1:])]

    block, wide = slots * rows, 2 * dim
    kv_mine = exchange(call(
        functools.partial(pack_kv_kernel, heads, rows, dim, a_of),
        [((rows, wide), BF16)] * slots, [pltpu.VMEM((rows * heads, wide), F32)],
        n_in=2, smem_first=True, micros=1.5, limit=56,
    )(tile_fill, key_value.reshape(rows * heads, wide)))
    qg_send = call(
        functools.partial(pack_qg_kernel, heads, rows, dim, a_of),
        [((wide, rows), BF16)] * slots, [pltpu.VMEM((heads, wide, rows), BF16)],
        n_in=4, smem_first=True, micros=1,
    )(tile_fill, jnp.transpose(queries, (1, 2, 0)), out_weight, grad_output)
    qg_mine = exchange(qg_send)
    own = call(
        functools.partial(join_kernel, slots), [((block, wide), BF16)], n_in=slots, after=1,
    )(*kv_mine, qg_send[0])[0]

    qa, q_all, grads, q_norm = call(
        functools.partial(join_q_kernel, slots, rows, dim),
        [((2 * wide, block), BF16), ((dim, block), BF16), ((dim, block), BF16), ((1, block), F32)], n_in=slots,
    )(*qg_mine)
    step = min(block, 512)
    scored, blocks = {}, {0: own}
    bit = columns // 2
    while bit:
        for r in sorted(blocks):
            blocks[r ^ bit] = swap(blocks[r], bit)
        bit //= 2
    for r in range(columns):
        if r == 2 and columns == 4:
            blocks[2] = call(functools.partial(join_kernel, 1), [((block, wide), BF16)], after=1)(
                blocks[2], scored[1][1])[0]
            blocks[3] = swap(blocks[2], 1)
        scored[r] = call(
            functools.partial(score_kernel, slots, rows, dim, step),
            [((block, block), BF16), ((1, block), F32), ((dim + 16, block), F32), ((block, wide), BF16), ((dim, block), BF16)],
            [pltpu.VMEM((block, 2 * wide), BF16), pltpu.VMEM((dim + 16, block), BF16), pltpu.VMEM((block, rows), F32)],
            n_in=3, after=min(r, 1), micros=5,
        )(blocks[r], qa, q_norm, *([scored[r - 1][1]] if r else []))
    combined = call(
        functools.partial(combine_kernel, slots, columns, rows, dim),
        [((dim, rows), BF16)] * slots + [((1, block), F32)] * (columns + 1), n_in=2 * columns + 1,
    )(*[scored[r][1] for r in range(columns)], *[scored[r][2] for r in range(columns)], grads)
    att_mine, factors, inner = exchange(combined[:slots]), combined[slots:-1], combined[-1]

    halves = columns == heads == 4
    order = sorted(range(columns), reverse=True)
    add = call(add_kernel, [((dim, width), BF16)], n_in=2, after=1)
    add_halves = call(add_kernel, [((wide, block), BF16)], n_in=2)
    z_masks = [columns << level for level in range(slots.bit_length() - 1)]
    dkv, dq, kept, summed, later = {}, None, None, {}, []
    for at, r in enumerate(order):
        if at and not halves and at == columns - 1 or halves and at == 1:
            terms, *weight_terms = call(
                functools.partial(project_kernel, slots, rows, a_of, b_of, halves),
                [((rows, width), BF16)] + ([((2, dim, width), BF16)] * 2 if halves else [((heads, dim, width), BF16)]),
                [pltpu.VMEM((heads, dim, width), BF16)],
                n_in=3 + slots, smem_first=True, after=1, micros=0.7,
            )(tile_fill, grad_output, out_weight, *att_mine, dkv[order[at - 1]])
            later, bit = [terms], 1
            while bit < mp // 2:
                terms = call(add_kernel, [((rows, width), BF16)], n_in=2)(terms, swap(terms, bit, "mp", mp))[0]
                bit *= 2
            terms_came = swap(terms, bit, "mp", mp)
            if halves:
                kept, sent = call(add_pairs_kernel, [((dim, width), BF16)] * 2, n_in=2, after=1)(
                    weight_terms[0], swap(weight_terms[1], 1), weight_terms[0])
                later = [kept]
        if at == 2 and halves:
            kept = add(kept, swap(sent, 2), dkv[order[at - 1]])[0]
            later = [kept]
        if at == 3 and halves:
            kept = add(kept, swap(kept, z_masks[0]), dkv[order[at - 1]])[0]
            later = [kept, summed[2], terms_came]
        operands = [scored[r][0], *scored[r][3:], q_all, grads, factors[r], inner] + ([] if dq is None else [dq])
        dkv[r], dq = call(
            functools.partial(back_kernel, slots, rows, dim, dq is None),
            [((wide, block), BF16), ((dim, block), F32)], [pltpu.VMEM((wide, block), BF16)],
            n_in=len(operands), after=len(later), micros=2,
        )(*operands, *later)
        later = []
        if columns == 4 and r == 2:
            summed[2] = swap(add_halves(dkv[2], swap(dkv[3], 1))[0], 2)

    if columns == 4:
        halved = add_halves(dkv[0], swap(dkv[1], 1))[0], summed[2]
    else:
        bit = 1
        while 2 * bit < columns:
            dkv = {r: add_halves(dkv[r], swap(dkv[r ^ bit], bit))[0] for r in order if r in dkv and not r & bit}
            bit *= 2
        halved = dkv[0], swap(dkv[bit], bit)
    pieces = call(
        functools.partial(add_pieces_kernel, slots, rows, dim), [((wide + dim, rows), BF16)] * slots, n_in=3,
    )(*halved, dq)
    returned = exchange(pieces)

    arrived = call(token_kernel, [((8, 128), F32)], n_in=0, after=slots)(*returned)[0]
    if halves:
        for mask in z_masks[1:]:
            kept = add(kept, swap(kept, mask), pieces[0])[0]
        across = call(functools.partial(join_kernel, 1), [((dim, width), BF16)], after=1)(swap(kept, 2), arrived)[0]
        weight_grad = call(
            functools.partial(place_kernel, columns, b_of), [((heads, dim, width), F32)], n_in=columns, micros=0.5,
        )(kept, swap(kept, 1), across, swap(across, 1))[0]
        arrived = across
    else:
        weight_grad = lax.psum(weight_terms[0].astype(F32), "seq")
    key_value_grad, query_grad, attention_out = call(
        functools.partial(unpack_kernel, slots, rows, dim, a_of),
        [((rows * heads, wide), F32), ((heads, dim, rows), F32), ((rows, width), BF16)],
        n_in=slots + 2, after=1, micros=5,
    )(*returned, terms, terms_came, arrived)
    return attention_out, jnp.transpose(query_grad, (2, 0, 1)), key_value_grad.reshape(rows, heads, wide), weight_grad


def solution(mesh):
    return jax.shard_map(
        functools.partial(shards, mesh.shape["seq"], mesh.shape["mp"]),
        mesh=mesh,
        in_specs=(
            P("seq", "mp", None),
            P("seq", "mp", None),
            P("seq"),
            P("mp", None, None),
            P("seq", None),
        ),
        out_specs=(P("seq", None), P("seq", "mp", None), P("seq", "mp", None), P("mp", None, None)),
        check_vma=False,
    )
```

```python
import functools

import jax
import jax.numpy as jnp
from jax import lax
from jax.experimental import pallas as pl
from jax.experimental.pallas import tpu as pltpu
from jax.sharding import PartitionSpec as P

TILE = 128
DEAD = 1024.0
BIAS = -1e30
LOG2_E = 1.4426950408889634
SAFE = 64.0
F32 = jnp.float32
BF16 = jnp.bfloat16
VMEM = pl.BlockSpec(memory_space=pltpu.VMEM)
SMEM = pl.BlockSpec(memory_space=pltpu.SMEM)
MIB = 1024 * 1024


def dot(a, b):
    return lax.dot_general(a, b, (((1,), (0,)), ((), ())), preferred_element_type=F32)


def dot_nt(a, b):
    return lax.dot_general(a, b, (((1,), (1,)), ((), ())), preferred_element_type=F32)


def call(kernel, outs, scratch=(), n_in=1, smem_first=False, after=0, micros=0.01, limit=16):
    specs = ([SMEM if smem_first else VMEM] + [VMEM] * (n_in - 1))[:n_in] + [pl.BlockSpec(memory_space=pl.ANY)] * after
    return pl.pallas_call(
        kernel,
        out_shape=[jax.ShapeDtypeStruct(shape, kind) for shape, kind in outs],
        in_specs=specs,
        out_specs=[VMEM] * len(outs),
        scratch_shapes=list(scratch),
        compiler_params=pltpu.CompilerParams(vmem_limit_bytes=limit * MIB),
        cost_estimate=pl.CostEstimate(flops=int(micros * 1.15e9), bytes_accessed=0, transcendentals=0),
    )


def live_column(fill_ref, rows):
    parts = []
    within = lax.broadcasted_iota(jnp.int32, (TILE, 1), 0)
    for tile in range(rows // TILE):
        parts.append(jnp.where(within < fill_ref[tile], 1.0, 0.0))
    return jnp.concatenate(parts, axis=0) if len(parts) > 1 else parts[0]


def live_row(fill_ref, rows):
    within = lax.broadcasted_iota(jnp.int32, (1, TILE), 1)
    parts = [jnp.where(within < fill_ref[tile], 1.0, 0.0) for tile in range(rows // TILE)]
    return jnp.concatenate(parts, axis=1) if len(parts) > 1 else parts[0]


def spread(slots):
    return [0] + list(range(slots - 1, 0, -1))


def pack_kv_kernel(heads, rows, dim, a_of, fill_ref, kv_ref, *refs):
    outs, (held,) = refs[:heads], refs[heads:]
    live = live_column(fill_ref, rows)
    lane = lax.broadcasted_iota(jnp.int32, (rows, 2 * dim), 1)
    mark = jnp.where(lane == 0, DEAD * (1.0 - live), 0.0)
    held[...] = kv_ref[...].astype(F32)
    me = a_of()
    for slot, mask in enumerate(spread(heads)):
        outs[slot][...] = (held[pl.ds(me ^ mask, rows, stride=heads), :] * live + mark).astype(BF16)


def pack_qg_kernel(heads, rows, dim, a_of, fill_ref, q_ref, w_ref, go_ref, *refs):
    outs, (held,) = refs[:heads], refs[heads:]
    grads = dot_nt(w_ref[...].reshape(heads * dim, go_ref.shape[1]), go_ref[...])
    grads = (grads * live_row(fill_ref, rows)).astype(BF16)
    for head in range(heads):
        held[head, 0:dim, :] = (q_ref[head].astype(F32) * dim**-0.5).astype(BF16)
        held[head, dim:, :] = grads[head * dim : (head + 1) * dim, :]
    me = a_of()
    for slot, mask in enumerate(spread(heads)):
        outs[slot][...] = held[me ^ mask]


def join_kernel(pieces, *refs):
    out_ref = refs[-1]
    rows = refs[0].shape[0]
    for index in range(pieces):
        out_ref[index * rows : (index + 1) * rows, :] = refs[index][...]


def join_q_kernel(slots, rows, dim, *refs):
    pieces, (qa_ref, q_ref, g_ref, norm_ref) = refs[:slots], refs[slots:]
    wide = 2 * dim
    row = lax.broadcasted_iota(jnp.int32, (dim, slots * rows), 0)
    qa_ref[wide : wide + dim, :] = jnp.zeros((dim, slots * rows), BF16)
    qa_ref[wide + dim :, :] = jnp.where(row == 0, 1.0, 0.0).astype(BF16)
    for slot in range(slots):
        here = slice(slot * rows, (slot + 1) * rows)
        queries = pieces[slot][0:dim, :]
        q_ref[:, here] = queries
        g_ref[:, here] = pieces[slot][dim:, :]
        scaled = queries.astype(F32) * LOG2_E
        high = scaled.astype(BF16)
        qa_ref[0:dim, here] = high
        qa_ref[dim:wide, here] = (scaled - high.astype(F32)).astype(BF16)
        norm_ref[:, here] = jnp.sum(scaled * scaled, axis=0, keepdims=True)


def score_kernel(slots, rows, dim, step, pair_ref, qa_ref, q_norm_ref, *refs):
    exp_ref, peak_ref, total_ref, v_ref, kt_ref, wide_ref, vt_ref, score_ref = refs[-8:]
    wide = 2 * dim
    keys = pair_ref.shape[0]
    full = pair_ref[...].astype(F32)
    turned = full.T
    norm = jnp.sum(turned[:dim, :] * turned[:dim, :], axis=0, keepdims=True)
    norm = jnp.where(turned[0:1, :] >= DEAD, 0.0, norm)
    small = jnp.max(norm) * jnp.max(q_norm_ref[...]) <= SAFE * SAFE
    lane = lax.broadcasted_iota(jnp.int32, (keys, wide), 1)
    bias = jnp.where(full[:, 0:1] >= DEAD, BIAS, 0.0)
    extra = jnp.where(lane == dim, bias, jnp.where(lane <= dim + 2, 1.0, 0.0))
    rolled = pltpu.roll(full, dim, 1)
    values = jnp.where(lane < dim, rolled, extra).astype(BF16)
    wide_ref[:, 0:wide] = jnp.where(lane < dim, full, rolled).astype(BF16)
    wide_ref[:, wide:] = values
    v_ref[...] = values
    kt_ref[...] = turned[:dim, :].astype(BF16)
    vt_ref[0:dim, :] = turned[dim:, :].astype(BF16)
    vt_ref[dim:, :] = jnp.ones((16, keys), BF16)

    @pl.when(small)
    def _():
        peak_ref[...] = jnp.zeros_like(peak_ref)
        ahead = dot(wide_ref[...], qa_ref[:, 0:rows])
        for slot in range(slots):
            here = slice(slot * rows, (slot + 1) * rows)
            scores = ahead
            if slot + 1 < slots:
                ahead = dot(wide_ref[...], qa_ref[:, (slot + 1) * rows : (slot + 2) * rows])
            exps = jnp.exp2(scores).astype(BF16)
            exp_ref[:, here] = exps
            total_ref[:, here] = dot(vt_ref[...], exps)

    @pl.when(jnp.logical_not(small))
    def _():
        for slot in range(slots):
            here = slice(slot * rows, (slot + 1) * rows)
            top = jnp.full((8, rows), BIAS, F32)
            for start in range(0, keys, step):
                part = slice(start, start + step)
                scores = dot(wide_ref[part, :], qa_ref[:, here])
                score_ref[part, :] = scores
                top = jnp.maximum(top, jnp.max(scores.reshape(step // 8, 8, rows), axis=0))
            peak = jnp.max(top, axis=0, keepdims=True)
            peak_ref[:, here] = peak
            total = jnp.zeros((dim + 16, rows), F32)
            for start in range(0, keys, step):
                part = slice(start, start + step)
                exps = jnp.exp2(score_ref[part, :] - peak).astype(BF16)
                exp_ref[part, here] = exps
                total = total + dot(vt_ref[:, part], exps)
            total_ref[:, here] = total


def combine_kernel(slots, columns, rows, dim, *refs):
    peaks, totals, (g_ref,), outs = refs[:columns], refs[columns : 2 * columns], refs[2 * columns : 2 * columns + 1], refs[2 * columns + 1 :]
    att_out, factors_out, inner_ref = outs[:slots], outs[slots : slots + columns], outs[-1]
    peak = functools.reduce(jnp.maximum, [ref[...] for ref in peaks])
    factors = [jnp.exp2(ref[...] - peak) for ref in peaks]
    total = sum(factor * ref[...] for factor, ref in zip(factors, totals))
    inverse = 1.0 / total[dim : dim + 1, :]
    attended = (total[0:dim, :] * inverse).astype(BF16)
    for slot in range(slots):
        att_out[slot][...] = attended[:, slot * rows : (slot + 1) * rows]
    for factor, ref in zip(factors, factors_out):
        ref[...] = factor * inverse
    inner_ref[...] = jnp.sum(g_ref[...].astype(F32) * attended.astype(F32), axis=0, keepdims=True)


def back_kernel(slots, rows, dim, first, exp_ref, v_ref, kt_ref, q_ref, g_ref, factor_ref, inner_ref, *refs):
    dkv_ref, dq_ref, ga_ref = refs[-3:]
    block = g_ref.shape[1]
    factor = factor_ref[...]
    inner = inner_ref[...] * factor
    high = inner.astype(BF16).astype(F32)
    row = lax.broadcasted_iota(jnp.int32, (dim, block), 0)
    ga_ref[0:dim, :] = (g_ref[...].astype(F32) * factor).astype(BF16)
    ga_ref[dim:, :] = jnp.where(row == 1, -high, jnp.where(row == 2, high - inner, 0.0)).astype(BF16)
    grad_k = grad_v = None
    ahead = dot(v_ref[...], ga_ref[:, 0:rows])
    for slot in range(slots):
        here = slice(slot * rows, (slot + 1) * rows)
        products = ahead
        if slot + 1 < slots:
            ahead = dot(v_ref[...], ga_ref[:, (slot + 1) * rows : (slot + 2) * rows])
        exps = exp_ref[:, here]
        grads = exps * products.astype(BF16)
        term_v = dot_nt(ga_ref[0:dim, here], exps)
        term_k = dot_nt(q_ref[:, here], grads)
        grad_v = term_v if grad_v is None else grad_v + term_v
        grad_k = term_k if grad_k is None else grad_k + term_k
        term = dot(kt_ref[...], grads)
        dq_ref[:, here] = term if first else refs[0][:, here] + term
    dkv_ref[dim:, :] = grad_v.astype(BF16)
    dkv_ref[0:dim, :] = grad_k.astype(BF16)


def project_kernel(slots, rows, a_of, b_of, halves, fill_ref, go_ref, w_ref, *refs):
    att, refs = refs[:slots], refs[slots + 1 :]
    terms_ref, held = refs[0], refs[-1]
    me = a_of()
    dim = held.shape[1]
    stacked = jnp.concatenate([ref[...].astype(F32) for ref in att], axis=0) * live_row(fill_ref, rows)
    grads = dot(stacked.astype(BF16), go_ref[...]).astype(BF16)
    for slot, mask in enumerate(spread(slots)):
        held[me ^ mask] = grads[slot * dim : (slot + 1) * dim, :]
    weights = jnp.concatenate([w_ref[me ^ mask] for mask in spread(slots)], axis=0)
    terms_ref[...] = dot(stacked.T.astype(BF16), weights).astype(BF16)
    if not halves:
        refs[1][...] = held[...]
        return
    me = b_of()
    kept_ref, sent_ref = refs[1], refs[2]
    for pair in range(slots // 2):
        kept_ref[pair] = held[me ^ (2 * pair)]
        sent_ref[pair] = held[me ^ (2 * pair) ^ 1]


def add_pairs_kernel(kept_ref, came_ref, _, first_ref, second_ref):
    for index, out_ref in enumerate((first_ref, second_ref)):
        out_ref[...] = (kept_ref[index].astype(F32) + came_ref[index].astype(F32)).astype(BF16)


def add_pieces_kernel(slots, rows, dim, kept_ref, came_ref, dq_ref, *outs):
    wide = 2 * dim
    for slot in range(slots):
        here = slice(slot * rows, (slot + 1) * rows)
        outs[slot][0:wide, :] = (kept_ref[:, here].astype(F32) + came_ref[:, here].astype(F32)).astype(BF16)
        outs[slot][wide:, :] = (dq_ref[:, here] * dim**-0.5).astype(BF16)


def add_kernel(a_ref, b_ref, *refs):
    refs[-1][...] = (a_ref[...].astype(F32) + b_ref[...].astype(F32)).astype(refs[-1].dtype)


def unpack_kernel(slots, rows, dim, a_of, order, *refs):
    pieces, (a_ref, b_ref, _, kv_out, q_out, sum_out) = refs[:slots], refs[slots:]
    sum_out[...] = (a_ref[...].astype(F32) + b_ref[...].astype(F32)).astype(BF16)
    wide = 2 * dim
    me = a_of()
    for slot, mask in enumerate(order):
        kv_out[pl.ds(me ^ mask, rows, stride=slots), :] = pieces[slot][0:wide, :].astype(F32).T
        q_out[me ^ mask] = pieces[slot][wide:, :].astype(F32)


def token_kernel(*refs):
    refs[-1][...] = jnp.zeros_like(refs[-1])


def place_kernel(columns, b_of, *refs):
    parts, (grad_out,) = refs[:columns], refs[columns:]
    me = b_of()
    for column in range(columns):
        grad_out[me ^ column] = parts[column][...].astype(F32)


def shards(seq, mp, queries, key_value, tile_fill, out_weight, grad_output):
    rows, heads, dim = queries.shape
    width = grad_output.shape[1]
    slots = heads
    columns = seq // slots
    assert slots * columns == seq and columns & (columns - 1) == 0 and slots & (slots - 1) == 0
    a_of = lambda: lax.axis_index("seq") // columns
    b_of = lambda: lax.axis_index("seq") % columns

    def swap(array, mask, axis="seq", size=seq):
        return lax.ppermute(array, axis, [(i, i ^ mask) for i in range(size)])

    def exchange(pieces):
        return [pieces[0]] + [swap(piece, mask * columns) for piece, mask in zip(pieces[1:], spread(slots)[1:])]

    block, wide = slots * rows, 2 * dim
    kv_mine = exchange(call(
        functools.partial(pack_kv_kernel, heads, rows, dim, a_of),
        [((rows, wide), BF16)] * slots, [pltpu.VMEM((rows * heads, wide), F32)],
        n_in=2, smem_first=True, micros=1.5, limit=56,
    )(tile_fill, key_value.reshape(rows * heads, wide)))
    qg_send = call(
        functools.partial(pack_qg_kernel, heads, rows, dim, a_of),
        [((wide, rows), BF16)] * slots, [pltpu.VMEM((heads, wide, rows), BF16)],
        n_in=4, smem_first=True, micros=1,
    )(tile_fill, jnp.transpose(queries, (1, 2, 0)), out_weight, grad_output)
    qg_mine = exchange(qg_send)
    own = call(
        functools.partial(join_kernel, slots), [((block, wide), BF16)], n_in=slots, after=1,
    )(*kv_mine, qg_send[0])[0]

    qa, q_all, grads, q_norm = call(
        functools.partial(join_q_kernel, slots, rows, dim),
        [((2 * wide, block), BF16), ((dim, block), BF16), ((dim, block), BF16), ((1, block), F32)], n_in=slots,
    )(*qg_mine)
    step = min(block, 512)
    scored, blocks = {}, {0: own}
    bit = columns // 2
    while bit:
        for r in sorted(blocks):
            blocks[r ^ bit] = swap(blocks[r], bit)
        bit //= 2
    for r in range(columns):
        if r == 2 and columns == 4:
            blocks[2] = call(functools.partial(join_kernel, 1), [((block, wide), BF16)], after=1)(
                blocks[2], scored[1][1])[0]
            blocks[3] = swap(blocks[2], 1)
        scored[r] = call(
            functools.partial(score_kernel, slots, rows, dim, step),
            [((block, block), BF16), ((1, block), F32), ((dim + 16, block), F32), ((block, wide), BF16), ((dim, block), BF16)],
            [pltpu.VMEM((block, 2 * wide), BF16), pltpu.VMEM((dim + 16, block), BF16), pltpu.VMEM((block, rows), F32)],
            n_in=3, after=min(r, 1), micros=5,
        )(blocks[r], qa, q_norm, *([scored[r - 1][1]] if r else []))
    combined = call(
        functools.partial(combine_kernel, slots, columns, rows, dim),
        [((dim, rows), BF16)] * slots + [((1, block), F32)] * (columns + 1), n_in=2 * columns + 1,
    )(*[scored[r][1] for r in range(columns)], *[scored[r][2] for r in range(columns)], grads)
    att_mine, factors, inner = exchange(combined[:slots]), combined[slots:-1], combined[-1]

    halves = columns == heads == 4
    order = sorted(range(columns), reverse=True)
    add = call(add_kernel, [((dim, width), BF16)], n_in=2, after=1)
    add_halves = call(add_kernel, [((wide, block), BF16)], n_in=2)
    z_masks = [columns << level for level in range(slots.bit_length() - 1)]
    dkv, dq, kept, summed, later = {}, None, None, {}, []
    for at, r in enumerate(order):
        if at and not halves and at == columns - 1 or halves and at == 1:
            terms, *weight_terms = call(
                functools.partial(project_kernel, slots, rows, a_of, b_of, halves),
                [((rows, width), BF16)] + ([((2, dim, width), BF16)] * 2 if halves else [((heads, dim, width), BF16)]),
                [pltpu.VMEM((heads, dim, width), BF16)],
                n_in=3 + slots, smem_first=True, after=1, micros=0.7,
            )(tile_fill, grad_output, out_weight, *att_mine, dkv[order[at - 1]])
            later, bit = [terms], 1
            while bit < mp // 2:
                terms = call(add_kernel, [((rows, width), BF16)], n_in=2)(terms, swap(terms, bit, "mp", mp))[0]
                bit *= 2
            terms_came = swap(terms, bit, "mp", mp)
            if halves:
                kept, sent = call(add_pairs_kernel, [((dim, width), BF16)] * 2, n_in=2, after=1)(
                    weight_terms[0], swap(weight_terms[1], 1), weight_terms[0])
                later = [kept]
        if at == 2 and halves:
            kept = add(kept, swap(sent, 2), dkv[order[at - 1]])[0]
            later = [kept]
        if at == 3 and halves:
            kept = add(kept, swap(kept, z_masks[0]), dkv[order[at - 1]])[0]
            later = [kept, summed[2], terms_came]
        operands = [scored[r][0], *scored[r][3:], q_all, grads, factors[r], inner] + ([] if dq is None else [dq])
        dkv[r], dq = call(
            functools.partial(back_kernel, slots, rows, dim, dq is None),
            [((wide, block), BF16), ((dim, block), F32)], [pltpu.VMEM((wide, block), BF16)],
            n_in=len(operands), after=len(later), micros=2,
        )(*operands, *later)
        later = []
        if columns == 4 and r == 2:
            summed[2] = swap(add_halves(dkv[2], swap(dkv[3], 1))[0], 2)

    if columns == 4:
        halved = add_halves(dkv[0], swap(dkv[1], 1))[0], summed[2]
    else:
        bit = 1
        while 2 * bit < columns:
            dkv = {r: add_halves(dkv[r], swap(dkv[r ^ bit], bit))[0] for r in order if r in dkv and not r & bit}
            bit *= 2
        halved = dkv[0], swap(dkv[bit], bit)
    pieces = call(
        functools.partial(add_pieces_kernel, slots, rows, dim), [((wide + dim, rows), BF16)] * slots, n_in=3,
    )(*halved, dq)
    returned = exchange(pieces)

    masks = spread(slots)
    order = [0] + sorted(masks[1:], key=lambda mask: (mask < slots // 2, mask))
    returned = [returned[masks.index(mask)] for mask in order]
    arrived = call(token_kernel, [((8, 128), F32)], n_in=0, after=slots)(*returned)[0]
    if halves:
        for mask in z_masks[1:]:
            kept = add(kept, swap(kept, mask), pieces[0])[0]
        across = call(functools.partial(join_kernel, 1), [((dim, width), BF16)], after=1)(swap(kept, 2), arrived)[0]
        weight_grad = call(
            functools.partial(place_kernel, columns, b_of), [((heads, dim, width), F32)], n_in=columns, micros=0.5,
        )(kept, swap(kept, 1), across, swap(across, 1))[0]
        arrived = across
    else:
        weight_grad = lax.psum(weight_terms[0].astype(F32), "seq")
    key_value_grad, query_grad, attention_out = call(
        functools.partial(unpack_kernel, slots, rows, dim, a_of, order),
        [((rows * heads, wide), F32), ((heads, dim, rows), F32), ((rows, width), BF16)],
        n_in=slots + 2, after=1, micros=5,
    )(*returned, terms, terms_came, arrived)
    return attention_out, jnp.transpose(query_grad, (2, 0, 1)), key_value_grad.reshape(rows, heads, wide), weight_grad


def solution(mesh):
    return jax.shard_map(
        functools.partial(shards, mesh.shape["seq"], mesh.shape["mp"]),
        mesh=mesh,
        in_specs=(
            P("seq", "mp", None),
            P("seq", "mp", None),
            P("seq"),
            P("mp", None, None),
            P("seq", None),
        ),
        out_specs=(P("seq", None), P("seq", "mp", None), P("seq", "mp", None), P("mp", None, None)),
        check_vma=False,
    )
```

```python
import functools

import jax
import jax.numpy as jnp
from jax import lax
from jax.experimental import pallas as pl
from jax.experimental.pallas import tpu as pltpu
from jax.sharding import PartitionSpec as P

TILE = 128
DEAD = 1024.0
BIAS = -1e30
LOG2_E = 1.4426950408889634
SAFE = 64.0
F32 = jnp.float32
BF16 = jnp.bfloat16
VMEM = pl.BlockSpec(memory_space=pltpu.VMEM)
SMEM = pl.BlockSpec(memory_space=pltpu.SMEM)
MIB = 1024 * 1024


def dot(a, b):
    return lax.dot_general(a, b, (((1,), (0,)), ((), ())), preferred_element_type=F32)


def dot_nt(a, b):
    return lax.dot_general(a, b, (((1,), (1,)), ((), ())), preferred_element_type=F32)


def call(kernel, outs, scratch=(), n_in=1, smem_first=False, after=0, micros=0.01, limit=16):
    specs = ([SMEM if smem_first else VMEM] + [VMEM] * (n_in - 1))[:n_in] + [pl.BlockSpec(memory_space=pl.ANY)] * after
    return pl.pallas_call(
        kernel,
        out_shape=[jax.ShapeDtypeStruct(shape, kind) for shape, kind in outs],
        in_specs=specs,
        out_specs=[VMEM] * len(outs),
        scratch_shapes=list(scratch),
        compiler_params=pltpu.CompilerParams(vmem_limit_bytes=limit * MIB),
        cost_estimate=pl.CostEstimate(flops=int(micros * 1.15e9), bytes_accessed=0, transcendentals=0),
    )


def live_column(fill_ref, rows):
    parts = []
    within = lax.broadcasted_iota(jnp.int32, (TILE, 1), 0)
    for tile in range(rows // TILE):
        parts.append(jnp.where(within < fill_ref[tile], 1.0, 0.0))
    return jnp.concatenate(parts, axis=0) if len(parts) > 1 else parts[0]


def live_row(fill_ref, rows):
    within = lax.broadcasted_iota(jnp.int32, (1, TILE), 1)
    parts = [jnp.where(within < fill_ref[tile], 1.0, 0.0) for tile in range(rows // TILE)]
    return jnp.concatenate(parts, axis=1) if len(parts) > 1 else parts[0]


def spread(slots):
    return [0] + list(range(slots - 1, 0, -1))


def pack_kv_kernel(heads, rows, dim, a_of, fill_ref, kv_ref, *refs):
    outs, (held,) = refs[:heads], refs[heads:]
    live = live_column(fill_ref, rows)
    lane = lax.broadcasted_iota(jnp.int32, (rows, 2 * dim), 1)
    mark = jnp.where(lane == 0, DEAD * (1.0 - live), 0.0)
    held[...] = kv_ref[...].astype(F32)
    me = a_of()
    for slot, mask in enumerate(spread(heads)):
        outs[slot][...] = (held[pl.ds(me ^ mask, rows, stride=heads), :] * live + mark).astype(BF16)


def pack_qg_kernel(heads, rows, dim, a_of, fill_ref, q_ref, w_ref, go_ref, *refs):
    outs, (held,) = refs[:heads], refs[heads:]
    grads = dot_nt(w_ref[...].reshape(heads * dim, go_ref.shape[1]), go_ref[...])
    grads = (grads * live_row(fill_ref, rows)).astype(BF16)
    for head in range(heads):
        held[head, 0:dim, :] = (q_ref[head].astype(F32) * dim**-0.5).astype(BF16)
        held[head, dim:, :] = grads[head * dim : (head + 1) * dim, :]
    me = a_of()
    for slot, mask in enumerate(spread(heads)):
        outs[slot][...] = held[me ^ mask]


def join_kernel(pieces, *refs):
    out_ref = refs[-1]
    rows = refs[0].shape[0]
    for index in range(pieces):
        out_ref[index * rows : (index + 1) * rows, :] = refs[index][...]


def join_q_kernel(slots, rows, dim, places, *refs):
    pieces, (qa_ref, q_ref, g_ref, norm_ref) = refs[:slots], refs[slots:]
    wide = 2 * dim
    row = lax.broadcasted_iota(jnp.int32, (dim, slots * rows), 0)
    qa_ref[wide : wide + dim, :] = jnp.zeros((dim, slots * rows), BF16)
    qa_ref[wide + dim :, :] = jnp.where(row == 0, 1.0, 0.0).astype(BF16)
    for piece, slot in zip(pieces, places):
        here = slice(slot * rows, (slot + 1) * rows)
        queries = piece[0:dim, :]
        q_ref[:, here] = queries
        g_ref[:, here] = piece[dim:, :]
        scaled = queries.astype(F32) * LOG2_E
        high = scaled.astype(BF16)
        qa_ref[0:dim, here] = high
        qa_ref[dim:wide, here] = (scaled - high.astype(F32)).astype(BF16)
        norm_ref[:, here] = jnp.sum(scaled * scaled, axis=0, keepdims=True)


def score_kernel(slots, rows, dim, step, pair_ref, qa_ref, q_norm_ref, *refs):
    exp_ref, peak_ref, total_ref, v_ref, kt_ref, wide_ref, vt_ref, score_ref = refs[-8:]
    wide = 2 * dim
    keys = pair_ref.shape[0]
    full = pair_ref[...].astype(F32)
    turned = full.T
    norm = jnp.sum(turned[:dim, :] * turned[:dim, :], axis=0, keepdims=True)
    norm = jnp.where(turned[0:1, :] >= DEAD, 0.0, norm)
    small = jnp.max(norm) * jnp.max(q_norm_ref[...]) <= SAFE * SAFE
    lane = lax.broadcasted_iota(jnp.int32, (keys, wide), 1)
    bias = jnp.where(full[:, 0:1] >= DEAD, BIAS, 0.0)
    extra = jnp.where(lane == dim, bias, jnp.where(lane <= dim + 2, 1.0, 0.0))
    rolled = pltpu.roll(full, dim, 1)
    values = jnp.where(lane < dim, rolled, extra).astype(BF16)
    wide_ref[:, 0:wide] = jnp.where(lane < dim, full, rolled).astype(BF16)
    wide_ref[:, wide:] = values
    v_ref[...] = values
    kt_ref[...] = turned[:dim, :].astype(BF16)
    vt_ref[0:dim, :] = turned[dim:, :].astype(BF16)
    vt_ref[dim:, :] = jnp.ones((16, keys), BF16)

    @pl.when(small)
    def _():
        peak_ref[...] = jnp.zeros_like(peak_ref)
        ahead = dot(wide_ref[...], qa_ref[:, 0:rows])
        for slot in range(slots):
            here = slice(slot * rows, (slot + 1) * rows)
            scores = ahead
            if slot + 1 < slots:
                ahead = dot(wide_ref[...], qa_ref[:, (slot + 1) * rows : (slot + 2) * rows])
            exps = jnp.exp2(scores).astype(BF16)
            exp_ref[:, here] = exps
            total_ref[:, here] = dot(vt_ref[...], exps)

    @pl.when(jnp.logical_not(small))
    def _():
        for slot in range(slots):
            here = slice(slot * rows, (slot + 1) * rows)
            top = jnp.full((8, rows), BIAS, F32)
            for start in range(0, keys, step):
                part = slice(start, start + step)
                scores = dot(wide_ref[part, :], qa_ref[:, here])
                score_ref[part, :] = scores
                top = jnp.maximum(top, jnp.max(scores.reshape(step // 8, 8, rows), axis=0))
            peak = jnp.max(top, axis=0, keepdims=True)
            peak_ref[:, here] = peak
            total = jnp.zeros((dim + 16, rows), F32)
            for start in range(0, keys, step):
                part = slice(start, start + step)
                exps = jnp.exp2(score_ref[part, :] - peak).astype(BF16)
                exp_ref[part, here] = exps
                total = total + dot(vt_ref[:, part], exps)
            total_ref[:, here] = total


def combine_kernel(slots, columns, rows, dim, *refs):
    peaks, totals, (g_ref,), outs = refs[:columns], refs[columns : 2 * columns], refs[2 * columns : 2 * columns + 1], refs[2 * columns + 1 :]
    att_out, factors_out, inner_ref = outs[:slots], outs[slots : slots + columns], outs[-1]
    peak = functools.reduce(jnp.maximum, [ref[...] for ref in peaks])
    factors = [jnp.exp2(ref[...] - peak) for ref in peaks]
    total = sum(factor * ref[...] for factor, ref in zip(factors, totals))
    inverse = 1.0 / total[dim : dim + 1, :]
    attended = (total[0:dim, :] * inverse).astype(BF16)
    for slot in range(slots):
        att_out[slot][...] = attended[:, slot * rows : (slot + 1) * rows]
    for factor, ref in zip(factors, factors_out):
        ref[...] = factor * inverse
    inner_ref[...] = jnp.sum(g_ref[...].astype(F32) * attended.astype(F32), axis=0, keepdims=True)


def back_kernel(slots, rows, dim, first, exp_ref, v_ref, kt_ref, q_ref, g_ref, factor_ref, inner_ref, *refs):
    dkv_ref, dq_ref, ga_ref = refs[-3:]
    block = g_ref.shape[1]
    factor = factor_ref[...]
    inner = inner_ref[...] * factor
    high = inner.astype(BF16).astype(F32)
    row = lax.broadcasted_iota(jnp.int32, (dim, block), 0)
    ga_ref[0:dim, :] = (g_ref[...].astype(F32) * factor).astype(BF16)
    ga_ref[dim:, :] = jnp.where(row == 1, -high, jnp.where(row == 2, high - inner, 0.0)).astype(BF16)
    grad_k = grad_v = None
    ahead = dot(v_ref[...], ga_ref[:, 0:rows])
    for slot in range(slots):
        here = slice(slot * rows, (slot + 1) * rows)
        products = ahead
        if slot + 1 < slots:
            ahead = dot(v_ref[...], ga_ref[:, (slot + 1) * rows : (slot + 2) * rows])
        exps = exp_ref[:, here]
        grads = exps * products.astype(BF16)
        term_v = dot_nt(ga_ref[0:dim, here], exps)
        term_k = dot_nt(q_ref[:, here], grads)
        grad_v = term_v if grad_v is None else grad_v + term_v
        grad_k = term_k if grad_k is None else grad_k + term_k
        term = dot(kt_ref[...], grads)
        dq_ref[:, here] = term if first else refs[0][:, here] + term
    dkv_ref[dim:, :] = grad_v.astype(BF16)
    dkv_ref[0:dim, :] = grad_k.astype(BF16)


def project_kernel(slots, rows, a_of, b_of, halves, fill_ref, go_ref, w_ref, *refs):
    att, refs = refs[:slots], refs[slots + 1 :]
    terms_ref, held = refs[0], refs[-1]
    me = a_of()
    dim = held.shape[1]
    stacked = jnp.concatenate([ref[...].astype(F32) for ref in att], axis=0) * live_row(fill_ref, rows)
    grads = dot(stacked.astype(BF16), go_ref[...]).astype(BF16)
    for slot, mask in enumerate(spread(slots)):
        held[me ^ mask] = grads[slot * dim : (slot + 1) * dim, :]
    weights = jnp.concatenate([w_ref[me ^ mask] for mask in spread(slots)], axis=0)
    terms_ref[...] = dot(stacked.T.astype(BF16), weights).astype(BF16)
    if not halves:
        refs[1][...] = held[...]
        return
    me = b_of()
    kept_ref, sent_ref = refs[1], refs[2]
    for pair in range(slots // 2):
        kept_ref[pair] = held[me ^ (2 * pair)]
        sent_ref[pair] = held[me ^ (2 * pair) ^ 1]


def add_pairs_kernel(kept_ref, came_ref, _, first_ref, second_ref):
    for index, out_ref in enumerate((first_ref, second_ref)):
        out_ref[...] = (kept_ref[index].astype(F32) + came_ref[index].astype(F32)).astype(BF16)


def add_pieces_kernel(slots, rows, dim, kept_ref, came_ref, dq_ref, *outs):
    wide = 2 * dim
    for slot in range(slots):
        here = slice(slot * rows, (slot + 1) * rows)
        outs[slot][0:wide, :] = (kept_ref[:, here].astype(F32) + came_ref[:, here].astype(F32)).astype(BF16)
        outs[slot][wide:, :] = (dq_ref[:, here] * dim**-0.5).astype(BF16)


def add_kernel(a_ref, b_ref, *refs):
    refs[-1][...] = (a_ref[...].astype(F32) + b_ref[...].astype(F32)).astype(refs[-1].dtype)


def unpack_kernel(slots, rows, dim, a_of, order, *refs):
    pieces, (a_ref, b_ref, _, kv_out, q_out, sum_out) = refs[:slots], refs[slots:]
    sum_out[...] = (a_ref[...].astype(F32) + b_ref[...].astype(F32)).astype(BF16)
    wide = 2 * dim
    me = a_of()
    for slot, mask in enumerate(order):
        kv_out[pl.ds(me ^ mask, rows, stride=slots), :] = pieces[slot][0:wide, :].astype(F32).T
        q_out[me ^ mask] = pieces[slot][wide:, :].astype(F32)


def token_kernel(*refs):
    refs[-1][...] = jnp.zeros_like(refs[-1])


def place_kernel(columns, b_of, *refs):
    parts, (grad_out,) = refs[:columns], refs[columns:]
    me = b_of()
    for column in range(columns):
        grad_out[me ^ column] = parts[column][...].astype(F32)


def shards(seq, mp, queries, key_value, tile_fill, out_weight, grad_output):
    rows, heads, dim = queries.shape
    width = grad_output.shape[1]
    slots = heads
    columns = seq // slots
    assert slots * columns == seq and columns & (columns - 1) == 0 and slots & (slots - 1) == 0
    a_of = lambda: lax.axis_index("seq") // columns
    b_of = lambda: lax.axis_index("seq") % columns

    def swap(array, mask, axis="seq", size=seq):
        return lax.ppermute(array, axis, [(i, i ^ mask) for i in range(size)])

    def exchange(pieces):
        return [pieces[0]] + [swap(piece, mask * columns) for piece, mask in zip(pieces[1:], spread(slots)[1:])]

    block, wide = slots * rows, 2 * dim
    kv_mine = exchange(call(
        functools.partial(pack_kv_kernel, heads, rows, dim, a_of),
        [((rows, wide), BF16)] * slots, [pltpu.VMEM((rows * heads, wide), F32)],
        n_in=2, smem_first=True, micros=1.5, limit=56,
    )(tile_fill, key_value.reshape(rows * heads, wide)))
    qg_send = call(
        functools.partial(pack_qg_kernel, heads, rows, dim, a_of),
        [((wide, rows), BF16)] * slots, [pltpu.VMEM((heads, wide, rows), BF16)],
        n_in=4, smem_first=True, micros=1,
    )(tile_fill, jnp.transpose(queries, (1, 2, 0)), out_weight, grad_output)
    qg_mine = exchange(qg_send)
    own = call(
        functools.partial(join_kernel, slots), [((block, wide), BF16)], n_in=slots, after=1,
    )(*kv_mine, qg_send[0])[0]

    places = [0] + sorted(range(1, slots), key=lambda slot: (spread(slots)[slot] < slots // 2, spread(slots)[slot]))
    qa, q_all, grads, q_norm = call(
        functools.partial(join_q_kernel, slots, rows, dim, places),
        [((2 * wide, block), BF16), ((dim, block), BF16), ((dim, block), BF16), ((1, block), F32)], n_in=slots,
    )(*[qg_mine[slot] for slot in places])
    step = min(block, 512)
    scored, blocks = {}, {0: own}
    bit = columns // 2
    while bit:
        for r in sorted(blocks):
            blocks[r ^ bit] = swap(blocks[r], bit)
        bit //= 2
    for r in range(columns):
        if r == 2 and columns == 4:
            blocks[2] = call(functools.partial(join_kernel, 1), [((block, wide), BF16)], after=1)(
                blocks[2], scored[1][1])[0]
            blocks[3] = swap(blocks[2], 1)
        scored[r] = call(
            functools.partial(score_kernel, slots, rows, dim, step),
            [((block, block), BF16), ((1, block), F32), ((dim + 16, block), F32), ((block, wide), BF16), ((dim, block), BF16)],
            [pltpu.VMEM((block, 2 * wide), BF16), pltpu.VMEM((dim + 16, block), BF16), pltpu.VMEM((block, rows), F32)],
            n_in=3, after=min(r, 1), micros=5,
        )(blocks[r], qa, q_norm, *([scored[r - 1][1]] if r else []))
    combined = call(
        functools.partial(combine_kernel, slots, columns, rows, dim),
        [((dim, rows), BF16)] * slots + [((1, block), F32)] * (columns + 1), n_in=2 * columns + 1,
    )(*[scored[r][1] for r in range(columns)], *[scored[r][2] for r in range(columns)], grads)
    att_mine, factors, inner = exchange(combined[:slots]), combined[slots:-1], combined[-1]

    halves = columns == heads == 4
    order = sorted(range(columns), reverse=True)
    add = call(add_kernel, [((dim, width), BF16)], n_in=2, after=1)
    add_halves = call(add_kernel, [((wide, block), BF16)], n_in=2)
    z_masks = [columns << level for level in range(slots.bit_length() - 1)]
    dkv, dq, kept, summed, later = {}, None, None, {}, []
    for at, r in enumerate(order):
        if at and not halves and at == columns - 1 or halves and at == 1:
            terms, *weight_terms = call(
                functools.partial(project_kernel, slots, rows, a_of, b_of, halves),
                [((rows, width), BF16)] + ([((2, dim, width), BF16)] * 2 if halves else [((heads, dim, width), BF16)]),
                [pltpu.VMEM((heads, dim, width), BF16)],
                n_in=3 + slots, smem_first=True, after=1, micros=0.7,
            )(tile_fill, grad_output, out_weight, *att_mine, dkv[order[at - 1]])
            later, bit = [terms], 1
            while bit < mp // 2:
                terms = call(add_kernel, [((rows, width), BF16)], n_in=2)(terms, swap(terms, bit, "mp", mp))[0]
                bit *= 2
            terms_came = swap(terms, bit, "mp", mp)
            if halves:
                kept, sent = call(add_pairs_kernel, [((dim, width), BF16)] * 2, n_in=2, after=1)(
                    weight_terms[0], swap(weight_terms[1], 1), weight_terms[0])
                later = [kept]
        if at == 2 and halves:
            kept = add(kept, swap(sent, 2), dkv[order[at - 1]])[0]
            later = [kept]
        if at == 3 and halves:
            kept = add(kept, swap(kept, z_masks[0]), dkv[order[at - 1]])[0]
            later = [kept, summed[2], terms_came]
        operands = [scored[r][0], *scored[r][3:], q_all, grads, factors[r], inner] + ([] if dq is None else [dq])
        dkv[r], dq = call(
            functools.partial(back_kernel, slots, rows, dim, dq is None),
            [((wide, block), BF16), ((dim, block), F32)], [pltpu.VMEM((wide, block), BF16)],
            n_in=len(operands), after=len(later), micros=2,
        )(*operands, *later)
        later = []
        if columns == 4 and r == 2:
            summed[2] = swap(add_halves(dkv[2], swap(dkv[3], 1))[0], 2)

    if columns == 4:
        halved = add_halves(dkv[0], swap(dkv[1], 1))[0], summed[2]
    else:
        bit = 1
        while 2 * bit < columns:
            dkv = {r: add_halves(dkv[r], swap(dkv[r ^ bit], bit))[0] for r in order if r in dkv and not r & bit}
            bit *= 2
        halved = dkv[0], swap(dkv[bit], bit)
    pieces = call(
        functools.partial(add_pieces_kernel, slots, rows, dim), [((wide + dim, rows), BF16)] * slots, n_in=3,
    )(*halved, dq)
    returned = exchange(pieces)

    masks = spread(slots)
    order = [0] + sorted(masks[1:], key=lambda mask: (mask < slots // 2, mask))
    returned = [returned[masks.index(mask)] for mask in order]
    arrived = call(token_kernel, [((8, 128), F32)], n_in=0, after=slots)(*returned)[0]
    if halves:
        for mask in z_masks[1:]:
            kept = add(kept, swap(kept, mask), pieces[0])[0]
        across = call(functools.partial(join_kernel, 1), [((dim, width), BF16)], after=1)(swap(kept, 2), arrived)[0]
        weight_grad = call(
            functools.partial(place_kernel, columns, b_of), [((heads, dim, width), F32)], n_in=columns, micros=0.5,
        )(kept, swap(kept, 1), across, swap(across, 1))[0]
        arrived = across
    else:
        weight_grad = lax.psum(weight_terms[0].astype(F32), "seq")
    key_value_grad, query_grad, attention_out = call(
        functools.partial(unpack_kernel, slots, rows, dim, a_of, order),
        [((rows * heads, wide), F32), ((heads, dim, rows), F32), ((rows, width), BF16)],
        n_in=slots + 2, after=1, micros=5,
    )(*returned, terms, terms_came, arrived)
    return attention_out, jnp.transpose(query_grad, (2, 0, 1)), key_value_grad.reshape(rows, heads, wide), weight_grad


def solution(mesh):
    return jax.shard_map(
        functools.partial(shards, mesh.shape["seq"], mesh.shape["mp"]),
        mesh=mesh,
        in_specs=(
            P("seq", "mp", None),
            P("seq", "mp", None),
            P("seq"),
            P("mp", None, None),
            P("seq", None),
        ),
        out_specs=(P("seq", None), P("seq", "mp", None), P("seq", "mp", None), P("mp", None, None)),
        check_vma=False,
    )
```
